32 devices in a mesh: leaf: 8 (over z, y), help: 4 (over x, core).
Axes of the slice: x: 2, y: 2, z: 4, core: 2. Of those that a mesh axis runs over, the one named last changes fastest.
Arguments:
- points: float32 [64, 32768], P(None, ('leaf', 'help')), may hold values from -3 to 3
- weights: float32 [256, 32768], P(None, ('leaf', 'help')), may hold values from -0.12 to 0.12
- interp: float32 [64, 512, 256], P(('leaf', 'help')), may hold values from -0.25 to 0.25
- transfer: float32 [6, 512, 256], replicated, may hold values from -0.25 to 0.25
- near_count: int32 [8, 8], P('leaf', 'help'), may hold values from 1 to 32, 128 in all within a row
- near_src: int32 [64, 32], P(('leaf', 'help')), may hold values from 0 to 63, as said below
- skel_group: int32 [8, 256], P('leaf'), may hold values from 0 to 4095, as said below
- skel_node: int32 [6, 256], replicated, may hold values from 0 to 511, as said below
- far_nodes: int32 [14, 4], replicated, may hold values from 0 to 7, as said below
Outputs:
- product: float32 [256, 32768], P(None, ('leaf', 'help'))
The draws below stay inside these ranges and needn't reach their ends.
Inputs may be any that keep to these rules, and one draw needn't show every extreme that they name: `near_src`: slot 0 of leaf i names leaf i itself; every source of a leaf of subtree g is a leaf of subtree g - 1, g or g + 1. Slots at or after the leaf's near_count are not used. `near_count`: the 8 counts of one subtree sum to exactly 128. `skel_group`: each row holds 256 distinct indices into its subtree's points, counted from the subtree's first point. `skel_node`: each row holds 256 distinct indices into its two children's skeleton points, the first child's first. `far_nodes`: rows 0 to 7 are the level-0 nodes, the next 4 rows the level-1 nodes, and so on down to the 2 nodes of the highest listed level; each entry is a node number of that row's level. On level 0, the first entry of node k's row is k - 1 (modulo 8) and no other entry is k, k + 1 or k - 1 (modulo 8); on a higher level of c >= 4 nodes, no entry of node k's row is k, k + 1 or k - 1 (modulo c); on the level of 2 nodes, every entry is the other node.
All inputs are finite; a program needn't handle non-finite values. No bound on the sum of `near_count` on one device may be relied on, other than what follows from the above.
Results may differ from the reference program's by a relative error of at most 0.0003.
Values sent between devices are 32-bit elements; how exact they have to be, the bound alone decides.
No kernel may reach another device: no remote copies, remote signals or barrier semaphores. Data moves between devices by JAX's collectives and lax.ppermute only.
A program may use at most 192 MiB of HBM per device.

```python
import math
import jax
import jax.numpy as jnp
import numpy as np
from jax import lax

F = 64
R = 256
LEAF = 512
SK = 256
NEAR = 32
NEAR_MEAN = 16
FL = 4
GROUPS = 8
LG = 8
NLEAF = 64
NPTS = 32768
NODES_UP = 6


def first_rows(key, rows, width, total):
    keys = jax.random.split(key, rows)
    return jax.vmap(lambda k: jax.random.permutation(k, total)[:width])(keys).astype(jnp.int32)


def draw_near_src(key, part):
    key = jax.random.fold_in(key, 11)
    leaf_ids = jnp.arange(NLEAF, dtype=jnp.int32)
    group = leaf_ids // LG
    step_key, pick_key = jax.random.split(key)
    offset = jax.random.randint(step_key, (NLEAF, NEAR), -1, 2).astype(jnp.int32)
    target = group[:, None] + offset
    target = jnp.where((target < 0) | (target >= GROUPS), group[:, None], target)
    within = jax.random.randint(pick_key, (NLEAF, NEAR), 0, LG).astype(jnp.int32)
    sources = target * LG + within
    sources = sources.at[:, 0].set(leaf_ids)
    return sources.astype(jnp.int32)


def draw_skel_group(key, part):
    key = jax.random.fold_in(key, 23)
    return first_rows(key, GROUPS, SK, LG * LEAF)


def draw_skel_node(key, part):
    key = jax.random.fold_in(key, 37)
    return first_rows(key, NODES_UP, SK, 2 * SK)


def draw_far_nodes(key, part):
    key = jax.random.fold_in(key, 41)
    pieces = []
    for level in range(GROUPS.bit_length() - 1):
        count = GROUPS >> level
        level_key = jax.random.fold_in(key, level)
        nodes = jnp.arange(count, dtype=jnp.int32)
        if count >= 4:
            if level == 0:
                first = ((nodes + count - 1) % count)[:, None]
            else:
                first = ((nodes + count // 2) % count)[:, None]
            steps = jax.random.randint(level_key, (count, FL - 1), 2, count - 1).astype(jnp.int32)
            others = (nodes[:, None] + steps) % count
            pieces.append(jnp.concatenate([first, others], axis=1))
        else:
            other = (nodes + 1) % count
            pieces.append(jnp.broadcast_to(other[:, None], (count, FL)))
    return jnp.concatenate(pieces, axis=0).astype(jnp.int32)


def level_of(rng, shape, cuts, smallest, top_value):
    factor_of = 1.0
    for axis_at, shards_of in cuts:
        draws = jax.random.uniform(jax.random.fold_in(jax.random.fold_in(rng, 6), axis_at), (shards_of,), jnp.float32, smallest / len(cuts), top_value / len(cuts))
        factor_of = factor_of * jnp.repeat(jnp.exp(draws), shape[axis_at] // shards_of).reshape((-1,) + (1,) * (len(shape) - 1 - axis_at))
    return factor_of


def profile(number_of, total, reach, slope):
    portions = [(1 << 20) // math.isqrt(standing ** slope) + 1 for standing in range(2, number_of + 1)]
    rest, given = total - reach - (number_of - 1), [1] * (number_of - 1)
    while rest > 0:
        candidates = [i for i in range(number_of - 1) if given[i] < reach]
        pool, remaining = sum([portions[i] for i in candidates]), rest
        for i in candidates:
            more = min(reach - given[i], max(1, remaining * portions[i] // pool), rest)
            given[i] = given[i] + more
            rest = rest - more
    return np.array([reach] + given)


def ragged_sizes(own_key, count, total, reach, lean):
    if count == 2:
        one = jax.random.randint(own_key, (), max(1, total - reach), min(reach, total - 1) + 1)
        return jnp.stack([one, total - one])
    sizes = jnp.asarray(profile(count, total, reach, lean), jnp.int32)
    couples = (count - 1) // 2
    source_of, sink = sizes[1:1 + 2 * couples:2], sizes[2:2 + 2 * couples:2]
    room = jnp.minimum(source_of - 1, reach - sink)
    shifted = jax.random.randint(jax.random.fold_in(own_key, 1), (couples,), 0, 1 << 20) % (room + 1)
    sizes = sizes.at[1:1 + 2 * couples:2].set(source_of - shifted).at[2:2 + 2 * couples:2].set(sink + shifted)
    return sizes[jax.random.permutation(jax.random.fold_in(own_key, 2), count)]


def normal_values(stream_key, extent, deviation, reach, cuts=(), held_as=jnp.bfloat16):
    values = jax.random.normal(stream_key, extent, jnp.float32) * deviation
    if len(cuts) > 0:
        values = level_of(stream_key, extent, cuts, -0.22, 0.18) * values
    return jnp.clip(values, min=-reach, max=reach).astype(held_as)


def setup_inputs(seed: int = 0) -> dict:
    streams_of = jax.random.split(jax.random.key(seed), 10)
    return {
        "points": normal_values(streams_of[0], (F, NPTS), 0.5, 3.0, ((1, 32),), jnp.float32),
        "weights": normal_values(streams_of[1], (R, NPTS), 0.02, 0.12, ((1, 32),), jnp.float32),
        "interp": normal_values(streams_of[2], (NLEAF, LEAF, SK), LEAF ** -0.5, 0.25, ((0, 32),), jnp.float32),
        "transfer": normal_values(streams_of[3], (NODES_UP, 2 * SK, SK), (2 * SK) ** -0.5, 0.25, (), jnp.float32),
        "near_count": jax.vmap(lambda own: ragged_sizes(own, LG, NEAR_MEAN * LG, NEAR, 2))(jax.random.split(streams_of[4], GROUPS)).reshape((GROUPS, LG)).astype(jnp.int32),
        "near_src": draw_near_src(jax.random.fold_in(streams_of[9], 71), 0),
        "skel_group": draw_skel_group(jax.random.fold_in(streams_of[9], 71), 0),
        "skel_node": draw_skel_node(jax.random.fold_in(streams_of[9], 71), 0),
        "far_nodes": draw_far_nodes(jax.random.fold_in(streams_of[9], 71), 0),
    }


HIGH = lax.Precision.HIGHEST


def kernel_block(source, target):
    cross = lax.dot_general(source, target, (((0,), (0,)), ((), ())), precision=HIGH, preferred_element_type=jnp.float32)
    source_sq = jnp.sum(source * source, axis=0)
    target_sq = jnp.sum(target * target, axis=0)
    dist = source_sq[:, None] + target_sq[None, :] - 2.0 * cross
    return jnp.exp((0.5 * F - dist) * 0.25)


def apply_block(source_pts, source_vals, target_pts):
    return jnp.dot(source_vals, kernel_block(source_pts, target_pts), precision=HIGH, preferred_element_type=jnp.float32)


def take_columns(cols, index):
    return jnp.take(cols, index, axis=1)


def reference(points, weights, interp, transfer, near_count, near_src, skel_group, skel_node, far_nodes):
    groups = GROUPS
    levels = groups.bit_length() - 1
    leaf_vals = weights.reshape(R, NLEAF, LEAF)
    leaf_up = jnp.einsum('rjl,jls->jrs', leaf_vals, interp, precision=HIGH)
    group_up = jnp.sum(leaf_up.reshape(groups, LG, R, SK), axis=1)
    group_pts = points.reshape(F, groups, LG * LEAF)
    group_skel = jax.vmap(take_columns, in_axes=(1, 0))(group_pts, skel_group)
    tier_pts = [group_skel]
    tier_vals = [group_up]
    row = 0
    for level in range(1, levels):
        count = groups >> level
        prev_pts = tier_pts[-1].reshape(count, 2, F, SK)
        prev_vals = tier_vals[-1].reshape(count, 2, R, SK)
        both_pts = jnp.concatenate([prev_pts[:, 0], prev_pts[:, 1]], axis=2)
        both_vals = jnp.concatenate([prev_vals[:, 0], prev_vals[:, 1]], axis=2)
        chosen = jax.vmap(take_columns)(both_pts, skel_node[row:row + count])
        merged = jnp.einsum('nrc,ncs->nrs', both_vals, transfer[row:row + count], precision=HIGH)
        tier_pts.append(chosen)
        tier_vals.append(merged)
        row += count
    far_parts = []
    start = 0
    for level in range(levels):
        count = groups >> level
        lists = far_nodes[start:start + count]
        pts = tier_pts[level]
        vals = tier_vals[level]

        def node_far(target, ids, pts=pts, vals=vals):
            total = jnp.zeros((R, SK), jnp.float32)
            for slot in range(FL):
                total = total + apply_block(pts[ids[slot]], vals[ids[slot]], target)
            return total

        far_parts.append(jax.vmap(node_far)(pts, lists))
        start += count
    local = far_parts[levels - 1]
    row = NODES_UP
    for level in range(levels - 1, 0, -1):
        count = groups >> level
        row -= count
        pushed = jnp.einsum('nrs,ncs->nrc', local, transfer[row:row + count], precision=HIGH)
        split = pushed.reshape(count, R, 2, SK).transpose(0, 2, 1, 3).reshape(2 * count, R, SK)
        local = far_parts[level - 1] + split
    far_out = jnp.einsum('grs,gjls->rgjl', local, interp.reshape(groups, LG, LEAF, SK), precision=HIGH).reshape(R, NPTS)
    counts = near_count.reshape(NLEAF)

    def leaf_near(inputs):
        leaf, count, sources = inputs
        target = lax.dynamic_slice_in_dim(points, leaf * LEAF, LEAF, 1)

        def one(slot, total):
            src = sources[slot]
            src_pts = lax.dynamic_slice_in_dim(points, src * LEAF, LEAF, 1)
            src_vals = lax.dynamic_slice_in_dim(weights, src * LEAF, LEAF, 1)
            term = apply_block(src_pts, src_vals, target)
            return total + jnp.where(slot < count, term, jnp.zeros_like(term))

        return lax.fori_loop(0, NEAR, one, jnp.zeros((R, LEAF), jnp.float32))

    near = lax.map(leaf_near, (jnp.arange(NLEAF, dtype=jnp.int32), counts, near_src))
    near_out = near.transpose(1, 0, 2).reshape(R, NPTS)
    return far_out + near_out
```

```python
import math
from functools import partial

import jax
import jax.numpy as jnp
from jax import lax
from jax.experimental import pallas as pl
from jax.experimental.pallas import tpu as pltpu
from jax.sharding import PartitionSpec as P

F = 64
R = 256
LEAF = 512
SK = 256
FL = 4
EXTRA = 8

BF = jnp.bfloat16
F32 = jnp.float32
LOG2E = 1.0 / math.log(2.0)
SCALE = math.sqrt(0.5 * LOG2E)
BIAS = 0.0625 * F * LOG2E
VMEM_LIMIT = 44 * 1024 * 1024


def dot(a, b):
    return jnp.dot(a, b, preferred_element_type=F32)


def dot_t(a, b):
    return lax.dot_general(a, b, (((1,), (1,)), ((), ())), preferred_element_type=F32)


def halves(x):
    hi = x.astype(BF)
    lo = (x - hi.astype(F32)).astype(BF)
    return hi, lo


def dot3(a, b, mul=dot):
    a_hi, a_lo = halves(a)
    b_hi, b_lo = halves(b)
    return mul(a_hi, b_hi) + mul(a_lo, b_hi) + mul(a_hi, b_lo)


def target_side(x):
    hi, lo = halves(x)
    both = hi.astype(F32) + lo.astype(F32)
    off = BIAS - 0.5 * jnp.sum(both * both, axis=0, keepdims=True)
    return jnp.concatenate([hi, lo, hi, lo], axis=0), off


def source_side(x):
    xt = x.T
    hi, lo = halves(xt)
    both = hi.astype(F32) + lo.astype(F32)
    off = BIAS - 0.5 * jnp.sum(both * both, axis=1, keepdims=True)
    return jnp.concatenate([hi, hi, lo, lo], axis=1), off


def near_body(nblk, nchunk, has_acc, mult_ref, *refs):
    targets = refs[:nblk]
    src_ref = refs[nblk]
    w_refs = refs[nblk + 1 : nblk + 1 + nchunk]
    at = nblk + 1 + nchunk
    if has_acc:
        acc_refs = refs[at : at + nblk]
        at += nblk
    outs = refs[at : at + nblk]
    t_scr, tb_scr, s_scr, sb_scr, w_scr, o_scr, list_ref = refs[at + nblk :]
    rows = R // nchunk
    for b in range(nblk):
        side, off = target_side(targets[b][:F, :] * SCALE)
        for leaf in range(2):
            cols = slice(leaf * LEAF, (leaf + 1) * LEAF)
            t_scr[2 * b + leaf] = side[:, cols]
            tb_scr[2 * b + leaf] = jnp.broadcast_to(off[:, cols], (8, LEAF))
            if has_acc:
                o_scr[2 * b + leaf] = acc_refs[b][:, cols]
            else:
                o_scr[2 * b + leaf] = jnp.zeros((R, LEAF), F32)
    for leaf in range(2):
        cols = slice(leaf * LEAF, (leaf + 1) * LEAF)
        side, off = source_side(src_ref[:F, cols] * SCALE)
        s_scr[leaf] = side
        sb_scr[leaf] = jnp.broadcast_to(off, (LEAF, 128))
        for c in range(nchunk):
            hi, lo = halves(w_refs[c][:, cols])
            w_scr[leaf, c * rows : (c + 1) * rows, :] = hi
            w_scr[leaf, R + c * rows : R + (c + 1) * rows, :] = lo

    def collect(n, count):
        @pl.when(mult_ref[n] > 0)
        def _():
            list_ref[count] = n

        return count + (mult_ref[n] > 0).astype(jnp.int32)

    count = lax.fori_loop(0, 4 * nblk, collect, jnp.int32(0))

    def tile(index, carry):
        n = list_ref[index]
        t, j = n // 2, n % 2
        side = t_scr[t]
        off = tb_scr[t][:1, :]
        total = jnp.zeros((R, LEAF), F32)
        for half in range(2):
            part = slice(half * 256, (half + 1) * 256)
            cross = dot(s_scr[j, part, :], side)
            src_off = sb_scr[j, part, :]
            src_off = jnp.concatenate([src_off] * (LEAF // 128), axis=1)
            k_hi, k_lo = halves(jnp.exp2(cross + src_off + off))
            total = total + dot(w_scr[j, :R, part], k_hi)
            total = total + dot(w_scr[j, R:, part], k_hi)
            total = total + dot(w_scr[j, :R, part], k_lo)
        o_scr[t] = o_scr[t] + mult_ref[n].astype(F32) * total
        return carry

    lax.fori_loop(0, count, tile, jnp.int32(0))
    for b in range(nblk):
        for leaf in range(2):
            outs[b][:, leaf * LEAF : (leaf + 1) * LEAF] = o_scr[2 * b + leaf]


def near_call(mult, targets, src, chunks, acc=None):
    nblk, nchunk = len(targets), len(chunks)
    cols = 2 * LEAF
    vmem = pl.BlockSpec(memory_space=pltpu.VMEM)
    n_in = nblk + 1 + nchunk
    aliases = {}
    extra = []
    if acc is not None:
        extra = list(acc)
        aliases = {1 + n_in + b: b for b in range(nblk)}
    tiles = nblk * 2
    return pl.pallas_call(
        partial(near_body, nblk, nchunk, acc is not None),
        out_shape=[jax.ShapeDtypeStruct((R, cols), F32)] * nblk,
        in_specs=[pl.BlockSpec(memory_space=pltpu.SMEM)] + [vmem] * (n_in + len(extra)),
        out_specs=[vmem] * nblk,
        scratch_shapes=[
            pltpu.VMEM((2 * nblk, 4 * F, LEAF), BF),
            pltpu.VMEM((2 * nblk, 8, LEAF), F32),
            pltpu.VMEM((2, LEAF, 4 * F), BF),
            pltpu.VMEM((2, LEAF, 128), F32),
            pltpu.VMEM((2, 2 * R, LEAF), BF),
            pltpu.VMEM((2 * nblk, R, LEAF), F32),
            pltpu.SMEM((4 * nblk,), jnp.int32),
        ],
        input_output_aliases=aliases,
        compiler_params=pltpu.CompilerParams(vmem_limit_bytes=VMEM_LIMIT),
        cost_estimate=pl.CostEstimate(
            flops=tiles * 2 * LEAF * LEAF * (4 * F + 3 * R) // 2,
            bytes_accessed=nblk * R * cols * 8,
            transcendentals=tiles * LEAF * LEAF // 2,
        ),
    )(mult, *targets, src, *chunks, *extra)


def up_body(xs, pos_ref, w_ref, interp_ref, keep_ref, give_ref, scr):
    total = jnp.zeros((R, SK), F32)
    for leaf in range(2):
        total = total + dot3(w_ref[:, leaf * LEAF : (leaf + 1) * LEAF], interp_ref[leaf])
    scr[...] = total
    rows = R // (2 * xs)
    x, core = pos_ref[0], pos_ref[1]
    for dx in range(xs):
        there = 2 * lax.rem(x + dx, xs)
        keep_ref[dx] = scr[pl.ds(pl.multiple_of((there + core) * rows, rows), rows), :]
        give_ref[dx] = scr[pl.ds(pl.multiple_of((there + 1 - core) * rows, rows), rows), :]


def up_call(xs, pos, weights, interp):
    rows = R // (2 * xs)
    vmem = pl.BlockSpec(memory_space=pltpu.VMEM)
    return pl.pallas_call(
        partial(up_body, xs),
        out_shape=[jax.ShapeDtypeStruct((xs, rows, SK), F32)] * 2,
        in_specs=[pl.BlockSpec(memory_space=pltpu.SMEM), vmem, vmem],
        out_specs=[vmem, vmem],
        scratch_shapes=[pltpu.VMEM((R, SK), F32)],
        compiler_params=pltpu.CompilerParams(vmem_limit_bytes=VMEM_LIMIT),
        cost_estimate=pl.CostEstimate(
            flops=6 * R * SK * 2 * LEAF, bytes_accessed=2 << 20, transcendentals=0
        ),
    )(pos, weights, interp)


def skel_body(xs, nblk, base_ref, index_ref, *refs):
    blocks = refs[:nblk]
    sums = refs[nblk:-1]
    out_ref = refs[-1]
    cols = 2 * LEAF
    total = jnp.zeros((2 * F, SK), F32)
    spot = lax.broadcasted_iota(jnp.int32, (cols, SK), 0)
    for b in range(nblk):
        hi, lo = halves(blocks[b][:F, :] * SCALE)
        hot = spot + base_ref[b] == index_ref[...]
        total = total + dot(jnp.concatenate([hi, lo], axis=0), hot.astype(F32).astype(BF))
    out_ref[:F, :] = total[:F] + total[F:]
    value = sums[0][...]
    for ref in sums[1:]:
        value = value + ref[...]
    out_ref[F:, :] = value


def skel_call(xs, bases, index, blocks, sums):
    rows = R // (2 * xs)
    vmem = pl.BlockSpec(memory_space=pltpu.VMEM)
    return pl.pallas_call(
        partial(skel_body, xs, len(blocks)),
        out_shape=jax.ShapeDtypeStruct((F + rows, SK), F32),
        in_specs=[pl.BlockSpec(memory_space=pltpu.SMEM)] + [vmem] * (1 + len(blocks) + len(sums)),
        out_specs=vmem,
        compiler_params=pltpu.CompilerParams(vmem_limit_bytes=VMEM_LIMIT),
        cost_estimate=pl.CostEstimate(
            flops=2 * 2 * F * SK * 2 * LEAF * len(blocks), bytes_accessed=1 << 20, transcendentals=0
        ),
    )(bases, index, *blocks, *sums)


def upper_start(level, groups):
    return sum((groups >> step for step in range(1, level)))


def list_start(level, groups):
    return sum((groups >> step for step in range(level)))


def far_body(groups, rows, steps, pos_ref, far_ref, node_ref, transfer_ref, *refs):
    pieces = refs[: len(steps) + 1]
    out_ref, p_scr, u_scr, f_scr = refs[len(steps) + 1 :]
    levels = groups.bit_length() - 1
    group = pos_ref[2]
    start = [sum(groups >> step for step in range(level)) for level in range(levels)]
    held = [0]
    p_scr[0] = pieces[0][:F, :]
    u_scr[0] = pieces[0][F:, :]
    for piece, step in zip(pieces[1:], steps):
        for at, mask in enumerate(held):
            p_scr[mask ^ step] = piece[at, :F, :]
            u_scr[mask ^ step] = piece[at, F:, :]
        held = held + [mask ^ step for mask in held]
    spot = lax.broadcasted_iota(jnp.int32, (2 * SK, SK), 0)
    for level in range(1, levels):
        bit = (group >> (level - 1)) & 1
        for m in range(groups >> level):
            row = upper_start(level, groups) + (m ^ (group >> level))
            left = start[level - 1] + 2 * m + bit
            right = start[level - 1] + 2 * m + 1 - bit
            hot = (spot == node_ref[row]).astype(F32).astype(BF)
            pts = jnp.concatenate([p_scr[left], p_scr[right]], axis=1)
            hi, lo = halves(pts)
            both = dot(jnp.concatenate([hi, lo], axis=0), hot)
            p_scr[start[level] + m] = both[:F] + both[F:]
            vals = jnp.concatenate([u_scr[left], u_scr[right]], axis=1)
            u_scr[start[level] + m] = dot3(vals, transfer_ref[row])
    for level in range(levels):
        node = group >> level
        side, off = target_side(p_scr[start[level]])
        f_scr[level] = jnp.zeros((rows, SK), F32)

        def one(m, carry, level=level, node=node, side=side, off=off):
            hits = jnp.int32(0)
            for slot in range(FL):
                entry = far_ref[list_start(level, groups) + node, slot]
                hits = hits + (entry == (m ^ node)).astype(jnp.int32)

            @pl.when(hits > 0)
            def _():
                src, src_off = source_side(p_scr[start[level] + m])
                block = jnp.exp2(dot(src, side) + src_off + off)
                term = dot3(u_scr[start[level] + m], block)
                f_scr[level] = f_scr[level] + hits.astype(F32) * term

            return carry

        lax.fori_loop(0, groups >> level, one, jnp.int32(0))
    local = f_scr[levels - 1]
    for level in range(levels - 1, 0, -1):
        row = upper_start(level, groups) + (group >> level)
        bit = (group >> (level - 1)) & 1
        matrix = transfer_ref[row, pl.ds(pl.multiple_of(bit * SK, SK), SK), :]
        local = f_scr[level - 1] + dot3(local, matrix, dot_t)
    out_ref[...] = local


def far_call(groups, pos, far_nodes, skel_node, transfer, pieces, steps):
    rows = pieces[0].shape[0] - F
    vmem = pl.BlockSpec(memory_space=pltpu.VMEM)
    smem = pl.BlockSpec(memory_space=pltpu.SMEM)
    nodes = 2 * groups
    return pl.pallas_call(
        partial(far_body, groups, rows, steps),
        out_shape=jax.ShapeDtypeStruct((rows, SK), F32),
        in_specs=[smem, smem, vmem, vmem] + [vmem] * len(pieces),
        out_specs=vmem,
        scratch_shapes=[
            pltpu.VMEM((nodes, F, SK), F32),
            pltpu.VMEM((nodes, rows, SK), F32),
            pltpu.VMEM((groups.bit_length(), rows, SK), F32),
        ],
        compiler_params=pltpu.CompilerParams(vmem_limit_bytes=VMEM_LIMIT),
        cost_estimate=pl.CostEstimate(
            flops=20 * 2 * 256 * SK * SK * 4, bytes_accessed=4 << 20, transcendentals=20 * SK * SK
        ),
    )(pos, far_nodes, skel_node[:, None, :], transfer, *pieces)


def final_body(xs, nsum, pos_ref, interp_ref, *refs):
    same = refs[:xs]
    mate = refs[xs]
    sums = refs[xs + 1 : xs + 1 + nsum]
    out_ref, v_scr = refs[xs + 1 + nsum :]
    rows = R // (2 * xs)
    x, core = pos_ref[0], pos_ref[1]
    for dx in range(xs):
        there = 2 * lax.rem(x + dx, xs)
        v_scr[pl.ds(pl.multiple_of((there + core) * rows, rows), rows), :] = same[dx][...]
        v_scr[pl.ds(pl.multiple_of((there + 1 - core) * rows, rows), rows), :] = mate[dx]
    value = v_scr[...]
    for leaf in range(2):
        cols = slice(leaf * LEAF, (leaf + 1) * LEAF)
        total = dot3(value, interp_ref[leaf], dot_t)
        for ref in sums:
            total = total + ref[:, cols]
        out_ref[:, cols] = total


def final_call(xs, pos, interp, same, mate, sums):
    vmem = pl.BlockSpec(memory_space=pltpu.VMEM)
    return pl.pallas_call(
        partial(final_body, xs, len(sums)),
        out_shape=jax.ShapeDtypeStruct((R, 2 * LEAF), F32),
        in_specs=[pl.BlockSpec(memory_space=pltpu.SMEM)] + [vmem] * (1 + xs + 1 + len(sums)),
        out_specs=vmem,
        scratch_shapes=[pltpu.VMEM((R, SK), F32)],
        compiler_params=pltpu.CompilerParams(vmem_limit_bytes=VMEM_LIMIT),
        cost_estimate=pl.CostEstimate(
            flops=6 * R * SK * 2 * LEAF, bytes_accessed=5 << 20, transcendentals=0
        ),
    )(pos, interp, *same, mate, *sums)


def help_pairs(xs, dx, dc):
    return [
        (2 * ((x + dx) % xs) + (core ^ dc), 2 * x + core) for x in range(xs) for core in range(2)
    ]


def shards(
    points, weights, interp, transfer, near_count, near_src, skel_group, skel_node, far_nodes
):
    helpers = lax.axis_size("help")
    groups = lax.axis_size("leaf")
    xs = helpers // 2
    helper = lax.axis_index("help")
    group = lax.axis_index("leaf")
    x, core = helper // 2, helper % 2
    leaves = 2 * helpers
    pos = jnp.stack([x, core, group]).astype(jnp.int32)
    nchunk = 2

    def from_help(value, dx, dc):
        return lax.ppermute(value, "help", help_pairs(xs, dx, dc))

    beside = [(i, i ^ 1) for i in range(groups)]
    across = [(i, i + 2) for i in range(0, groups - 2, 2)]
    across += [(i, i - 2) for i in range(3, groups, 2)]

    slots = near_src.shape[1]
    relative = near_src - (group - 1) * leaves
    used = lax.broadcasted_iota(jnp.int32, near_src.shape, 1) < near_count[0][:, None]
    names = lax.broadcasted_iota(jnp.int32, (2, slots, 3 * leaves), 2)
    times = jnp.sum(((relative[:, :, None] == names) & used[:, :, None]).astype(F32), axis=1)
    times = times.reshape(2, 3, leaves)
    even = group % 2 == 0
    before, own, after = times[:, 0], times[:, 1], times[:, 2]
    times = jnp.stack([own, jnp.where(even, after, before), jnp.where(even, before, after)], axis=1)
    flat = times.reshape(1, 6 * leaves)
    flat = jnp.pad(flat, ((0, EXTRA - 1), (0, points.shape[1] - 6 * leaves)))
    packed = jnp.concatenate([points, flat], axis=0)

    rows = R // nchunk
    w_own = [weights[c * rows : (c + 1) * rows] for c in range(nchunk)]
    pts_y = lax.ppermute(points, "leaf", beside)
    w_y = [lax.ppermute(chunk, "leaf", beside) for chunk in w_own]
    pts_z = lax.ppermute(pts_y, "leaf", across)
    w_z = [lax.ppermute(chunk, "leaf", across) for chunk in w_y]

    order = [(dx, dc) for dx in range(xs) for dc in range(2)]
    blocks = [packed if o == (0, 0) else from_help(packed, *o) for o in order]
    keep, give = up_call(xs, pos, weights, interp)
    half = keep + from_help(give, 0, 1)
    sums = [half[0]] + [
        lax.ppermute(half[dx], "help", help_pairs(xs, -dx, 0)) for dx in range(1, xs)
    ]

    mult = jnp.stack([block[F, : 6 * leaves].reshape(2, 3, helpers, 2) for block in blocks])
    mult = lax.dynamic_index_in_dim(mult, helper, 3, keepdims=False).astype(jnp.int32)
    mult = mult.transpose(2, 0, 1, 3).reshape(3, len(order) * 4)

    bases = jnp.stack([(2 * ((x + dx) % xs) + (core ^ dc)) for dx, dc in order]) * (2 * LEAF)
    payload = skel_call(xs, bases.astype(jnp.int32), skel_group, blocks, sums)

    steps = [1 << k for k in range(groups.bit_length() - 1)]
    steps = steps[:1] + steps[:0:-1]
    pieces = [payload]
    held = payload[None]
    for step in steps:
        got = lax.ppermute(held, "leaf", [(i, i ^ step) for i in range(groups)])
        pieces.append(got)
        held = jnp.concatenate([held, got], axis=0)

    near = near_call(mult[0], blocks, points, w_own)
    near = near_call(mult[1], blocks, pts_y, w_y, near)

    v_own = far_call(groups, pos, far_nodes, skel_node, transfer, pieces, steps)
    v_same = [v_own] + [from_help(v_own, dx, 0) for dx in range(1, xs)]
    v_mate = from_help(jnp.stack(v_same), 0, 1)

    away = near_call(mult[2][8:], blocks[2:], pts_z, w_z, near[2:])
    home = near_call(mult[2][:8], blocks[:2], pts_z, w_z, near[:2])
    parts = [home[0], from_help(home[1], 0, 1)]
    for dx in range(1, xs):
        keep_dx, give_dx = away[2 * dx - 2], away[2 * dx - 1]
        part = keep_dx + from_help(give_dx, 0, 1)
        parts.append(lax.ppermute(part, "help", help_pairs(xs, -dx, 0)))
    return final_call(xs, pos, interp, v_same, v_mate, parts)


def solution(mesh):
    placed = (
        P(None, ("leaf", "help")),
        P(None, ("leaf", "help")),
        P(("leaf", "help"), None, None),
        P(),
        P("leaf", "help"),
        P(("leaf", "help"), None),
        P("leaf", None),
        P(),
        P(),
    )
    return jax.shard_map(
        shards, mesh=mesh, in_specs=placed, out_specs=P(None, ("leaf", "help")), check_vma=False
    )
```

```python
import math
from functools import partial

import jax
import jax.numpy as jnp
from jax import lax
from jax.experimental import pallas as pl
from jax.experimental.pallas import tpu as pltpu
from jax.sharding import PartitionSpec as P

F = 64
R = 256
LEAF = 512
SK = 256
FL = 4
EXTRA = 8

BF = jnp.bfloat16
F32 = jnp.float32
LOG2E = 1.0 / math.log(2.0)
SCALE = math.sqrt(0.5 * LOG2E)
BIAS = 0.0625 * F * LOG2E
VMEM_LIMIT = 24 * 1024 * 1024


def dot(a, b):
    return jnp.dot(a, b, preferred_element_type=F32)


def dot_t(a, b):
    return lax.dot_general(a, b, (((1,), (1,)), ((), ())), preferred_element_type=F32)


def halves(x):
    hi = x.astype(BF)
    lo = (x - hi.astype(F32)).astype(BF)
    return hi, lo


def dot3(a, b, mul=dot):
    a_hi, a_lo = halves(a)
    b_hi, b_lo = halves(b)
    return mul(a_hi, b_hi) + mul(a_lo, b_hi) + mul(a_hi, b_lo)


def target_side(x):
    hi, lo = halves(x)
    both = hi.astype(F32) + lo.astype(F32)
    off = BIAS - 0.5 * jnp.sum(both * both, axis=0, keepdims=True)
    return jnp.concatenate([hi, lo, hi, lo], axis=0), off


def source_side(x):
    xt = x.T
    hi, lo = halves(xt)
    both = hi.astype(F32) + lo.astype(F32)
    off = BIAS - 0.5 * jnp.sum(both * both, axis=1, keepdims=True)
    return jnp.concatenate([hi, hi, lo, lo], axis=1), off


def near_body(nblk, nset, nchunk, rows, acc_row, mult_ref, *refs):
    tiles_of = 4 * nset * nblk
    t_refs = refs[: 2 * nblk]
    at = 2 * nblk
    s_refs = refs[at : at + nset * (2 + nchunk)]
    at += nset * (2 + nchunk)
    acc_refs = refs[at : at + nblk] if acc_row is not None else ()
    outs = refs[-9 - nblk : -9]
    t_scr, tb_scr, s_scr, sb_scr, w_scr, o_scr, kh_scr, kl_scr, list_ref = refs[-9:]
    each = rows // nchunk
    for b in range(nblk):
        for leaf in range(2):
            cols = slice(leaf * LEAF, (leaf + 1) * LEAF)
            t_scr[2 * b + leaf] = t_refs[2 * b][leaf]
            tb_scr[2 * b + leaf] = t_refs[2 * b + 1][leaf]
            if acc_refs:
                o_scr[2 * b + leaf] = acc_refs[b][acc_row : acc_row + rows, cols]
            else:
                o_scr[2 * b + leaf] = jnp.zeros((rows, LEAF), F32)
    for k in range(nset):
        side_ref, off_ref = s_refs[k * (2 + nchunk) : k * (2 + nchunk) + 2]
        chunks = s_refs[k * (2 + nchunk) + 2 : (k + 1) * (2 + nchunk)]
        for leaf in range(2):
            cols = slice(leaf * LEAF, (leaf + 1) * LEAF)
            j = 2 * k + leaf
            s_scr[j] = side_ref[leaf]
            sb_scr[j] = off_ref[leaf]
            for c in range(nchunk):
                hi, lo = halves(chunks[c][:, cols])
                w_scr[j, c * each : (c + 1) * each, :] = hi
                w_scr[j, rows + c * each : rows + (c + 1) * each, :] = lo

    def collect(n, count):
        @pl.when(mult_ref[n] > 0)
        def _():
            list_ref[count] = n

        return count + (mult_ref[n] > 0).astype(jnp.int32)

    list_ref[0] = 0
    count = lax.fori_loop(0, tiles_of, collect, jnp.int32(0))

    def block(index, slot):
        n = list_ref[jnp.minimum(index, jnp.maximum(count - 1, 0))]
        t, j = n // (2 * nset), n % (2 * nset)
        side = t_scr[t]
        off = tb_scr[t][:1, :]
        for half in range(2):
            part = slice(half * 256, (half + 1) * 256)
            cross = dot(s_scr[j, part, :], side)
            src_off = sb_scr[j, part, :]
            src_off = jnp.concatenate([src_off] * (LEAF // 128), axis=1)
            k_hi, k_lo = halves(jnp.exp2(cross + src_off + off))
            kh_scr[slot, part, :] = k_hi
            kl_scr[slot, part, :] = k_lo

    def apply(index, slot):
        n = list_ref[index]
        t, j = n // (2 * nset), n % (2 * nset)
        factor = mult_ref[n].astype(F32)
        for half in range(2):
            cols = slice(half * 256, (half + 1) * 256)
            both = dot(w_scr[j], kh_scr[slot, :, cols])
            low = dot(w_scr[j, :rows, :], kl_scr[slot, :, cols])
            o_scr[t, :, cols] = o_scr[t, :, cols] + factor * (both[:rows] + both[rows:] + low)

    @pl.when(count > 0)
    def _():
        block(0, 0)

    def pair(index, carry):
        block(2 * index + 1, 1)
        apply(2 * index, 0)

        @pl.when(2 * index + 1 < count)
        def _():
            block(2 * index + 2, 0)
            apply(2 * index + 1, 1)

        return carry

    lax.fori_loop(0, (count + 1) // 2, pair, jnp.int32(0))
    for b in range(nblk):
        for leaf in range(2):
            outs[b][:, leaf * LEAF : (leaf + 1) * LEAF] = o_scr[2 * b + leaf]


def near_call(name, mult, targets, sources, rows, acc=None, acc_row=None, after=()):
    nblk, nset, nchunk = len(targets), len(sources), len(sources[0]) - 2
    cols = 2 * LEAF
    vmem = pl.BlockSpec(memory_space=pltpu.VMEM)
    operands = [a for t in targets for a in t] + [a for s in sources for a in s]
    operands += list(acc) if acc is not None else []
    return pl.pallas_call(
        partial(near_body, nblk, nset, nchunk, rows, acc_row),
        name=name,
        out_shape=[jax.ShapeDtypeStruct((rows, cols), F32)] * nblk,
        in_specs=[pl.BlockSpec(memory_space=pltpu.SMEM)]
        + [vmem] * len(operands)
        + [pl.BlockSpec(memory_space=pl.ANY)] * len(after),
        out_specs=[vmem] * nblk,
        scratch_shapes=[
            pltpu.VMEM((2 * nblk, 4 * F, LEAF), BF),
            pltpu.VMEM((2 * nblk, 8, LEAF), F32),
            pltpu.VMEM((2 * nset, LEAF, 4 * F), BF),
            pltpu.VMEM((2 * nset, LEAF, 128), F32),
            pltpu.VMEM((2 * nset, 2 * rows, LEAF), BF),
            pltpu.VMEM((2 * nblk, rows, LEAF), F32),
            pltpu.VMEM((2, LEAF, LEAF), BF),
            pltpu.VMEM((2, LEAF, LEAF), BF),
            pltpu.SMEM((4 * nset * nblk,), jnp.int32),
        ],
        compiler_params=pltpu.CompilerParams(vmem_limit_bytes=VMEM_LIMIT),
    )(mult, *operands, *after)


def source_body(pts_ref, side_ref, off_ref):
    for leaf in range(2):
        cols = slice(leaf * LEAF, (leaf + 1) * LEAF)
        side, off = source_side(pts_ref[:, cols] * SCALE)
        side_ref[leaf] = side
        off_ref[leaf] = jnp.broadcast_to(off, (LEAF, 128))


def source_call(pts):
    vmem = pl.BlockSpec(memory_space=pltpu.VMEM)
    return pl.pallas_call(
        source_body,
        name="source_side",
        out_shape=[
            jax.ShapeDtypeStruct((2, LEAF, 4 * F), BF),
            jax.ShapeDtypeStruct((2, LEAF, 128), F32),
        ],
        in_specs=[vmem],
        out_specs=[vmem, vmem],
        compiler_params=pltpu.CompilerParams(vmem_limit_bytes=VMEM_LIMIT),
    )(pts)


def up_body(xs, pos_ref, w_ref, interp_ref, keep_ref, give_ref, scr):
    total = jnp.zeros((R, SK), F32)
    for leaf in range(2):
        total = total + dot3(w_ref[:, leaf * LEAF : (leaf + 1) * LEAF], interp_ref[leaf])
    scr[...] = total
    rows = R // (2 * xs)
    x, core = pos_ref[0], pos_ref[1]
    for dx in range(xs):
        there = 2 * lax.rem(x + dx, xs)
        keep_ref[dx] = scr[pl.ds(pl.multiple_of((there + core) * rows, rows), rows), :]
        give_ref[dx] = scr[pl.ds(pl.multiple_of((there + 1 - core) * rows, rows), rows), :]


def up_call(xs, pos, weights, interp):
    rows = R // (2 * xs)
    vmem = pl.BlockSpec(memory_space=pltpu.VMEM)
    return pl.pallas_call(
        partial(up_body, xs),
        name="leaf_up",
        out_shape=[jax.ShapeDtypeStruct((xs, rows, SK), F32)] * 2,
        in_specs=[pl.BlockSpec(memory_space=pltpu.SMEM), vmem, vmem],
        out_specs=[vmem, vmem],
        scratch_shapes=[pltpu.VMEM((R, SK), F32)],
        compiler_params=pltpu.CompilerParams(vmem_limit_bytes=VMEM_LIMIT),
    )(pos, weights, interp)


def skel_body(xs, nsum, base_ref, index_ref, same_ref, mate_ref, *refs):
    nblk = 2 * xs
    sums = refs[:nsum]
    out_ref = refs[nsum]
    sides = refs[nsum + 1 :]
    cols = 2 * LEAF
    total = jnp.zeros((2 * F, SK), F32)
    spot = lax.broadcasted_iota(jnp.int32, (cols, SK), 0)
    for b in range(nblk):
        pts = (same_ref, mate_ref)[b % 2][b // 2, :F, :] * SCALE
        side, off = target_side(pts)
        for leaf in range(2):
            part = slice(leaf * LEAF, (leaf + 1) * LEAF)
            sides[2 * b][leaf] = side[:, part]
            sides[2 * b + 1][leaf] = jnp.broadcast_to(off[:, part], (8, LEAF))
        hot = spot + base_ref[b] == index_ref[...]
        total = total + dot(side[: 2 * F], hot.astype(F32).astype(BF))
    out_ref[:F, :] = total[:F] + total[F:]
    value = sums[0][...]
    for ref in sums[1:]:
        value = value + ref[...]
    out_ref[F:, :] = value


def skel_call(xs, bases, index, same, mate, sums):
    rows = R // (2 * xs)
    nblk = 2 * xs
    vmem = pl.BlockSpec(memory_space=pltpu.VMEM)
    side = [
        jax.ShapeDtypeStruct((2, 4 * F, LEAF), BF),
        jax.ShapeDtypeStruct((2, 8, LEAF), F32),
    ]
    out = pl.pallas_call(
        partial(skel_body, xs, len(sums)),
        name="skeleton",
        out_shape=[jax.ShapeDtypeStruct((F + rows, SK), F32)] + side * nblk,
        in_specs=[pl.BlockSpec(memory_space=pltpu.SMEM)] + [vmem] * (3 + len(sums)),
        out_specs=[vmem] * (1 + 2 * nblk),
        compiler_params=pltpu.CompilerParams(vmem_limit_bytes=VMEM_LIMIT),
    )(bases, index, same, mate, *sums)
    return out[0], [(out[1 + 2 * b], out[2 + 2 * b]) for b in range(nblk)]


def upper_start(level, groups):
    return sum((groups >> step for step in range(1, level)))


def list_start(level, groups):
    return sum((groups >> step for step in range(level)))


def far_body(groups, rows, steps, pos_ref, far_ref, node_ref, transfer_ref, *refs):
    pieces = refs[: len(steps) + 1]
    out_ref, p_scr, u_scr, f_scr = refs[-4:]
    levels = groups.bit_length() - 1
    group = pos_ref[2]
    start = [sum(groups >> step for step in range(level)) for level in range(levels)]
    held = [0]
    p_scr[0] = pieces[0][:F, :]
    u_scr[0] = pieces[0][F:, :]
    for piece, step in zip(pieces[1:], steps):
        for at, mask in enumerate(held):
            p_scr[mask ^ step] = piece[at, :F, :]
            u_scr[mask ^ step] = piece[at, F:, :]
        held = held + [mask ^ step for mask in held]
    spot = lax.broadcasted_iota(jnp.int32, (2 * SK, SK), 0)
    for level in range(1, levels):
        bit = (group >> (level - 1)) & 1
        for m in range(groups >> level):
            row = upper_start(level, groups) + (m ^ (group >> level))
            left = start[level - 1] + 2 * m + bit
            right = start[level - 1] + 2 * m + 1 - bit
            hot = (spot == node_ref[row]).astype(F32).astype(BF)
            pts = jnp.concatenate([p_scr[left], p_scr[right]], axis=1)
            hi, lo = halves(pts)
            both = dot(jnp.concatenate([hi, lo], axis=0), hot)
            p_scr[start[level] + m] = both[:F] + both[F:]
            vals = jnp.concatenate([u_scr[left], u_scr[right]], axis=1)
            u_scr[start[level] + m] = dot3(vals, transfer_ref[row])
    for level in range(levels):
        node = group >> level
        side, off = target_side(p_scr[start[level]])
        f_scr[level] = jnp.zeros((rows, SK), F32)

        def one(m, carry, level=level, node=node, side=side, off=off):
            hits = jnp.int32(0)
            for slot in range(FL):
                entry = far_ref[list_start(level, groups) + node, slot]
                hits = hits + (entry == (m ^ node)).astype(jnp.int32)

            @pl.when(hits > 0)
            def _():
                src, src_off = source_side(p_scr[start[level] + m])
                block = jnp.exp2(dot(src, side) + src_off + off)
                term = dot3(u_scr[start[level] + m], block)
                f_scr[level] = f_scr[level] + hits.astype(F32) * term

            return carry

        lax.fori_loop(0, groups >> level, one, jnp.int32(0))
    local = f_scr[levels - 1]
    for level in range(levels - 1, 0, -1):
        row = upper_start(level, groups) + (group >> level)
        bit = (group >> (level - 1)) & 1
        matrix = transfer_ref[row, pl.ds(pl.multiple_of(bit * SK, SK), SK), :]
        local = f_scr[level - 1] + dot3(local, matrix, dot_t)
    out_ref[...] = local


def far_call(groups, pos, far_nodes, skel_node, transfer, pieces, steps, after=()):
    rows = pieces[0].shape[0] - F
    vmem = pl.BlockSpec(memory_space=pltpu.VMEM)
    smem = pl.BlockSpec(memory_space=pltpu.SMEM)
    nodes = 2 * groups
    return pl.pallas_call(
        partial(far_body, groups, rows, steps),
        name="far",
        out_shape=jax.ShapeDtypeStruct((rows, SK), F32),
        in_specs=[smem, smem, vmem, vmem]
        + [vmem] * len(pieces)
        + [pl.BlockSpec(memory_space=pl.ANY)] * len(after),
        out_specs=vmem,
        scratch_shapes=[
            pltpu.VMEM((nodes, F, SK), F32),
            pltpu.VMEM((nodes, rows, SK), F32),
            pltpu.VMEM((groups.bit_length(), rows, SK), F32),
        ],
        compiler_params=pltpu.CompilerParams(vmem_limit_bytes=VMEM_LIMIT),
    )(pos, far_nodes, skel_node[:, None, :], transfer, *pieces, *after)


def final_body(xs, pos_ref, interp_ref, home_ref, mate_ref, *refs):
    same = refs[:xs]
    v_mate = refs[xs]
    parts = refs[xs + 1 : -2]
    out_ref, v_scr = refs[-2:]
    rows = R // (2 * xs)
    x, core = pos_ref[0], pos_ref[1]
    for dx in range(xs):
        there = 2 * lax.rem(x + dx, xs)
        v_scr[pl.ds(pl.multiple_of((there + core) * rows, rows), rows), :] = same[dx][...]
        v_scr[pl.ds(pl.multiple_of((there + 1 - core) * rows, rows), rows), :] = v_mate[dx]
    value = v_scr[...]
    for leaf in range(2):
        cols = slice(leaf * LEAF, (leaf + 1) * LEAF)
        total = dot3(value, interp_ref[leaf], dot_t)
        out_ref[:, cols] = total + home_ref[:, cols] + mate_ref[:, cols]
    for n, ref in enumerate(parts):
        part = slice(n % 2 * (R // 2), (n % 2 + 1) * (R // 2))
        out_ref[part, :] = out_ref[part, :] + ref[...]


def final_call(xs, pos, interp, home, mate, same, v_mate, parts):
    vmem = pl.BlockSpec(memory_space=pltpu.VMEM)
    return pl.pallas_call(
        partial(final_body, xs),
        name="join",
        out_shape=jax.ShapeDtypeStruct((R, 2 * LEAF), F32),
        in_specs=[pl.BlockSpec(memory_space=pltpu.SMEM)] + [vmem] * (3 + xs + 1 + len(parts)),
        out_specs=vmem,
        scratch_shapes=[pltpu.VMEM((R, SK), F32)],
        compiler_params=pltpu.CompilerParams(vmem_limit_bytes=VMEM_LIMIT),
    )(pos, interp, home, mate, *same, v_mate, *parts)


def help_pairs(xs, dx, dc):
    return [
        (2 * ((x + dx) % xs) + (core ^ dc), 2 * x + core) for x in range(xs) for core in range(2)
    ]


def shards(
    points, weights, interp, transfer, near_count, near_src, skel_group, skel_node, far_nodes
):
    helpers = lax.axis_size("help")
    groups = lax.axis_size("leaf")
    xs = helpers // 2
    helper = lax.axis_index("help")
    group = lax.axis_index("leaf")
    x, core = helper // 2, helper % 2
    leaves = 2 * helpers
    pos = jnp.stack([x, core, group]).astype(jnp.int32)
    nchunk = 2

    def from_help(value, dx, dc):
        return lax.ppermute(value, "help", help_pairs(xs, dx, dc))

    beside = [(i, i ^ 1) for i in range(groups)]
    across = [(i, i + 2) for i in range(0, groups - 2, 2)]
    across += [(i, i - 2) for i in range(3, groups, 2)]

    slots = near_src.shape[1]
    relative = near_src - (group - 1) * leaves
    used = lax.broadcasted_iota(jnp.int32, near_src.shape, 1) < near_count[0][:, None]
    names = lax.broadcasted_iota(jnp.int32, (2, slots, 3 * leaves), 2)
    times = jnp.sum(((relative[:, :, None] == names) & used[:, :, None]).astype(F32), axis=1)
    times = times.reshape(2, 3, leaves)
    even = group % 2 == 0
    before, own, after = times[:, 0], times[:, 1], times[:, 2]
    times = jnp.stack([own, jnp.where(even, after, before), jnp.where(even, before, after)], axis=1)
    flat = times.reshape(1, 6 * leaves)
    flat = jnp.pad(flat, ((0, EXTRA - 1), (0, points.shape[1] - 6 * leaves)))
    packed = jnp.concatenate([points, flat], axis=0)

    rows = R // nchunk
    w_own = [weights[c * rows : (c + 1) * rows] for c in range(nchunk)]
    pts_y = lax.ppermute(points, "leaf", beside)
    w_y = [lax.ppermute(chunk, "leaf", beside) for chunk in w_own]

    order = [(dx, dc) for dx in range(xs) for dc in range(2)]
    packed, w_own = lax.optimization_barrier((packed, w_own))
    same = jnp.stack([packed] + [from_help(packed, dx, 0) for dx in range(1, xs)])
    mate = from_help(same, 0, 1)
    keep, give = up_call(xs, pos, weights, interp)
    half = keep + from_help(give, 0, 1)
    sums = [half[0]] + [
        lax.ppermute(half[dx], "help", help_pairs(xs, -dx, 0)) for dx in range(1, xs)
    ]

    mult = jnp.stack([same[:, F, : 6 * leaves], mate[:, F, : 6 * leaves]], axis=1)
    mult = mult.reshape(helpers, 2, 3, helpers, 2)
    mult = lax.dynamic_index_in_dim(mult, helper, 3, keepdims=False).astype(jnp.int32)

    def mult_of(blocks, sets):
        return mult[blocks][:, :, sets].reshape(-1)

    bases = jnp.stack([(2 * ((x + dx) % xs) + (core ^ dc)) for dx, dc in order]) * (2 * LEAF)
    payload, targets = skel_call(xs, bases.astype(jnp.int32), skel_group, same, mate, sums)
    home, away = slice(0, 2), slice(2, None)
    own_src = (*source_call(points), *w_own)
    y_src = (*source_call(pts_y), *w_y)

    pts_z = lax.ppermute(pts_y, "leaf", across)
    z_side = source_call(pts_z)

    n0a = near_call("near_own_away", mult_of(away, slice(0, 1)), targets[away], [own_src], R)
    w_y[0], n0a = lax.optimization_barrier((w_y[0], n0a))
    w_z = [lax.ppermute(w_y[0], "leaf", across)]
    n0h = near_call(
        "near_own_home", mult_of(home, slice(0, 1)), targets[home], [own_src], R, after=n0a[:1]
    )
    w_y[1], n0h = lax.optimization_barrier((w_y[1], n0h))
    w_z.append(lax.ppermute(w_y[1], "leaf", across))

    steps = [1 << k for k in range(groups.bit_length() - 1)][::-1]
    pieces = [payload]
    held = payload[None]
    for step in steps:
        got = lax.ppermute(held, "leaf", [(i, i ^ step) for i in range(groups)])
        pieces.append(got)
        held = jnp.concatenate([held, got], axis=0)

    n1a = near_call(
        "near_pair_away", mult_of(away, slice(1, 2)), targets[away], [y_src], R, n0a, 0,
        after=n0h[:1],
    )
    n1h = near_call(
        "near_pair_home", mult_of(home, slice(1, 2)), targets[home], [y_src], R, n0h, 0,
        after=n1a[:1],
    )
    m2a = mult_of(away, slice(2, 3))
    last = n1h[:1]
    parts = []
    for c in range(nchunk):
        blocks = near_call(
            "near_next_away", m2a, targets[away], [(*z_side, w_z[c])], rows, n1a, c * rows,
            after=last,
        )
        part = [
            blocks[2 * dx - 2] + from_help(blocks[2 * dx - 1], 0, 1) for dx in range(1, xs)
        ]
        parts.append(
            [lax.ppermute(part[dx - 1], "help", help_pairs(xs, -dx, 0)) for dx in range(1, xs)]
        )
        last = part[:1]
        if c == 0:
            v_own = far_call(
                groups, pos, far_nodes, skel_node, transfer, pieces, steps, after=last
            )
            last = [v_own]
            v_same = [v_own] + [from_help(v_own, dx, 0) for dx in range(1, xs)]
            v_mate = from_help(jnp.stack(v_same), 0, 1)
    n2h = near_call(
        "near_next_home", mult_of(home, slice(2, 3)), targets[home], [(*z_side, *w_z)], R, n1h, 0,
        after=last,
    )
    flat_parts = [parts[c][dx] for dx in range(xs - 1) for c in range(nchunk)]
    return final_call(
        xs, pos, interp, n2h[0], from_help(n2h[1], 0, 1), v_same, v_mate, flat_parts
    )


def solution(mesh):
    placed = (
        P(None, ("leaf", "help")),
        P(None, ("leaf", "help")),
        P(("leaf", "help"), None, None),
        P(),
        P("leaf", "help"),
        P(("leaf", "help"), None),
        P("leaf", None),
        P(),
        P(),
    )
    return jax.shard_map(
        shards, mesh=mesh, in_specs=placed, out_specs=P(None, ("leaf", "help")), check_vma=False
    )
```

```python
import math
from functools import partial

import jax
import jax.numpy as jnp
from jax import lax
from jax.experimental import pallas as pl
from jax.experimental.pallas import tpu as pltpu
from jax.sharding import PartitionSpec as P

F = 64
R = 256
LEAF = 512
SK = 256
FL = 4
EXTRA = 8

BF = jnp.bfloat16
F32 = jnp.float32
LOG2E = 1.0 / math.log(2.0)
SCALE = math.sqrt(0.5 * LOG2E)
BIAS = 0.0625 * F * LOG2E
VMEM_LIMIT = 24 * 1024 * 1024


def dot(a, b):
    return jnp.dot(a, b, preferred_element_type=F32)


def dot_t(a, b):
    return lax.dot_general(a, b, (((1,), (1,)), ((), ())), preferred_element_type=F32)


def halves(x):
    hi = x.astype(BF)
    lo = (x - hi.astype(F32)).astype(BF)
    return hi, lo


def dot3(a, b, mul=dot):
    a_hi, a_lo = halves(a)
    b_hi, b_lo = halves(b)
    return mul(a_hi, b_hi) + mul(a_lo, b_hi) + mul(a_hi, b_lo)


def target_side(x):
    hi, lo = halves(x)
    both = hi.astype(F32) + lo.astype(F32)
    off = BIAS - 0.5 * jnp.sum(both * both, axis=0, keepdims=True)
    return jnp.concatenate([hi, lo, hi, lo], axis=0), off


def source_side(x):
    xt = x.T
    hi, lo = halves(xt)
    both = hi.astype(F32) + lo.astype(F32)
    off = BIAS - 0.5 * jnp.sum(both * both, axis=1, keepdims=True)
    return jnp.concatenate([hi, hi, lo, lo], axis=1), off


def near_body(nblk, kinds, nchunk, rows, acc_row, first, pos_ref, times_ref, *refs):
    nset = len(kinds)
    t_refs = refs[: 2 * nblk]
    at = 2 * nblk
    s_refs = refs[at : at + nset * (1 + nchunk)]
    at += nset * (1 + nchunk)
    acc_refs = refs[at : at + nblk] if acc_row is not None else ()
    outs = refs[-8 - nblk : -8]
    t_scr, tb_scr, s_scr, sb_scr, w_scr, o_scr, k_scr, list_ref = refs[-8:]
    each = rows // nchunk
    for b in range(nblk):
        for leaf in range(2):
            cols = slice(leaf * LEAF, (leaf + 1) * LEAF)
            t_scr[2 * b + leaf] = t_refs[2 * b][leaf]
            tb_scr[2 * b + leaf] = t_refs[2 * b + 1][leaf]
            if acc_refs:
                o_scr[2 * b + leaf] = acc_refs[b][acc_row : acc_row + rows, cols]
            else:
                o_scr[2 * b + leaf] = jnp.zeros((rows, LEAF), F32)
    for k in range(nset):
        pts_ref = s_refs[k * (1 + nchunk)]
        chunks = s_refs[k * (1 + nchunk) + 1 : (k + 1) * (1 + nchunk)]
        for leaf in range(2):
            cols = slice(leaf * LEAF, (leaf + 1) * LEAF)
            j = 2 * k + leaf
            side, off = source_side(pts_ref[:F, cols] * SCALE)
            s_scr[j] = side
            sb_scr[j] = jnp.broadcast_to(off, (LEAF, 128))
            for c in range(nchunk):
                hi, lo = halves(chunks[c][:, cols])
                w_scr[j, c * each : (c + 1) * each, :] = hi
                w_scr[j, rows + c * each : rows + (c + 1) * each, :] = lo

    x, core, group, leaves = pos_ref[0], pos_ref[1], pos_ref[2], pos_ref[3]
    odd = group % 2
    column = []
    for kind in kinds:
        relative = {"own": 1, "pair": 2 - 2 * odd, "next": 2 * odd}[kind]
        column.append(relative * leaves + 2 * (2 * x + core))

    count = jnp.int32(0)
    list_ref[0] = 0
    for t in range(2 * nblk):
        for j in range(2 * nset):
            times = times_ref[(2 * first + t) * 128 + column[j // 2] + j % 2]

            @pl.when(times > 0)
            def _(count=count, t=t, j=j, times=times):
                list_ref[count] = (times * 64 + t) * 8 + j

            count = count + (times > 0).astype(jnp.int32)

    def entry(index):
        code = list_ref[index]
        return (code >> 3) & 63, code & 7, (code >> 9).astype(F32)

    def block(index, slot):
        t, j, _ = entry(jnp.minimum(index, jnp.maximum(count - 1, 0)))
        side = t_scr[t]
        off = tb_scr[t][:1, :]
        for half in range(2):
            part = slice(half * 256, (half + 1) * 256)
            cross = dot(s_scr[j, part, :], side)
            src_off = sb_scr[j, part, :]
            src_off = jnp.concatenate([src_off] * (LEAF // 128), axis=1)
            k_hi, k_lo = halves(jnp.exp2(cross + src_off + off))
            k_scr[slot, part, :] = k_hi
            k_scr[slot, LEAF + half * 256 : LEAF + (half + 1) * 256, :] = k_lo

    def apply(index, slot):
        t, j, factor = entry(index)
        for half in range(2):
            cols = slice(half * 256, (half + 1) * 256)
            both = dot(w_scr[j], k_scr[slot, :LEAF, cols])
            low = dot(w_scr[j, :rows, :], k_scr[slot, LEAF:, cols])
            o_scr[t, :, cols] = o_scr[t, :, cols] + factor * (both[:rows] + both[rows:] + low)

    @pl.when(count > 0)
    def _():
        block(0, 0)

    def pair(index, carry):
        block(2 * index + 1, 1)
        apply(2 * index, 0)

        @pl.when(2 * index + 1 < count)
        def _():
            block(2 * index + 2, 0)
            apply(2 * index + 1, 1)

        return carry

    lax.fori_loop(0, (count + 1) // 2, pair, jnp.int32(0))
    for b in range(nblk):
        for leaf in range(2):
            outs[b][:, leaf * LEAF : (leaf + 1) * LEAF] = o_scr[2 * b + leaf]


def near_call(name, where, targets, first, sources, rows, acc=None, acc_row=None, after=()):
    nblk, nchunk = len(targets), len(next(iter(sources.values()))) - 1
    nset = len(sources)
    cols = 2 * LEAF
    vmem = pl.BlockSpec(memory_space=pltpu.VMEM)
    smem = pl.BlockSpec(memory_space=pltpu.SMEM)
    operands = [a for t in targets for a in t] + [a for s in sources.values() for a in s]
    operands += list(acc) if acc is not None else []
    return pl.pallas_call(
        partial(near_body, nblk, tuple(sources), nchunk, rows, acc_row, first),
        name=name,
        out_shape=[jax.ShapeDtypeStruct((rows, cols), F32)] * nblk,
        in_specs=[smem, smem]
        + [vmem] * len(operands)
        + [pl.BlockSpec(memory_space=pl.ANY)] * len(after),
        out_specs=[vmem] * nblk,
        scratch_shapes=[
            pltpu.VMEM((2 * nblk, 4 * F, LEAF), BF),
            pltpu.VMEM((2 * nblk, 8, LEAF), F32),
            pltpu.VMEM((2 * nset, LEAF, 4 * F), BF),
            pltpu.VMEM((2 * nset, LEAF, 128), F32),
            pltpu.VMEM((2 * nset, 2 * rows, LEAF), BF),
            pltpu.VMEM((2 * nblk, rows, LEAF), F32),
            pltpu.VMEM((2, 2 * LEAF, LEAF), BF),
            pltpu.SMEM((4 * nset * nblk,), jnp.int32),
        ],
        compiler_params=pltpu.CompilerParams(vmem_limit_bytes=VMEM_LIMIT),
    )(*where, *operands, *after)


def share_rows(xs):
    return R // (2 * xs) * SK // (2 * LEAF)


def leaf_body(xs, pos_ref, count_ref, src_ref, pts_ref, w_ref, interp_ref, *refs):
    msgs, scr = refs[:-1], refs[-1]
    total = jnp.zeros((R, SK), F32)
    for leaf in range(2):
        total = total + dot3(w_ref[:, leaf * LEAF : (leaf + 1) * LEAF], interp_ref[leaf])
    scr[...] = total
    x, core, group, leaves = pos_ref[0], pos_ref[1], pos_ref[2], pos_ref[3]
    slots = src_ref.shape[0]
    name = lax.broadcasted_iota(jnp.int32, (slots, 128), 1) + (group - 1) * leaves
    slot = lax.broadcasted_iota(jnp.int32, (slots, 128), 0)
    times = []
    for leaf in range(2):
        hit = (src_ref[:, leaf : leaf + 1] == name) & (slot < count_ref[0, leaf])
        times.append(jnp.sum(hit.astype(F32), axis=0, keepdims=True))
    times = jnp.concatenate(times + [jnp.zeros((EXTRA - 2, 128), F32)], axis=0)
    rows = R // (2 * xs)
    tall = share_rows(xs)
    for n, msg in enumerate(msgs):
        helper = 2 * lax.rem(x + n // 2, xs) + (core if n % 2 == 0 else 1 - core)
        msg[:F, :] = pts_ref[...]
        msg[F : F + EXTRA, :] = jnp.zeros((EXTRA, 2 * LEAF), F32)
        msg[F : F + EXTRA, :128] = times
        for i in range(rows // tall):
            at = pl.multiple_of(helper * rows + i * tall, tall)
            msg[F + EXTRA :, i * SK : (i + 1) * SK] = scr[pl.ds(at, tall), :]


def leaf_call(xs, pos, near_count, near_src, points, weights, interp):
    vmem = pl.BlockSpec(memory_space=pltpu.VMEM)
    smem = pl.BlockSpec(memory_space=pltpu.SMEM)
    height = F + EXTRA + share_rows(xs)
    return pl.pallas_call(
        partial(leaf_body, xs),
        name="leaf_up",
        out_shape=[jax.ShapeDtypeStruct((height, 2 * LEAF), F32)] * (2 * xs),
        in_specs=[smem, smem, vmem, vmem, vmem, vmem],
        out_specs=[vmem] * (2 * xs),
        scratch_shapes=[pltpu.VMEM((R, SK), F32)],
        compiler_params=pltpu.CompilerParams(vmem_limit_bytes=VMEM_LIMIT),
    )(pos, near_count, near_src.T, points, weights, interp)


def skel_body(xs, pos_ref, index_ref, *refs):
    nblk = 2 * xs
    msgs = refs[:nblk]
    out_ref = refs[nblk]
    sides = refs[nblk + 1 :]
    rows = R // nblk
    tall = share_rows(xs)
    total = jnp.zeros((2 * F, SK), F32)
    value = jnp.zeros((tall, 2 * LEAF), F32)
    spot = lax.broadcasted_iota(jnp.int32, (2 * LEAF, SK), 0)
    x, core = pos_ref[0], pos_ref[1]
    for b in range(nblk):
        helper = 2 * lax.rem(x + b // 2, xs) + (core if b % 2 == 0 else 1 - core)
        side, off = target_side(msgs[b][:F, :] * SCALE)
        for leaf in range(2):
            part = slice(leaf * LEAF, (leaf + 1) * LEAF)
            sides[2 * b][leaf] = side[:, part]
            sides[2 * b + 1][leaf] = jnp.broadcast_to(off[:, part], (8, LEAF))
        hot = spot + helper * (2 * LEAF) == index_ref[...]
        total = total + dot(side[: 2 * F], hot.astype(F32).astype(BF))
        value = value + msgs[b][F + EXTRA :, :]
    out_ref[:F, :] = total[:F] + total[F:]
    for i in range(rows // tall):
        out_ref[F + i * tall : F + (i + 1) * tall, :] = value[:, i * SK : (i + 1) * SK]


def skel_call(xs, pos, index, msgs):
    rows = R // (2 * xs)
    nblk = 2 * xs
    vmem = pl.BlockSpec(memory_space=pltpu.VMEM)
    side = [
        jax.ShapeDtypeStruct((2, 4 * F, LEAF), BF),
        jax.ShapeDtypeStruct((2, 8, LEAF), F32),
    ]
    out = pl.pallas_call(
        partial(skel_body, xs),
        name="skeleton",
        out_shape=[jax.ShapeDtypeStruct((F + rows, SK), F32)] + side * nblk,
        in_specs=[pl.BlockSpec(memory_space=pltpu.SMEM)] + [vmem] * (1 + nblk),
        out_specs=[vmem] * (1 + 2 * nblk),
        compiler_params=pltpu.CompilerParams(vmem_limit_bytes=VMEM_LIMIT),
    )(pos, index, *msgs)
    return out[0], [(out[1 + 2 * b], out[2 + 2 * b]) for b in range(nblk)]


def upper_start(level, groups):
    return sum((groups >> step for step in range(1, level)))


def list_start(level, groups):
    return sum((groups >> step for step in range(level)))


def far_body(groups, rows, pos_ref, far_ref, node_ref, transfer_ref, *refs):
    pieces, beside = refs[: groups // 2], refs[groups // 2]
    out_ref, p_scr, u_scr, f_scr = refs[-4:]
    levels = groups.bit_length() - 1
    group = pos_ref[2]
    start = [sum(groups >> step for step in range(level)) for level in range(levels)]
    for n, piece in enumerate(pieces):
        p_scr[2 * n] = piece[:F, :]
        u_scr[2 * n] = piece[F:, :]
        p_scr[2 * n + 1] = beside[n, :F, :]
        u_scr[2 * n + 1] = beside[n, F:, :]
    spot = lax.broadcasted_iota(jnp.int32, (2 * SK, SK), 0)
    for level in range(1, levels):
        bit = (group >> (level - 1)) & 1
        for m in range(groups >> level):
            row = upper_start(level, groups) + (m ^ (group >> level))
            left = start[level - 1] + 2 * m + bit
            right = start[level - 1] + 2 * m + 1 - bit
            hot = (spot == node_ref[row]).astype(F32).astype(BF)
            pts = jnp.concatenate([p_scr[left], p_scr[right]], axis=1)
            hi, lo = halves(pts)
            both = dot(jnp.concatenate([hi, lo], axis=0), hot)
            p_scr[start[level] + m] = both[:F] + both[F:]
            vals = jnp.concatenate([u_scr[left], u_scr[right]], axis=1)
            u_scr[start[level] + m] = dot3(vals, transfer_ref[row])
    for level in range(levels):
        node = group >> level
        side, off = target_side(p_scr[start[level]])
        f_scr[level] = jnp.zeros((rows, SK), F32)

        def one(m, carry, level=level, node=node, side=side, off=off):
            hits = jnp.int32(0)
            for slot in range(FL):
                entry = far_ref[list_start(level, groups) + node, slot]
                hits = hits + (entry == (m ^ node)).astype(jnp.int32)

            @pl.when(hits > 0)
            def _():
                src, src_off = source_side(p_scr[start[level] + m])
                block = jnp.exp2(dot(src, side) + src_off + off)
                term = dot3(u_scr[start[level] + m], block)
                f_scr[level] = f_scr[level] + hits.astype(F32) * term

            return carry

        lax.fori_loop(0, groups >> level, one, jnp.int32(0))
    local = f_scr[levels - 1]
    for level in range(levels - 1, 0, -1):
        row = upper_start(level, groups) + (group >> level)
        bit = (group >> (level - 1)) & 1
        matrix = transfer_ref[row, pl.ds(pl.multiple_of(bit * SK, SK), SK), :]
        local = f_scr[level - 1] + dot3(local, matrix, dot_t)
    out_ref[...] = local


def far_call(groups, pos, far_nodes, skel_node, transfer, pieces, beside, after):
    rows = pieces[0].shape[0] - F
    vmem = pl.BlockSpec(memory_space=pltpu.VMEM)
    smem = pl.BlockSpec(memory_space=pltpu.SMEM)
    nodes = 2 * groups
    return pl.pallas_call(
        partial(far_body, groups, rows),
        name="far",
        out_shape=jax.ShapeDtypeStruct((rows, SK), F32),
        in_specs=[smem, smem, vmem, vmem]
        + [vmem] * (len(pieces) + 1)
        + [pl.BlockSpec(memory_space=pl.ANY)] * len(after),
        out_specs=vmem,
        scratch_shapes=[
            pltpu.VMEM((nodes, F, SK), F32),
            pltpu.VMEM((nodes, rows, SK), F32),
            pltpu.VMEM((groups.bit_length(), rows, SK), F32),
        ],
        compiler_params=pltpu.CompilerParams(vmem_limit_bytes=VMEM_LIMIT),
    )(pos, far_nodes, skel_node[:, None, :], transfer, *pieces, beside, *after)


def final_body(xs, pos_ref, interp_ref, home_ref, mate_ref, *refs):
    values = refs[: 2 * xs]
    out_ref, v_scr = refs[-2:]
    rows = R // (2 * xs)
    x, core = pos_ref[0], pos_ref[1]
    for n, ref in enumerate(values):
        helper = 2 * lax.rem(x + n // 2, xs) + (core if n % 2 == 0 else 1 - core)
        v_scr[pl.ds(pl.multiple_of(helper * rows, rows), rows), :] = ref[...]
    value = v_scr[...]
    for leaf in range(2):
        cols = slice(leaf * LEAF, (leaf + 1) * LEAF)
        total = dot3(value, interp_ref[leaf], dot_t)
        out_ref[:, cols] = total + home_ref[:, cols] + mate_ref[:, cols]


def add_body(value_ref, *refs):
    out_ref = refs[-1]
    rows = R // 2
    count = (len(refs) - 1) // 2
    for c in range(2):
        part = slice(c * rows, (c + 1) * rows)
        total = value_ref[part, :]
        for ref in refs[c * count : (c + 1) * count]:
            total = total + ref[...]
        out_ref[part, :] = total


def add_call(value, parts):
    vmem = pl.BlockSpec(memory_space=pltpu.VMEM)
    operands = [value] + parts[0] + parts[1]
    return pl.pallas_call(
        add_body,
        name="add_parts",
        out_shape=jax.ShapeDtypeStruct(value.shape, F32),
        in_specs=[vmem] * len(operands),
        out_specs=vmem,
        compiler_params=pltpu.CompilerParams(vmem_limit_bytes=VMEM_LIMIT),
    )(*operands)


def final_call(xs, pos, interp, home, mate, values):
    vmem = pl.BlockSpec(memory_space=pltpu.VMEM)
    return pl.pallas_call(
        partial(final_body, xs),
        name="join",
        out_shape=jax.ShapeDtypeStruct((R, 2 * LEAF), F32),
        in_specs=[pl.BlockSpec(memory_space=pltpu.SMEM)] + [vmem] * (3 + 2 * xs),
        out_specs=vmem,
        scratch_shapes=[pltpu.VMEM((R, SK), F32)],
        compiler_params=pltpu.CompilerParams(vmem_limit_bytes=VMEM_LIMIT),
    )(pos, interp, home, mate, *values)


def help_pairs(xs, dx, dc):
    return [
        (2 * ((x + dx) % xs) + (core ^ dc), 2 * x + core) for x in range(xs) for core in range(2)
    ]


def shards(
    points, weights, interp, transfer, near_count, near_src, skel_group, skel_node, far_nodes
):
    helpers = lax.axis_size("help")
    groups = lax.axis_size("leaf")
    xs = helpers // 2
    helper = lax.axis_index("help")
    group = lax.axis_index("leaf")
    x, core = helper // 2, helper % 2
    leaves = 2 * helpers
    pos = jnp.stack([x, core, group, jnp.int32(leaves)]).astype(jnp.int32)
    rows = R // 2

    def from_help(value, dx, dc):
        return lax.ppermute(value, "help", help_pairs(xs, dx, dc))

    def to_help(value, dx):
        return lax.ppermute(value, "help", help_pairs(xs, -dx, 0))

    def together(*values):
        return lax.optimization_barrier(values)

    beside = [(i, i ^ 1) for i in range(groups)]
    across = [(i, i + 2) for i in range(0, groups - 2, 2)]
    across += [(i, i - 2) for i in range(3, groups, 2)]
    order = [(dx, dc) for dx in range(xs) for dc in range(2)]

    pts_y = lax.ppermute(points, "leaf", beside)
    msgs = leaf_call(xs, pos, near_count, near_src, points, weights, interp)
    w_own = [weights[:rows], weights[rows:]]
    got = [lax.ppermute(msgs[n], "help", help_pairs(xs, -dx, dc)) for n, (dx, dc) in enumerate(order) if n]
    w_y = [lax.ppermute(chunk, "leaf", beside) for chunk in w_own]

    pts_y, got = together(pts_y, got)
    pts_z = lax.ppermute(pts_y, "leaf", across)
    blocks = [msgs[0]] + [got[order.index((-dx % xs, dc)) - 1] for dx, dc in order[1:]]
    times = jnp.stack([block[F : F + 2, :128] for block in blocks]).astype(jnp.int32).reshape(-1)
    where = (pos, times)
    payload, targets = skel_call(xs, pos, skel_group, blocks)
    home, away = slice(0, 2), slice(2, None)

    pieces = [payload]
    for mask in range(2, groups, 2):
        pieces.append(lax.ppermute(payload, "leaf", [(i, i ^ mask) for i in range(groups)]))
    n0 = near_call("near_own", where, targets, 0, {"own": (points, *w_own)}, R)
    w_z = [lax.ppermute(w_y[0], "leaf", across)]
    w_y = list(together(*w_y))
    w_z.append(lax.ppermute(w_y[1], "leaf", across))
    pieces, w_y = together(pieces, w_y)
    side = lax.ppermute(jnp.stack(pieces), "leaf", beside)

    n1 = near_call("near_pair", where, targets, 0, {"pair": (pts_y, *w_y)}, R, n0, 0)
    sums = []
    for c in range(2):
        source = {"next": (pts_z, w_z[c])}
        part = near_call(
            "near_next_away", where, targets[away], 2, source, rows, n1[away], c * rows
        )
        kept, given = part[::2], part[1::2]
        sums.append((kept, [from_help(value, 0, 1) for value in given]))
    parts = []
    for c in range(2):
        kept, mates = sums[c]
        if c == 0:
            mates, side, w_z = together(mates, side, w_z)
        both = [k + m for k, m in zip(kept, mates)]
        parts.append([to_help(value, dx + 1) for dx, value in enumerate(both)])
    v_own = far_call(groups, pos, far_nodes, skel_node, transfer, pieces, side, both[:1])
    values = [v_own] + [from_help(v_own, dx, dc) for dx, dc in order[1:]]
    source = {"next": (pts_z, *w_z)}
    n2 = near_call("near_next_home", where, targets[home], 0, source, R, n1[home], 0, [v_own])
    mine = add_call(n2[0], parts)
    return final_call(xs, pos, interp, mine, from_help(n2[1], 0, 1), values)


def solution(mesh):
    placed = (
        P(None, ("leaf", "help")),
        P(None, ("leaf", "help")),
        P(("leaf", "help"), None, None),
        P(),
        P("leaf", "help"),
        P(("leaf", "help"), None),
        P("leaf", None),
        P(),
        P(),
    )
    return jax.shard_map(
        shards, mesh=mesh, in_specs=placed, out_specs=P(None, ("leaf", "help")), check_vma=False
    )
```

```python
import math
from functools import partial

import jax
import jax.numpy as jnp
from jax import lax
from jax.experimental import pallas as pl
from jax.experimental.pallas import tpu as pltpu
from jax.sharding import PartitionSpec as P

F = 64
R = 256
LEAF = 512
SK = 256
FL = 4
EXTRA = 8

BF = jnp.bfloat16
F32 = jnp.float32
LOG2E = 1.0 / math.log(2.0)
SCALE = math.sqrt(0.5 * LOG2E)
BIAS = 0.0625 * F * LOG2E
VMEM_LIMIT = 24 * 1024 * 1024


def dot(a, b):
    return jnp.dot(a, b, preferred_element_type=F32)


def dot_t(a, b):
    return lax.dot_general(a, b, (((1,), (1,)), ((), ())), preferred_element_type=F32)


def halves(x):
    hi = x.astype(BF)
    lo = (x - hi.astype(F32)).astype(BF)
    return hi, lo


def dot3(a, b, mul=dot):
    a_hi, a_lo = halves(a)
    b_hi, b_lo = halves(b)
    return mul(a_hi, b_hi) + mul(a_lo, b_hi) + mul(a_hi, b_lo)


def target_side(x):
    hi, lo = halves(x)
    both = hi.astype(F32) + lo.astype(F32)
    off = BIAS - 0.5 * jnp.sum(both * both, axis=0, keepdims=True)
    return jnp.concatenate([hi, lo, hi, lo], axis=0), off


def source_side(x):
    xt = x.T
    hi, lo = halves(xt)
    both = hi.astype(F32) + lo.astype(F32)
    off = BIAS - 0.5 * jnp.sum(both * both, axis=1, keepdims=True)
    return jnp.concatenate([hi, hi, lo, lo], axis=1), off


def near_body(
    xs, sets, leaves_at, rows, row, has_acc, nout, pos_ref, times_ref, t_ref, tb_ref, *refs
):
    nset = len(sets)
    if has_acc:
        s_scr, sb_scr, w_scr, o_scr, k_scr, times_scr, list_ref = refs[-7:]
        outs = refs[-7 - nout : -7]
    else:
        o_scr, s_scr, sb_scr, w_scr, k_scr, times_scr, list_ref = refs[-7:]
    at = 0
    for k, (_, ready, chunks) in enumerate(sets):
        heads = refs[at : at + 1 + ready]
        parts = refs[at + 1 + ready : at + 1 + ready + chunks]
        at += 1 + ready + chunks
        each = rows // chunks
        for leaf in range(2):
            cols = slice(leaf * LEAF, (leaf + 1) * LEAF)
            j = 2 * k + leaf
            if ready:
                s_scr[j] = heads[0][leaf]
                sb_scr[j] = heads[1][leaf]
            else:
                side, off = source_side(heads[0][:F, cols] * SCALE)
                s_scr[j] = side
                sb_scr[j] = jnp.broadcast_to(off, (LEAF, 128))
            for c in range(chunks):
                hi, lo = halves(parts[c][:, cols])
                w_scr[j, c * each : (c + 1) * each, :] = hi
                w_scr[j, rows + c * each : rows + (c + 1) * each, :] = lo
    start, stop = leaves_at
    for t in range(start, stop):
        if has_acc:
            o_scr[t - start] = refs[at][t, row : row + rows, :]
        else:
            o_scr[t - start] = jnp.zeros((rows, LEAF), F32)

    x, core, group, leaves = pos_ref[0], pos_ref[1], pos_ref[2], pos_ref[3]
    odd = group % 2
    column = []
    for kind, _, _ in sets:
        relative = {"own": 1, "pair": 2 - 2 * odd, "next": 2 * odd}[kind]
        column.append(relative * leaves + 2 * (2 * x + core))

    count = jnp.int32(0)
    list_ref[0] = 0
    times_scr[0] = 0
    for t in range(start, stop):
        for j in range(2 * nset):
            helper = 2 * lax.rem(x + t // 4, xs) + (core if t // 2 % 2 == 0 else 1 - core)
            times = times_ref[(2 * helper + t % 2) * 128 + column[j // 2] + j % 2]

            @pl.when(times > 0)
            def _(count=count, t=t, j=j, times=times):
                list_ref[count] = t * 8 + j
                times_scr[count] = times

            count = count + (times > 0).astype(jnp.int32)

    def block(index, slot):
        code = list_ref[jnp.minimum(index, jnp.maximum(count - 1, 0))]
        t, j = code // 8, code % 8
        side = t_ref[t]
        off = tb_ref[t][:1, :]
        for half in range(2):
            part = slice(half * 256, (half + 1) * 256)
            cross = dot(s_scr[j, part, :], side)
            src_off = sb_scr[j, part, :]
            src_off = jnp.concatenate([src_off] * (LEAF // 128), axis=1)
            k_hi, k_lo = halves(jnp.exp2(cross + src_off + off))
            k_scr[slot, part, :] = k_hi
            k_scr[slot, LEAF + half * 256 : LEAF + (half + 1) * 256, :] = k_lo

    def apply(index, slot):
        code = list_ref[index]
        t, j = code // 8 - start, code % 8
        factor = times_scr[index].astype(F32)
        for half in range(2):
            cols = slice(half * 256, (half + 1) * 256)
            both = dot(w_scr[j], k_scr[slot, :LEAF, cols])
            low = dot(w_scr[j, :rows, :], k_scr[slot, LEAF:, cols])
            o_scr[t, :, cols] = o_scr[t, :, cols] + factor * (both[:rows] + both[rows:] + low)

    @pl.when(count > 0)
    def _():
        block(0, 0)

    def pair(index, carry):
        block(2 * index + 1, 1)
        apply(2 * index, 0)

        @pl.when(2 * index + 1 < count)
        def _():
            block(2 * index + 2, 0)
            apply(2 * index + 1, 1)

        return carry

    lax.fori_loop(0, (count + 1) // 2, pair, jnp.int32(0))
    if has_acc:
        tall = outs[0].shape[0]
        for n, ref in enumerate(outs):
            t, top = 2 * (n // (rows // tall)), n % (rows // tall) * tall
            for leaf in range(2):
                cols = slice(leaf * LEAF, (leaf + 1) * LEAF)
                ref[:, cols] = o_scr[t + leaf, top : top + tall, :]


def near_call(name, where, targets, leaves_at, sources, rows, row=0, acc=None, after=()):
    nset = len(sources)
    start, stop = leaves_at
    tall = R // 2
    vmem = pl.BlockSpec(memory_space=pltpu.VMEM)
    smem = pl.BlockSpec(memory_space=pltpu.SMEM)
    operands = [a for _, heads, chunks in sources for a in (*heads, *chunks)]
    scratch = [
        pltpu.VMEM((2 * nset, LEAF, 4 * F), BF),
        pltpu.VMEM((2 * nset, LEAF, 128), F32),
        pltpu.VMEM((2 * nset, 2 * rows, LEAF), BF),
        pltpu.VMEM((stop - start, rows, LEAF), F32),
        pltpu.VMEM((2, 2 * LEAF, LEAF), BF),
        pltpu.SMEM((2 * nset * (stop - start),), jnp.int32),
        pltpu.SMEM((2 * nset * (stop - start),), jnp.int32),
    ]
    if acc is None:
        out = [jax.ShapeDtypeStruct((stop - start, rows, LEAF), F32)]
        scratch.pop(3)
    else:
        operands.append(acc)
        out = [jax.ShapeDtypeStruct((tall, 2 * LEAF), F32)] * ((stop - start) // 2 * (rows // tall))
    sets = tuple((kind, len(heads) - 1, len(chunks)) for kind, heads, chunks in sources)
    return pl.pallas_call(
        partial(
            near_body, targets[0].shape[0] // 4, sets, leaves_at, rows, row, acc is not None, len(out)
        ),
        name=name,
        out_shape=out,
        in_specs=[smem, smem]
        + [vmem] * (2 + len(operands))
        + [pl.BlockSpec(memory_space=pl.ANY)] * len(after),
        out_specs=[vmem] * len(out),
        scratch_shapes=scratch,
        compiler_params=pltpu.CompilerParams(vmem_limit_bytes=VMEM_LIMIT),
    )(*where, *targets, *operands, *after)


def source_body(pts_ref, side_ref, off_ref):
    for leaf in range(2):
        cols = slice(leaf * LEAF, (leaf + 1) * LEAF)
        side, off = source_side(pts_ref[:, cols] * SCALE)
        side_ref[leaf] = side
        off_ref[leaf] = jnp.broadcast_to(off, (LEAF, 128))


def source_call(pts):
    vmem = pl.BlockSpec(memory_space=pltpu.VMEM)
    return pl.pallas_call(
        source_body,
        name="source_side",
        out_shape=[
            jax.ShapeDtypeStruct((2, LEAF, 4 * F), BF),
            jax.ShapeDtypeStruct((2, LEAF, 128), F32),
        ],
        in_specs=[vmem],
        out_specs=[vmem, vmem],
        compiler_params=pltpu.CompilerParams(vmem_limit_bytes=VMEM_LIMIT),
    )(pts)


def share_rows(xs):
    return R // (2 * xs) * SK // (2 * LEAF)


def leaf_body(xs, pos_ref, count_ref, src_ref, pts_in, w_in, interp_in, *refs):
    msg, pts_ref, w_ref, interp_ref, scr, sems = refs
    copies = [
        pltpu.make_async_copy(pts_in, pts_ref, sems.at[0]),
        pltpu.make_async_copy(w_in, w_ref, sems.at[1]),
        pltpu.make_async_copy(interp_in, interp_ref, sems.at[2]),
    ]
    for copy in copies:
        copy.start()
    group, leaves = pos_ref[2], pos_ref[3]
    lane = lax.broadcasted_iota(jnp.int32, (1, 128), 1) + (group - 1) * leaves
    times = []
    for leaf in range(2):
        row = jnp.zeros((1, 128), F32)
        for slot in range(src_ref.shape[1]):
            name = jnp.where(slot < count_ref[0, leaf], src_ref[leaf, slot], -1 - 128 * leaves)
            row = row + (lane == name).astype(F32)
        times.append(row)
    times = jnp.concatenate(times + [jnp.zeros((EXTRA - 2, 128), F32)], axis=0)
    for copy in copies:
        copy.wait()
    total = jnp.zeros((R, SK), F32)
    for leaf in range(2):
        total = total + dot3(w_ref[:, leaf * LEAF : (leaf + 1) * LEAF], interp_ref[leaf])
    scr[...] = total
    rows = R // (2 * xs)
    tall = share_rows(xs)
    for helper in range(2 * xs):
        msg[helper, :F, :] = pts_ref[...]
        msg[helper, F : F + EXTRA, :] = jnp.zeros((EXTRA, 2 * LEAF), F32)
        msg[helper, F : F + EXTRA, :128] = times
        for i in range(rows // tall):
            at = helper * rows + i * tall
            msg[helper, F + EXTRA :, i * SK : (i + 1) * SK] = scr[at : at + tall, :]


def leaf_call(xs, pos, near_count, near_src, points, weights, interp):
    vmem = pl.BlockSpec(memory_space=pltpu.VMEM)
    smem = pl.BlockSpec(memory_space=pltpu.SMEM)
    anywhere = pl.BlockSpec(memory_space=pl.ANY)
    height = F + EXTRA + share_rows(xs)
    return pl.pallas_call(
        partial(leaf_body, xs),
        name="leaf_up",
        out_shape=jax.ShapeDtypeStruct((2 * xs, height, 2 * LEAF), F32),
        in_specs=[smem, smem, smem, anywhere, anywhere, anywhere],
        out_specs=vmem,
        scratch_shapes=[
            pltpu.VMEM(points.shape, F32),
            pltpu.VMEM(weights.shape, F32),
            pltpu.VMEM(interp.shape, F32),
            pltpu.VMEM((R, SK), F32),
            pltpu.SemaphoreType.DMA((3,)),
        ],
        compiler_params=pltpu.CompilerParams(vmem_limit_bytes=VMEM_LIMIT),
    )(pos, near_count, near_src, points, weights, interp)


def skel_body(xs, pos_ref, index_ref, msgs, out_ref, side_ref, off_ref):
    nblk = 2 * xs
    rows = R // nblk
    tall = share_rows(xs)
    total = jnp.zeros((2 * F, SK), F32)
    value = jnp.zeros((tall, 2 * LEAF), F32)
    spot = lax.broadcasted_iota(jnp.int32, (2 * LEAF, SK), 0)
    x, core = pos_ref[0], pos_ref[1]
    for b in range(nblk):
        helper = 2 * lax.rem(x + b // 2, xs) + (core if b % 2 == 0 else 1 - core)
        side, off = target_side(msgs[helper, :F, :] * SCALE)
        for leaf in range(2):
            part = slice(leaf * LEAF, (leaf + 1) * LEAF)
            side_ref[2 * b + leaf] = side[:, part]
            off_ref[2 * b + leaf] = jnp.broadcast_to(off[:, part], (8, LEAF))
        hot = spot + helper * (2 * LEAF) == index_ref[...]
        total = total + dot(side[: 2 * F], hot.astype(F32).astype(BF))
        value = value + msgs[helper, F + EXTRA :, :]
    out_ref[:F, :] = total[:F] + total[F:]
    for i in range(rows // tall):
        out_ref[F + i * tall : F + (i + 1) * tall, :] = value[:, i * SK : (i + 1) * SK]


def skel_call(xs, pos, index, msgs):
    rows = R // (2 * xs)
    nblk = 2 * xs
    vmem = pl.BlockSpec(memory_space=pltpu.VMEM)
    return pl.pallas_call(
        partial(skel_body, xs),
        name="skeleton",
        out_shape=[
            jax.ShapeDtypeStruct((F + rows, SK), F32),
            jax.ShapeDtypeStruct((2 * nblk, 4 * F, LEAF), BF),
            jax.ShapeDtypeStruct((2 * nblk, 8, LEAF), F32),
        ],
        in_specs=[pl.BlockSpec(memory_space=pltpu.SMEM)] + [vmem] * 2,
        out_specs=[vmem] * 3,
        compiler_params=pltpu.CompilerParams(vmem_limit_bytes=VMEM_LIMIT),
    )(pos, index, msgs)


def upper_start(level, groups):
    return sum((groups >> step for step in range(1, level)))


def list_start(level, groups):
    return sum((groups >> step for step in range(level)))


def far_body(groups, rows, pos_ref, far_ref, node_ref, transfer_ref, *refs):
    pieces, beside = refs[: groups // 2], refs[groups // 2]
    out_ref, p_scr, u_scr, f_scr = refs[-4:]
    levels = groups.bit_length() - 1
    group = pos_ref[2]
    start = [sum(groups >> step for step in range(level)) for level in range(levels)]
    for n, piece in enumerate(pieces):
        p_scr[2 * n] = piece[:F, :]
        u_scr[2 * n] = piece[F:, :]
        p_scr[2 * n + 1] = beside[n, :F, :]
        u_scr[2 * n + 1] = beside[n, F:, :]
    spot = lax.broadcasted_iota(jnp.int32, (2 * SK, SK), 0)
    for level in range(1, levels):
        bit = (group >> (level - 1)) & 1
        for m in range(groups >> level):
            row = upper_start(level, groups) + (m ^ (group >> level))
            left = start[level - 1] + 2 * m + bit
            right = start[level - 1] + 2 * m + 1 - bit
            hot = (spot == node_ref[row]).astype(F32).astype(BF)
            pts = jnp.concatenate([p_scr[left], p_scr[right]], axis=1)
            hi, lo = halves(pts)
            both = dot(jnp.concatenate([hi, lo], axis=0), hot)
            p_scr[start[level] + m] = both[:F] + both[F:]
            vals = jnp.concatenate([u_scr[left], u_scr[right]], axis=1)
            u_scr[start[level] + m] = dot3(vals, transfer_ref[row])
    for level in range(levels):
        node = group >> level
        side, off = target_side(p_scr[start[level]])
        f_scr[level] = jnp.zeros((rows, SK), F32)

        def one(m, carry, level=level, node=node, side=side, off=off):
            hits = jnp.int32(0)
            for slot in range(FL):
                entry = far_ref[list_start(level, groups) + node, slot]
                hits = hits + (entry == (m ^ node)).astype(jnp.int32)

            @pl.when(hits > 0)
            def _():
                src, src_off = source_side(p_scr[start[level] + m])
                block = jnp.exp2(dot(src, side) + src_off + off)
                term = dot3(u_scr[start[level] + m], block)
                f_scr[level] = f_scr[level] + hits.astype(F32) * term

            return carry

        lax.fori_loop(0, groups >> level, one, jnp.int32(0))
    local = f_scr[levels - 1]
    for level in range(levels - 1, 0, -1):
        row = upper_start(level, groups) + (group >> level)
        bit = (group >> (level - 1)) & 1
        matrix = transfer_ref[row, pl.ds(pl.multiple_of(bit * SK, SK), SK), :]
        local = f_scr[level - 1] + dot3(local, matrix, dot_t)
    out_ref[...] = local


def far_call(groups, pos, far_nodes, skel_node, transfer, pieces, beside, after):
    rows = pieces[0].shape[0] - F
    vmem = pl.BlockSpec(memory_space=pltpu.VMEM)
    smem = pl.BlockSpec(memory_space=pltpu.SMEM)
    nodes = 2 * groups
    return pl.pallas_call(
        partial(far_body, groups, rows),
        name="far",
        out_shape=jax.ShapeDtypeStruct((rows, SK), F32),
        in_specs=[smem, smem, vmem, vmem]
        + [vmem] * (len(pieces) + 1)
        + [pl.BlockSpec(memory_space=pl.ANY)] * len(after),
        out_specs=vmem,
        scratch_shapes=[
            pltpu.VMEM((nodes, F, SK), F32),
            pltpu.VMEM((nodes, rows, SK), F32),
            pltpu.VMEM((groups.bit_length(), rows, SK), F32),
        ],
        compiler_params=pltpu.CompilerParams(vmem_limit_bytes=VMEM_LIMIT),
    )(pos, far_nodes, skel_node[:, None, :], transfer, *pieces, beside, *after)


def final_body(xs, pos_ref, interp_ref, *refs):
    values, sums = refs[: 2 * xs], refs[2 * xs : -2]
    out_ref, v_scr = refs[-2:]
    rows = R // (2 * xs)
    x, core = pos_ref[0], pos_ref[1]
    for n, ref in enumerate(values):
        helper = 2 * lax.rem(x + n // 2, xs) + (core if n % 2 == 0 else 1 - core)
        v_scr[pl.ds(pl.multiple_of(helper * rows, rows), rows), :] = ref[...]
    value = v_scr[...]
    for leaf in range(2):
        cols = slice(leaf * LEAF, (leaf + 1) * LEAF)
        total = dot3(value, interp_ref[leaf], dot_t)
        for c in range(2):
            part = slice(c * R // 2, (c + 1) * R // 2)
            out_ref[part, cols] = total[part] + sums[c][:, cols] + sums[2 + c][:, cols]


def add_body(*refs):
    count = (len(refs) - 2) // 2
    for c in range(2):
        total = refs[c * count][...]
        for ref in refs[c * count + 1 : (c + 1) * count]:
            total = total + ref[...]
        refs[c - 2][...] = total


def add_call(home, parts):
    vmem = pl.BlockSpec(memory_space=pltpu.VMEM)
    operands = [home[0], *parts[0], home[1], *parts[1]]
    return pl.pallas_call(
        add_body,
        name="add_parts",
        out_shape=[jax.ShapeDtypeStruct(home[0].shape, F32)] * 2,
        in_specs=[vmem] * len(operands),
        out_specs=[vmem] * 2,
        compiler_params=pltpu.CompilerParams(vmem_limit_bytes=VMEM_LIMIT),
    )(*operands)


def final_call(xs, pos, interp, home, mate, values):
    vmem = pl.BlockSpec(memory_space=pltpu.VMEM)
    return pl.pallas_call(
        partial(final_body, xs),
        name="join",
        out_shape=jax.ShapeDtypeStruct((R, 2 * LEAF), F32),
        in_specs=[pl.BlockSpec(memory_space=pltpu.SMEM)] + [vmem] * (1 + 2 * xs + 4),
        out_specs=vmem,
        scratch_shapes=[pltpu.VMEM((R, SK), F32)],
        compiler_params=pltpu.CompilerParams(vmem_limit_bytes=VMEM_LIMIT),
    )(pos, interp, *values, *home, *mate)


def help_pairs(xs, dx, dc):
    return [
        (2 * ((x + dx) % xs) + (core ^ dc), 2 * x + core) for x in range(xs) for core in range(2)
    ]


def shards(
    points, weights, interp, transfer, near_count, near_src, skel_group, skel_node, far_nodes
):
    helpers = lax.axis_size("help")
    groups = lax.axis_size("leaf")
    xs = helpers // 2
    helper = lax.axis_index("help")
    group = lax.axis_index("leaf")
    x, core = helper // 2, helper % 2
    leaves = 2 * helpers
    pos = jnp.stack([x, core, group, jnp.int32(leaves)]).astype(jnp.int32)
    rows = R // 2

    def from_help(value, dx, dc):
        return lax.ppermute(value, "help", help_pairs(xs, dx, dc))

    def to_help(value, dx):
        return lax.ppermute(value, "help", help_pairs(xs, -dx, 0))

    def together(*values):
        return lax.optimization_barrier(values)

    beside = [(i, i ^ 1) for i in range(groups)]
    across = [(i, i + 2) for i in range(0, groups - 2, 2)]
    across += [(i, i - 2) for i in range(3, groups, 2)]
    order = [(dx, dc) for dx in range(xs) for dc in range(2)]

    pts_y = lax.ppermute(points, "leaf", beside)
    w_own = [weights[:rows], weights[rows:]]
    w_y = [lax.ppermute(chunk, "leaf", beside) for chunk in w_own]
    msgs = leaf_call(xs, pos, near_count, near_src, points, weights, interp)
    got = lax.all_to_all(msgs, "help", 0, 0)
    pts_z = lax.ppermute(pts_y, "leaf", across)
    pts_z, w_y[0] = together(pts_z, w_y[0])
    w_z = [lax.ppermute(w_y[0], "leaf", across)]
    got, w_y = together(got, w_y)
    w_z.append(lax.ppermute(w_y[1], "leaf", across))

    times = got[:, F : F + 2, :128].astype(jnp.int32).reshape(-1)
    where = (pos, times)
    payload, *targets = skel_call(xs, pos, skel_group, got)
    pieces = [payload]
    for mask in range(2, groups, 2):
        pieces.append(lax.ppermute(payload, "leaf", [(i, i ^ mask) for i in range(groups)]))

    sources = [("own", (points,), w_own), ("pair", (pts_y,), w_y)]
    (near,) = near_call("near_own_pair", where, targets, (0, 2 * helpers), sources, R)
    z_side = source_call(pts_z)
    sums, part = [], []
    for c in range(2):
        part = near_call(
            "near_next_away", where, targets, (4, 2 * helpers), [("next", z_side, w_z[c : c + 1])],
            rows, c * rows, near, part[:1],
        )
        kept, given = part[::2], part[1::2]
        sums.append((kept, [from_help(value, 0, 1) for value in given]))
    pieces, part = together(pieces, part)
    side = lax.ppermute(jnp.stack(pieces), "leaf", beside)
    parts = []
    for c in range(2):
        kept, mates = sums[c]
        if c == 0:
            mates, pieces = together(mates, pieces)
        both = [k + m for k, m in zip(kept, mates)]
        parts.append([to_help(value, dx + 1) for dx, value in enumerate(both)])
    v_own = far_call(groups, pos, far_nodes, skel_node, transfer, pieces, side, both[:1])
    values = [v_own] + [from_help(v_own, dx, dc) for dx, dc in order[1:]]
    home = near_call(
        "near_next_home", where, targets, (0, 4), [("next", z_side, w_z)], R, 0, near, [v_own]
    )
    mate = [from_help(value, 0, 1) for value in home[2:]]
    return final_call(xs, pos, interp, add_call(home[:2], parts), mate, values)


def solution(mesh):
    placed = (
        P(None, ("leaf", "help")),
        P(None, ("leaf", "help")),
        P(("leaf", "help"), None, None),
        P(),
        P("leaf", "help"),
        P(("leaf", "help"), None),
        P("leaf", None),
        P(),
        P(),
    )
    return jax.shard_map(
        shards, mesh=mesh, in_specs=placed, out_specs=P(None, ("leaf", "help")), check_vma=False
    )
```

```python
import math
from functools import partial

import jax
import jax.numpy as jnp
from jax import lax
from jax.experimental import pallas as pl
from jax.experimental.pallas import tpu as pltpu
from jax.sharding import PartitionSpec as P

F = 64
R = 256
LEAF = 512
SK = 256
FL = 4
EXTRA = 8

BF = jnp.bfloat16
F32 = jnp.float32
LOG2E = 1.0 / math.log(2.0)
SCALE = math.sqrt(0.5 * LOG2E)
BIAS = 0.0625 * F * LOG2E
VMEM_LIMIT = 24 * 1024 * 1024


def dot(a, b):
    return jnp.dot(a, b, preferred_element_type=F32)


def dot_t(a, b):
    return lax.dot_general(a, b, (((1,), (1,)), ((), ())), preferred_element_type=F32)


def halves(x):
    hi = x.astype(BF)
    lo = (x - hi.astype(F32)).astype(BF)
    return hi, lo


def dot3(a, b, mul=dot):
    a_hi, a_lo = halves(a)
    b_hi, b_lo = halves(b)
    return mul(a_hi, b_hi) + mul(a_lo, b_hi) + mul(a_hi, b_lo)


def target_side(x):
    hi, lo = halves(x)
    both = hi.astype(F32) + lo.astype(F32)
    off = BIAS - 0.5 * jnp.sum(both * both, axis=0, keepdims=True)
    return jnp.concatenate([hi, lo, hi, lo], axis=0), off


def source_side(x):
    xt = x.T
    hi, lo = halves(xt)
    both = hi.astype(F32) + lo.astype(F32)
    off = BIAS - 0.5 * jnp.sum(both * both, axis=1, keepdims=True)
    return jnp.concatenate([hi, hi, lo, lo], axis=1), off


def near_body(
    xs, sets, leaves_at, rows, row, nacc, nout, pos_ref, got_ref, t_ref, tb_ref, *refs
):
    nset = len(sets)
    if nacc:
        s_scr, sb_scr, w_scr, o_scr, k_scr, times_scr, list_ref, times_ref, sem = refs[-9:]
        outs = refs[-9 - nout : -9]
    else:
        o_scr, s_scr, sb_scr, w_scr, k_scr, times_scr, list_ref, times_ref, sem = refs[-9:]
    copy = pltpu.make_async_copy(got_ref.at[:, F : F + EXTRA, :128], times_ref, sem)
    copy.start()
    at = 0
    for k, (_, ready, chunks) in enumerate(sets):
        heads = refs[at : at + 1 + ready]
        parts = refs[at + 1 + ready : at + 1 + ready + chunks]
        at += 1 + ready + chunks
        each = rows // chunks
        for leaf in range(2):
            cols = slice(leaf * LEAF, (leaf + 1) * LEAF)
            j = 2 * k + leaf
            if ready:
                s_scr[j] = heads[0][leaf]
                sb_scr[j] = heads[1][leaf]
            else:
                side, off = source_side(heads[0][:F, cols] * SCALE)
                s_scr[j] = side
                sb_scr[j] = jnp.broadcast_to(off, (LEAF, 128))
            for c in range(chunks):
                hi, lo = halves(parts[c][:, cols])
                w_scr[j, c * each : (c + 1) * each, :] = hi
                w_scr[j, rows + c * each : rows + (c + 1) * each, :] = lo
    start, stop = leaves_at
    for t in range(start, stop):
        if nacc:
            o_scr[t - start] = sum(ref[t, row : row + rows, :] for ref in refs[at : at + nacc])
        else:
            o_scr[t - start] = jnp.zeros((rows, LEAF), F32)

    x, core, group, leaves = pos_ref[0], pos_ref[1], pos_ref[2], pos_ref[3]
    odd = group % 2
    column = []
    for kind, _, _ in sets:
        relative = {"own": 1, "pair": 2 - 2 * odd, "next": 2 * odd}[kind]
        column.append(relative * leaves + 2 * (2 * x + core))

    copy.wait()
    count = jnp.int32(0)
    list_ref[0] = 0
    for t in range(start, stop):
        for j in range(2 * nset):
            helper = 2 * lax.rem(x + t // 4, xs) + (core if t // 2 % 2 == 0 else 1 - core)
            times = times_ref[helper, t % 2, column[j // 2] + j % 2]

            @pl.when(times > 0)
            def _(count=count, t=t, j=j, times=times):
                list_ref[count] = t * 8 + j
                times_scr[count] = times

            count = count + (times > 0).astype(jnp.int32)

    def block(index, slot):
        code = list_ref[jnp.minimum(index, jnp.maximum(count - 1, 0))]
        t, j = code // 8, code % 8
        side = t_ref[t]
        off = tb_ref[t][:1, :]
        for half in range(2):
            part = slice(half * 256, (half + 1) * 256)
            cross = dot(s_scr[j, part, :], side)
            src_off = sb_scr[j, part, :]
            src_off = jnp.concatenate([src_off] * (LEAF // 128), axis=1)
            k_hi, k_lo = halves(jnp.exp2(cross + src_off + off))
            k_scr[slot, part, :] = k_hi
            k_scr[slot, LEAF + half * 256 : LEAF + (half + 1) * 256, :] = k_lo

    def apply(index, slot):
        code = list_ref[index]
        t, j = code // 8 - start, code % 8
        factor = times_scr[index]
        for half in range(2):
            cols = slice(half * 256, (half + 1) * 256)
            both = dot(w_scr[j], k_scr[slot, :LEAF, cols])
            low = dot(w_scr[j, :rows, :], k_scr[slot, LEAF:, cols])
            o_scr[t, :, cols] = o_scr[t, :, cols] + factor * (both[:rows] + both[rows:] + low)

    @pl.when(count > 0)
    def _():
        block(0, 0)

    def pair(index, carry):
        block(2 * index + 1, 1)
        apply(2 * index, 0)

        @pl.when(2 * index + 1 < count)
        def _():
            block(2 * index + 2, 0)
            apply(2 * index + 1, 1)

        return carry

    lax.fori_loop(0, (count + 1) // 2, pair, jnp.int32(0))
    if nacc:
        tall = outs[0].shape[0]
        for n, ref in enumerate(outs):
            t, top = 2 * (n // (rows // tall)), n % (rows // tall) * tall
            for leaf in range(2):
                cols = slice(leaf * LEAF, (leaf + 1) * LEAF)
                ref[:, cols] = o_scr[t + leaf, top : top + tall, :]


def near_call(name, where, targets, leaves_at, sources, rows, row=0, acc=(), after=()):
    nset = len(sources)
    start, stop = leaves_at
    tall = R // 2
    vmem = pl.BlockSpec(memory_space=pltpu.VMEM)
    smem = pl.BlockSpec(memory_space=pltpu.SMEM)
    operands = [a for _, heads, chunks in sources for a in (*heads, *chunks)]
    scratch = [
        pltpu.VMEM((2 * nset, LEAF, 4 * F), BF),
        pltpu.VMEM((2 * nset, LEAF, 128), F32),
        pltpu.VMEM((2 * nset, 2 * rows, LEAF), BF),
        pltpu.VMEM((stop - start, rows, LEAF), F32),
        pltpu.VMEM((2, 2 * LEAF, LEAF), BF),
        pltpu.SMEM((2 * nset * (stop - start),), F32),
        pltpu.SMEM((2 * nset * (stop - start),), jnp.int32),
        pltpu.SMEM((where[1].shape[0], EXTRA, 128), F32),
        pltpu.SemaphoreType.DMA,
    ]
    if not acc:
        out = [jax.ShapeDtypeStruct((stop - start, rows, LEAF), F32)]
        scratch.pop(3)
    else:
        operands += list(acc)
        out = [jax.ShapeDtypeStruct((tall, 2 * LEAF), F32)] * ((stop - start) // 2 * (rows // tall))
    sets = tuple((kind, len(heads) - 1, len(chunks)) for kind, heads, chunks in sources)
    return pl.pallas_call(
        partial(
            near_body, targets[0].shape[0] // 4, sets, leaves_at, rows, row, len(acc), len(out)
        ),
        name=name,
        out_shape=out,
        in_specs=[smem, pl.BlockSpec(memory_space=pl.ANY)]
        + [vmem] * (2 + len(operands))
        + [pl.BlockSpec(memory_space=pl.ANY)] * len(after),
        out_specs=[vmem] * len(out),
        scratch_shapes=scratch,
        compiler_params=pltpu.CompilerParams(vmem_limit_bytes=VMEM_LIMIT),
    )(*where, *targets, *operands, *after)


def source_body(pts_ref, side_ref, off_ref):
    for leaf in range(2):
        cols = slice(leaf * LEAF, (leaf + 1) * LEAF)
        side, off = source_side(pts_ref[:, cols] * SCALE)
        side_ref[leaf] = side
        off_ref[leaf] = jnp.broadcast_to(off, (LEAF, 128))


def source_call(pts):
    vmem = pl.BlockSpec(memory_space=pltpu.VMEM)
    return pl.pallas_call(
        source_body,
        name="source_side",
        out_shape=[
            jax.ShapeDtypeStruct((2, LEAF, 4 * F), BF),
            jax.ShapeDtypeStruct((2, LEAF, 128), F32),
        ],
        in_specs=[vmem],
        out_specs=[vmem, vmem],
        compiler_params=pltpu.CompilerParams(vmem_limit_bytes=VMEM_LIMIT),
    )(pts)


def share_rows(xs):
    return R // (2 * xs) * SK // (2 * LEAF)


def leaf_body(xs, pos_ref, count_ref, src_ref, pts_in, w_in, interp_in, *refs):
    msg, pts_ref, w_ref, interp_ref, scr, sems = refs
    copies = [
        pltpu.make_async_copy(pts_in, pts_ref, sems.at[0]),
        pltpu.make_async_copy(w_in, w_ref, sems.at[1]),
        pltpu.make_async_copy(interp_in, interp_ref, sems.at[2]),
    ]
    for copy in copies:
        copy.start()
    group, leaves = pos_ref[2], pos_ref[3]
    lane = lax.broadcasted_iota(jnp.int32, (1, 128), 1) + (group - 1) * leaves
    times = []
    for leaf in range(2):
        row = jnp.zeros((1, 128), F32)
        for slot in range(src_ref.shape[1]):
            name = jnp.where(slot < count_ref[0, leaf], src_ref[leaf, slot], -1 - 128 * leaves)
            row = row + (lane == name).astype(F32)
        times.append(row)
    times = jnp.concatenate(times + [jnp.zeros((EXTRA - 2, 128), F32)], axis=0)
    for copy in copies:
        copy.wait()
    total = jnp.zeros((R, SK), F32)
    for leaf in range(2):
        total = total + dot3(w_ref[:, leaf * LEAF : (leaf + 1) * LEAF], interp_ref[leaf])
    scr[...] = total
    rows = R // (2 * xs)
    tall = share_rows(xs)
    for helper in range(2 * xs):
        msg[helper, :F, :] = pts_ref[...]
        msg[helper, F : F + EXTRA, :] = jnp.zeros((EXTRA, 2 * LEAF), F32)
        msg[helper, F : F + EXTRA, :128] = times
        for i in range(rows // tall):
            at = helper * rows + i * tall
            msg[helper, F + EXTRA :, i * SK : (i + 1) * SK] = scr[at : at + tall, :]


def leaf_call(xs, pos, near_count, near_src, points, weights, interp):
    vmem = pl.BlockSpec(memory_space=pltpu.VMEM)
    smem = pl.BlockSpec(memory_space=pltpu.SMEM)
    hbm = pl.BlockSpec(memory_space=pltpu.HBM)
    height = F + EXTRA + share_rows(xs)
    return pl.pallas_call(
        partial(leaf_body, xs),
        name="leaf_up",
        out_shape=jax.ShapeDtypeStruct((2 * xs, height, 2 * LEAF), F32),
        in_specs=[smem, smem, smem, hbm, hbm, hbm],
        out_specs=vmem,
        scratch_shapes=[
            pltpu.VMEM(points.shape, F32),
            pltpu.VMEM(weights.shape, F32),
            pltpu.VMEM(interp.shape, F32),
            pltpu.VMEM((R, SK), F32),
            pltpu.SemaphoreType.DMA((3,)),
        ],
        compiler_params=pltpu.CompilerParams(vmem_limit_bytes=VMEM_LIMIT),
    )(pos, near_count, near_src, points, weights, interp)


def skel_body(xs, pos_ref, index_ref, msgs, out_ref, side_ref, off_ref):
    nblk = 2 * xs
    rows = R // nblk
    tall = share_rows(xs)
    total = jnp.zeros((2 * F, SK), F32)
    value = jnp.zeros((tall, 2 * LEAF), F32)
    spot = lax.broadcasted_iota(jnp.int32, (2 * LEAF, SK), 0)
    x, core = pos_ref[0], pos_ref[1]
    for b in range(nblk):
        helper = 2 * lax.rem(x + b // 2, xs) + (core if b % 2 == 0 else 1 - core)
        side, off = target_side(msgs[helper, :F, :] * SCALE)
        for leaf in range(2):
            part = slice(leaf * LEAF, (leaf + 1) * LEAF)
            side_ref[2 * b + leaf] = side[:, part]
            off_ref[2 * b + leaf] = jnp.broadcast_to(off[:, part], (8, LEAF))
        hot = spot + helper * (2 * LEAF) == index_ref[...]
        total = total + dot(side[: 2 * F], hot.astype(F32).astype(BF))
        value = value + msgs[helper, F + EXTRA :, :]
    for n in range(out_ref.shape[0]):
        out_ref[n, :F, :] = total[:F] + total[F:]
        for i in range(rows // tall):
            part = slice(F + i * tall, F + (i + 1) * tall)
            out_ref[n, part, :] = value[:, i * SK : (i + 1) * SK]


def skel_call(xs, copies, pos, index, msgs):
    rows = R // (2 * xs)
    nblk = 2 * xs
    vmem = pl.BlockSpec(memory_space=pltpu.VMEM)
    return pl.pallas_call(
        partial(skel_body, xs),
        name="skeleton",
        out_shape=[
            jax.ShapeDtypeStruct((copies, F + rows, SK), F32),
            jax.ShapeDtypeStruct((2 * nblk, 4 * F, LEAF), BF),
            jax.ShapeDtypeStruct((2 * nblk, 8, LEAF), F32),
        ],
        in_specs=[pl.BlockSpec(memory_space=pltpu.SMEM)] + [vmem] * 2,
        out_specs=[vmem] * 3,
        compiler_params=pltpu.CompilerParams(vmem_limit_bytes=VMEM_LIMIT),
    )(pos, index, msgs)


def upper_start(level, groups):
    return sum((groups >> step for step in range(1, level)))


def list_start(level, groups):
    return sum((groups >> step for step in range(level)))


def far_body(groups, rows, pos_ref, far_ref, node_ref, transfer_ref, alike_ref, beside_ref, *refs):
    out_ref, p_scr, u_scr, f_scr = refs[-4:]
    levels = groups.bit_length() - 1
    group = pos_ref[2]
    odd = group % 2
    start = [list_start(level, groups) for level in range(levels)]
    for n in range(groups // 2):
        p_scr[2 * n + odd] = alike_ref[n, :F, :]
        u_scr[2 * n + odd] = alike_ref[n, F:, :]
        p_scr[2 * n + 1 - odd] = beside_ref[n, :F, :]
        u_scr[2 * n + 1 - odd] = beside_ref[n, F:, :]
    spot = lax.broadcasted_iota(jnp.int32, (2 * SK, SK), 0)
    for level in range(1, levels):
        for n in range(groups >> level):
            row = upper_start(level, groups) + n
            left = start[level - 1] + 2 * n
            hot = (spot == node_ref[row]).astype(F32).astype(BF)
            hi, lo = halves(jnp.concatenate([p_scr[left], p_scr[left + 1]], axis=1))
            both = dot(jnp.concatenate([hi, lo], axis=0), hot)
            p_scr[start[level] + n] = both[:F] + both[F:]
            vals = jnp.concatenate([u_scr[left], u_scr[left + 1]], axis=1)
            u_scr[start[level] + n] = dot3(vals, transfer_ref[row])
    for level in range(levels):
        node = group >> level
        side, off = target_side(p_scr[start[level] + node])
        f_scr[level] = jnp.zeros((rows, SK), F32)

        def one(n, carry, level=level, node=node, side=side, off=off):
            hits = jnp.int32(0)
            for slot in range(FL):
                hits = hits + (far_ref[slot, start[level] + node] == n).astype(jnp.int32)

            @pl.when(hits > 0)
            def _():
                src, src_off = source_side(p_scr[start[level] + n])
                block = jnp.exp2(dot(src, side) + src_off + off)
                term = dot3(u_scr[start[level] + n], block)
                f_scr[level] = f_scr[level] + hits.astype(F32) * term

            return carry

        lax.fori_loop(0, groups >> level, one, jnp.int32(0))
    local = f_scr[levels - 1]
    for level in range(levels - 1, 0, -1):
        row = upper_start(level, groups) + (group >> level)
        bit = (group >> (level - 1)) & 1
        matrix = transfer_ref[row, pl.ds(pl.multiple_of(bit * SK, SK), SK), :]
        local = f_scr[level - 1] + dot3(local, matrix, dot_t)
    out_ref[...] = local


def far_call(groups, pos, far_nodes, skel_node, transfer, alike, beside, after):
    rows = alike.shape[1] - F
    vmem = pl.BlockSpec(memory_space=pltpu.VMEM)
    smem = pl.BlockSpec(memory_space=pltpu.SMEM)
    nodes = 2 * groups
    return pl.pallas_call(
        partial(far_body, groups, rows),
        name="far",
        out_shape=jax.ShapeDtypeStruct((rows, SK), F32),
        in_specs=[smem, smem, vmem, vmem, vmem, vmem]
        + [pl.BlockSpec(memory_space=pl.ANY)] * len(after),
        out_specs=vmem,
        scratch_shapes=[
            pltpu.VMEM((nodes, F, SK), F32),
            pltpu.VMEM((nodes, rows, SK), F32),
            pltpu.VMEM((groups.bit_length(), rows, SK), F32),
        ],
        compiler_params=pltpu.CompilerParams(vmem_limit_bytes=VMEM_LIMIT),
    )(pos, far_nodes.T, skel_node[:, None, :], transfer, alike, beside, *after)


def final_body(xs, pos_ref, interp_ref, *refs):
    values, sums = refs[: 2 * xs], refs[2 * xs : -2]
    out_ref, v_scr = refs[-2:]
    rows = R // (2 * xs)
    x, core = pos_ref[0], pos_ref[1]
    for n, ref in enumerate(values):
        helper = 2 * lax.rem(x + n // 2, xs) + (core if n % 2 == 0 else 1 - core)
        v_scr[pl.ds(pl.multiple_of(helper * rows, rows), rows), :] = ref[...]
    value = v_scr[...]
    for leaf in range(2):
        cols = slice(leaf * LEAF, (leaf + 1) * LEAF)
        total = dot3(value, interp_ref[leaf], dot_t)
        for c in range(2):
            part = slice(c * R // 2, (c + 1) * R // 2)
            out_ref[part, cols] = total[part] + sums[c][:, cols] + sums[2 + c][:, cols]


def add_body(count, *refs):
    for n, out_ref in enumerate(refs[-(len(refs) // (count + 1)) :]):
        total = refs[n * count][...]
        for ref in refs[n * count + 1 : (n + 1) * count]:
            total = total + ref[...]
        out_ref[...] = total


def add_call(*sums):
    vmem = pl.BlockSpec(memory_space=pltpu.VMEM)
    operands = [value for terms in sums for value in terms]
    return pl.pallas_call(
        partial(add_body, len(sums[0])),
        name="add_parts",
        out_shape=[jax.ShapeDtypeStruct(sums[0][0].shape, F32)] * len(sums),
        in_specs=[vmem] * len(operands),
        out_specs=[vmem] * len(sums),
        compiler_params=pltpu.CompilerParams(vmem_limit_bytes=VMEM_LIMIT),
    )(*operands)


def final_call(xs, pos, interp, home, mate, values):
    vmem = pl.BlockSpec(memory_space=pltpu.VMEM)
    return pl.pallas_call(
        partial(final_body, xs),
        name="join",
        out_shape=jax.ShapeDtypeStruct((R, 2 * LEAF), F32),
        in_specs=[pl.BlockSpec(memory_space=pltpu.SMEM)] + [vmem] * (1 + 2 * xs + 4),
        out_specs=vmem,
        scratch_shapes=[pltpu.VMEM((R, SK), F32)],
        compiler_params=pltpu.CompilerParams(vmem_limit_bytes=VMEM_LIMIT),
    )(pos, interp, *values, *home, *mate)


def help_pairs(xs, dx, dc):
    return [
        (2 * ((x + dx) % xs) + (core ^ dc), 2 * x + core) for x in range(xs) for core in range(2)
    ]


def shards(
    points, weights, interp, transfer, near_count, near_src, skel_group, skel_node, far_nodes
):
    helpers = lax.axis_size("help")
    groups = lax.axis_size("leaf")
    xs = helpers // 2
    helper = lax.axis_index("help")
    group = lax.axis_index("leaf")
    x, core = helper // 2, helper % 2
    leaves = 2 * helpers
    pos = jnp.stack([x, core, group, jnp.int32(leaves)]).astype(jnp.int32)
    rows = R // 2

    def from_help(value, dx, dc):
        return lax.ppermute(value, "help", help_pairs(xs, dx, dc))

    def to_help(value, dx):
        return lax.ppermute(value, "help", help_pairs(xs, -dx, 0))

    def together(*values):
        return lax.optimization_barrier(values)

    beside = [(i, i ^ 1) for i in range(groups)]
    across = [(i, i + 2) for i in range(0, groups - 2, 2)]
    across += [(i, i - 2) for i in range(3, groups, 2)]
    order = [(dx, dc) for dx in range(xs) for dc in range(2)]

    pts_y = lax.ppermute(points, "leaf", beside)
    w_y = [lax.ppermute(weights[c * rows : (c + 1) * rows], "leaf", beside) for c in range(2)]
    msgs = leaf_call(xs, pos, near_count, near_src, points, weights, interp)
    got = lax.all_to_all(msgs, "help", 0, 0)
    pts_z = lax.ppermute(pts_y, "leaf", across)

    payload, *targets = skel_call(xs, groups // 2, pos, skel_group, got)
    where = (pos, got)
    parity = [[n for n in range(groups) if n % 2 == odd] for odd in range(2)]
    alike = lax.all_to_all(payload, "leaf", 0, 0, axis_index_groups=parity)
    pts_z, w_y[0] = together(pts_z, w_y[0])
    w_z = [lax.ppermute(w_y[0], "leaf", across)]
    (own,) = near_call(
        "near_own", where, targets, (0, 2 * helpers), [("own", (points,), [weights])], R
    )
    own, w_y[1] = together(own, w_y[1])
    w_z.append(lax.ppermute(w_y[1], "leaf", across))
    z_side = source_call(pts_z)
    alike, w_y[1] = together(alike, w_y[1])
    side = lax.ppermute(alike, "leaf", beside)
    (pair,) = near_call(
        "near_pair", where, targets, (0, 2 * helpers), [("pair", (pts_y,), w_y)], R
    )

    sums, part = [], []
    for c in range(2):
        part = near_call(
            "near_next_away", where, targets, (4, 2 * helpers), [("next", z_side, w_z[c : c + 1])],
            rows, c * rows, (own, pair), part[:1],
        )
        kept, given = part[::2], part[1::2]
        sums.append((kept, [from_help(value, 0, 1) for value in given]))
    parts = []
    for c in range(2):
        kept, mates = sums[c]
        if c == 0:
            mates, side = together(mates, side)
        both = add_call(*zip(kept, mates))
        parts.append([to_help(value, dx + 1) for dx, value in enumerate(both)])
    v_own = far_call(groups, pos, far_nodes, skel_node, transfer, alike, side, both[:1])
    values = [v_own] + [from_help(v_own, dx, dc) for dx, dc in order[1:]]
    home = near_call(
        "near_next_home", where, targets, (0, 4), [("next", z_side, w_z)], R, 0, (own, pair), [v_own]
    )
    mate = [from_help(value, 0, 1) for value in home[2:]]
    mine = add_call(*[[home[c], *parts[c]] for c in range(2)])
    return final_call(xs, pos, interp, mine, mate, values)


def solution(mesh):
    placed = (
        P(None, ("leaf", "help")),
        P(None, ("leaf", "help")),
        P(("leaf", "help"), None, None),
        P(),
        P("leaf", "help"),
        P(("leaf", "help"), None),
        P("leaf", None),
        P(),
        P(),
    )
    return jax.shard_map(
        shards, mesh=mesh, in_specs=placed, out_specs=P(None, ("leaf", "help")), check_vma=False
    )
```

```python
import math
from functools import partial

import jax
import jax.numpy as jnp
from jax import lax
from jax.experimental import pallas as pl
from jax.experimental.pallas import tpu as pltpu
from jax.sharding import PartitionSpec as P

F = 64
R = 256
LEAF = 512
SK = 256
FL = 4
EXTRA = 8

BF = jnp.bfloat16
F32 = jnp.float32
LOG2E = 1.0 / math.log(2.0)
SCALE = math.sqrt(0.5 * LOG2E)
BIAS = 0.0625 * F * LOG2E
VMEM_LIMIT = 64 * 1024 * 1024


def dot(a, b):
    return jnp.dot(a, b, preferred_element_type=F32)


def dot_t(a, b):
    return lax.dot_general(a, b, (((1,), (1,)), ((), ())), preferred_element_type=F32)


def halves(x):
    hi = x.astype(BF)
    lo = (x - hi.astype(F32)).astype(BF)
    return hi, lo


def dot3(a, b, mul=dot):
    a_hi, a_lo = halves(a)
    b_hi, b_lo = halves(b)
    return mul(a_hi, b_hi) + mul(a_lo, b_hi) + mul(a_hi, b_lo)


def target_side(x):
    hi, lo = halves(x)
    both = hi.astype(F32) + lo.astype(F32)
    off = BIAS - 0.5 * jnp.sum(both * both, axis=0, keepdims=True)
    return jnp.concatenate([hi, lo, hi, lo], axis=0), off


def source_side(x):
    xt = x.T
    hi, lo = halves(xt)
    both = hi.astype(F32) + lo.astype(F32)
    off = BIAS - 0.5 * jnp.sum(both * both, axis=1, keepdims=True)
    return jnp.concatenate([hi, hi, lo, lo], axis=1), off


def near_body(xs, sets, blocks_at, rows, row, nacc, nout, pos_ref, *refs):
    nset = len(sets)
    first, last = blocks_at
    nblk = last - first
    msgs, refs = refs[:nblk], refs[nblk:]
    tp_scr, sp_scr, wf_scr, t_scr, tb_scr, s_scr, sb_scr, w_scr, k_scr = refs[-13:-4]
    times_ref, times_scr, list_ref, sems = refs[-4:]
    outs = refs[-13 - (2 if nacc else 0) - nout : -13 - (2 if nacc else 0)]
    o_scr, acc_scr = refs[-15:-13] if nacc else (outs[0], None)
    copies = []

    def fetch(source, target):
        copies.append(pltpu.make_async_copy(source, target, sems.at[len(copies)]))
        copies[-1].start()
        return copies[-1]

    counts = [fetch(msgs[b].at[F : F + EXTRA, :128], times_ref.at[b]) for b in range(nblk)]
    at = 0
    heads, parts = [], []
    for k, (_, chunks) in enumerate(sets):
        each = rows // chunks
        heads.append(fetch(refs[at], sp_scr.at[k]))
        parts.append((refs[at + 1 : at + 1 + chunks], each))
        at += 1 + chunks
    targets = [fetch(msgs[b].at[:F, :], tp_scr.at[b]) for b in range(nblk)]
    weights = [
        [fetch(ref, wf_scr.at[k, c * each : (c + 1) * each, :]) for c, ref in enumerate(chunks)]
        for k, (chunks, each) in enumerate(parts)
    ]
    accs = [
        fetch(refs[at + n].at[2 * first : 2 * last, row : row + rows, :], acc_scr.at[n])
        for n in range(nacc)
    ]

    x, core, group, leaves = pos_ref[0], pos_ref[1], pos_ref[2], pos_ref[3]
    odd = group % 2
    column = []
    for kind, _ in sets:
        relative = {"own": 1, "pair": 2 - 2 * odd, "next": 2 * odd}[kind]
        column.append(relative * leaves + 2 * (2 * x + core))
    for copy in counts:
        copy.wait()
    count = jnp.int32(0)
    list_ref[0] = 0
    for t in range(2 * nblk):
        for j in range(2 * nset):
            times = times_ref[t // 2, t % 2, column[j // 2] + j % 2]

            @pl.when(times > 0)
            def _(count=count, t=t, j=j, times=times):
                list_ref[count] = t * 8 + j
                times_scr[count] = times

            count = count + (times > 0).astype(jnp.int32)

    for k in range(nset):
        heads[k].wait()
        for leaf in range(2):
            cols = slice(leaf * LEAF, (leaf + 1) * LEAF)
            side, off = source_side(sp_scr[k, :, cols] * SCALE)
            s_scr[2 * k + leaf] = side
            sb_scr[2 * k + leaf] = jnp.broadcast_to(off, (LEAF, 128))
    for b in range(nblk):
        targets[b].wait()
        for leaf in range(2):
            side, off = target_side(tp_scr[b, :, leaf * LEAF : (leaf + 1) * LEAF] * SCALE)
            t_scr[2 * b + leaf] = side
            tb_scr[2 * b + leaf] = jnp.broadcast_to(off, (8, LEAF))
    for t in range(2 * nblk):
        o_scr[t] = jnp.zeros((rows, LEAF), F32)
    for k in range(nset):
        for copy in weights[k]:
            copy.wait()
        for leaf in range(2):
            hi, lo = halves(wf_scr[k, :, leaf * LEAF : (leaf + 1) * LEAF])
            w_scr[2 * k + leaf, :rows, :] = hi
            w_scr[2 * k + leaf, rows:, :] = lo

    def block(index, slot):
        code = list_ref[jnp.minimum(index, jnp.maximum(count - 1, 0))]
        t, j = code // 8, code % 8
        side = t_scr[t]
        off = tb_scr[t][:1, :]
        for half in range(2):
            part = slice(half * 256, (half + 1) * 256)
            cross = dot(s_scr[j, part, :], side)
            src_off = sb_scr[j, part, :]
            src_off = jnp.concatenate([src_off] * (LEAF // 128), axis=1)
            k_hi, k_lo = halves(jnp.exp2(cross + src_off + off))
            k_scr[slot, part, :] = k_hi
            k_scr[slot, LEAF + half * 256 : LEAF + (half + 1) * 256, :] = k_lo

    def apply(index, slot):
        code = list_ref[index]
        t, j = code // 8, code % 8
        factor = times_scr[index]
        for half in range(2):
            cols = slice(half * 256, (half + 1) * 256)
            both = dot(w_scr[j], k_scr[slot, :LEAF, cols])
            low = dot(w_scr[j, :rows, :], k_scr[slot, LEAF:, cols])
            o_scr[t, :, cols] = o_scr[t, :, cols] + factor * (both[:rows] + both[rows:] + low)

    @pl.when(count > 0)
    def _():
        block(0, 0)

    def pair(index, carry):
        block(2 * index + 1, 1)
        apply(2 * index, 0)

        @pl.when(2 * index + 1 < count)
        def _():
            block(2 * index + 2, 0)
            apply(2 * index + 1, 1)

        return carry

    lax.fori_loop(0, (count + 1) // 2, pair, jnp.int32(0))
    for copy in accs:
        copy.wait()
    if nacc:
        tall = outs[0].shape[0]
        for n, ref in enumerate(outs):
            t, top = 2 * (n // (rows // tall)), n % (rows // tall) * tall
            part = slice(top, top + tall)
            for leaf in range(2):
                cols = slice(leaf * LEAF, (leaf + 1) * LEAF)
                total = o_scr[t + leaf, part, :]
                for m in range(nacc):
                    total = total + acc_scr[m, t + leaf, part, :]
                ref[:, cols] = total


def near_call(name, pos, msgs, blocks_at, sources, rows, row=0, acc=(), after=()):
    nset = len(sources)
    first, last = blocks_at
    nblk = last - first
    nt = 2 * nblk
    tall = R // 2
    vmem = pl.BlockSpec(memory_space=pltpu.VMEM)
    smem = pl.BlockSpec(memory_space=pltpu.SMEM)
    operands = list(msgs[first:last])
    operands += [a for _, points, chunks in sources for a in (points, *chunks)]
    operands += list(acc)
    scratch = [
        pltpu.VMEM((nblk, F, 2 * LEAF), F32),
        pltpu.VMEM((nset, F, 2 * LEAF), F32),
        pltpu.VMEM((nset, rows, 2 * LEAF), F32),
        pltpu.VMEM((nt, 4 * F, LEAF), BF),
        pltpu.VMEM((nt, 8, LEAF), F32),
        pltpu.VMEM((2 * nset, LEAF, 4 * F), BF),
        pltpu.VMEM((2 * nset, LEAF, 128), F32),
        pltpu.VMEM((2 * nset, 2 * rows, LEAF), BF),
        pltpu.VMEM((2, 2 * LEAF, LEAF), BF),
        pltpu.SMEM((nblk, EXTRA, 128), F32),
        pltpu.SMEM((2 * nset * nt,), F32),
        pltpu.SMEM((2 * nset * nt,), jnp.int32),
        pltpu.SemaphoreType.DMA((2 * nblk + len(operands),)),
    ]
    if acc:
        out = [jax.ShapeDtypeStruct((tall, 2 * LEAF), F32)] * (nblk * (rows // tall))
        scratch = [
            pltpu.VMEM((nt, rows, LEAF), F32),
            pltpu.VMEM((len(acc), nt, rows, LEAF), F32),
        ] + scratch
    else:
        out = [jax.ShapeDtypeStruct((nt, rows, LEAF), F32)]
    sets = tuple((kind, len(chunks)) for kind, _, chunks in sources)
    return pl.pallas_call(
        partial(near_body, len(msgs) // 2, sets, blocks_at, rows, row, len(acc), len(out)),
        name=name,
        out_shape=out,
        in_specs=[smem] + [pl.BlockSpec(memory_space=pl.ANY)] * (len(operands) + len(after)),
        out_specs=[vmem] * len(out),
        scratch_shapes=scratch,
        compiler_params=pltpu.CompilerParams(vmem_limit_bytes=VMEM_LIMIT),
    )(pos, *operands, *after)


def share_rows(xs):
    return R // (2 * xs) * SK // (2 * LEAF)


def leaf_body(xs, pos_ref, count_ref, src_ref, pts_in, w_in, interp_in, *refs):
    msgs = refs[: 2 * xs]
    pts_ref, w_ref, interp_ref, scr, sems = refs[2 * xs :]
    copies = [
        pltpu.make_async_copy(pts_in, pts_ref, sems.at[0]),
        pltpu.make_async_copy(w_in, w_ref, sems.at[1]),
        pltpu.make_async_copy(interp_in, interp_ref, sems.at[2]),
    ]
    for copy in copies:
        copy.start()
    x, core, group, leaves = pos_ref[0], pos_ref[1], pos_ref[2], pos_ref[3]
    lane = lax.broadcasted_iota(jnp.int32, (1, 128), 1) + (group - 1) * leaves
    times = []
    for leaf in range(2):
        row = jnp.zeros((1, 128), F32)
        for slot in range(src_ref.shape[1]):
            name = jnp.where(slot < count_ref[0, leaf], src_ref[leaf, slot], -1 - 128 * leaves)
            row = row + (lane == name).astype(F32)
        times.append(row)
    times = jnp.concatenate(times + [jnp.zeros((EXTRA - 2, 128), F32)], axis=0)
    for copy in copies:
        copy.wait()
    total = jnp.zeros((R, SK), F32)
    for leaf in range(2):
        total = total + dot3(w_ref[:, leaf * LEAF : (leaf + 1) * LEAF], interp_ref[leaf])
    scr[...] = total
    rows = R // (2 * xs)
    tall = share_rows(xs)
    for n, msg in enumerate(msgs):
        helper = 2 * lax.rem(x + n // 2, xs) + (core if n % 2 == 0 else 1 - core)
        msg[:F, :] = pts_ref[...]
        msg[F : F + EXTRA, :] = jnp.zeros((EXTRA, 2 * LEAF), F32)
        msg[F : F + EXTRA, :128] = times
        for i in range(rows // tall):
            at = pl.multiple_of(helper * rows + i * tall, tall)
            msg[F + EXTRA :, i * SK : (i + 1) * SK] = scr[pl.ds(at, tall), :]


def leaf_call(xs, pos, near_count, near_src, points, weights, interp):
    vmem = pl.BlockSpec(memory_space=pltpu.VMEM)
    smem = pl.BlockSpec(memory_space=pltpu.SMEM)
    anywhere = pl.BlockSpec(memory_space=pl.ANY)
    height = F + EXTRA + share_rows(xs)
    return pl.pallas_call(
        partial(leaf_body, xs),
        name="leaf_up",
        out_shape=[jax.ShapeDtypeStruct((height, 2 * LEAF), F32)] * (2 * xs),
        in_specs=[smem, smem, smem, anywhere, anywhere, anywhere],
        out_specs=[vmem] * (2 * xs),
        scratch_shapes=[
            pltpu.VMEM(points.shape, F32),
            pltpu.VMEM(weights.shape, F32),
            pltpu.VMEM(interp.shape, F32),
            pltpu.VMEM((R, SK), F32),
            pltpu.SemaphoreType.DMA((3,)),
        ],
        compiler_params=pltpu.CompilerParams(vmem_limit_bytes=VMEM_LIMIT),
    )(pos, near_count, near_src, points, weights, interp)


def skel_body(xs, pos_ref, index_ref, *refs):
    msgs, out_ref = refs[:-1], refs[-1]
    rows = R // (2 * xs)
    tall = share_rows(xs)
    total = jnp.zeros((2 * F, SK), F32)
    value = jnp.zeros((tall, 2 * LEAF), F32)
    spot = lax.broadcasted_iota(jnp.int32, (2 * LEAF, SK), 0)
    x, core = pos_ref[0], pos_ref[1]
    for b, msg in enumerate(msgs):
        helper = 2 * lax.rem(x + b // 2, xs) + (core if b % 2 == 0 else 1 - core)
        hi, lo = halves(msg[:F, :] * SCALE)
        hot = spot + helper * (2 * LEAF) == index_ref[...]
        total = total + dot(jnp.concatenate([hi, lo], axis=0), hot.astype(F32).astype(BF))
        value = value + msg[F + EXTRA :, :]
    for n in range(out_ref.shape[0]):
        out_ref[n, :F, :] = total[:F] + total[F:]
        for i in range(rows // tall):
            part = slice(F + i * tall, F + (i + 1) * tall)
            out_ref[n, part, :] = value[:, i * SK : (i + 1) * SK]


def skel_call(xs, copies, pos, index, msgs):
    rows = R // (2 * xs)
    vmem = pl.BlockSpec(memory_space=pltpu.VMEM)
    return pl.pallas_call(
        partial(skel_body, xs),
        name="skeleton",
        out_shape=jax.ShapeDtypeStruct((copies, F + rows, SK), F32),
        in_specs=[pl.BlockSpec(memory_space=pltpu.SMEM)] + [vmem] * (1 + len(msgs)),
        out_specs=vmem,
        compiler_params=pltpu.CompilerParams(vmem_limit_bytes=VMEM_LIMIT),
    )(pos, index, *msgs)


def upper_start(level, groups):
    return sum((groups >> step for step in range(1, level)))


def list_start(level, groups):
    return sum((groups >> step for step in range(level)))


def far_body(groups, rows, pos_ref, far_ref, node_ref, transfer_ref, alike_ref, beside_ref, *refs):
    out_ref, p_scr, u_scr, f_scr = refs[-4:]
    levels = groups.bit_length() - 1
    group = pos_ref[2]
    odd = group % 2
    start = [list_start(level, groups) for level in range(levels)]
    for n in range(groups // 2):
        p_scr[2 * n + odd] = alike_ref[n, :F, :]
        u_scr[2 * n + odd] = alike_ref[n, F:, :]
        p_scr[2 * n + 1 - odd] = beside_ref[n, :F, :]
        u_scr[2 * n + 1 - odd] = beside_ref[n, F:, :]
    spot = lax.broadcasted_iota(jnp.int32, (2 * SK, SK), 0)
    for level in range(1, levels):
        for n in range(groups >> level):
            row = upper_start(level, groups) + n
            left = start[level - 1] + 2 * n
            hot = (spot == node_ref[row]).astype(F32).astype(BF)
            hi, lo = halves(jnp.concatenate([p_scr[left], p_scr[left + 1]], axis=1))
            both = dot(jnp.concatenate([hi, lo], axis=0), hot)
            p_scr[start[level] + n] = both[:F] + both[F:]
            vals = jnp.concatenate([u_scr[left], u_scr[left + 1]], axis=1)
            u_scr[start[level] + n] = dot3(vals, transfer_ref[row])
    for level in range(levels):
        node = group >> level
        side, off = target_side(p_scr[start[level] + node])
        f_scr[level] = jnp.zeros((rows, SK), F32)

        def one(n, carry, level=level, node=node, side=side, off=off):
            hits = jnp.int32(0)
            for slot in range(FL):
                hits = hits + (far_ref[slot, start[level] + node] == n).astype(jnp.int32)

            @pl.when(hits > 0)
            def _():
                src, src_off = source_side(p_scr[start[level] + n])
                block = jnp.exp2(dot(src, side) + src_off + off)
                term = dot3(u_scr[start[level] + n], block)
                f_scr[level] = f_scr[level] + hits.astype(F32) * term

            return carry

        lax.fori_loop(0, groups >> level, one, jnp.int32(0))
    local = f_scr[levels - 1]
    for level in range(levels - 1, 0, -1):
        row = upper_start(level, groups) + (group >> level)
        bit = (group >> (level - 1)) & 1
        matrix = transfer_ref[row, pl.ds(pl.multiple_of(bit * SK, SK), SK), :]
        local = f_scr[level - 1] + dot3(local, matrix, dot_t)
    out_ref[...] = local


def far_call(groups, pos, far_nodes, skel_node, transfer, alike, beside, after):
    rows = alike.shape[1] - F
    vmem = pl.BlockSpec(memory_space=pltpu.VMEM)
    smem = pl.BlockSpec(memory_space=pltpu.SMEM)
    nodes = 2 * groups
    return pl.pallas_call(
        partial(far_body, groups, rows),
        name="far",
        out_shape=jax.ShapeDtypeStruct((rows, SK), F32),
        in_specs=[smem, smem, vmem, vmem, vmem, vmem]
        + [pl.BlockSpec(memory_space=pl.ANY)] * len(after),
        out_specs=vmem,
        scratch_shapes=[
            pltpu.VMEM((nodes, F, SK), F32),
            pltpu.VMEM((nodes, rows, SK), F32),
            pltpu.VMEM((groups.bit_length(), rows, SK), F32),
        ],
        compiler_params=pltpu.CompilerParams(vmem_limit_bytes=VMEM_LIMIT),
    )(pos, far_nodes.T, skel_node[:, None, :], transfer, alike, beside, *after)


def final_body(xs, pos_ref, interp_ref, *refs):
    values, sums = refs[: 2 * xs], refs[2 * xs : -2]
    out_ref, v_scr = refs[-2:]
    rows = R // (2 * xs)
    x, core = pos_ref[0], pos_ref[1]
    for n, ref in enumerate(values):
        helper = 2 * lax.rem(x + n // 2, xs) + (core if n % 2 == 0 else 1 - core)
        v_scr[pl.ds(pl.multiple_of(helper * rows, rows), rows), :] = ref[...]
    value = v_scr[...]
    for leaf in range(2):
        cols = slice(leaf * LEAF, (leaf + 1) * LEAF)
        total = dot3(value, interp_ref[leaf], dot_t)
        for c in range(2):
            part = slice(c * R // 2, (c + 1) * R // 2)
            out_ref[part, cols] = total[part] + sums[c][:, cols] + sums[2 + c][:, cols]


def add_body(count, *refs):
    for n, out_ref in enumerate(refs[-(len(refs) // (count + 1)) :]):
        total = refs[n * count][...]
        for ref in refs[n * count + 1 : (n + 1) * count]:
            total = total + ref[...]
        out_ref[...] = total


def add_call(*sums):
    vmem = pl.BlockSpec(memory_space=pltpu.VMEM)
    operands = [value for terms in sums for value in terms]
    return pl.pallas_call(
        partial(add_body, len(sums[0])),
        name="add_parts",
        out_shape=[jax.ShapeDtypeStruct(sums[0][0].shape, F32)] * len(sums),
        in_specs=[vmem] * len(operands),
        out_specs=[vmem] * len(sums),
        compiler_params=pltpu.CompilerParams(vmem_limit_bytes=VMEM_LIMIT),
    )(*operands)


def final_call(xs, pos, interp, home, mate, values):
    vmem = pl.BlockSpec(memory_space=pltpu.VMEM)
    return pl.pallas_call(
        partial(final_body, xs),
        name="join",
        out_shape=jax.ShapeDtypeStruct((R, 2 * LEAF), F32),
        in_specs=[pl.BlockSpec(memory_space=pltpu.SMEM)] + [vmem] * (1 + 2 * xs + 4),
        out_specs=vmem,
        scratch_shapes=[pltpu.VMEM((R, SK), F32)],
        compiler_params=pltpu.CompilerParams(vmem_limit_bytes=VMEM_LIMIT),
    )(pos, interp, *values, *home, *mate)


def help_pairs(xs, dx, dc):
    return [
        (2 * ((x + dx) % xs) + (core ^ dc), 2 * x + core) for x in range(xs) for core in range(2)
    ]


def shards(
    points, weights, interp, transfer, near_count, near_src, skel_group, skel_node, far_nodes
):
    helpers = lax.axis_size("help")
    groups = lax.axis_size("leaf")
    xs = helpers // 2
    helper = lax.axis_index("help")
    group = lax.axis_index("leaf")
    x, core = helper // 2, helper % 2
    leaves = 2 * helpers
    pos = jnp.stack([x, core, group, jnp.int32(leaves)]).astype(jnp.int32)
    rows = R // 2

    def from_help(value, dx, dc):
        return lax.ppermute(value, "help", help_pairs(xs, dx, dc))

    def to_help(value, dx):
        return lax.ppermute(value, "help", help_pairs(xs, -dx, 0))

    def together(*values):
        return lax.optimization_barrier(values)

    beside = [(i, i ^ 1) for i in range(groups)]
    across = [(i, i + 2) for i in range(0, groups - 2, 2)]
    across += [(i, i - 2) for i in range(3, groups, 2)]
    order = [(dx, dc) for dx in range(xs) for dc in range(2)]

    pts_y = lax.ppermute(points, "leaf", beside)
    w_y = [lax.ppermute(weights[c * rows : (c + 1) * rows], "leaf", beside) for c in range(2)]
    sent = leaf_call(xs, pos, near_count, near_src, points, weights, interp)
    got = [
        lax.ppermute(sent[n], "help", help_pairs(xs, -dx, dc))
        for n, (dx, dc) in enumerate(order)
        if n
    ]
    pts_z = lax.ppermute(pts_y, "leaf", across)
    got, pts_z = together(got, pts_z)
    msgs = [sent[0]] + [got[order.index((-dx % xs, dc)) - 1] for dx, dc in order[1:]]

    payload = skel_call(xs, groups // 2, pos, skel_group, msgs)
    parity = [[n for n in range(groups) if n % 2 == odd] for odd in range(2)]
    alike = lax.all_to_all(payload, "leaf", 0, 0, axis_index_groups=parity)
    w_z = [lax.ppermute(w_y[0], "leaf", across)]
    (own,) = near_call(
        "near_own", pos, msgs, (0, helpers), [("own", points, [weights])], R, after=[payload]
    )
    own, w_y[1] = together(own, w_y[1])
    w_z.append(lax.ppermute(w_y[1], "leaf", across))
    alike, w_y[1] = together(alike, w_y[1])
    side = lax.ppermute(alike, "leaf", beside)
    (pair,) = near_call("near_pair", pos, msgs, (0, helpers), [("pair", pts_y, w_y)], R)

    sums, part = [], []
    for c in range(2):
        part = near_call(
            "near_next_away", pos, msgs, (2, helpers), [("next", pts_z, w_z[c : c + 1])],
            rows, c * rows, (own, pair), part[:1],
        )
        kept, given = part[::2], part[1::2]
        sums.append((kept, [from_help(value, 0, 1) for value in given]))
    parts = []
    for c in range(2):
        kept, mates = sums[c]
        if c == 0:
            mates, side = together(mates, side)
        both = add_call(*zip(kept, mates))
        parts.append([to_help(value, dx + 1) for dx, value in enumerate(both)])
    v_own = far_call(groups, pos, far_nodes, skel_node, transfer, alike, side, both[:1])
    values = [v_own] + [from_help(v_own, dx, dc) for dx, dc in order[1:]]
    home = near_call(
        "near_next_home", pos, msgs, (0, 2), [("next", pts_z, w_z)], R, 0, (own, pair), [v_own]
    )
    mate = [from_help(value, 0, 1) for value in home[2:]]
    mine = add_call(*[[home[c], *parts[c]] for c in range(2)])
    return final_call(xs, pos, interp, mine, mate, values)


def solution(mesh):
    placed = (
        P(None, ("leaf", "help")),
        P(None, ("leaf", "help")),
        P(("leaf", "help"), None, None),
        P(),
        P("leaf", "help"),
        P(("leaf", "help"), None),
        P("leaf", None),
        P(),
        P(),
    )
    return jax.shard_map(
        shards, mesh=mesh, in_specs=placed, out_specs=P(None, ("leaf", "help")), check_vma=False
    )
```

```python
import math
from functools import partial

import jax
import jax.numpy as jnp
from jax import lax
from jax.experimental import pallas as pl
from jax.experimental.pallas import tpu as pltpu
from jax.sharding import PartitionSpec as P

F = 64
R = 256
LEAF = 512
SK = 256
FL = 4
EXTRA = 8

BF = jnp.bfloat16
F32 = jnp.float32
LOG2E = 1.0 / math.log(2.0)
SCALE = math.sqrt(0.5 * LOG2E)
BIAS = 0.0625 * F * LOG2E
VMEM_LIMIT = 24 * 1024 * 1024


def dot(a, b):
    return jnp.dot(a, b, preferred_element_type=F32)


def dot_t(a, b):
    return lax.dot_general(a, b, (((1,), (1,)), ((), ())), preferred_element_type=F32)


def halves(x):
    hi = x.astype(BF)
    lo = (x - hi.astype(F32)).astype(BF)
    return hi, lo


def dot3(a, b, mul=dot):
    a_hi, a_lo = halves(a)
    b_hi, b_lo = halves(b)
    return mul(a_hi, b_hi) + mul(a_lo, b_hi) + mul(a_hi, b_lo)


def target_side(x):
    hi, lo = halves(x)
    both = hi.astype(F32) + lo.astype(F32)
    off = BIAS - 0.5 * jnp.sum(both * both, axis=0, keepdims=True)
    return jnp.concatenate([hi, lo, hi, lo], axis=0), off


def source_side(x):
    xt = x.T
    hi, lo = halves(xt)
    both = hi.astype(F32) + lo.astype(F32)
    off = BIAS - 0.5 * jnp.sum(both * both, axis=1, keepdims=True)
    return jnp.concatenate([hi, hi, lo, lo], axis=1), off


def near_body(
    xs, sets, leaves_at, rows, row, nacc, nout, pos_ref, *refs
):
    nset = len(sets)
    start, stop = leaves_at
    msgs, (t_ref, tb_ref), refs = refs[: 2 * xs], refs[2 * xs : 2 * xs + 2], refs[2 * xs + 2 :]
    if nacc:
        s_scr, sb_scr, w_scr, o_scr, k_scr, times_scr, list_ref, times_ref, sems = refs[-9:]
        outs = refs[-9 - nout : -9]
    else:
        o_scr, s_scr, sb_scr, w_scr, k_scr, times_scr, list_ref, times_ref, sems = refs[-9:]
    copies = [
        pltpu.make_async_copy(msgs[b].at[F : F + EXTRA, :128], times_ref.at[b], sems.at[b])
        for b in range(start // 2, stop // 2)
    ]
    for copy in copies:
        copy.start()
    at = 0
    for k, (_, ready, chunks) in enumerate(sets):
        heads = refs[at : at + 1 + ready]
        parts = refs[at + 1 + ready : at + 1 + ready + chunks]
        at += 1 + ready + chunks
        each = rows // chunks
        for leaf in range(2):
            cols = slice(leaf * LEAF, (leaf + 1) * LEAF)
            j = 2 * k + leaf
            if ready:
                s_scr[j] = heads[0][leaf]
                sb_scr[j] = heads[1][leaf]
            else:
                side, off = source_side(heads[0][:F, cols] * SCALE)
                s_scr[j] = side
                sb_scr[j] = jnp.broadcast_to(off, (LEAF, 128))
            for c in range(chunks):
                hi, lo = halves(parts[c][:, cols])
                w_scr[j, c * each : (c + 1) * each, :] = hi
                w_scr[j, rows + c * each : rows + (c + 1) * each, :] = lo
    for t in range(start, stop):
        if nacc:
            o_scr[t - start] = sum(ref[t, row : row + rows, :] for ref in refs[at : at + nacc])
        else:
            o_scr[t - start] = jnp.zeros((rows, LEAF), F32)

    x, core, group, leaves = pos_ref[0], pos_ref[1], pos_ref[2], pos_ref[3]
    odd = group % 2
    column = []
    for kind, _, _ in sets:
        relative = {"own": 1, "pair": 2 - 2 * odd, "next": 2 * odd}[kind]
        column.append(relative * leaves + 2 * (2 * x + core))

    for copy in copies:
        copy.wait()
    count = jnp.int32(0)
    list_ref[0] = 0
    for t in range(start, stop):
        for j in range(2 * nset):
            times = times_ref[t // 2, t % 2, column[j // 2] + j % 2]

            @pl.when(times > 0)
            def _(count=count, t=t, j=j, times=times):
                list_ref[count] = t * 8 + j
                times_scr[count] = times

            count = count + (times > 0).astype(jnp.int32)

    def block(index, slot):
        code = list_ref[jnp.minimum(index, jnp.maximum(count - 1, 0))]
        t, j = code // 8, code % 8
        side = t_ref[t]
        off = tb_ref[t][:1, :]
        for half in range(2):
            part = slice(half * 256, (half + 1) * 256)
            cross = dot(s_scr[j, part, :], side)
            src_off = sb_scr[j, part, :]
            src_off = jnp.concatenate([src_off] * (LEAF // 128), axis=1)
            k_hi, k_lo = halves(jnp.exp2(cross + src_off + off))
            k_scr[slot, part, :] = k_hi
            k_scr[slot, LEAF + half * 256 : LEAF + (half + 1) * 256, :] = k_lo

    def apply(index, slot):
        code = list_ref[index]
        t, j = code // 8 - start, code % 8
        factor = times_scr[index]
        for half in range(2):
            cols = slice(half * 256, (half + 1) * 256)
            both = dot(w_scr[j], k_scr[slot, :LEAF, cols])
            low = dot(w_scr[j, :rows, :], k_scr[slot, LEAF:, cols])
            o_scr[t, :, cols] = o_scr[t, :, cols] + factor * (both[:rows] + both[rows:] + low)

    @pl.when(count > 0)
    def _():
        block(0, 0)

    def pair(index, carry):
        block(2 * index + 1, 1)
        apply(2 * index, 0)

        @pl.when(2 * index + 1 < count)
        def _():
            block(2 * index + 2, 0)
            apply(2 * index + 1, 1)

        return carry

    lax.fori_loop(0, (count + 1) // 2, pair, jnp.int32(0))
    if nacc:
        tall = outs[0].shape[0]
        for n, ref in enumerate(outs):
            t, top = 2 * (n // (rows // tall)), n % (rows // tall) * tall
            for leaf in range(2):
                cols = slice(leaf * LEAF, (leaf + 1) * LEAF)
                ref[:, cols] = o_scr[t + leaf, top : top + tall, :]


def near_call(name, pos, msgs, targets, leaves_at, sources, rows, row=0, acc=(), after=()):
    nset = len(sources)
    start, stop = leaves_at
    tall = R // 2
    vmem = pl.BlockSpec(memory_space=pltpu.VMEM)
    smem = pl.BlockSpec(memory_space=pltpu.SMEM)
    operands = [a for _, heads, chunks in sources for a in (*heads, *chunks)]
    scratch = [
        pltpu.VMEM((2 * nset, LEAF, 4 * F), BF),
        pltpu.VMEM((2 * nset, LEAF, 128), F32),
        pltpu.VMEM((2 * nset, 2 * rows, LEAF), BF),
        pltpu.VMEM((stop - start, rows, LEAF), F32),
        pltpu.VMEM((2, 2 * LEAF, LEAF), BF),
        pltpu.SMEM((2 * nset * (stop - start),), F32),
        pltpu.SMEM((2 * nset * (stop - start),), jnp.int32),
        pltpu.SMEM((len(msgs), EXTRA, 128), F32),
        pltpu.SemaphoreType.DMA((len(msgs),)),
    ]
    if not acc:
        out = [jax.ShapeDtypeStruct((stop - start, rows, LEAF), F32)]
        scratch.pop(3)
    else:
        operands += list(acc)
        out = [jax.ShapeDtypeStruct((tall, 2 * LEAF), F32)] * ((stop - start) // 2 * (rows // tall))
    sets = tuple((kind, len(heads) - 1, len(chunks)) for kind, heads, chunks in sources)
    return pl.pallas_call(
        partial(
            near_body, len(msgs) // 2, sets, leaves_at, rows, row, len(acc), len(out)
        ),
        name=name,
        out_shape=out,
        in_specs=[smem]
        + [pl.BlockSpec(memory_space=pl.ANY)] * len(msgs)
        + [vmem] * (2 + len(operands))
        + [pl.BlockSpec(memory_space=pl.ANY)] * len(after),
        out_specs=[vmem] * len(out),
        scratch_shapes=scratch,
        compiler_params=pltpu.CompilerParams(vmem_limit_bytes=VMEM_LIMIT),
    )(pos, *msgs, *targets, *operands, *after)


def source_body(pts_ref, side_ref, off_ref):
    for leaf in range(2):
        cols = slice(leaf * LEAF, (leaf + 1) * LEAF)
        side, off = source_side(pts_ref[:, cols] * SCALE)
        side_ref[leaf] = side
        off_ref[leaf] = jnp.broadcast_to(off, (LEAF, 128))


def source_call(pts):
    vmem = pl.BlockSpec(memory_space=pltpu.VMEM)
    return pl.pallas_call(
        source_body,
        name="source_side",
        out_shape=[
            jax.ShapeDtypeStruct((2, LEAF, 4 * F), BF),
            jax.ShapeDtypeStruct((2, LEAF, 128), F32),
        ],
        in_specs=[vmem],
        out_specs=[vmem, vmem],
        compiler_params=pltpu.CompilerParams(vmem_limit_bytes=VMEM_LIMIT),
    )(pts)


def share_rows(xs):
    return R // (2 * xs) * SK // (2 * LEAF)


def leaf_body(xs, pos_ref, count_ref, src_ref, pts_in, w_in, interp_in, *refs):
    msgs = refs[: 2 * xs]
    pts_ref, w_ref, interp_ref, scr, sems = refs[2 * xs :]
    copies = [
        pltpu.make_async_copy(pts_in, pts_ref, sems.at[0]),
        pltpu.make_async_copy(w_in, w_ref, sems.at[1]),
        pltpu.make_async_copy(interp_in, interp_ref, sems.at[2]),
    ]
    for copy in copies:
        copy.start()
    x, core, group, leaves = pos_ref[0], pos_ref[1], pos_ref[2], pos_ref[3]
    lane = lax.broadcasted_iota(jnp.int32, (1, 128), 1) + (group - 1) * leaves
    times = []
    for leaf in range(2):
        row = jnp.zeros((1, 128), F32)
        for slot in range(src_ref.shape[1]):
            name = jnp.where(slot < count_ref[0, leaf], src_ref[leaf, slot], -1 - 128 * leaves)
            row = row + (lane == name).astype(F32)
        times.append(row)
    times = jnp.concatenate(times + [jnp.zeros((EXTRA - 2, 128), F32)], axis=0)
    for copy in copies:
        copy.wait()
    total = jnp.zeros((R, SK), F32)
    for leaf in range(2):
        total = total + dot3(w_ref[:, leaf * LEAF : (leaf + 1) * LEAF], interp_ref[leaf])
    scr[...] = total
    rows = R // (2 * xs)
    tall = share_rows(xs)
    for n, msg in enumerate(msgs):
        helper = 2 * lax.rem(x + n // 2, xs) + (core if n % 2 == 0 else 1 - core)
        msg[:F, :] = pts_ref[...]
        msg[F : F + EXTRA, :] = jnp.zeros((EXTRA, 2 * LEAF), F32)
        msg[F : F + EXTRA, :128] = times
        for i in range(rows // tall):
            at = pl.multiple_of(helper * rows + i * tall, tall)
            msg[F + EXTRA :, i * SK : (i + 1) * SK] = scr[pl.ds(at, tall), :]


def leaf_call(xs, pos, near_count, near_src, points, weights, interp):
    vmem = pl.BlockSpec(memory_space=pltpu.VMEM)
    smem = pl.BlockSpec(memory_space=pltpu.SMEM)
    anywhere = pl.BlockSpec(memory_space=pl.ANY)
    height = F + EXTRA + share_rows(xs)
    return pl.pallas_call(
        partial(leaf_body, xs),
        name="leaf_up",
        out_shape=[jax.ShapeDtypeStruct((height, 2 * LEAF), F32)] * (2 * xs),
        in_specs=[smem, smem, smem, anywhere, anywhere, anywhere],
        out_specs=[vmem] * (2 * xs),
        scratch_shapes=[
            pltpu.VMEM(points.shape, F32),
            pltpu.VMEM(weights.shape, F32),
            pltpu.VMEM(interp.shape, F32),
            pltpu.VMEM((R, SK), F32),
            pltpu.SemaphoreType.DMA((3,)),
        ],
        compiler_params=pltpu.CompilerParams(vmem_limit_bytes=VMEM_LIMIT),
    )(pos, near_count, near_src, points, weights, interp)


def skel_body(xs, pos_ref, index_ref, *refs):
    msgs, (out_ref, side_ref, off_ref) = refs[:-3], refs[-3:]
    rows = R // (2 * xs)
    tall = share_rows(xs)
    total = jnp.zeros((2 * F, SK), F32)
    value = jnp.zeros((tall, 2 * LEAF), F32)
    spot = lax.broadcasted_iota(jnp.int32, (2 * LEAF, SK), 0)
    x, core = pos_ref[0], pos_ref[1]
    for b, msg in enumerate(msgs):
        helper = 2 * lax.rem(x + b // 2, xs) + (core if b % 2 == 0 else 1 - core)
        side, off = target_side(msg[:F, :] * SCALE)
        for leaf in range(2):
            part = slice(leaf * LEAF, (leaf + 1) * LEAF)
            side_ref[2 * b + leaf] = side[:, part]
            off_ref[2 * b + leaf] = jnp.broadcast_to(off[:, part], (8, LEAF))
        hot = spot + helper * (2 * LEAF) == index_ref[...]
        total = total + dot(side[: 2 * F], hot.astype(F32).astype(BF))
        value = value + msg[F + EXTRA :, :]
    out_ref[:F, :] = total[:F] + total[F:]
    for i in range(rows // tall):
        out_ref[F + i * tall : F + (i + 1) * tall, :] = value[:, i * SK : (i + 1) * SK]


def skel_call(xs, pos, index, msgs):
    rows = R // (2 * xs)
    leaves = 2 * len(msgs)
    vmem = pl.BlockSpec(memory_space=pltpu.VMEM)
    payload, *targets = pl.pallas_call(
        partial(skel_body, xs),
        name="skeleton",
        out_shape=[
            jax.ShapeDtypeStruct((F + rows, SK), F32),
            jax.ShapeDtypeStruct((leaves, 4 * F, LEAF), BF),
            jax.ShapeDtypeStruct((leaves, 8, LEAF), F32),
        ],
        in_specs=[pl.BlockSpec(memory_space=pltpu.SMEM)] + [vmem] * (1 + len(msgs)),
        out_specs=[vmem] * 3,
        compiler_params=pltpu.CompilerParams(vmem_limit_bytes=VMEM_LIMIT),
    )(pos, index, *msgs)
    return payload, targets


def stack_body(*refs):
    for n, ref in enumerate(refs[:-1]):
        refs[-1][n] = ref[...]


def stack_call(pieces):
    vmem = pl.BlockSpec(memory_space=pltpu.VMEM)
    return pl.pallas_call(
        stack_body,
        name="stack",
        out_shape=jax.ShapeDtypeStruct((len(pieces), *pieces[0].shape), F32),
        in_specs=[vmem] * len(pieces),
        out_specs=vmem,
        compiler_params=pltpu.CompilerParams(vmem_limit_bytes=VMEM_LIMIT),
    )(*pieces)


def upper_start(level, groups):
    return sum((groups >> step for step in range(1, level)))


def list_start(level, groups):
    return sum((groups >> step for step in range(level)))


def far_body(groups, rows, pos_ref, far_ref, node_ref, transfer_ref, alike_ref, beside_ref, *refs):
    out_ref, p_scr, u_scr, f_scr = refs[-4:]
    levels = groups.bit_length() - 1
    group = pos_ref[2]
    start = [list_start(level, groups) for level in range(levels)]
    for n in range(groups // 2):
        same, other = group ^ (2 * n), group ^ (2 * n + 1)
        p_scr[same] = alike_ref[n, :F, :]
        u_scr[same] = alike_ref[n, F:, :]
        p_scr[other] = beside_ref[n, :F, :]
        u_scr[other] = beside_ref[n, F:, :]
    spot = lax.broadcasted_iota(jnp.int32, (2 * SK, SK), 0)
    for level in range(1, levels):
        for n in range(groups >> level):
            row = upper_start(level, groups) + n
            left = start[level - 1] + 2 * n
            hot = (spot == node_ref[row : row + 1, :]).astype(F32).astype(BF)
            hi, lo = halves(jnp.concatenate([p_scr[left], p_scr[left + 1]], axis=1))
            both = dot(jnp.concatenate([hi, lo], axis=0), hot)
            p_scr[start[level] + n] = both[:F] + both[F:]
            vals = jnp.concatenate([u_scr[left], u_scr[left + 1]], axis=1)
            u_scr[start[level] + n] = dot3(vals, transfer_ref[row])
    for level in range(levels):
        node = group >> level
        side, off = target_side(p_scr[start[level] + node])
        f_scr[level] = jnp.zeros((rows, SK), F32)

        def one(n, carry, level=level, node=node, side=side, off=off):
            hits = jnp.int32(0)
            for slot in range(FL):
                hits = hits + (far_ref[slot, start[level] + node] == n).astype(jnp.int32)

            @pl.when(hits > 0)
            def _():
                src, src_off = source_side(p_scr[start[level] + n])
                block = jnp.exp2(dot(src, side) + src_off + off)
                term = dot3(u_scr[start[level] + n], block)
                f_scr[level] = f_scr[level] + hits.astype(F32) * term

            return carry

        lax.fori_loop(0, groups >> level, one, jnp.int32(0))
    local = f_scr[levels - 1]
    for level in range(levels - 1, 0, -1):
        row = upper_start(level, groups) + (group >> level)
        bit = (group >> (level - 1)) & 1
        matrix = transfer_ref[row, pl.ds(pl.multiple_of(bit * SK, SK), SK), :]
        local = f_scr[level - 1] + dot3(local, matrix, dot_t)
    out_ref[...] = local


def far_call(groups, pos, far_nodes, skel_node, transfer, alike, beside, after):
    rows = alike.shape[1] - F
    vmem = pl.BlockSpec(memory_space=pltpu.VMEM)
    smem = pl.BlockSpec(memory_space=pltpu.SMEM)
    nodes = 2 * groups
    return pl.pallas_call(
        partial(far_body, groups, rows),
        name="far",
        out_shape=jax.ShapeDtypeStruct((rows, SK), F32),
        in_specs=[smem, smem, vmem, vmem, vmem, vmem]
        + [pl.BlockSpec(memory_space=pl.ANY)] * len(after),
        out_specs=vmem,
        scratch_shapes=[
            pltpu.VMEM((nodes, F, SK), F32),
            pltpu.VMEM((nodes, rows, SK), F32),
            pltpu.VMEM((groups.bit_length(), rows, SK), F32),
        ],
        compiler_params=pltpu.CompilerParams(vmem_limit_bytes=VMEM_LIMIT),
    )(pos, far_nodes.T, skel_node, transfer, alike, beside, *after)


def final_body(xs, pos_ref, interp_ref, *refs):
    values, sums = refs[: 2 * xs], refs[2 * xs : -2]
    out_ref, v_scr = refs[-2:]
    rows = R // (2 * xs)
    x, core = pos_ref[0], pos_ref[1]
    for n, ref in enumerate(values):
        helper = 2 * lax.rem(x + n // 2, xs) + (core if n % 2 == 0 else 1 - core)
        v_scr[pl.ds(pl.multiple_of(helper * rows, rows), rows), :] = ref[...]
    value = v_scr[...]
    for leaf in range(2):
        cols = slice(leaf * LEAF, (leaf + 1) * LEAF)
        total = dot3(value, interp_ref[leaf], dot_t)
        for c in range(2):
            part = slice(c * R // 2, (c + 1) * R // 2)
            out_ref[part, cols] = total[part] + sums[c][:, cols] + sums[2 + c][:, cols]


def add_body(count, *refs):
    for n, out_ref in enumerate(refs[-(len(refs) // (count + 1)) :]):
        total = refs[n * count][...]
        for ref in refs[n * count + 1 : (n + 1) * count]:
            total = total + ref[...]
        out_ref[...] = total


def add_call(*sums):
    vmem = pl.BlockSpec(memory_space=pltpu.VMEM)
    operands = [value for terms in sums for value in terms]
    return pl.pallas_call(
        partial(add_body, len(sums[0])),
        name="add_parts",
        out_shape=[jax.ShapeDtypeStruct(sums[0][0].shape, F32)] * len(sums),
        in_specs=[vmem] * len(operands),
        out_specs=[vmem] * len(sums),
        compiler_params=pltpu.CompilerParams(vmem_limit_bytes=VMEM_LIMIT),
    )(*operands)


def final_call(xs, pos, interp, home, mate, values):
    vmem = pl.BlockSpec(memory_space=pltpu.VMEM)
    return pl.pallas_call(
        partial(final_body, xs),
        name="join",
        out_shape=jax.ShapeDtypeStruct((R, 2 * LEAF), F32),
        in_specs=[pl.BlockSpec(memory_space=pltpu.SMEM)] + [vmem] * (1 + 2 * xs + 4),
        out_specs=vmem,
        scratch_shapes=[pltpu.VMEM((R, SK), F32)],
        compiler_params=pltpu.CompilerParams(vmem_limit_bytes=VMEM_LIMIT),
    )(pos, interp, *values, *home, *mate)


def help_pairs(xs, dx, dc):
    return [
        (2 * ((x + dx) % xs) + (core ^ dc), 2 * x + core) for x in range(xs) for core in range(2)
    ]


def shards(
    points, weights, interp, transfer, near_count, near_src, skel_group, skel_node, far_nodes
):
    helpers = lax.axis_size("help")
    groups = lax.axis_size("leaf")
    xs = helpers // 2
    helper = lax.axis_index("help")
    group = lax.axis_index("leaf")
    x, core = helper // 2, helper % 2
    leaves = 2 * helpers
    pos = jnp.stack([x, core, group, jnp.int32(leaves)]).astype(jnp.int32)
    rows = R // 2

    def from_help(value, dx, dc):
        return lax.ppermute(value, "help", help_pairs(xs, dx, dc))

    def to_help(value, dx):
        return lax.ppermute(value, "help", help_pairs(xs, -dx, 0))

    def together(*values):
        return lax.optimization_barrier(values)

    beside = [(i, i ^ 1) for i in range(groups)]
    across = [(i, i + 2) for i in range(0, groups - 2, 2)]
    across += [(i, i - 2) for i in range(3, groups, 2)]
    order = [(dx, dc) for dx in range(xs) for dc in range(2)]

    pts_y = lax.ppermute(points, "leaf", beside)
    w_own = [weights[:rows], weights[rows:]]
    w_y = [lax.ppermute(chunk, "leaf", beside) for chunk in w_own]
    sent = leaf_call(xs, pos, near_count, near_src, points, weights, interp)
    got = [
        lax.ppermute(sent[n], "help", help_pairs(xs, -dx, dc))
        for n, (dx, dc) in enumerate(order)
        if n
    ]
    pts_z = lax.ppermute(pts_y, "leaf", across)
    w_z = [lax.ppermute(w_y[0], "leaf", across)]
    w_y = list(together(*w_y))
    w_z.append(lax.ppermute(w_y[1], "leaf", across))

    got, w_y = together(got, w_y)
    msgs = [sent[0]] + [got[order.index((-dx % xs, dc)) - 1] for dx, dc in order[1:]]
    payload, targets = skel_call(xs, pos, skel_group, msgs)
    pieces = [payload]
    for mask in range(2, groups, 2):
        pieces.append(lax.ppermute(payload, "leaf", [(i, i ^ mask) for i in range(groups)]))

    sources = [("own", (points,), [weights]), ("pair", (pts_y,), w_y)]
    (near,) = near_call("near_own_pair", pos, msgs, targets, (0, 2 * helpers), sources, R)
    z_side = source_call(pts_z)
    sums, part = [], []
    for c in range(2):
        if c == 1:
            pieces, w_z[1], part = together(pieces, w_z[1], part)
            alike = stack_call(pieces)
            side = lax.ppermute(alike, "leaf", beside)
        part = near_call(
            "near_next_away", pos, msgs, targets, (4, 2 * helpers),
            [("next", z_side, w_z[c : c + 1])], rows, c * rows, [near], part[:1],
        )
        kept, given = part[::2], part[1::2]
        sums.append((kept, [from_help(value, 0, 1) for value in given]))
    parts = []
    for c in range(2):
        kept, mates = sums[c]
        both = add_call(*zip(kept, mates))
        parts.append([to_help(value, dx + 1) for dx, value in enumerate(both)])
    v_own = far_call(groups, pos, far_nodes, skel_node, transfer, alike, side, both[:1])
    values = [v_own] + [from_help(v_own, dx, dc) for dx, dc in order[1:]]
    home = near_call(
        "near_next_home", pos, msgs, targets, (0, 4), [("next", z_side, w_z)], R, 0, [near], [v_own]
    )
    mate = [from_help(value, 0, 1) for value in home[2:]]
    mine = add_call(*[[home[c], *parts[c]] for c in range(2)])
    return final_call(xs, pos, interp, mine, mate, values)


def solution(mesh):
    placed = (
        P(None, ("leaf", "help")),
        P(None, ("leaf", "help")),
        P(("leaf", "help"), None, None),
        P(),
        P("leaf", "help"),
        P(("leaf", "help"), None),
        P("leaf", None),
        P(),
        P(),
    )
    return jax.shard_map(
        shards, mesh=mesh, in_specs=placed, out_specs=P(None, ("leaf", "help")), check_vma=False
    )
```

```python
import math
from functools import partial

import jax
import jax.numpy as jnp
from jax import lax
from jax.experimental import pallas as pl
from jax.experimental.pallas import tpu as pltpu
from jax.sharding import PartitionSpec as P

F = 64
R = 256
LEAF = 512
SK = 256
FL = 4
EXTRA = 8

BF = jnp.bfloat16
F32 = jnp.float32
LOG2E = 1.0 / math.log(2.0)
SCALE = math.sqrt(0.5 * LOG2E)
BIAS = 0.0625 * F * LOG2E
VMEM_LIMIT = 24 * 1024 * 1024
VMEM_WHOLE = 64 * 1024 * 1024


def dot(a, b):
    return jnp.dot(a, b, preferred_element_type=F32)


def dot_t(a, b):
    return lax.dot_general(a, b, (((1,), (1,)), ((), ())), preferred_element_type=F32)


def halves(x):
    hi = x.astype(BF)
    lo = (x - hi.astype(F32)).astype(BF)
    return hi, lo


def dot3(a, b, mul=dot):
    a_hi, a_lo = halves(a)
    b_hi, b_lo = halves(b)
    return mul(a_hi, b_hi) + mul(a_lo, b_hi) + mul(a_hi, b_lo)


def target_side(x):
    hi, lo = halves(x)
    both = hi.astype(F32) + lo.astype(F32)
    off = BIAS - 0.5 * jnp.sum(both * both, axis=0, keepdims=True)
    return jnp.concatenate([hi, lo, hi, lo], axis=0), off


def source_side(x):
    xt = x.T
    hi, lo = halves(xt)
    both = hi.astype(F32) + lo.astype(F32)
    off = BIAS - 0.5 * jnp.sum(both * both, axis=1, keepdims=True)
    return jnp.concatenate([hi, hi, lo, lo], axis=1), off


def near_body(
    xs, sets, leaves_at, rows, row, nacc, nout, pos_ref, *refs
):
    nset = len(sets)
    start, stop = leaves_at
    msgs, (t_ref, tb_ref), refs = refs[: 2 * xs], refs[2 * xs : 2 * xs + 2], refs[2 * xs + 2 :]
    if nacc:
        s_scr, sb_scr, w_scr, o_scr, k_scr, times_scr, list_ref, times_ref, sems = refs[-9:]
        outs = refs[-9 - nout : -9]
    else:
        o_scr, s_scr, sb_scr, w_scr, k_scr, times_scr, list_ref, times_ref, sems = refs[-9:]
    copies = [
        pltpu.make_async_copy(msgs[b].at[F : F + EXTRA, :128], times_ref.at[b], sems.at[b])
        for b in range(start // 2, stop // 2)
    ]
    for copy in copies:
        copy.start()
    at = 0
    for k, (_, ready, chunks) in enumerate(sets):
        heads = refs[at : at + 1 + ready]
        parts = refs[at + 1 + ready : at + 1 + ready + chunks]
        at += 1 + ready + chunks
        each = rows // chunks
        for leaf in range(2):
            cols = slice(leaf * LEAF, (leaf + 1) * LEAF)
            j = 2 * k + leaf
            if ready:
                s_scr[j] = heads[0][leaf]
                sb_scr[j] = heads[1][leaf]
            else:
                side, off = source_side(heads[0][:F, cols] * SCALE)
                s_scr[j] = side
                sb_scr[j] = jnp.broadcast_to(off, (LEAF, 128))
            for c in range(chunks):
                hi, lo = halves(parts[c][:, cols])
                w_scr[j, c * each : (c + 1) * each, :] = hi
                w_scr[j, rows + c * each : rows + (c + 1) * each, :] = lo
    for t in range(start, stop):
        if nacc:
            o_scr[t - start] = sum(ref[t, row : row + rows, :] for ref in refs[at : at + nacc])
        else:
            o_scr[t - start] = jnp.zeros((rows, LEAF), F32)

    x, core, group, leaves = pos_ref[0], pos_ref[1], pos_ref[2], pos_ref[3]
    odd = group % 2
    column = []
    for kind, _, _ in sets:
        relative = {"own": 1, "pair": 2 - 2 * odd, "next": 2 * odd}[kind]
        column.append(relative * leaves + 2 * (2 * x + core))

    for copy in copies:
        copy.wait()
    count = jnp.int32(0)
    list_ref[0] = 0
    for t in range(start, stop):
        for j in range(2 * nset):
            times = times_ref[t // 2, t % 2, column[j // 2] + j % 2]

            @pl.when(times > 0)
            def _(count=count, t=t, j=j, times=times):
                list_ref[count] = t * 8 + j
                times_scr[count] = times

            count = count + (times > 0).astype(jnp.int32)

    def block(index, slot):
        code = list_ref[jnp.minimum(index, jnp.maximum(count - 1, 0))]
        t, j = code // 8, code % 8
        side = t_ref[t]
        off = tb_ref[t][:1, :]
        for half in range(2):
            part = slice(half * 256, (half + 1) * 256)
            cross = dot(s_scr[j, part, :], side)
            src_off = sb_scr[j, part, :]
            src_off = jnp.concatenate([src_off] * (LEAF // 128), axis=1)
            k_hi, k_lo = halves(jnp.exp2(cross + src_off + off))
            k_scr[slot, part, :] = k_hi
            k_scr[slot, LEAF + half * 256 : LEAF + (half + 1) * 256, :] = k_lo

    def apply(index, slot):
        code = list_ref[index]
        t, j = code // 8 - start, code % 8
        factor = times_scr[index]
        for half in range(2):
            cols = slice(half * 256, (half + 1) * 256)
            both = dot(w_scr[j], k_scr[slot, :LEAF, cols])
            low = dot(w_scr[j, :rows, :], k_scr[slot, LEAF:, cols])
            o_scr[t, :, cols] = o_scr[t, :, cols] + factor * (both[:rows] + both[rows:] + low)

    @pl.when(count > 0)
    def _():
        block(0, 0)

    def pair(index, carry):
        block(2 * index + 1, 1)
        apply(2 * index, 0)

        @pl.when(2 * index + 1 < count)
        def _():
            block(2 * index + 2, 0)
            apply(2 * index + 1, 1)

        return carry

    lax.fori_loop(0, (count + 1) // 2, pair, jnp.int32(0))
    if nacc:
        tall = outs[0].shape[0]
        for n, ref in enumerate(outs):
            t, top = 2 * (n // (rows // tall)), n % (rows // tall) * tall
            for leaf in range(2):
                cols = slice(leaf * LEAF, (leaf + 1) * LEAF)
                ref[:, cols] = o_scr[t + leaf, top : top + tall, :]


def near_call(name, pos, msgs, targets, leaves_at, sources, rows, row=0, acc=(), after=()):
    nset = len(sources)
    start, stop = leaves_at
    tall = R // 2
    vmem = pl.BlockSpec(memory_space=pltpu.VMEM)
    smem = pl.BlockSpec(memory_space=pltpu.SMEM)
    operands = [a for _, heads, chunks in sources for a in (*heads, *chunks)]
    scratch = [
        pltpu.VMEM((2 * nset, LEAF, 4 * F), BF),
        pltpu.VMEM((2 * nset, LEAF, 128), F32),
        pltpu.VMEM((2 * nset, 2 * rows, LEAF), BF),
        pltpu.VMEM((stop - start, rows, LEAF), F32),
        pltpu.VMEM((2, 2 * LEAF, LEAF), BF),
        pltpu.SMEM((2 * nset * (stop - start),), F32),
        pltpu.SMEM((2 * nset * (stop - start),), jnp.int32),
        pltpu.SMEM((len(msgs), EXTRA, 128), F32),
        pltpu.SemaphoreType.DMA((len(msgs),)),
    ]
    if not acc:
        out = [jax.ShapeDtypeStruct((stop - start, rows, LEAF), F32)]
        scratch.pop(3)
    else:
        operands += list(acc)
        out = [jax.ShapeDtypeStruct((tall, 2 * LEAF), F32)] * ((stop - start) // 2 * (rows // tall))
    sets = tuple((kind, len(heads) - 1, len(chunks)) for kind, heads, chunks in sources)
    return pl.pallas_call(
        partial(
            near_body, len(msgs) // 2, sets, leaves_at, rows, row, len(acc), len(out)
        ),
        name=name,
        out_shape=out,
        in_specs=[smem]
        + [pl.BlockSpec(memory_space=pl.ANY)] * len(msgs)
        + [vmem] * (2 + len(operands))
        + [pl.BlockSpec(memory_space=pl.ANY)] * len(after),
        out_specs=[vmem] * len(out),
        scratch_shapes=scratch,
        compiler_params=pltpu.CompilerParams(vmem_limit_bytes=VMEM_LIMIT),
    )(pos, *msgs, *targets, *operands, *after)


def source_body(pts_ref, side_ref, off_ref):
    for leaf in range(2):
        cols = slice(leaf * LEAF, (leaf + 1) * LEAF)
        side, off = source_side(pts_ref[:, cols] * SCALE)
        side_ref[leaf] = side
        off_ref[leaf] = jnp.broadcast_to(off, (LEAF, 128))


def source_call(pts):
    vmem = pl.BlockSpec(memory_space=pltpu.VMEM)
    return pl.pallas_call(
        source_body,
        name="source_side",
        out_shape=[
            jax.ShapeDtypeStruct((2, LEAF, 4 * F), BF),
            jax.ShapeDtypeStruct((2, LEAF, 128), F32),
        ],
        in_specs=[vmem],
        out_specs=[vmem, vmem],
        compiler_params=pltpu.CompilerParams(vmem_limit_bytes=VMEM_LIMIT),
    )(pts)


def share_rows(xs):
    return R // (2 * xs) * SK // (2 * LEAF)


def leaf_body(xs, pos_ref, count_ref, src_ref, pts_in, w_in, interp_in, *refs):
    msgs = refs[: 2 * xs]
    pts_ref, w_ref, interp_ref, scr, sems = refs[2 * xs :]
    copies = [
        pltpu.make_async_copy(pts_in, pts_ref, sems.at[0]),
        pltpu.make_async_copy(w_in, w_ref, sems.at[1]),
        pltpu.make_async_copy(interp_in, interp_ref, sems.at[2]),
    ]
    for copy in copies:
        copy.start()
    x, core, group, leaves = pos_ref[0], pos_ref[1], pos_ref[2], pos_ref[3]
    lane = lax.broadcasted_iota(jnp.int32, (1, 128), 1) + (group - 1) * leaves
    times = []
    for leaf in range(2):
        row = jnp.zeros((1, 128), F32)
        for slot in range(src_ref.shape[1]):
            name = jnp.where(slot < count_ref[0, leaf], src_ref[leaf, slot], -1 - 128 * leaves)
            row = row + (lane == name).astype(F32)
        times.append(row)
    times = jnp.concatenate(times + [jnp.zeros((EXTRA - 2, 128), F32)], axis=0)
    for copy in copies:
        copy.wait()
    total = jnp.zeros((R, SK), F32)
    for leaf in range(2):
        total = total + dot3(w_ref[:, leaf * LEAF : (leaf + 1) * LEAF], interp_ref[leaf])
    scr[...] = total
    rows = R // (2 * xs)
    tall = share_rows(xs)
    for n, msg in enumerate(msgs):
        helper = 2 * lax.rem(x + n // 2, xs) + (core if n % 2 == 0 else 1 - core)
        msg[:F, :] = pts_ref[...]
        msg[F : F + EXTRA, :] = jnp.zeros((EXTRA, 2 * LEAF), F32)
        msg[F : F + EXTRA, :128] = times
        for i in range(rows // tall):
            at = pl.multiple_of(helper * rows + i * tall, tall)
            msg[F + EXTRA :, i * SK : (i + 1) * SK] = scr[pl.ds(at, tall), :]


def leaf_call(xs, pos, near_count, near_src, points, weights, interp):
    vmem = pl.BlockSpec(memory_space=pltpu.VMEM)
    smem = pl.BlockSpec(memory_space=pltpu.SMEM)
    anywhere = pl.BlockSpec(memory_space=pl.ANY)
    height = F + EXTRA + share_rows(xs)
    return pl.pallas_call(
        partial(leaf_body, xs),
        name="leaf_up",
        out_shape=[jax.ShapeDtypeStruct((height, 2 * LEAF), F32)] * (2 * xs),
        in_specs=[smem, smem, smem, anywhere, anywhere, anywhere],
        out_specs=[vmem] * (2 * xs),
        scratch_shapes=[
            pltpu.VMEM(points.shape, F32),
            pltpu.VMEM(weights.shape, F32),
            pltpu.VMEM(interp.shape, F32),
            pltpu.VMEM((R, SK), F32),
            pltpu.SemaphoreType.DMA((3,)),
        ],
        compiler_params=pltpu.CompilerParams(vmem_limit_bytes=VMEM_WHOLE),
    )(pos, near_count, near_src, points, weights, interp)


def skel_body(xs, pos_ref, index_ref, *refs):
    msgs, (out_ref, side_ref, off_ref) = refs[:-3], refs[-3:]
    rows = R // (2 * xs)
    tall = share_rows(xs)
    total = jnp.zeros((2 * F, SK), F32)
    value = jnp.zeros((tall, 2 * LEAF), F32)
    spot = lax.broadcasted_iota(jnp.int32, (2 * LEAF, SK), 0)
    x, core = pos_ref[0], pos_ref[1]
    for b, msg in enumerate(msgs):
        helper = 2 * lax.rem(x + b // 2, xs) + (core if b % 2 == 0 else 1 - core)
        side, off = target_side(msg[:F, :] * SCALE)
        for leaf in range(2):
            part = slice(leaf * LEAF, (leaf + 1) * LEAF)
            side_ref[2 * b + leaf] = side[:, part]
            off_ref[2 * b + leaf] = jnp.broadcast_to(off[:, part], (8, LEAF))
        hot = spot + helper * (2 * LEAF) == index_ref[...]
        total = total + dot(side[: 2 * F], hot.astype(F32).astype(BF))
        value = value + msg[F + EXTRA :, :]
    out_ref[:F, :] = total[:F] + total[F:]
    for i in range(rows // tall):
        out_ref[F + i * tall : F + (i + 1) * tall, :] = value[:, i * SK : (i + 1) * SK]


def skel_call(xs, pos, index, msgs):
    rows = R // (2 * xs)
    leaves = 2 * len(msgs)
    vmem = pl.BlockSpec(memory_space=pltpu.VMEM)
    payload, *targets = pl.pallas_call(
        partial(skel_body, xs),
        name="skeleton",
        out_shape=[
            jax.ShapeDtypeStruct((F + rows, SK), F32),
            jax.ShapeDtypeStruct((leaves, 4 * F, LEAF), BF),
            jax.ShapeDtypeStruct((leaves, 8, LEAF), F32),
        ],
        in_specs=[pl.BlockSpec(memory_space=pltpu.SMEM)] + [vmem] * (1 + len(msgs)),
        out_specs=[vmem] * 3,
        compiler_params=pltpu.CompilerParams(vmem_limit_bytes=VMEM_LIMIT),
        cost_estimate=pl.CostEstimate(
            flops=5_000_000_000, bytes_accessed=8_000_000, transcendentals=0
        ),
    )(pos, index, *msgs)
    return payload, targets


def stack_body(*refs):
    for n, ref in enumerate(refs[:-1]):
        refs[-1][n] = ref[...]


def stack_call(pieces):
    vmem = pl.BlockSpec(memory_space=pltpu.VMEM)
    return pl.pallas_call(
        stack_body,
        name="stack",
        out_shape=jax.ShapeDtypeStruct((len(pieces), *pieces[0].shape), F32),
        in_specs=[vmem] * len(pieces),
        out_specs=vmem,
        compiler_params=pltpu.CompilerParams(vmem_limit_bytes=VMEM_LIMIT),
    )(*pieces)


def upper_start(level, groups):
    return sum((groups >> step for step in range(1, level)))


def list_start(level, groups):
    return sum((groups >> step for step in range(level)))


def far_body(groups, rows, pos_ref, far_ref, node_ref, transfer_ref, alike_ref, beside_ref, *refs):
    out_ref, p_scr, u_scr, f_scr = refs[-4:]
    levels = groups.bit_length() - 1
    group = pos_ref[2]
    start = [list_start(level, groups) for level in range(levels)]
    for n in range(groups // 2):
        same, other = group ^ (2 * n), group ^ (2 * n + 1)
        p_scr[same] = alike_ref[n, :F, :]
        u_scr[same] = alike_ref[n, F:, :]
        p_scr[other] = beside_ref[n, :F, :]
        u_scr[other] = beside_ref[n, F:, :]
    spot = lax.broadcasted_iota(jnp.int32, (2 * SK, SK), 0)
    for level in range(1, levels):
        for n in range(groups >> level):
            row = upper_start(level, groups) + n
            left = start[level - 1] + 2 * n
            hot = (spot == node_ref[row : row + 1, :]).astype(F32).astype(BF)
            hi, lo = halves(jnp.concatenate([p_scr[left], p_scr[left + 1]], axis=1))
            both = dot(jnp.concatenate([hi, lo], axis=0), hot)
            p_scr[start[level] + n] = both[:F] + both[F:]
            vals = jnp.concatenate([u_scr[left], u_scr[left + 1]], axis=1)
            u_scr[start[level] + n] = dot3(vals, transfer_ref[row])
    for level in range(levels):
        node = group >> level
        side, off = target_side(p_scr[start[level] + node])
        f_scr[level] = jnp.zeros((rows, SK), F32)

        def one(n, carry, level=level, node=node, side=side, off=off):
            hits = jnp.int32(0)
            for slot in range(FL):
                hits = hits + (far_ref[slot, start[level] + node] == n).astype(jnp.int32)

            @pl.when(hits > 0)
            def _():
                src, src_off = source_side(p_scr[start[level] + n])
                block = jnp.exp2(dot(src, side) + src_off + off)
                term = dot3(u_scr[start[level] + n], block)
                f_scr[level] = f_scr[level] + hits.astype(F32) * term

            return carry

        lax.fori_loop(0, groups >> level, one, jnp.int32(0))
    local = f_scr[levels - 1]
    for level in range(levels - 1, 0, -1):
        row = upper_start(level, groups) + (group >> level)
        bit = (group >> (level - 1)) & 1
        matrix = transfer_ref[row, pl.ds(pl.multiple_of(bit * SK, SK), SK), :]
        local = f_scr[level - 1] + dot3(local, matrix, dot_t)
    out_ref[...] = local


def far_call(groups, pos, far_nodes, skel_node, transfer, alike, beside, after):
    rows = alike.shape[1] - F
    vmem = pl.BlockSpec(memory_space=pltpu.VMEM)
    smem = pl.BlockSpec(memory_space=pltpu.SMEM)
    nodes = 2 * groups
    return pl.pallas_call(
        partial(far_body, groups, rows),
        name="far",
        out_shape=jax.ShapeDtypeStruct((rows, SK), F32),
        in_specs=[smem, smem, vmem, vmem, vmem, vmem]
        + [pl.BlockSpec(memory_space=pl.ANY)] * len(after),
        out_specs=vmem,
        scratch_shapes=[
            pltpu.VMEM((nodes, F, SK), F32),
            pltpu.VMEM((nodes, rows, SK), F32),
            pltpu.VMEM((groups.bit_length(), rows, SK), F32),
        ],
        compiler_params=pltpu.CompilerParams(vmem_limit_bytes=VMEM_LIMIT),
    )(pos, far_nodes.T, skel_node, transfer, alike, beside, *after)


def final_body(xs, pos_ref, interp_ref, *refs):
    values, sums = refs[: 2 * xs], refs[2 * xs : -2]
    out_ref, v_scr = refs[-2:]
    rows = R // (2 * xs)
    x, core = pos_ref[0], pos_ref[1]
    for n, ref in enumerate(values):
        helper = 2 * lax.rem(x + n // 2, xs) + (core if n % 2 == 0 else 1 - core)
        v_scr[pl.ds(pl.multiple_of(helper * rows, rows), rows), :] = ref[...]
    value = v_scr[...]
    for leaf in range(2):
        cols = slice(leaf * LEAF, (leaf + 1) * LEAF)
        total = dot3(value, interp_ref[leaf], dot_t)
        for c in range(2):
            part = slice(c * R // 2, (c + 1) * R // 2)
            out_ref[part, cols] = total[part] + sums[c][:, cols] + sums[2 + c][:, cols]


def add_body(count, *refs):
    for n, out_ref in enumerate(refs[-(len(refs) // (count + 1)) :]):
        total = refs[n * count][...]
        for ref in refs[n * count + 1 : (n + 1) * count]:
            total = total + ref[...]
        out_ref[...] = total


def add_call(*sums):
    vmem = pl.BlockSpec(memory_space=pltpu.VMEM)
    operands = [value for terms in sums for value in terms]
    return pl.pallas_call(
        partial(add_body, len(sums[0])),
        name="add_parts",
        out_shape=[jax.ShapeDtypeStruct(sums[0][0].shape, F32)] * len(sums),
        in_specs=[vmem] * len(operands),
        out_specs=[vmem] * len(sums),
        compiler_params=pltpu.CompilerParams(vmem_limit_bytes=VMEM_LIMIT),
    )(*operands)


def final_call(xs, pos, interp, home, mate, values):
    vmem = pl.BlockSpec(memory_space=pltpu.VMEM)
    return pl.pallas_call(
        partial(final_body, xs),
        name="join",
        out_shape=jax.ShapeDtypeStruct((R, 2 * LEAF), F32),
        in_specs=[pl.BlockSpec(memory_space=pltpu.SMEM)] + [vmem] * (1 + 2 * xs + 4),
        out_specs=vmem,
        scratch_shapes=[pltpu.VMEM((R, SK), F32)],
        compiler_params=pltpu.CompilerParams(vmem_limit_bytes=VMEM_LIMIT),
    )(pos, interp, *values, *home, *mate)


def help_pairs(xs, dx, dc):
    return [
        (2 * ((x + dx) % xs) + (core ^ dc), 2 * x + core) for x in range(xs) for core in range(2)
    ]


def shards(
    points, weights, interp, transfer, near_count, near_src, skel_group, skel_node, far_nodes
):
    helpers = lax.axis_size("help")
    groups = lax.axis_size("leaf")
    xs = helpers // 2
    helper = lax.axis_index("help")
    group = lax.axis_index("leaf")
    x, core = helper // 2, helper % 2
    leaves = 2 * helpers
    pos = jnp.stack([x, core, group, jnp.int32(leaves)]).astype(jnp.int32)
    rows = R // 2

    def from_help(value, dx, dc):
        return lax.ppermute(value, "help", help_pairs(xs, dx, dc))

    def to_help(value, dx):
        return lax.ppermute(value, "help", help_pairs(xs, -dx, 0))

    def together(*values):
        return lax.optimization_barrier(values)

    beside = [(i, i ^ 1) for i in range(groups)]
    across = [(i, i + 2) for i in range(0, groups - 2, 2)]
    across += [(i, i - 2) for i in range(3, groups, 2)]
    order = [(dx, dc) for dx in range(xs) for dc in range(2)]

    pts_y = lax.ppermute(points, "leaf", beside)
    w_own = [weights[:rows], weights[rows:]]
    w_y = [lax.ppermute(chunk, "leaf", beside) for chunk in w_own]
    sent = leaf_call(xs, pos, near_count, near_src, points, weights, interp)
    got = [
        lax.ppermute(sent[n], "help", help_pairs(xs, -dx, dc))
        for n, (dx, dc) in enumerate(order)
        if n
    ]
    pts_z = lax.ppermute(pts_y, "leaf", across)
    w_z = [lax.ppermute(w_y[0], "leaf", across)]

    got, pts_z = together(got, pts_z)
    msgs = [sent[0]] + [got[order.index((-dx % xs, dc)) - 1] for dx, dc in order[1:]]
    payload, targets = skel_call(xs, pos, skel_group, msgs)
    every = (0, 2 * helpers)
    (own,) = near_call("near_own", pos, msgs, targets, every, [("own", (points,), [weights])], R)
    own, w_y[1], payload, w_z[0] = together(own, w_y[1], payload, w_z[0])
    w_z.append(lax.ppermute(w_y[1], "leaf", across))
    pieces = [payload]
    for mask in range(2, groups, 2):
        pieces.append(lax.ppermute(payload, "leaf", [(i, i ^ mask) for i in range(groups)]))

    (pair,) = near_call("near_pair", pos, msgs, targets, every, [("pair", (pts_y,), w_y)], R)
    pieces, pair = together(pieces, pair)
    alike = stack_call(pieces)
    side = lax.ppermute(alike, "leaf", beside)
    z_side = source_call(pts_z)
    near = [own, pair]
    sums, part = [], [alike]
    for c in range(2):
        part = near_call(
            "near_next_away", pos, msgs, targets, (4, 2 * helpers),
            [("next", z_side, w_z[c : c + 1])], rows, c * rows, near, part[:1],
        )
        kept, given = part[::2], part[1::2]
        sums.append((kept, [from_help(value, 0, 1) for value in given]))
    parts = []
    for c in range(2):
        kept, mates = sums[c]
        both = add_call(*zip(kept, mates))
        parts.append([to_help(value, dx + 1) for dx, value in enumerate(both)])
    v_own = far_call(groups, pos, far_nodes, skel_node, transfer, alike, side, both[:1])
    values = [v_own] + [from_help(v_own, dx, dc) for dx, dc in order[1:]]
    home = near_call(
        "near_next_home", pos, msgs, targets, (0, 4), [("next", z_side, w_z)], R, 0, near, [v_own]
    )
    mate = [from_help(value, 0, 1) for value in home[2:]]
    mine = add_call(*[[home[c], *parts[c]] for c in range(2)])
    return final_call(xs, pos, interp, mine, mate, values)


def solution(mesh):
    placed = (
        P(None, ("leaf", "help")),
        P(None, ("leaf", "help")),
        P(("leaf", "help"), None, None),
        P(),
        P("leaf", "help"),
        P(("leaf", "help"), None),
        P("leaf", None),
        P(),
        P(),
    )
    return jax.shard_map(
        shards, mesh=mesh, in_specs=placed, out_specs=P(None, ("leaf", "help")), check_vma=False
    )
```

```python
import math
from functools import partial

import jax
import jax.numpy as jnp
from jax import lax
from jax.experimental import pallas as pl
from jax.experimental.pallas import tpu as pltpu
from jax.sharding import PartitionSpec as P

F = 64
R = 256
LEAF = 512
SK = 256
FL = 4
EXTRA = 8

BF = jnp.bfloat16
F32 = jnp.float32
LOG2E = 1.0 / math.log(2.0)
SCALE = math.sqrt(0.5 * LOG2E)
BIAS = 0.0625 * F * LOG2E
VMEM_LIMIT = 24 * 1024 * 1024
VMEM_WHOLE = 64 * 1024 * 1024


def dot(a, b):
    return jnp.dot(a, b, preferred_element_type=F32)


def dot_t(a, b):
    return lax.dot_general(a, b, (((1,), (1,)), ((), ())), preferred_element_type=F32)


def halves(x):
    hi = x.astype(BF)
    lo = (x - hi.astype(F32)).astype(BF)
    return hi, lo


def dot3(a, b, mul=dot):
    a_hi, a_lo = halves(a)
    b_hi, b_lo = halves(b)
    return mul(a_hi, b_hi) + mul(a_lo, b_hi) + mul(a_hi, b_lo)


def target_side(x):
    hi, lo = halves(x)
    both = hi.astype(F32) + lo.astype(F32)
    off = BIAS - 0.5 * jnp.sum(both * both, axis=0, keepdims=True)
    return jnp.concatenate([hi, lo, hi, lo], axis=0), off


def source_side(x):
    xt = x.T
    hi, lo = halves(xt)
    both = hi.astype(F32) + lo.astype(F32)
    off = BIAS - 0.5 * jnp.sum(both * both, axis=1, keepdims=True)
    return jnp.concatenate([hi, hi, lo, lo], axis=1), off


def near_body(
    xs, sets, leaves_at, rows, row, nacc, nout, pos_ref, *refs
):
    nset = len(sets)
    start, stop = leaves_at
    msgs, (t_ref, tb_ref), refs = refs[: 2 * xs], refs[2 * xs : 2 * xs + 2], refs[2 * xs + 2 :]
    if nacc:
        s_scr, sb_scr, w_scr, o_scr, k_scr, times_scr, list_ref, times_ref, sems = refs[-9:]
        outs = refs[-9 - nout : -9]
    else:
        o_scr, s_scr, sb_scr, w_scr, k_scr, times_scr, list_ref, times_ref, sems = refs[-9:]
    copies = [
        pltpu.make_async_copy(msgs[b].at[F : F + EXTRA, :128], times_ref.at[b], sems.at[b])
        for b in range(start // 2, stop // 2)
    ]
    for copy in copies:
        copy.start()
    at = 0
    for k, (_, ready, chunks) in enumerate(sets):
        heads = refs[at : at + 1 + ready]
        parts = refs[at + 1 + ready : at + 1 + ready + chunks]
        at += 1 + ready + chunks
        each = rows // chunks
        for leaf in range(2):
            cols = slice(leaf * LEAF, (leaf + 1) * LEAF)
            j = 2 * k + leaf
            if ready:
                s_scr[j] = heads[0][leaf]
                sb_scr[j] = heads[1][leaf]
            else:
                side, off = source_side(heads[0][:F, cols] * SCALE)
                s_scr[j] = side
                sb_scr[j] = jnp.broadcast_to(off, (LEAF, 128))
            for c in range(chunks):
                hi, lo = halves(parts[c][parts[c].shape[0] - each :, cols])
                w_scr[j, c * each : (c + 1) * each, :] = hi
                w_scr[j, rows + c * each : rows + (c + 1) * each, :] = lo
    for t in range(start, stop):
        if nacc:
            o_scr[t - start] = sum(
                ref[t - (4 * xs - ref.shape[0]), row : row + rows, :] for ref in refs[at : at + nacc]
            )
        else:
            o_scr[t - start] = jnp.zeros((rows, LEAF), F32)

    x, core, group, leaves = pos_ref[0], pos_ref[1], pos_ref[2], pos_ref[3]
    odd = group % 2
    column = []
    for kind, _, _ in sets:
        relative = {"own": 1, "pair": 2 - 2 * odd, "next": 2 * odd}[kind]
        column.append(relative * leaves + 2 * (2 * x + core))

    for copy in copies:
        copy.wait()
    count = jnp.int32(0)
    list_ref[0] = 0
    for t in range(start, stop):
        for j in range(2 * nset):
            times = times_ref[t // 2, t % 2, column[j // 2] + j % 2]

            @pl.when(times > 0)
            def _(count=count, t=t, j=j, times=times):
                list_ref[count] = t * 8 + j
                times_scr[count] = times

            count = count + (times > 0).astype(jnp.int32)

    def block(index, slot):
        code = list_ref[jnp.minimum(index, jnp.maximum(count - 1, 0))]
        t, j = code // 8, code % 8
        side = t_ref[t]
        off = tb_ref[t][:1, :]
        for half in range(2):
            part = slice(half * 256, (half + 1) * 256)
            cross = dot(s_scr[j, part, :], side)
            src_off = sb_scr[j, part, :]
            src_off = jnp.concatenate([src_off] * (LEAF // 128), axis=1)
            k_hi, k_lo = halves(jnp.exp2(cross + src_off + off))
            k_scr[slot, part, :] = k_hi
            k_scr[slot, LEAF + half * 256 : LEAF + (half + 1) * 256, :] = k_lo

    def apply(index, slot):
        code = list_ref[index]
        t, j = code // 8 - start, code % 8
        factor = times_scr[index]
        for half in range(2):
            cols = slice(half * 256, (half + 1) * 256)
            both = dot(w_scr[j], k_scr[slot, :LEAF, cols])
            low = dot(w_scr[j, :rows, :], k_scr[slot, LEAF:, cols])
            o_scr[t, :, cols] = o_scr[t, :, cols] + factor * (both[:rows] + both[rows:] + low)

    @pl.when(count > 0)
    def _():
        block(0, 0)

    def pair(index, carry):
        block(2 * index + 1, 1)
        apply(2 * index, 0)

        @pl.when(2 * index + 1 < count)
        def _():
            block(2 * index + 2, 0)
            apply(2 * index + 1, 1)

        return carry

    lax.fori_loop(0, (count + 1) // 2, pair, jnp.int32(0))
    if nacc:
        tall = outs[0].shape[0]
        for n, ref in enumerate(outs):
            t, top = 2 * (n // (rows // tall)), n % (rows // tall) * tall
            for leaf in range(2):
                cols = slice(leaf * LEAF, (leaf + 1) * LEAF)
                ref[:, cols] = o_scr[t + leaf, top : top + tall, :]


def near_call(name, pos, msgs, targets, leaves_at, sources, rows, row=0, acc=(), after=()):
    nset = len(sources)
    start, stop = leaves_at
    tall = R // 2
    vmem = pl.BlockSpec(memory_space=pltpu.VMEM)
    smem = pl.BlockSpec(memory_space=pltpu.SMEM)
    operands = [a for _, heads, chunks in sources for a in (*heads, *chunks)]
    scratch = [
        pltpu.VMEM((2 * nset, LEAF, 4 * F), BF),
        pltpu.VMEM((2 * nset, LEAF, 128), F32),
        pltpu.VMEM((2 * nset, 2 * rows, LEAF), BF),
        pltpu.VMEM((stop - start, rows, LEAF), F32),
        pltpu.VMEM((2, 2 * LEAF, LEAF), BF),
        pltpu.SMEM((2 * nset * (stop - start),), F32),
        pltpu.SMEM((2 * nset * (stop - start),), jnp.int32),
        pltpu.SMEM((len(msgs), EXTRA, 128), F32),
        pltpu.SemaphoreType.DMA((len(msgs),)),
    ]
    if not acc:
        out = [jax.ShapeDtypeStruct((stop - start, rows, LEAF), F32)]
        scratch.pop(3)
    else:
        operands += list(acc)
        out = [jax.ShapeDtypeStruct((tall, 2 * LEAF), F32)] * ((stop - start) // 2 * (rows // tall))
    sets = tuple((kind, len(heads) - 1, len(chunks)) for kind, heads, chunks in sources)
    return pl.pallas_call(
        partial(
            near_body, len(msgs) // 2, sets, leaves_at, rows, row, len(acc), len(out)
        ),
        name=name,
        out_shape=out,
        in_specs=[smem]
        + [pl.BlockSpec(memory_space=pl.ANY)] * len(msgs)
        + [vmem] * (2 + len(operands))
        + [pl.BlockSpec(memory_space=pl.ANY)] * len(after),
        out_specs=[vmem] * len(out),
        scratch_shapes=scratch,
        compiler_params=pltpu.CompilerParams(vmem_limit_bytes=VMEM_LIMIT),
    )(pos, *msgs, *targets, *operands, *after)


def source_body(pts_ref, side_ref, off_ref):
    for leaf in range(2):
        cols = slice(leaf * LEAF, (leaf + 1) * LEAF)
        side, off = source_side(pts_ref[:F, cols] * SCALE)
        side_ref[leaf] = side
        off_ref[leaf] = jnp.broadcast_to(off, (LEAF, 128))


def source_call(pts):
    vmem = pl.BlockSpec(memory_space=pltpu.VMEM)
    return pl.pallas_call(
        source_body,
        name="source_side",
        out_shape=[
            jax.ShapeDtypeStruct((2, LEAF, 4 * F), BF),
            jax.ShapeDtypeStruct((2, LEAF, 128), F32),
        ],
        in_specs=[vmem],
        out_specs=[vmem, vmem],
        compiler_params=pltpu.CompilerParams(vmem_limit_bytes=VMEM_LIMIT),
    )(pts)


def share_rows(xs):
    return R // (2 * xs) * SK // (2 * LEAF)


def leaf_body(xs, pos_ref, count_ref, src_ref, pts_in, w_in, interp_in, *refs):
    msgs = refs[: 2 * xs]
    pts_ref, w_ref, interp_ref, scr, sems = refs[2 * xs :]
    copies = [
        pltpu.make_async_copy(pts_in, pts_ref, sems.at[0]),
        pltpu.make_async_copy(w_in, w_ref, sems.at[1]),
        pltpu.make_async_copy(interp_in, interp_ref, sems.at[2]),
    ]
    for copy in copies:
        copy.start()
    x, core, group, leaves = pos_ref[0], pos_ref[1], pos_ref[2], pos_ref[3]
    lane = lax.broadcasted_iota(jnp.int32, (1, 128), 1) + (group - 1) * leaves
    times = []
    for leaf in range(2):
        row = jnp.zeros((1, 128), F32)
        for slot in range(src_ref.shape[1]):
            name = jnp.where(slot < count_ref[0, leaf], src_ref[leaf, slot], -1 - 128 * leaves)
            row = row + (lane == name).astype(F32)
        times.append(row)
    times = jnp.concatenate(times + [jnp.zeros((EXTRA - 2, 128), F32)], axis=0)
    for copy in copies:
        copy.wait()
    total = jnp.zeros((R, SK), F32)
    for leaf in range(2):
        total = total + dot3(w_ref[:, leaf * LEAF : (leaf + 1) * LEAF], interp_ref[leaf])
    scr[...] = total
    rows = R // (2 * xs)
    tall = share_rows(xs)
    for n, msg in enumerate(msgs):
        helper = 2 * lax.rem(x + n // 2, xs) + (core if n % 2 == 0 else 1 - core)
        msg[:F, :] = pts_ref[...]
        msg[F : F + EXTRA, :] = jnp.zeros((EXTRA, 2 * LEAF), F32)
        msg[F : F + EXTRA, :128] = times
        for i in range(rows // tall):
            at = pl.multiple_of(helper * rows + i * tall, tall)
            msg[F + EXTRA :, i * SK : (i + 1) * SK] = scr[pl.ds(at, tall), :]


def leaf_call(xs, pos, near_count, near_src, points, weights, interp):
    vmem = pl.BlockSpec(memory_space=pltpu.VMEM)
    smem = pl.BlockSpec(memory_space=pltpu.SMEM)
    anywhere = pl.BlockSpec(memory_space=pl.ANY)
    height = F + EXTRA + share_rows(xs)
    return pl.pallas_call(
        partial(leaf_body, xs),
        name="leaf_up",
        out_shape=[jax.ShapeDtypeStruct((height, 2 * LEAF), F32)] * (2 * xs),
        in_specs=[smem, smem, smem, anywhere, anywhere, anywhere],
        out_specs=[vmem] * (2 * xs),
        scratch_shapes=[
            pltpu.VMEM(points.shape, F32),
            pltpu.VMEM(weights.shape, F32),
            pltpu.VMEM(interp.shape, F32),
            pltpu.VMEM((R, SK), F32),
            pltpu.SemaphoreType.DMA((3,)),
        ],
        compiler_params=pltpu.CompilerParams(vmem_limit_bytes=VMEM_WHOLE),
    )(pos, near_count, near_src, points, weights, interp)


def skel_body(xs, pos_ref, index_ref, *refs):
    msgs, (out_ref, side_ref, off_ref) = refs[:-3], refs[-3:]
    rows = R // (2 * xs)
    tall = share_rows(xs)
    total = jnp.zeros((2 * F, SK), F32)
    value = jnp.zeros((tall, 2 * LEAF), F32)
    spot = lax.broadcasted_iota(jnp.int32, (2 * LEAF, SK), 0)
    x, core = pos_ref[0], pos_ref[1]
    for b, msg in enumerate(msgs):
        helper = 2 * lax.rem(x + b // 2, xs) + (core if b % 2 == 0 else 1 - core)
        side, off = target_side(msg[:F, :] * SCALE)
        for leaf in range(2):
            part = slice(leaf * LEAF, (leaf + 1) * LEAF)
            side_ref[2 * b + leaf] = side[:, part]
            off_ref[2 * b + leaf] = jnp.broadcast_to(off[:, part], (8, LEAF))
        hot = spot + helper * (2 * LEAF) == index_ref[...]
        total = total + dot(side[: 2 * F], hot.astype(F32).astype(BF))
        value = value + msg[F + EXTRA :, :]
    out_ref[:F, :] = total[:F] + total[F:]
    for i in range(rows // tall):
        out_ref[F + i * tall : F + (i + 1) * tall, :] = value[:, i * SK : (i + 1) * SK]


def skel_call(xs, pos, index, msgs):
    rows = R // (2 * xs)
    leaves = 2 * len(msgs)
    vmem = pl.BlockSpec(memory_space=pltpu.VMEM)
    payload, *targets = pl.pallas_call(
        partial(skel_body, xs),
        name="skeleton",
        out_shape=[
            jax.ShapeDtypeStruct((F + rows, SK), F32),
            jax.ShapeDtypeStruct((leaves, 4 * F, LEAF), BF),
            jax.ShapeDtypeStruct((leaves, 8, LEAF), F32),
        ],
        in_specs=[pl.BlockSpec(memory_space=pltpu.SMEM)] + [vmem] * (1 + len(msgs)),
        out_specs=[vmem] * 3,
        compiler_params=pltpu.CompilerParams(vmem_limit_bytes=VMEM_LIMIT),
        cost_estimate=pl.CostEstimate(
            flops=5_000_000_000, bytes_accessed=8_000_000, transcendentals=0
        ),
    )(pos, index, *msgs)
    return payload, targets


def stack_body(*refs):
    for n, ref in enumerate(refs[:-1]):
        refs[-1][n] = ref[...]


def stack_call(pieces):
    vmem = pl.BlockSpec(memory_space=pltpu.VMEM)
    return pl.pallas_call(
        stack_body,
        name="stack",
        out_shape=jax.ShapeDtypeStruct((len(pieces), *pieces[0].shape), F32),
        in_specs=[vmem] * len(pieces),
        out_specs=vmem,
        compiler_params=pltpu.CompilerParams(vmem_limit_bytes=VMEM_LIMIT),
    )(*pieces)


def upper_start(level, groups):
    return sum((groups >> step for step in range(1, level)))


def list_start(level, groups):
    return sum((groups >> step for step in range(level)))


def far_body(groups, rows, pos_ref, far_ref, node_ref, transfer_ref, alike_ref, beside_ref, *refs):
    out_ref, p_scr, u_scr, f_scr = refs[-4:]
    levels = groups.bit_length() - 1
    group = pos_ref[2]
    start = [list_start(level, groups) for level in range(levels)]
    for n in range(groups // 2):
        same, other = group ^ (2 * n), group ^ (2 * n + 1)
        p_scr[same] = alike_ref[n, :F, :]
        u_scr[same] = alike_ref[n, F:, :]
        p_scr[other] = beside_ref[n, :F, :]
        u_scr[other] = beside_ref[n, F:, :]
    spot = lax.broadcasted_iota(jnp.int32, (2 * SK, SK), 0)
    for level in range(1, levels):
        for n in range(groups >> level):
            row = upper_start(level, groups) + n
            left = start[level - 1] + 2 * n
            hot = (spot == node_ref[row : row + 1, :]).astype(F32).astype(BF)
            hi, lo = halves(jnp.concatenate([p_scr[left], p_scr[left + 1]], axis=1))
            both = dot(jnp.concatenate([hi, lo], axis=0), hot)
            p_scr[start[level] + n] = both[:F] + both[F:]
            vals = jnp.concatenate([u_scr[left], u_scr[left + 1]], axis=1)
            u_scr[start[level] + n] = dot3(vals, transfer_ref[row])
    for level in range(levels):
        node = group >> level
        side, off = target_side(p_scr[start[level] + node])
        f_scr[level] = jnp.zeros((rows, SK), F32)

        def one(n, carry, level=level, node=node, side=side, off=off):
            hits = jnp.int32(0)
            for slot in range(FL):
                hits = hits + (far_ref[slot, start[level] + node] == n).astype(jnp.int32)

            @pl.when(hits > 0)
            def _():
                src, src_off = source_side(p_scr[start[level] + n])
                block = jnp.exp2(dot(src, side) + src_off + off)
                term = dot3(u_scr[start[level] + n], block)
                f_scr[level] = f_scr[level] + hits.astype(F32) * term

            return carry

        lax.fori_loop(0, groups >> level, one, jnp.int32(0))
    local = f_scr[levels - 1]
    for level in range(levels - 1, 0, -1):
        row = upper_start(level, groups) + (group >> level)
        bit = (group >> (level - 1)) & 1
        matrix = transfer_ref[row, pl.ds(pl.multiple_of(bit * SK, SK), SK), :]
        local = f_scr[level - 1] + dot3(local, matrix, dot_t)
    out_ref[...] = local


def far_call(groups, pos, far_nodes, skel_node, transfer, alike, beside, after):
    rows = alike.shape[1] - F
    vmem = pl.BlockSpec(memory_space=pltpu.VMEM)
    smem = pl.BlockSpec(memory_space=pltpu.SMEM)
    nodes = 2 * groups
    return pl.pallas_call(
        partial(far_body, groups, rows),
        name="far",
        out_shape=jax.ShapeDtypeStruct((rows, SK), F32),
        in_specs=[smem, smem, vmem, vmem, vmem, vmem]
        + [pl.BlockSpec(memory_space=pl.ANY)] * len(after),
        out_specs=vmem,
        scratch_shapes=[
            pltpu.VMEM((nodes, F, SK), F32),
            pltpu.VMEM((nodes, rows, SK), F32),
            pltpu.VMEM((groups.bit_length(), rows, SK), F32),
        ],
        compiler_params=pltpu.CompilerParams(vmem_limit_bytes=VMEM_LIMIT),
    )(pos, far_nodes.T, skel_node, transfer, alike, beside, *after)


def final_body(xs, pos_ref, interp_ref, *refs):
    values, sums = refs[: 2 * xs], refs[2 * xs : -2]
    out_ref, v_scr = refs[-2:]
    rows = R // (2 * xs)
    x, core = pos_ref[0], pos_ref[1]
    for n, ref in enumerate(values):
        helper = 2 * lax.rem(x + n // 2, xs) + (core if n % 2 == 0 else 1 - core)
        v_scr[pl.ds(pl.multiple_of(helper * rows, rows), rows), :] = ref[...]
    value = v_scr[...]
    for leaf in range(2):
        cols = slice(leaf * LEAF, (leaf + 1) * LEAF)
        total = dot3(value, interp_ref[leaf], dot_t)
        for c in range(2):
            part = slice(c * R // 2, (c + 1) * R // 2)
            out_ref[part, cols] = total[part] + sums[c][:, cols] + sums[2 + c][:, cols]


def add_body(count, *refs):
    for n, out_ref in enumerate(refs[-(len(refs) // (count + 1)) :]):
        total = refs[n * count][...]
        for ref in refs[n * count + 1 : (n + 1) * count]:
            total = total + ref[...]
        out_ref[...] = total


def add_call(*sums):
    vmem = pl.BlockSpec(memory_space=pltpu.VMEM)
    operands = [value for terms in sums for value in terms]
    return pl.pallas_call(
        partial(add_body, len(sums[0])),
        name="add_parts",
        out_shape=[jax.ShapeDtypeStruct(sums[0][0].shape, F32)] * len(sums),
        in_specs=[vmem] * len(operands),
        out_specs=[vmem] * len(sums),
        compiler_params=pltpu.CompilerParams(vmem_limit_bytes=VMEM_LIMIT),
    )(*operands)


def final_call(xs, pos, interp, home, mate, values):
    vmem = pl.BlockSpec(memory_space=pltpu.VMEM)
    return pl.pallas_call(
        partial(final_body, xs),
        name="join",
        out_shape=jax.ShapeDtypeStruct((R, 2 * LEAF), F32),
        in_specs=[pl.BlockSpec(memory_space=pltpu.SMEM)] + [vmem] * (1 + 2 * xs + 4),
        out_specs=vmem,
        scratch_shapes=[pltpu.VMEM((R, SK), F32)],
        compiler_params=pltpu.CompilerParams(vmem_limit_bytes=VMEM_LIMIT),
    )(pos, interp, *values, *home, *mate)


def help_pairs(xs, dx, dc):
    return [
        (2 * ((x + dx) % xs) + (core ^ dc), 2 * x + core) for x in range(xs) for core in range(2)
    ]


def shards(
    points, weights, interp, transfer, near_count, near_src, skel_group, skel_node, far_nodes
):
    helpers = lax.axis_size("help")
    groups = lax.axis_size("leaf")
    xs = helpers // 2
    helper = lax.axis_index("help")
    group = lax.axis_index("leaf")
    x, core = helper // 2, helper % 2
    leaves = 2 * helpers
    pos = jnp.stack([x, core, group, jnp.int32(leaves)]).astype(jnp.int32)
    rows = R // 2

    def from_help(value, dx, dc):
        return lax.ppermute(value, "help", help_pairs(xs, dx, dc))

    def to_help(value, dx):
        return lax.ppermute(value, "help", help_pairs(xs, -dx, 0))

    def together(*values):
        return lax.optimization_barrier(values)

    beside = [(i, i ^ 1) for i in range(groups)]
    across = [(i, i + 2) for i in range(0, groups - 2, 2)]
    across += [(i, i - 2) for i in range(3, groups, 2)]
    order = [(dx, dc) for dx in range(xs) for dc in range(2)]

    w_y = [jnp.concatenate([points, weights[:rows]], axis=0), weights[rows:]]
    w_y = [lax.ppermute(chunk, "leaf", beside) for chunk in w_y]
    sent = leaf_call(xs, pos, near_count, near_src, points, weights, interp)
    got = [
        lax.ppermute(sent[n], "help", help_pairs(xs, -dx, dc))
        for n, (dx, dc) in enumerate(order)
        if n
    ]
    w_z = [lax.ppermute(w_y[0], "leaf", across)]
    msgs = [sent[0]] + [got[order.index((-dx % xs, dc)) - 1] for dx, dc in order[1:]]
    payload, targets = skel_call(xs, pos, skel_group, msgs)
    pieces = [payload]
    for mask in range(2, groups, 2):
        pieces.append(lax.ppermute(payload, "leaf", [(i, i ^ mask) for i in range(groups)]))

    every, away, home = (0, 2 * helpers), (4, 2 * helpers), (0, 4)
    (own,) = near_call("near_own", pos, msgs, targets, every, [("own", (points,), [weights])], R)
    w_z.append(lax.ppermute(w_y[1], "leaf", across))
    pieces, own = together(pieces, own)
    alike = stack_call(pieces)
    side = lax.ppermute(alike, "leaf", beside)
    pair_src = ("pair", (w_y[0],), w_y)
    (pair,) = near_call("near_pair", pos, msgs, targets, away, [pair_src], R, after=[alike])
    z_side = source_call(w_z[0])
    sums, part = [], []
    for c in range(2):
        part = near_call(
            "near_next_away", pos, msgs, targets, away,
            [("next", z_side, w_z[c : c + 1])], rows, c * rows, [own, pair], part[:1],
        )
        kept, given = part[::2], part[1::2]
        sums.append((kept, [from_help(value, 0, 1) for value in given]))
    parts = []
    for c in range(2):
        kept, mates = sums[c]
        if c == 1:
            mates, side = together(mates, side)
        both = add_call(*zip(kept, mates))
        parts.append([to_help(value, dx + 1) for dx, value in enumerate(both)])
    v_own = far_call(groups, pos, far_nodes, skel_node, transfer, alike, side, both[:1])
    values = [v_own] + [from_help(v_own, dx, dc) for dx, dc in order[1:]]
    sources = [pair_src, ("next", z_side, w_z)]
    home = near_call("near_home", pos, msgs, targets, home, sources, R, 0, [own], [v_own])
    mate = [from_help(value, 0, 1) for value in home[2:]]
    mine = add_call(*[[home[c], *parts[c]] for c in range(2)])
    return final_call(xs, pos, interp, mine, mate, values)


def solution(mesh):
    placed = (
        P(None, ("leaf", "help")),
        P(None, ("leaf", "help")),
        P(("leaf", "help"), None, None),
        P(),
        P("leaf", "help"),
        P(("leaf", "help"), None),
        P("leaf", None),
        P(),
        P(),
    )
    return jax.shard_map(
        shards, mesh=mesh, in_specs=placed, out_specs=P(None, ("leaf", "help")), check_vma=False
    )
```

```python
import math
from functools import partial

import jax
import jax.numpy as jnp
from jax import lax
from jax.experimental import pallas as pl
from jax.experimental.pallas import tpu as pltpu
from jax.sharding import PartitionSpec as P

F = 64
R = 256
LEAF = 512
SK = 256
FL = 4
EXTRA = 8
SIZES = (128, 128)

BF = jnp.bfloat16
F32 = jnp.float32
LOG2E = 1.0 / math.log(2.0)
SCALE = math.sqrt(0.5 * LOG2E)
BIAS = 0.0625 * F * LOG2E
VMEM_LIMIT = 24 * 1024 * 1024
VMEM_WHOLE = 64 * 1024 * 1024


def dot(a, b):
    return jnp.dot(a, b, preferred_element_type=F32)


def dot_t(a, b):
    return lax.dot_general(a, b, (((1,), (1,)), ((), ())), preferred_element_type=F32)


def halves(x):
    hi = x.astype(BF)
    lo = (x - hi.astype(F32)).astype(BF)
    return hi, lo


def dot3(a, b, mul=dot):
    a_hi, a_lo = halves(a)
    b_hi, b_lo = halves(b)
    return mul(a_hi, b_hi) + mul(a_lo, b_hi) + mul(a_hi, b_lo)


def target_side(x):
    hi, lo = halves(x)
    both = hi.astype(F32) + lo.astype(F32)
    off = BIAS - 0.5 * jnp.sum(both * both, axis=0, keepdims=True)
    return jnp.concatenate([hi, lo, hi, lo], axis=0), off


def source_side(x):
    xt = x.T
    hi, lo = halves(xt)
    both = hi.astype(F32) + lo.astype(F32)
    off = BIAS - 0.5 * jnp.sum(both * both, axis=1, keepdims=True)
    return jnp.concatenate([hi, hi, lo, lo], axis=1), off


def near_body(
    xs, sets, leaves_at, rows, row, nacc, nout, pos_ref, *refs
):
    nset = len(sets)
    start, stop = leaves_at
    msgs, (t_ref, tb_ref), refs = refs[: 2 * xs], refs[2 * xs : 2 * xs + 2], refs[2 * xs + 2 :]
    if nacc:
        s_scr, sb_scr, w_scr, o_scr, k_scr, times_scr, list_ref, times_ref, sems = refs[-9:]
        outs = refs[-9 - nout : -9]
    else:
        o_scr, s_scr, sb_scr, w_scr, k_scr, times_scr, list_ref, times_ref, sems = refs[-9:]
    copies = [
        pltpu.make_async_copy(msgs[b].at[F : F + EXTRA, :128], times_ref.at[b], sems.at[b])
        for b in range(start // 2, stop // 2)
    ]
    for copy in copies:
        copy.start()
    at = 0
    for k, (_, ready, chunks) in enumerate(sets):
        heads = refs[at : at + 1 + ready]
        parts = refs[at + 1 + ready : at + 1 + ready + chunks]
        at += 1 + ready + chunks
        for leaf in range(2):
            cols = slice(leaf * LEAF, (leaf + 1) * LEAF)
            j = 2 * k + leaf
            if ready:
                s_scr[j] = heads[0][leaf]
                sb_scr[j] = heads[1][leaf]
            else:
                side, off = source_side(heads[0][:F, cols] * SCALE)
                s_scr[j] = side
                sb_scr[j] = jnp.broadcast_to(off, (LEAF, 128))
            top = 0
            for part in parts:
                hi, lo = halves(part[:, cols])
                w_scr[j, top : top + part.shape[0], :] = hi
                w_scr[j, rows + top : rows + top + part.shape[0], :] = lo
                top += part.shape[0]
    for t in range(start, stop):
        if nacc:
            o_scr[t - start] = sum(
                ref[t - (4 * xs - ref.shape[0]), row : row + rows, :] for ref in refs[at : at + nacc]
            )
        else:
            o_scr[t - start] = jnp.zeros((rows, LEAF), F32)

    x, core, group, leaves = pos_ref[0], pos_ref[1], pos_ref[2], pos_ref[3]
    odd = group % 2
    column = []
    for kind, _, _ in sets:
        relative = {"own": 1, "pair": 2 - 2 * odd, "next": 2 * odd}[kind]
        column.append(relative * leaves + 2 * (2 * x + core))

    for copy in copies:
        copy.wait()
    count = jnp.int32(0)
    list_ref[0] = 0
    for t in range(start, stop):
        for j in range(2 * nset):
            times = times_ref[t // 2, t % 2, column[j // 2] + j % 2]

            @pl.when(times > 0)
            def _(count=count, t=t, j=j, times=times):
                list_ref[count] = t * 8 + j
                times_scr[count] = times

            count = count + (times > 0).astype(jnp.int32)

    def block(index, slot):
        code = list_ref[jnp.minimum(index, jnp.maximum(count - 1, 0))]
        t, j = code // 8, code % 8
        side = t_ref[t]
        off = tb_ref[t][:1, :]
        for half in range(2):
            part = slice(half * 256, (half + 1) * 256)
            cross = dot(s_scr[j, part, :], side)
            src_off = sb_scr[j, part, :]
            src_off = jnp.concatenate([src_off] * (LEAF // 128), axis=1)
            k_hi, k_lo = halves(jnp.exp2(cross + src_off + off))
            k_scr[slot, part, :] = k_hi
            k_scr[slot, LEAF + half * 256 : LEAF + (half + 1) * 256, :] = k_lo

    def apply(index, slot):
        code = list_ref[index]
        t, j = code // 8 - start, code % 8
        factor = times_scr[index]
        for half in range(2):
            cols = slice(half * 256, (half + 1) * 256)
            both = dot(w_scr[j], k_scr[slot, :LEAF, cols])
            low = dot(w_scr[j, :rows, :], k_scr[slot, LEAF:, cols])
            o_scr[t, :, cols] = o_scr[t, :, cols] + factor * (both[:rows] + both[rows:] + low)

    @pl.when(count > 0)
    def _():
        block(0, 0)

    def pair(index, carry):
        block(2 * index + 1, 1)
        apply(2 * index, 0)

        @pl.when(2 * index + 1 < count)
        def _():
            block(2 * index + 2, 0)
            apply(2 * index + 1, 1)

        return carry

    lax.fori_loop(0, (count + 1) // 2, pair, jnp.int32(0))
    if nacc:
        t, top = 0, 0
        for ref in outs:
            tall = ref.shape[0]
            for leaf in range(2):
                cols = slice(leaf * LEAF, (leaf + 1) * LEAF)
                ref[:, cols] = o_scr[t + leaf, top : top + tall, :]
            t, top = (t, top + tall) if top + tall < rows else (t + 2, 0)


def near_call(name, pos, msgs, targets, leaves_at, sources, rows, row=0, acc=(), after=()):
    nset = len(sources)
    start, stop = leaves_at
    vmem = pl.BlockSpec(memory_space=pltpu.VMEM)
    smem = pl.BlockSpec(memory_space=pltpu.SMEM)
    operands = [a for _, heads, chunks in sources for a in (*heads, *chunks)]
    scratch = [
        pltpu.VMEM((2 * nset, LEAF, 4 * F), BF),
        pltpu.VMEM((2 * nset, LEAF, 128), F32),
        pltpu.VMEM((2 * nset, 2 * rows, LEAF), BF),
        pltpu.VMEM((stop - start, rows, LEAF), F32),
        pltpu.VMEM((2, 2 * LEAF, LEAF), BF),
        pltpu.SMEM((2 * nset * (stop - start),), F32),
        pltpu.SMEM((2 * nset * (stop - start),), jnp.int32),
        pltpu.SMEM((len(msgs), EXTRA, 128), F32),
        pltpu.SemaphoreType.DMA((len(msgs),)),
    ]
    if not acc:
        out = [jax.ShapeDtypeStruct((stop - start, rows, LEAF), F32)]
        scratch.pop(3)
    else:
        operands += list(acc)
        talls = SIZES if rows == R else (rows,)
        out = [jax.ShapeDtypeStruct((tall, 2 * LEAF), F32) for tall in talls] * ((stop - start) // 2)
    sets = tuple((kind, len(heads) - 1, len(chunks)) for kind, heads, chunks in sources)
    return pl.pallas_call(
        partial(
            near_body, len(msgs) // 2, sets, leaves_at, rows, row, len(acc), len(out)
        ),
        name=name,
        out_shape=out,
        in_specs=[smem]
        + [pl.BlockSpec(memory_space=pl.ANY)] * len(msgs)
        + [vmem] * (2 + len(operands))
        + [pl.BlockSpec(memory_space=pl.ANY)] * len(after),
        out_specs=[vmem] * len(out),
        scratch_shapes=scratch,
        compiler_params=pltpu.CompilerParams(vmem_limit_bytes=VMEM_LIMIT),
    )(pos, *msgs, *targets, *operands, *after)


def source_body(pts_ref, side_ref, off_ref):
    for leaf in range(2):
        cols = slice(leaf * LEAF, (leaf + 1) * LEAF)
        side, off = source_side(pts_ref[:F, cols] * SCALE)
        side_ref[leaf] = side
        off_ref[leaf] = jnp.broadcast_to(off, (LEAF, 128))


def source_call(pts):
    vmem = pl.BlockSpec(memory_space=pltpu.VMEM)
    return pl.pallas_call(
        source_body,
        name="source_side",
        out_shape=[
            jax.ShapeDtypeStruct((2, LEAF, 4 * F), BF),
            jax.ShapeDtypeStruct((2, LEAF, 128), F32),
        ],
        in_specs=[vmem],
        out_specs=[vmem, vmem],
        compiler_params=pltpu.CompilerParams(vmem_limit_bytes=VMEM_LIMIT),
    )(pts)


def share_rows(xs):
    return R // (2 * xs) * SK // (2 * LEAF)


def leaf_body(xs, pos_ref, count_ref, src_ref, pts_in, w_in, interp_in, *refs):
    msgs = refs[: 2 * xs]
    pts_ref, w_ref, interp_ref, scr, sems = refs[2 * xs :]
    copies = [
        pltpu.make_async_copy(pts_in, pts_ref, sems.at[0]),
        pltpu.make_async_copy(w_in, w_ref, sems.at[1]),
        pltpu.make_async_copy(interp_in, interp_ref, sems.at[2]),
    ]
    for copy in copies:
        copy.start()
    x, core, group, leaves = pos_ref[0], pos_ref[1], pos_ref[2], pos_ref[3]
    lane = lax.broadcasted_iota(jnp.int32, (1, 128), 1) + (group - 1) * leaves
    times = []
    for leaf in range(2):
        row = jnp.zeros((1, 128), F32)
        for slot in range(src_ref.shape[1]):
            name = jnp.where(slot < count_ref[0, leaf], src_ref[leaf, slot], -1 - 128 * leaves)
            row = row + (lane == name).astype(F32)
        times.append(row)
    times = jnp.concatenate(times + [jnp.zeros((EXTRA - 2, 128), F32)], axis=0)
    for copy in copies:
        copy.wait()
    total = jnp.zeros((R, SK), F32)
    for leaf in range(2):
        total = total + dot3(w_ref[:, leaf * LEAF : (leaf + 1) * LEAF], interp_ref[leaf])
    scr[...] = total
    rows = R // (2 * xs)
    tall = share_rows(xs)
    for n, msg in enumerate(msgs):
        helper = 2 * lax.rem(x + n // 2, xs) + (core if n % 2 == 0 else 1 - core)
        msg[:F, :] = pts_ref[...]
        msg[F : F + EXTRA, :] = jnp.zeros((EXTRA, 2 * LEAF), F32)
        msg[F : F + EXTRA, :128] = times
        for i in range(rows // tall):
            at = pl.multiple_of(helper * rows + i * tall, tall)
            msg[F + EXTRA :, i * SK : (i + 1) * SK] = scr[pl.ds(at, tall), :]


def leaf_call(xs, pos, near_count, near_src, points, weights, interp):
    vmem = pl.BlockSpec(memory_space=pltpu.VMEM)
    smem = pl.BlockSpec(memory_space=pltpu.SMEM)
    anywhere = pl.BlockSpec(memory_space=pl.ANY)
    height = F + EXTRA + share_rows(xs)
    return pl.pallas_call(
        partial(leaf_body, xs),
        name="leaf_up",
        out_shape=[jax.ShapeDtypeStruct((height, 2 * LEAF), F32)] * (2 * xs),
        in_specs=[smem, smem, smem, anywhere, anywhere, anywhere],
        out_specs=[vmem] * (2 * xs),
        scratch_shapes=[
            pltpu.VMEM(points.shape, F32),
            pltpu.VMEM(weights.shape, F32),
            pltpu.VMEM(interp.shape, F32),
            pltpu.VMEM((R, SK), F32),
            pltpu.SemaphoreType.DMA((3,)),
        ],
        compiler_params=pltpu.CompilerParams(vmem_limit_bytes=VMEM_WHOLE),
    )(pos, near_count, near_src, points, weights, interp)


def skel_body(xs, pos_ref, index_ref, *refs):
    msgs, (out_ref, side_ref, off_ref) = refs[:-3], refs[-3:]
    rows = R // (2 * xs)
    tall = share_rows(xs)
    total = jnp.zeros((2 * F, SK), F32)
    value = jnp.zeros((tall, 2 * LEAF), F32)
    spot = lax.broadcasted_iota(jnp.int32, (2 * LEAF, SK), 0)
    x, core = pos_ref[0], pos_ref[1]
    for b, msg in enumerate(msgs):
        helper = 2 * lax.rem(x + b // 2, xs) + (core if b % 2 == 0 else 1 - core)
        side, off = target_side(msg[:F, :] * SCALE)
        for leaf in range(2):
            part = slice(leaf * LEAF, (leaf + 1) * LEAF)
            side_ref[2 * b + leaf] = side[:, part]
            off_ref[2 * b + leaf] = jnp.broadcast_to(off[:, part], (8, LEAF))
        hot = spot + helper * (2 * LEAF) == index_ref[...]
        total = total + dot(side[: 2 * F], hot.astype(F32).astype(BF))
        value = value + msg[F + EXTRA :, :]
    out_ref[:F, :] = total[:F] + total[F:]
    for i in range(rows // tall):
        out_ref[F + i * tall : F + (i + 1) * tall, :] = value[:, i * SK : (i + 1) * SK]


def skel_call(xs, pos, index, msgs):
    rows = R // (2 * xs)
    leaves = 2 * len(msgs)
    vmem = pl.BlockSpec(memory_space=pltpu.VMEM)
    payload, *targets = pl.pallas_call(
        partial(skel_body, xs),
        name="skeleton",
        out_shape=[
            jax.ShapeDtypeStruct((F + rows, SK), F32),
            jax.ShapeDtypeStruct((leaves, 4 * F, LEAF), BF),
            jax.ShapeDtypeStruct((leaves, 8, LEAF), F32),
        ],
        in_specs=[pl.BlockSpec(memory_space=pltpu.SMEM)] + [vmem] * (1 + len(msgs)),
        out_specs=[vmem] * 3,
        compiler_params=pltpu.CompilerParams(vmem_limit_bytes=VMEM_LIMIT),
        cost_estimate=pl.CostEstimate(
            flops=5_000_000_000, bytes_accessed=8_000_000, transcendentals=0
        ),
    )(pos, index, *msgs)
    return payload, targets


def stack_body(*refs):
    for n, ref in enumerate(refs[:-1]):
        refs[-1][n] = ref[...]


def stack_call(pieces):
    vmem = pl.BlockSpec(memory_space=pltpu.VMEM)
    return pl.pallas_call(
        stack_body,
        name="stack",
        out_shape=jax.ShapeDtypeStruct((len(pieces), *pieces[0].shape), F32),
        in_specs=[vmem] * len(pieces),
        out_specs=vmem,
        compiler_params=pltpu.CompilerParams(vmem_limit_bytes=VMEM_LIMIT),
    )(*pieces)


def upper_start(level, groups):
    return sum((groups >> step for step in range(1, level)))


def list_start(level, groups):
    return sum((groups >> step for step in range(level)))


def far_body(groups, rows, pos_ref, far_ref, node_ref, transfer_ref, alike_ref, beside_ref, *refs):
    out_ref, p_scr, u_scr, f_scr = refs[-4:]
    levels = groups.bit_length() - 1
    group = pos_ref[2]
    start = [list_start(level, groups) for level in range(levels)]
    for n in range(groups // 2):
        same, other = group ^ (2 * n), group ^ (2 * n + 1)
        p_scr[same] = alike_ref[n, :F, :]
        u_scr[same] = alike_ref[n, F:, :]
        p_scr[other] = beside_ref[n, :F, :]
        u_scr[other] = beside_ref[n, F:, :]
    spot = lax.broadcasted_iota(jnp.int32, (2 * SK, SK), 0)
    for level in range(1, levels):
        for n in range(groups >> level):
            row = upper_start(level, groups) + n
            left = start[level - 1] + 2 * n
            hot = (spot == node_ref[row : row + 1, :]).astype(F32).astype(BF)
            hi, lo = halves(jnp.concatenate([p_scr[left], p_scr[left + 1]], axis=1))
            both = dot(jnp.concatenate([hi, lo], axis=0), hot)
            p_scr[start[level] + n] = both[:F] + both[F:]
            vals = jnp.concatenate([u_scr[left], u_scr[left + 1]], axis=1)
            u_scr[start[level] + n] = dot3(vals, transfer_ref[row])
    for level in range(levels):
        node = group >> level
        side, off = target_side(p_scr[start[level] + node])
        f_scr[level] = jnp.zeros((rows, SK), F32)

        def one(n, carry, level=level, node=node, side=side, off=off):
            hits = jnp.int32(0)
            for slot in range(FL):
                hits = hits + (far_ref[slot, start[level] + node] == n).astype(jnp.int32)

            @pl.when(hits > 0)
            def _():
                src, src_off = source_side(p_scr[start[level] + n])
                block = jnp.exp2(dot(src, side) + src_off + off)
                term = dot3(u_scr[start[level] + n], block)
                f_scr[level] = f_scr[level] + hits.astype(F32) * term

            return carry

        lax.fori_loop(0, groups >> level, one, jnp.int32(0))
    local = f_scr[levels - 1]
    for level in range(levels - 1, 0, -1):
        row = upper_start(level, groups) + (group >> level)
        bit = (group >> (level - 1)) & 1
        matrix = transfer_ref[row, pl.ds(pl.multiple_of(bit * SK, SK), SK), :]
        local = f_scr[level - 1] + dot3(local, matrix, dot_t)
    out_ref[...] = local


def far_call(groups, pos, far_nodes, skel_node, transfer, alike, beside, after):
    rows = alike.shape[1] - F
    vmem = pl.BlockSpec(memory_space=pltpu.VMEM)
    smem = pl.BlockSpec(memory_space=pltpu.SMEM)
    nodes = 2 * groups
    return pl.pallas_call(
        partial(far_body, groups, rows),
        name="far",
        out_shape=jax.ShapeDtypeStruct((rows, SK), F32),
        in_specs=[smem, smem, vmem, vmem, vmem, vmem]
        + [pl.BlockSpec(memory_space=pl.ANY)] * len(after),
        out_specs=vmem,
        scratch_shapes=[
            pltpu.VMEM((nodes, F, SK), F32),
            pltpu.VMEM((nodes, rows, SK), F32),
            pltpu.VMEM((groups.bit_length(), rows, SK), F32),
        ],
        compiler_params=pltpu.CompilerParams(vmem_limit_bytes=VMEM_LIMIT),
    )(pos, far_nodes.T, skel_node, transfer, alike, beside, *after)


def final_body(xs, pos_ref, interp_ref, *refs):
    values, sums = refs[: 2 * xs], refs[2 * xs : -2]
    out_ref, v_scr = refs[-2:]
    rows = R // (2 * xs)
    x, core = pos_ref[0], pos_ref[1]
    for n, ref in enumerate(values):
        helper = 2 * lax.rem(x + n // 2, xs) + (core if n % 2 == 0 else 1 - core)
        v_scr[pl.ds(pl.multiple_of(helper * rows, rows), rows), :] = ref[...]
    value = v_scr[...]
    for leaf in range(2):
        cols = slice(leaf * LEAF, (leaf + 1) * LEAF)
        total = dot3(value, interp_ref[leaf], dot_t)
        for c in range(2):
            part = slice(c * SIZES[0], SIZES[0] + c * SIZES[1])
            out_ref[part, cols] = total[part] + sums[c][:, cols] + sums[2 + c][:, cols]


def add_body(count, *refs):
    for n, out_ref in enumerate(refs[-(len(refs) // (count + 1)) :]):
        total = refs[n * count][...]
        for ref in refs[n * count + 1 : (n + 1) * count]:
            total = total + ref[...]
        out_ref[...] = total


def add_call(*sums):
    vmem = pl.BlockSpec(memory_space=pltpu.VMEM)
    operands = [value for terms in sums for value in terms]
    return pl.pallas_call(
        partial(add_body, len(sums[0])),
        name="add_parts",
        out_shape=[jax.ShapeDtypeStruct(terms[0].shape, F32) for terms in sums],
        in_specs=[vmem] * len(operands),
        out_specs=[vmem] * len(sums),
        compiler_params=pltpu.CompilerParams(vmem_limit_bytes=VMEM_LIMIT),
    )(*operands)


def final_call(xs, pos, interp, home, mate, values):
    vmem = pl.BlockSpec(memory_space=pltpu.VMEM)
    return pl.pallas_call(
        partial(final_body, xs),
        name="join",
        out_shape=jax.ShapeDtypeStruct((R, 2 * LEAF), F32),
        in_specs=[pl.BlockSpec(memory_space=pltpu.SMEM)] + [vmem] * (1 + 2 * xs + 4),
        out_specs=vmem,
        scratch_shapes=[pltpu.VMEM((R, SK), F32)],
        compiler_params=pltpu.CompilerParams(vmem_limit_bytes=VMEM_LIMIT),
    )(pos, interp, *values, *home, *mate)


def help_pairs(xs, dx, dc):
    return [
        (2 * ((x + dx) % xs) + (core ^ dc), 2 * x + core) for x in range(xs) for core in range(2)
    ]


def shards(
    points, weights, interp, transfer, near_count, near_src, skel_group, skel_node, far_nodes
):
    helpers = lax.axis_size("help")
    groups = lax.axis_size("leaf")
    xs = helpers // 2
    helper = lax.axis_index("help")
    group = lax.axis_index("leaf")
    x, core = helper // 2, helper % 2
    leaves = 2 * helpers
    pos = jnp.stack([x, core, group, jnp.int32(leaves)]).astype(jnp.int32)
    rows = R // 2

    def from_help(value, dx, dc):
        return lax.ppermute(value, "help", help_pairs(xs, dx, dc))

    def to_help(value, dx):
        return lax.ppermute(value, "help", help_pairs(xs, -dx, 0))

    def together(*values):
        return lax.optimization_barrier(values)

    beside = [(i, i ^ 1) for i in range(groups)]
    across = [(i, i + 2) for i in range(0, groups - 2, 2)]
    across += [(i, i - 2) for i in range(3, groups, 2)]
    order = [(dx, dc) for dx in range(xs) for dc in range(2)]

    cut = SIZES[0]
    pts_y = lax.ppermute(points, "leaf", beside)
    w_y = [lax.ppermute(chunk, "leaf", beside) for chunk in (weights[:cut], weights[cut:])]
    sent = leaf_call(xs, pos, near_count, near_src, points, weights, interp)
    got = [
        lax.ppermute(sent[n], "help", help_pairs(xs, -dx, dc))
        for n, (dx, dc) in enumerate(order)
        if n
    ]
    pts_z = lax.ppermute(pts_y, "leaf", across)
    pts_z, w_y[0] = together(pts_z, w_y[0])
    w_z = [lax.ppermute(w_y[0], "leaf", across)]
    msgs = [sent[0]] + [got[order.index((-dx % xs, dc)) - 1] for dx, dc in order[1:]]
    payload, targets = skel_call(xs, pos, skel_group, msgs)
    pieces = [payload]
    for mask in range(2, groups, 2):
        pieces.append(lax.ppermute(payload, "leaf", [(i, i ^ mask) for i in range(groups)]))

    payload, w_y[1] = together(payload, w_y[1])
    every, away, home = (0, 2 * helpers), (4, 2 * helpers), (0, 4)
    (own,) = near_call("near_own", pos, msgs, targets, every, [("own", (points,), [weights])], R)
    w_z.append(lax.ppermute(w_y[1], "leaf", across))
    pair_src = ("pair", (pts_y,), w_y)
    (pair,) = near_call("near_pair", pos, msgs, targets, away, [pair_src], R, after=[own])
    z_side = source_call(pts_z)
    sums, part = [], [pair]
    for c in range(2):
        if c == 1:
            pieces, part = together(pieces, part)
            alike = stack_call(pieces)
            side = lax.ppermute(alike, "leaf", beside)
            part = [alike]
        part = near_call(
            "near_next_away", pos, msgs, targets, away, [("next", z_side, w_z[c : c + 1])],
            SIZES[c], c * SIZES[0], [own, pair], part[:1],
        )
        kept, given = part[::2], part[1::2]
        sums.append((kept, [from_help(value, 0, 1) for value in given]))
    parts = []
    for c in range(2):
        kept, mates = sums[c]
        if c == 1:
            mates, side = together(mates, side)
        both = add_call(*zip(kept, mates))
        parts.append([to_help(value, dx + 1) for dx, value in enumerate(both)])
    v_own = far_call(groups, pos, far_nodes, skel_node, transfer, alike, side, both[:1])
    values = [v_own] + [from_help(v_own, dx, dc) for dx, dc in order[1:]]
    sources = [pair_src, ("next", z_side, w_z)]
    home = near_call("near_home", pos, msgs, targets, home, sources, R, 0, [own], [v_own])
    mate = [from_help(value, 0, 1) for value in home[2:]]
    mine = add_call(*[[home[c], *parts[c]] for c in range(2)])
    return final_call(xs, pos, interp, mine, mate, values)


def solution(mesh):
    placed = (
        P(None, ("leaf", "help")),
        P(None, ("leaf", "help")),
        P(("leaf", "help"), None, None),
        P(),
        P("leaf", "help"),
        P(("leaf", "help"), None),
        P("leaf", None),
        P(),
        P(),
    )
    return jax.shard_map(
        shards, mesh=mesh, in_specs=placed, out_specs=P(None, ("leaf", "help")), check_vma=False
    )
```

```python
import math
from functools import partial

import jax
import jax.numpy as jnp
from jax import lax
from jax.experimental import pallas as pl
from jax.experimental.pallas import tpu as pltpu
from jax.sharding import PartitionSpec as P

F = 64
R = 256
LEAF = 512
SK = 256
FL = 4
EXTRA = 8
SIZES = (128, 128)

BF = jnp.bfloat16
F32 = jnp.float32
LOG2E = 1.0 / math.log(2.0)
SCALE = math.sqrt(0.5 * LOG2E)
BIAS = 0.0625 * F * LOG2E
VMEM_LIMIT = 24 * 1024 * 1024
VMEM_WHOLE = 64 * 1024 * 1024


def dot(a, b):
    return jnp.dot(a, b, preferred_element_type=F32)


def dot_t(a, b):
    return lax.dot_general(a, b, (((1,), (1,)), ((), ())), preferred_element_type=F32)


def halves(x):
    hi = x.astype(BF)
    lo = (x - hi.astype(F32)).astype(BF)
    return hi, lo


def dot3(a, b, mul=dot):
    a_hi, a_lo = halves(a)
    b_hi, b_lo = halves(b)
    return mul(a_hi, b_hi) + mul(a_lo, b_hi) + mul(a_hi, b_lo)


def target_side(x):
    hi, lo = halves(x)
    both = hi.astype(F32) + lo.astype(F32)
    off = BIAS - 0.5 * jnp.sum(both * both, axis=0, keepdims=True)
    return jnp.concatenate([hi, lo, hi, lo], axis=0), off


def source_side(x):
    xt = x.T
    hi, lo = halves(xt)
    both = hi.astype(F32) + lo.astype(F32)
    off = BIAS - 0.5 * jnp.sum(both * both, axis=1, keepdims=True)
    return jnp.concatenate([hi, hi, lo, lo], axis=1), off


def near_body(
    xs, sets, leaves_at, rows, row, nacc, nout, pos_ref, *refs
):
    nset = len(sets)
    start, stop = leaves_at
    msgs, (t_ref, tb_ref), refs = refs[: 2 * xs], refs[2 * xs : 2 * xs + 2], refs[2 * xs + 2 :]
    if nacc:
        s_scr, sb_scr, w_scr, o_scr, k_scr, times_scr, list_ref, times_ref, sems = refs[-9:]
        outs = refs[-9 - nout : -9]
    else:
        o_scr, s_scr, sb_scr, w_scr, k_scr, times_scr, list_ref, times_ref, sems = refs[-9:]
    copies = [
        pltpu.make_async_copy(msgs[b].at[F : F + EXTRA, :128], times_ref.at[b], sems.at[b])
        for b in range(start // 2, stop // 2)
    ]
    for copy in copies:
        copy.start()
    at = 0
    for k, (_, ready, chunks) in enumerate(sets):
        heads = refs[at : at + 1 + ready]
        parts = refs[at + 1 + ready : at + 1 + ready + chunks]
        at += 1 + ready + chunks
        for leaf in range(2):
            cols = slice(leaf * LEAF, (leaf + 1) * LEAF)
            j = 2 * k + leaf
            if ready:
                s_scr[j] = heads[0][leaf]
                sb_scr[j] = heads[1][leaf]
            else:
                side, off = source_side(heads[0][:F, cols] * SCALE)
                s_scr[j] = side
                sb_scr[j] = jnp.broadcast_to(off, (LEAF, 128))
            top = 0
            for part in parts:
                hi, lo = halves(part[:, cols])
                w_scr[j, top : top + part.shape[0], :] = hi
                w_scr[j, rows + top : rows + top + part.shape[0], :] = lo
                top += part.shape[0]
    for t in range(start, stop):
        if nacc:
            o_scr[t - start] = sum(
                ref[t - (4 * xs - ref.shape[0]), row : row + rows, :] for ref in refs[at : at + nacc]
            )
        else:
            o_scr[t - start] = jnp.zeros((rows, LEAF), F32)

    x, core, group, leaves = pos_ref[0], pos_ref[1], pos_ref[2], pos_ref[3]
    odd = group % 2
    column = []
    for kind, _, _ in sets:
        relative = {"own": 1, "pair": 2 - 2 * odd, "next": 2 * odd}[kind]
        column.append(relative * leaves + 2 * (2 * x + core))

    for copy in copies:
        copy.wait()
    count = jnp.int32(0)
    list_ref[0] = 0
    for t in range(start, stop):
        for j in range(2 * nset):
            times = times_ref[t // 2, t % 2, column[j // 2] + j % 2]

            @pl.when(times > 0)
            def _(count=count, t=t, j=j, times=times):
                list_ref[count] = t * 8 + j
                times_scr[count] = times

            count = count + (times > 0).astype(jnp.int32)

    def block(index, slot):
        code = list_ref[jnp.minimum(index, jnp.maximum(count - 1, 0))]
        t, j = code // 8, code % 8
        side = t_ref[t]
        off = tb_ref[t][:1, :]
        for half in range(2):
            part = slice(half * 256, (half + 1) * 256)
            cross = dot(s_scr[j, part, :], side)
            src_off = sb_scr[j, part, :]
            src_off = jnp.concatenate([src_off] * (LEAF // 128), axis=1)
            k_hi, k_lo = halves(jnp.exp2(cross + src_off + off))
            k_scr[slot, part, :] = k_hi
            k_scr[slot, LEAF + half * 256 : LEAF + (half + 1) * 256, :] = k_lo

    def apply(index, slot):
        code = list_ref[index]
        t, j = code // 8 - start, code % 8
        factor = times_scr[index]
        for half in range(2):
            cols = slice(half * 256, (half + 1) * 256)
            both = dot(w_scr[j], k_scr[slot, :LEAF, cols])
            low = dot(w_scr[j, :rows, :], k_scr[slot, LEAF:, cols])
            o_scr[t, :, cols] = o_scr[t, :, cols] + factor * (both[:rows] + both[rows:] + low)

    @pl.when(count > 0)
    def _():
        block(0, 0)

    def pair(index, carry):
        block(2 * index + 1, 1)
        apply(2 * index, 0)

        @pl.when(2 * index + 1 < count)
        def _():
            block(2 * index + 2, 0)
            apply(2 * index + 1, 1)

        return carry

    lax.fori_loop(0, (count + 1) // 2, pair, jnp.int32(0))
    if nacc:
        t, top = 0, 0
        for ref in outs:
            tall = ref.shape[0]
            for leaf in range(2):
                cols = slice(leaf * LEAF, (leaf + 1) * LEAF)
                ref[:, cols] = o_scr[t + leaf, top : top + tall, :]
            t, top = (t, top + tall) if top + tall < rows else (t + 2, 0)


def near_call(name, pos, msgs, targets, leaves_at, sources, rows, row=0, acc=(), after=()):
    nset = len(sources)
    start, stop = leaves_at
    vmem = pl.BlockSpec(memory_space=pltpu.VMEM)
    smem = pl.BlockSpec(memory_space=pltpu.SMEM)
    operands = [a for _, heads, chunks in sources for a in (*heads, *chunks)]
    scratch = [
        pltpu.VMEM((2 * nset, LEAF, 4 * F), BF),
        pltpu.VMEM((2 * nset, LEAF, 128), F32),
        pltpu.VMEM((2 * nset, 2 * rows, LEAF), BF),
        pltpu.VMEM((stop - start, rows, LEAF), F32),
        pltpu.VMEM((2, 2 * LEAF, LEAF), BF),
        pltpu.SMEM((2 * nset * (stop - start),), F32),
        pltpu.SMEM((2 * nset * (stop - start),), jnp.int32),
        pltpu.SMEM((len(msgs), EXTRA, 128), F32),
        pltpu.SemaphoreType.DMA((len(msgs),)),
    ]
    if not acc:
        out = [jax.ShapeDtypeStruct((stop - start, rows, LEAF), F32)]
        scratch.pop(3)
    else:
        operands += list(acc)
        talls = SIZES if rows == R else (rows,)
        out = [jax.ShapeDtypeStruct((tall, 2 * LEAF), F32) for tall in talls] * ((stop - start) // 2)
    sets = tuple((kind, len(heads) - 1, len(chunks)) for kind, heads, chunks in sources)
    return pl.pallas_call(
        partial(
            near_body, len(msgs) // 2, sets, leaves_at, rows, row, len(acc), len(out)
        ),
        name=name,
        out_shape=out,
        in_specs=[smem]
        + [pl.BlockSpec(memory_space=pl.ANY)] * len(msgs)
        + [vmem] * (2 + len(operands))
        + [pl.BlockSpec(memory_space=pl.ANY)] * len(after),
        out_specs=[vmem] * len(out),
        scratch_shapes=scratch,
        compiler_params=pltpu.CompilerParams(vmem_limit_bytes=VMEM_LIMIT),
    )(pos, *msgs, *targets, *operands, *after)


def source_body(pts_ref, side_ref, off_ref):
    for leaf in range(2):
        cols = slice(leaf * LEAF, (leaf + 1) * LEAF)
        side, off = source_side(pts_ref[:F, cols] * SCALE)
        side_ref[leaf] = side
        off_ref[leaf] = jnp.broadcast_to(off, (LEAF, 128))


def source_call(pts):
    vmem = pl.BlockSpec(memory_space=pltpu.VMEM)
    return pl.pallas_call(
        source_body,
        name="source_side",
        out_shape=[
            jax.ShapeDtypeStruct((2, LEAF, 4 * F), BF),
            jax.ShapeDtypeStruct((2, LEAF, 128), F32),
        ],
        in_specs=[vmem],
        out_specs=[vmem, vmem],
        compiler_params=pltpu.CompilerParams(vmem_limit_bytes=VMEM_LIMIT),
    )(pts)


def share_rows(xs):
    return R // (2 * xs) * SK // (2 * LEAF)


def leaf_body(xs, pos_ref, count_ref, src_ref, pts_in, w_in, interp_in, *refs):
    msgs = refs[: 2 * xs]
    pts_ref, w_ref, interp_ref, scr, sems = refs[2 * xs :]
    copies = [
        pltpu.make_async_copy(pts_in, pts_ref, sems.at[0]),
        pltpu.make_async_copy(w_in, w_ref, sems.at[1]),
        pltpu.make_async_copy(interp_in, interp_ref, sems.at[2]),
    ]
    for copy in copies:
        copy.start()
    x, core, group, leaves = pos_ref[0], pos_ref[1], pos_ref[2], pos_ref[3]
    lane = lax.broadcasted_iota(jnp.int32, (1, 128), 1) + (group - 1) * leaves
    times = []
    for leaf in range(2):
        row = jnp.zeros((1, 128), F32)
        for slot in range(src_ref.shape[1]):
            name = jnp.where(slot < count_ref[0, leaf], src_ref[leaf, slot], -1 - 128 * leaves)
            row = row + (lane == name).astype(F32)
        times.append(row)
    times = jnp.concatenate(times + [jnp.zeros((EXTRA - 2, 128), F32)], axis=0)
    for copy in copies:
        copy.wait()
    total = jnp.zeros((R, SK), F32)
    for leaf in range(2):
        total = total + dot3(w_ref[:, leaf * LEAF : (leaf + 1) * LEAF], interp_ref[leaf])
    scr[...] = total
    rows = R // (2 * xs)
    tall = share_rows(xs)
    for n, msg in enumerate(msgs):
        helper = 2 * lax.rem(x + n // 2, xs) + (core if n % 2 == 0 else 1 - core)
        msg[:F, :] = pts_ref[...]
        msg[F : F + EXTRA, :] = jnp.zeros((EXTRA, 2 * LEAF), F32)
        msg[F : F + EXTRA, :128] = times
        for i in range(rows // tall):
            at = pl.multiple_of(helper * rows + i * tall, tall)
            msg[F + EXTRA :, i * SK : (i + 1) * SK] = scr[pl.ds(at, tall), :]


def leaf_call(xs, pos, near_count, near_src, points, weights, interp):
    vmem = pl.BlockSpec(memory_space=pltpu.VMEM)
    smem = pl.BlockSpec(memory_space=pltpu.SMEM)
    anywhere = pl.BlockSpec(memory_space=pl.ANY)
    height = F + EXTRA + share_rows(xs)
    return pl.pallas_call(
        partial(leaf_body, xs),
        name="leaf_up",
        out_shape=[jax.ShapeDtypeStruct((height, 2 * LEAF), F32)] * (2 * xs),
        in_specs=[smem, smem, smem, anywhere, anywhere, anywhere],
        out_specs=[vmem] * (2 * xs),
        scratch_shapes=[
            pltpu.VMEM(points.shape, F32),
            pltpu.VMEM(weights.shape, F32),
            pltpu.VMEM(interp.shape, F32),
            pltpu.VMEM((R, SK), F32),
            pltpu.SemaphoreType.DMA((3,)),
        ],
        compiler_params=pltpu.CompilerParams(vmem_limit_bytes=VMEM_WHOLE),
    )(pos, near_count, near_src, points, weights, interp)


def skel_body(xs, pos_ref, index_ref, *refs):
    msgs, (out_ref, side_ref, off_ref) = refs[:-3], refs[-3:]
    rows = R // (2 * xs)
    tall = share_rows(xs)
    total = jnp.zeros((2 * F, SK), F32)
    value = jnp.zeros((tall, 2 * LEAF), F32)
    spot = lax.broadcasted_iota(jnp.int32, (2 * LEAF, SK), 0)
    x, core = pos_ref[0], pos_ref[1]
    for b, msg in enumerate(msgs):
        helper = 2 * lax.rem(x + b // 2, xs) + (core if b % 2 == 0 else 1 - core)
        side, off = target_side(msg[:F, :] * SCALE)
        for leaf in range(2):
            part = slice(leaf * LEAF, (leaf + 1) * LEAF)
            side_ref[2 * b + leaf] = side[:, part]
            off_ref[2 * b + leaf] = jnp.broadcast_to(off[:, part], (8, LEAF))
        hot = spot + helper * (2 * LEAF) == index_ref[...]
        total = total + dot(side[: 2 * F], hot.astype(F32).astype(BF))
        value = value + msg[F + EXTRA :, :]
    out_ref[:F, :] = total[:F] + total[F:]
    for i in range(rows // tall):
        out_ref[F + i * tall : F + (i + 1) * tall, :] = value[:, i * SK : (i + 1) * SK]


def skel_call(xs, pos, index, msgs):
    rows = R // (2 * xs)
    leaves = 2 * len(msgs)
    vmem = pl.BlockSpec(memory_space=pltpu.VMEM)
    payload, *targets = pl.pallas_call(
        partial(skel_body, xs),
        name="skeleton",
        out_shape=[
            jax.ShapeDtypeStruct((F + rows, SK), F32),
            jax.ShapeDtypeStruct((leaves, 4 * F, LEAF), BF),
            jax.ShapeDtypeStruct((leaves, 8, LEAF), F32),
        ],
        in_specs=[pl.BlockSpec(memory_space=pltpu.SMEM)] + [vmem] * (1 + len(msgs)),
        out_specs=[vmem] * 3,
        compiler_params=pltpu.CompilerParams(vmem_limit_bytes=VMEM_LIMIT),
        cost_estimate=pl.CostEstimate(
            flops=5_000_000_000, bytes_accessed=8_000_000, transcendentals=0
        ),
    )(pos, index, *msgs)
    return payload, targets


def stack_body(*refs):
    for n, ref in enumerate(refs[:-1]):
        refs[-1][n] = ref[...]


def stack_call(pieces):
    vmem = pl.BlockSpec(memory_space=pltpu.VMEM)
    return pl.pallas_call(
        stack_body,
        name="stack",
        out_shape=jax.ShapeDtypeStruct((len(pieces), *pieces[0].shape), F32),
        in_specs=[vmem] * len(pieces),
        out_specs=vmem,
        compiler_params=pltpu.CompilerParams(vmem_limit_bytes=VMEM_LIMIT),
    )(*pieces)


def upper_start(level, groups):
    return sum((groups >> step for step in range(1, level)))


def list_start(level, groups):
    return sum((groups >> step for step in range(level)))


def far_body(groups, rows, pos_ref, far_ref, node_ref, transfer_ref, alike_ref, beside_ref, *refs):
    out_ref, p_scr, u_scr, f_scr = refs[-4:]
    levels = groups.bit_length() - 1
    group = pos_ref[2]
    start = [list_start(level, groups) for level in range(levels)]
    for n in range(groups // 2):
        same, other = group ^ (2 * n), group ^ (2 * n + 1)
        p_scr[same] = alike_ref[n, :F, :]
        u_scr[same] = alike_ref[n, F:, :]
        p_scr[other] = beside_ref[n, :F, :]
        u_scr[other] = beside_ref[n, F:, :]
    spot = lax.broadcasted_iota(jnp.int32, (2 * SK, SK), 0)
    for level in range(1, levels):
        for n in range(groups >> level):
            row = upper_start(level, groups) + n
            left = start[level - 1] + 2 * n
            hot = (spot == node_ref[row : row + 1, :]).astype(F32).astype(BF)
            hi, lo = halves(jnp.concatenate([p_scr[left], p_scr[left + 1]], axis=1))
            both = dot(jnp.concatenate([hi, lo], axis=0), hot)
            p_scr[start[level] + n] = both[:F] + both[F:]
            vals = jnp.concatenate([u_scr[left], u_scr[left + 1]], axis=1)
            u_scr[start[level] + n] = dot3(vals, transfer_ref[row])
    for level in range(levels):
        node = group >> level
        side, off = target_side(p_scr[start[level] + node])
        f_scr[level] = jnp.zeros((rows, SK), F32)

        def one(n, carry, level=level, node=node, side=side, off=off):
            hits = jnp.int32(0)
            for slot in range(FL):
                hits = hits + (far_ref[slot, start[level] + node] == n).astype(jnp.int32)

            @pl.when(hits > 0)
            def _():
                src, src_off = source_side(p_scr[start[level] + n])
                block = jnp.exp2(dot(src, side) + src_off + off)
                term = dot3(u_scr[start[level] + n], block)
                f_scr[level] = f_scr[level] + hits.astype(F32) * term

            return carry

        lax.fori_loop(0, groups >> level, one, jnp.int32(0))
    local = f_scr[levels - 1]
    for level in range(levels - 1, 0, -1):
        row = upper_start(level, groups) + (group >> level)
        bit = (group >> (level - 1)) & 1
        matrix = transfer_ref[row, pl.ds(pl.multiple_of(bit * SK, SK), SK), :]
        local = f_scr[level - 1] + dot3(local, matrix, dot_t)
    out_ref[...] = local


def far_call(groups, pos, far_nodes, skel_node, transfer, alike, beside, after):
    rows = alike.shape[1] - F
    vmem = pl.BlockSpec(memory_space=pltpu.VMEM)
    smem = pl.BlockSpec(memory_space=pltpu.SMEM)
    nodes = 2 * groups
    return pl.pallas_call(
        partial(far_body, groups, rows),
        name="far",
        out_shape=jax.ShapeDtypeStruct((rows, SK), F32),
        in_specs=[smem, smem, vmem, vmem, vmem, vmem]
        + [pl.BlockSpec(memory_space=pl.ANY)] * len(after),
        out_specs=vmem,
        scratch_shapes=[
            pltpu.VMEM((nodes, F, SK), F32),
            pltpu.VMEM((nodes, rows, SK), F32),
            pltpu.VMEM((groups.bit_length(), rows, SK), F32),
        ],
        compiler_params=pltpu.CompilerParams(vmem_limit_bytes=VMEM_LIMIT),
    )(pos, far_nodes.T, skel_node, transfer, alike, beside, *after)


def final_body(xs, pos_ref, interp_ref, *refs):
    values, sums = refs[: 2 * xs], refs[2 * xs : -2]
    out_ref, v_scr = refs[-2:]
    rows = R // (2 * xs)
    x, core = pos_ref[0], pos_ref[1]
    for n, ref in enumerate(values):
        helper = 2 * lax.rem(x + n // 2, xs) + (core if n % 2 == 0 else 1 - core)
        v_scr[pl.ds(pl.multiple_of(helper * rows, rows), rows), :] = ref[...]
    value = v_scr[...]
    for leaf in range(2):
        cols = slice(leaf * LEAF, (leaf + 1) * LEAF)
        total = dot3(value, interp_ref[leaf], dot_t)
        for c in range(2):
            part = slice(c * SIZES[0], SIZES[0] + c * SIZES[1])
            out_ref[part, cols] = total[part] + sums[c][:, cols] + sums[2 + c][:, cols]


def add_body(count, *refs):
    for n, out_ref in enumerate(refs[-(len(refs) // (count + 1)) :]):
        total = refs[n * count][...]
        for ref in refs[n * count + 1 : (n + 1) * count]:
            total = total + ref[...]
        out_ref[...] = total


def add_call(*sums):
    vmem = pl.BlockSpec(memory_space=pltpu.VMEM)
    operands = [value for terms in sums for value in terms]
    return pl.pallas_call(
        partial(add_body, len(sums[0])),
        name="add_parts",
        out_shape=[jax.ShapeDtypeStruct(terms[0].shape, F32) for terms in sums],
        in_specs=[vmem] * len(operands),
        out_specs=[vmem] * len(sums),
        compiler_params=pltpu.CompilerParams(vmem_limit_bytes=VMEM_LIMIT),
    )(*operands)


def final_call(xs, pos, interp, home, mate, values):
    vmem = pl.BlockSpec(memory_space=pltpu.VMEM)
    return pl.pallas_call(
        partial(final_body, xs),
        name="join",
        out_shape=jax.ShapeDtypeStruct((R, 2 * LEAF), F32),
        in_specs=[pl.BlockSpec(memory_space=pltpu.SMEM)] + [vmem] * (1 + 2 * xs + 4),
        out_specs=vmem,
        scratch_shapes=[pltpu.VMEM((R, SK), F32)],
        compiler_params=pltpu.CompilerParams(vmem_limit_bytes=VMEM_LIMIT),
    )(pos, interp, *values, *home, *mate)


def help_pairs(xs, dx, dc):
    return [
        (2 * ((x + dx) % xs) + (core ^ dc), 2 * x + core) for x in range(xs) for core in range(2)
    ]


def shards(
    points, weights, interp, transfer, near_count, near_src, skel_group, skel_node, far_nodes
):
    helpers = lax.axis_size("help")
    groups = lax.axis_size("leaf")
    xs = helpers // 2
    helper = lax.axis_index("help")
    group = lax.axis_index("leaf")
    x, core = helper // 2, helper % 2
    leaves = 2 * helpers
    pos = jnp.stack([x, core, group, jnp.int32(leaves)]).astype(jnp.int32)
    rows = R // 2

    def from_help(value, dx, dc):
        return lax.ppermute(value, "help", help_pairs(xs, dx, dc))

    def to_help(value, dx):
        return lax.ppermute(value, "help", help_pairs(xs, -dx, 0))

    def together(*values):
        return lax.optimization_barrier(values)

    beside = [(i, i ^ 1) for i in range(groups)]
    across = [(i, i + 2) for i in range(0, groups - 2, 2)]
    across += [(i, i - 2) for i in range(3, groups, 2)]
    order = [(dx, dc) for dx in range(xs) for dc in range(2)]

    cut = SIZES[0]
    pts_y = lax.ppermute(points, "leaf", beside)
    w_y = [lax.ppermute(chunk, "leaf", beside) for chunk in (weights[:cut], weights[cut:])]
    sent = leaf_call(xs, pos, near_count, near_src, points, weights, interp)
    got = [
        lax.ppermute(sent[n], "help", help_pairs(xs, -dx, dc))
        for n, (dx, dc) in enumerate(order)
        if n
    ]
    pts_z = lax.ppermute(pts_y, "leaf", across)
    pts_z, w_y[0] = together(pts_z, w_y[0])
    w_z = [lax.ppermute(w_y[0], "leaf", across)]
    msgs = [sent[0]] + [got[order.index((-dx % xs, dc)) - 1] for dx, dc in order[1:]]
    payload, targets = skel_call(xs, pos, skel_group, msgs)
    pieces = [payload]
    for mask in range(2, groups, 2):
        pieces.append(lax.ppermute(payload, "leaf", [(i, i ^ mask) for i in range(groups)]))

    payload, w_y[1] = together(payload, w_y[1])
    every, away, home = (0, 2 * helpers), (4, 2 * helpers), (0, 4)
    (own,) = near_call("near_own", pos, msgs, targets, every, [("own", (points,), [weights])], R)
    w_z.append(lax.ppermute(w_y[1], "leaf", across))
    pair_src = ("pair", (pts_y,), w_y)
    (pair,) = near_call("near_pair", pos, msgs, targets, away, [pair_src], R, after=[own])
    z_side = source_call(pts_z)
    sums, part = [], [pair]
    for c in range(2):
        if c == 1:
            pieces, part = together(pieces, part)
            alike = stack_call(pieces)
            side = lax.ppermute(alike, "leaf", beside)
            part = [alike]
        part = near_call(
            "near_next_away", pos, msgs, targets, away, [("next", z_side, w_z[c : c + 1])],
            SIZES[c], c * SIZES[0], [own, pair], part[:1],
        )
        kept, given = part[::2], part[1::2]
        sums.append((kept, [from_help(value, 0, 1) for value in given]))
    parts = []
    for c in range(2):
        kept, mates = sums[c]
        both = add_call(*zip(kept, mates))
        parts.append([to_help(value, dx + 1) for dx, value in enumerate(both)])
    sources = [pair_src, ("next", z_side, w_z)]
    home = near_call("near_home", pos, msgs, targets, home, sources, R, 0, [own], both[:1])
    v_own = far_call(groups, pos, far_nodes, skel_node, transfer, alike, side, home[:1])
    values = [v_own] + [from_help(v_own, dx, dc) for dx, dc in order[1:]]
    mate = [from_help(value, 0, 1) for value in home[2:]]
    mine = add_call(*[[home[c], *parts[c]] for c in range(2)])
    return final_call(xs, pos, interp, mine, mate, values)


def solution(mesh):
    placed = (
        P(None, ("leaf", "help")),
        P(None, ("leaf", "help")),
        P(("leaf", "help"), None, None),
        P(),
        P("leaf", "help"),
        P(("leaf", "help"), None),
        P("leaf", None),
        P(),
        P(),
    )
    return jax.shard_map(
        shards, mesh=mesh, in_specs=placed, out_specs=P(None, ("leaf", "help")), check_vma=False
    )
```

```python
import math
from functools import partial

import jax
import jax.numpy as jnp
from jax import lax
from jax.experimental import pallas as pl
from jax.experimental.pallas import tpu as pltpu
from jax.sharding import PartitionSpec as P

F = 64
R = 256
LEAF = 512
SK = 256
FL = 4
EXTRA = 8
SIZES = (128, 128)

BF = jnp.bfloat16
F32 = jnp.float32
LOG2E = 1.0 / math.log(2.0)
SCALE = math.sqrt(0.5 * LOG2E)
BIAS = 0.0625 * F * LOG2E
VMEM_LIMIT = 24 * 1024 * 1024
VMEM_WHOLE = 64 * 1024 * 1024


def dot(a, b):
    return jnp.dot(a, b, preferred_element_type=F32)


def dot_t(a, b):
    return lax.dot_general(a, b, (((1,), (1,)), ((), ())), preferred_element_type=F32)


def halves(x):
    hi = x.astype(BF)
    lo = (x - hi.astype(F32)).astype(BF)
    return hi, lo


def dot3(a, b, mul=dot):
    a_hi, a_lo = halves(a)
    b_hi, b_lo = halves(b)
    return mul(a_hi, b_hi) + mul(a_lo, b_hi) + mul(a_hi, b_lo)


def target_side(x):
    hi, lo = halves(x)
    both = hi.astype(F32) + lo.astype(F32)
    off = BIAS - 0.5 * jnp.sum(both * both, axis=0, keepdims=True)
    return jnp.concatenate([hi, lo, hi, lo], axis=0), off


def source_side(x):
    xt = x.T
    hi, lo = halves(xt)
    both = hi.astype(F32) + lo.astype(F32)
    off = BIAS - 0.5 * jnp.sum(both * both, axis=1, keepdims=True)
    return jnp.concatenate([hi, hi, lo, lo], axis=1), off


def near_body(
    xs, sets, leaves_at, rows, row, nacc, nout, pos_ref, *refs
):
    nset = len(sets)
    start, stop = leaves_at
    msgs, (t_ref, tb_ref), refs = refs[: 2 * xs], refs[2 * xs : 2 * xs + 2], refs[2 * xs + 2 :]
    if nacc:
        s_scr, sb_scr, w_scr, o_scr, k_scr, times_scr, list_ref, times_ref, sems = refs[-9:]
        outs = refs[-9 - nout : -9]
    else:
        o_scr, s_scr, sb_scr, w_scr, k_scr, times_scr, list_ref, times_ref, sems = refs[-9:]
    copies = [
        pltpu.make_async_copy(msgs[b].at[F : F + EXTRA, :128], times_ref.at[b], sems.at[b])
        for b in range(start // 2, stop // 2)
    ]
    for copy in copies:
        copy.start()
    at = 0
    for k, (_, ready, chunks) in enumerate(sets):
        heads = refs[at : at + 1 + ready]
        parts = refs[at + 1 + ready : at + 1 + ready + chunks]
        at += 1 + ready + chunks
        for leaf in range(2):
            cols = slice(leaf * LEAF, (leaf + 1) * LEAF)
            j = 2 * k + leaf
            if ready:
                s_scr[j] = heads[0][leaf]
                sb_scr[j] = heads[1][leaf]
            else:
                side, off = source_side(heads[0][:F, cols] * SCALE)
                s_scr[j] = side
                sb_scr[j] = jnp.broadcast_to(off, (LEAF, 128))
            top = 0
            for part in parts:
                hi, lo = halves(part[:, cols])
                w_scr[j, top : top + part.shape[0], :] = hi
                w_scr[j, rows + top : rows + top + part.shape[0], :] = lo
                top += part.shape[0]
    for t in range(start, stop):
        if nacc:
            o_scr[t - start] = sum(
                ref[t - (4 * xs - ref.shape[0]), row : row + rows, :] for ref in refs[at : at + nacc]
            )
        else:
            o_scr[t - start] = jnp.zeros((rows, LEAF), F32)

    x, core, group, leaves = pos_ref[0], pos_ref[1], pos_ref[2], pos_ref[3]
    odd = group % 2
    column = []
    for kind, _, _ in sets:
        relative = {"own": 1, "pair": 2 - 2 * odd, "next": 2 * odd}[kind]
        column.append(relative * leaves + 2 * (2 * x + core))

    for copy in copies:
        copy.wait()
    count = jnp.int32(0)
    list_ref[0] = 0
    for t in range(start, stop):
        for j in range(2 * nset):
            times = times_ref[t // 2, t % 2, column[j // 2] + j % 2]

            @pl.when(times > 0)
            def _(count=count, t=t, j=j, times=times):
                list_ref[count] = t * 8 + j
                times_scr[count] = times

            count = count + (times > 0).astype(jnp.int32)

    def block(index, slot):
        code = list_ref[jnp.minimum(index, jnp.maximum(count - 1, 0))]
        t, j = code // 8, code % 8
        side = t_ref[t]
        off = tb_ref[t][:1, :]
        for half in range(2):
            part = slice(half * 256, (half + 1) * 256)
            cross = dot(s_scr[j, part, :], side)
            src_off = sb_scr[j, part, :]
            src_off = jnp.concatenate([src_off] * (LEAF // 128), axis=1)
            k_hi, k_lo = halves(jnp.exp2(cross + src_off + off))
            k_scr[slot, part, :] = k_hi
            k_scr[slot, LEAF + half * 256 : LEAF + (half + 1) * 256, :] = k_lo

    def apply(index, slot):
        code = list_ref[index]
        t, j = code // 8 - start, code % 8
        factor = times_scr[index]
        for half in range(2):
            cols = slice(half * 256, (half + 1) * 256)
            both = dot(w_scr[j], k_scr[slot, :LEAF, cols])
            low = dot(w_scr[j, :rows, :], k_scr[slot, LEAF:, cols])
            o_scr[t, :, cols] = o_scr[t, :, cols] + factor * (both[:rows] + both[rows:] + low)

    @pl.when(count > 0)
    def _():
        block(0, 0)

    def pair(index, carry):
        block(2 * index + 1, 1)
        apply(2 * index, 0)

        @pl.when(2 * index + 1 < count)
        def _():
            block(2 * index + 2, 0)
            apply(2 * index + 1, 1)

        return carry

    lax.fori_loop(0, (count + 1) // 2, pair, jnp.int32(0))
    if nacc:
        t, top = 0, 0
        for ref in outs:
            tall = ref.shape[0]
            for leaf in range(2):
                cols = slice(leaf * LEAF, (leaf + 1) * LEAF)
                ref[:, cols] = o_scr[t + leaf, top : top + tall, :]
            t, top = (t, top + tall) if top + tall < rows else (t + 2, 0)


def near_call(name, pos, msgs, targets, leaves_at, sources, rows, row=0, acc=(), after=()):
    nset = len(sources)
    start, stop = leaves_at
    vmem = pl.BlockSpec(memory_space=pltpu.VMEM)
    smem = pl.BlockSpec(memory_space=pltpu.SMEM)
    operands = [a for _, heads, chunks in sources for a in (*heads, *chunks)]
    scratch = [
        pltpu.VMEM((2 * nset, LEAF, 4 * F), BF),
        pltpu.VMEM((2 * nset, LEAF, 128), F32),
        pltpu.VMEM((2 * nset, 2 * rows, LEAF), BF),
        pltpu.VMEM((stop - start, rows, LEAF), F32),
        pltpu.VMEM((2, 2 * LEAF, LEAF), BF),
        pltpu.SMEM((2 * nset * (stop - start),), F32),
        pltpu.SMEM((2 * nset * (stop - start),), jnp.int32),
        pltpu.SMEM((len(msgs), EXTRA, 128), F32),
        pltpu.SemaphoreType.DMA((len(msgs),)),
    ]
    if not acc:
        out = [jax.ShapeDtypeStruct((stop - start, rows, LEAF), F32)]
        scratch.pop(3)
    else:
        operands += list(acc)
        talls = SIZES if rows == R else (rows,)
        out = [jax.ShapeDtypeStruct((tall, 2 * LEAF), F32) for tall in talls] * ((stop - start) // 2)
    sets = tuple((kind, len(heads) - 1, len(chunks)) for kind, heads, chunks in sources)
    return pl.pallas_call(
        partial(
            near_body, len(msgs) // 2, sets, leaves_at, rows, row, len(acc), len(out)
        ),
        name=name,
        out_shape=out,
        in_specs=[smem]
        + [pl.BlockSpec(memory_space=pl.ANY)] * len(msgs)
        + [vmem] * (2 + len(operands))
        + [pl.BlockSpec(memory_space=pl.ANY)] * len(after),
        out_specs=[vmem] * len(out),
        scratch_shapes=scratch,
        compiler_params=pltpu.CompilerParams(vmem_limit_bytes=VMEM_LIMIT),
    )(pos, *msgs, *targets, *operands, *after)


def source_body(pts_ref, side_ref, off_ref):
    for leaf in range(2):
        cols = slice(leaf * LEAF, (leaf + 1) * LEAF)
        side, off = source_side(pts_ref[:F, cols] * SCALE)
        side_ref[leaf] = side
        off_ref[leaf] = jnp.broadcast_to(off, (LEAF, 128))


def source_call(pts):
    vmem = pl.BlockSpec(memory_space=pltpu.VMEM)
    return pl.pallas_call(
        source_body,
        name="source_side",
        out_shape=[
            jax.ShapeDtypeStruct((2, LEAF, 4 * F), BF),
            jax.ShapeDtypeStruct((2, LEAF, 128), F32),
        ],
        in_specs=[vmem],
        out_specs=[vmem, vmem],
        compiler_params=pltpu.CompilerParams(vmem_limit_bytes=VMEM_LIMIT),
    )(pts)


def share_rows(xs):
    return R // (2 * xs) * SK // (2 * LEAF)


def leaf_body(xs, pos_ref, count_ref, src_ref, pts_in, w_in, interp_in, *refs):
    msgs = refs[: 2 * xs]
    pts_ref, w_ref, interp_ref, scr, sems = refs[2 * xs :]
    copies = [
        pltpu.make_async_copy(pts_in, pts_ref, sems.at[0]),
        pltpu.make_async_copy(w_in, w_ref, sems.at[1]),
        pltpu.make_async_copy(interp_in, interp_ref, sems.at[2]),
    ]
    for copy in copies:
        copy.start()
    x, core, group, leaves = pos_ref[0], pos_ref[1], pos_ref[2], pos_ref[3]
    lane = lax.broadcasted_iota(jnp.int32, (1, 128), 1) + (group - 1) * leaves
    times = []
    for leaf in range(2):
        row = jnp.zeros((1, 128), F32)
        for slot in range(src_ref.shape[1]):
            name = jnp.where(slot < count_ref[0, leaf], src_ref[leaf, slot], -1 - 128 * leaves)
            row = row + (lane == name).astype(F32)
        times.append(row)
    times = jnp.concatenate(times + [jnp.zeros((EXTRA - 2, 128), F32)], axis=0)
    for copy in copies:
        copy.wait()
    total = jnp.zeros((R, SK), F32)
    for leaf in range(2):
        total = total + dot3(w_ref[:, leaf * LEAF : (leaf + 1) * LEAF], interp_ref[leaf])
    scr[...] = total
    rows = R // (2 * xs)
    tall = share_rows(xs)
    for n, msg in enumerate(msgs):
        helper = 2 * lax.rem(x + n // 2, xs) + (core if n % 2 == 0 else 1 - core)
        msg[:F, :] = pts_ref[...]
        msg[F : F + EXTRA, :] = jnp.zeros((EXTRA, 2 * LEAF), F32)
        msg[F : F + EXTRA, :128] = times
        for i in range(rows // tall):
            at = pl.multiple_of(helper * rows + i * tall, tall)
            msg[F + EXTRA :, i * SK : (i + 1) * SK] = scr[pl.ds(at, tall), :]


def leaf_call(xs, pos, near_count, near_src, points, weights, interp):
    vmem = pl.BlockSpec(memory_space=pltpu.VMEM)
    smem = pl.BlockSpec(memory_space=pltpu.SMEM)
    anywhere = pl.BlockSpec(memory_space=pl.ANY)
    height = F + EXTRA + share_rows(xs)
    return pl.pallas_call(
        partial(leaf_body, xs),
        name="leaf_up",
        out_shape=[jax.ShapeDtypeStruct((height, 2 * LEAF), F32)] * (2 * xs),
        in_specs=[smem, smem, smem, anywhere, anywhere, anywhere],
        out_specs=[vmem] * (2 * xs),
        scratch_shapes=[
            pltpu.VMEM(points.shape, F32),
            pltpu.VMEM(weights.shape, F32),
            pltpu.VMEM(interp.shape, F32),
            pltpu.VMEM((R, SK), F32),
            pltpu.SemaphoreType.DMA((3,)),
        ],
        compiler_params=pltpu.CompilerParams(vmem_limit_bytes=VMEM_WHOLE),
    )(pos, near_count, near_src, points, weights, interp)


def skel_body(xs, pos_ref, index_ref, *refs):
    msgs, (out_ref, side_ref, off_ref) = refs[:-3], refs[-3:]
    rows = R // (2 * xs)
    tall = share_rows(xs)
    total = jnp.zeros((2 * F, SK), F32)
    value = jnp.zeros((tall, 2 * LEAF), F32)
    spot = lax.broadcasted_iota(jnp.int32, (2 * LEAF, SK), 0)
    x, core = pos_ref[0], pos_ref[1]
    for b, msg in enumerate(msgs):
        helper = 2 * lax.rem(x + b // 2, xs) + (core if b % 2 == 0 else 1 - core)
        side, off = target_side(msg[:F, :] * SCALE)
        for leaf in range(2):
            part = slice(leaf * LEAF, (leaf + 1) * LEAF)
            side_ref[2 * b + leaf] = side[:, part]
            off_ref[2 * b + leaf] = jnp.broadcast_to(off[:, part], (8, LEAF))
        hot = spot + helper * (2 * LEAF) == index_ref[...]
        total = total + dot(side[: 2 * F], hot.astype(F32).astype(BF))
        value = value + msg[F + EXTRA :, :]
    out_ref[:F, :] = total[:F] + total[F:]
    for i in range(rows // tall):
        out_ref[F + i * tall : F + (i + 1) * tall, :] = value[:, i * SK : (i + 1) * SK]


def skel_call(xs, pos, index, msgs):
    rows = R // (2 * xs)
    leaves = 2 * len(msgs)
    vmem = pl.BlockSpec(memory_space=pltpu.VMEM)
    payload, *targets = pl.pallas_call(
        partial(skel_body, xs),
        name="skeleton",
        out_shape=[
            jax.ShapeDtypeStruct((F + rows, SK), F32),
            jax.ShapeDtypeStruct((leaves, 4 * F, LEAF), BF),
            jax.ShapeDtypeStruct((leaves, 8, LEAF), F32),
        ],
        in_specs=[pl.BlockSpec(memory_space=pltpu.SMEM)] + [vmem] * (1 + len(msgs)),
        out_specs=[vmem] * 3,
        compiler_params=pltpu.CompilerParams(vmem_limit_bytes=VMEM_LIMIT),
        cost_estimate=pl.CostEstimate(
            flops=5_000_000_000, bytes_accessed=8_000_000, transcendentals=0
        ),
    )(pos, index, *msgs)
    return payload, targets


def stack_body(*refs):
    for n, ref in enumerate(refs[:-1]):
        refs[-1][n] = ref[...]


def stack_call(pieces):
    vmem = pl.BlockSpec(memory_space=pltpu.VMEM)
    return pl.pallas_call(
        stack_body,
        name="stack",
        out_shape=jax.ShapeDtypeStruct((len(pieces), *pieces[0].shape), F32),
        in_specs=[vmem] * len(pieces),
        out_specs=vmem,
        compiler_params=pltpu.CompilerParams(vmem_limit_bytes=VMEM_LIMIT),
    )(*pieces)


def upper_start(level, groups):
    return sum((groups >> step for step in range(1, level)))


def list_start(level, groups):
    return sum((groups >> step for step in range(level)))


def far_body(groups, rows, pos_ref, far_ref, node_ref, transfer_ref, alike_ref, beside_ref, *refs):
    out_ref, p_scr, u_scr, f_scr = refs[-4:]
    levels = groups.bit_length() - 1
    group = pos_ref[2]
    start = [list_start(level, groups) for level in range(levels)]
    for n in range(groups // 2):
        same, other = group ^ (2 * n), group ^ (2 * n + 1)
        p_scr[same] = alike_ref[n, :F, :]
        u_scr[same] = alike_ref[n, F:, :]
        p_scr[other] = beside_ref[n, :F, :]
        u_scr[other] = beside_ref[n, F:, :]
    spot = lax.broadcasted_iota(jnp.int32, (2 * SK, SK), 0)
    for level in range(1, levels):
        for n in range(groups >> level):
            row = upper_start(level, groups) + n
            left = start[level - 1] + 2 * n
            hot = (spot == node_ref[row : row + 1, :]).astype(F32).astype(BF)
            hi, lo = halves(jnp.concatenate([p_scr[left], p_scr[left + 1]], axis=1))
            both = dot(jnp.concatenate([hi, lo], axis=0), hot)
            p_scr[start[level] + n] = both[:F] + both[F:]
            vals = jnp.concatenate([u_scr[left], u_scr[left + 1]], axis=1)
            u_scr[start[level] + n] = dot3(vals, transfer_ref[row])
    for level in range(levels):
        node = group >> level
        side, off = target_side(p_scr[start[level] + node])
        f_scr[level] = jnp.zeros((rows, SK), F32)

        def one(n, carry, level=level, node=node, side=side, off=off):
            hits = jnp.int32(0)
            for slot in range(FL):
                hits = hits + (far_ref[slot, start[level] + node] == n).astype(jnp.int32)

            @pl.when(hits > 0)
            def _():
                src, src_off = source_side(p_scr[start[level] + n])
                block = jnp.exp2(dot(src, side) + src_off + off)
                term = dot3(u_scr[start[level] + n], block)
                f_scr[level] = f_scr[level] + hits.astype(F32) * term

            return carry

        lax.fori_loop(0, groups >> level, one, jnp.int32(0))
    local = f_scr[levels - 1]
    for level in range(levels - 1, 0, -1):
        row = upper_start(level, groups) + (group >> level)
        bit = (group >> (level - 1)) & 1
        matrix = transfer_ref[row, pl.ds(pl.multiple_of(bit * SK, SK), SK), :]
        local = f_scr[level - 1] + dot3(local, matrix, dot_t)
    out_ref[...] = local


def far_call(groups, pos, far_nodes, skel_node, transfer, alike, beside, after):
    rows = alike.shape[1] - F
    vmem = pl.BlockSpec(memory_space=pltpu.VMEM)
    smem = pl.BlockSpec(memory_space=pltpu.SMEM)
    nodes = 2 * groups
    return pl.pallas_call(
        partial(far_body, groups, rows),
        name="far",
        out_shape=jax.ShapeDtypeStruct((rows, SK), F32),
        in_specs=[smem, smem, vmem, vmem, vmem, vmem]
        + [pl.BlockSpec(memory_space=pl.ANY)] * len(after),
        out_specs=vmem,
        scratch_shapes=[
            pltpu.VMEM((nodes, F, SK), F32),
            pltpu.VMEM((nodes, rows, SK), F32),
            pltpu.VMEM((groups.bit_length(), rows, SK), F32),
        ],
        compiler_params=pltpu.CompilerParams(vmem_limit_bytes=VMEM_LIMIT),
    )(pos, far_nodes.T, skel_node, transfer, alike, beside, *after)


def final_body(xs, pos_ref, interp_ref, *refs):
    values, sums = refs[:xs], refs[xs:-2]
    out_ref, v_scr = refs[-2:]
    rows = R // (2 * xs)
    x, core = pos_ref[0], pos_ref[1]
    for dx, ref in enumerate(values):
        for dc in range(2):
            helper = 2 * lax.rem(x + dx, xs) + (core if dc == 0 else 1 - core)
            v_scr[pl.ds(pl.multiple_of(helper * rows, rows), rows), :] = ref[dc]
    value = v_scr[...]
    for leaf in range(2):
        cols = slice(leaf * LEAF, (leaf + 1) * LEAF)
        total = dot3(value, interp_ref[leaf], dot_t)
        for c in range(2):
            part = slice(c * SIZES[0], SIZES[0] + c * SIZES[1])
            out_ref[part, cols] = total[part] + sums[c][:, cols] + sums[2 + c][:, cols]


def add_body(count, *refs):
    for n, out_ref in enumerate(refs[-(len(refs) // (count + 1)) :]):
        total = refs[n * count][...]
        for ref in refs[n * count + 1 : (n + 1) * count]:
            total = total + ref[...]
        out_ref[...] = total


def add_call(*sums):
    vmem = pl.BlockSpec(memory_space=pltpu.VMEM)
    operands = [value for terms in sums for value in terms]
    return pl.pallas_call(
        partial(add_body, len(sums[0])),
        name="add_parts",
        out_shape=[jax.ShapeDtypeStruct(terms[0].shape, F32) for terms in sums],
        in_specs=[vmem] * len(operands),
        out_specs=[vmem] * len(sums),
        compiler_params=pltpu.CompilerParams(vmem_limit_bytes=VMEM_LIMIT),
    )(*operands)


def final_call(xs, pos, interp, home, mate, values):
    vmem = pl.BlockSpec(memory_space=pltpu.VMEM)
    return pl.pallas_call(
        partial(final_body, xs),
        name="join",
        out_shape=jax.ShapeDtypeStruct((R, 2 * LEAF), F32),
        in_specs=[pl.BlockSpec(memory_space=pltpu.SMEM)] + [vmem] * (1 + xs + 4),
        out_specs=vmem,
        scratch_shapes=[pltpu.VMEM((R, SK), F32)],
        compiler_params=pltpu.CompilerParams(vmem_limit_bytes=VMEM_LIMIT),
    )(pos, interp, *values, *home, *mate)


def help_pairs(xs, dx, dc):
    return [
        (2 * ((x + dx) % xs) + (core ^ dc), 2 * x + core) for x in range(xs) for core in range(2)
    ]


def shards(
    points, weights, interp, transfer, near_count, near_src, skel_group, skel_node, far_nodes
):
    helpers = lax.axis_size("help")
    groups = lax.axis_size("leaf")
    xs = helpers // 2
    helper = lax.axis_index("help")
    group = lax.axis_index("leaf")
    x, core = helper // 2, helper % 2
    leaves = 2 * helpers
    pos = jnp.stack([x, core, group, jnp.int32(leaves)]).astype(jnp.int32)
    rows = R // 2

    def from_help(value, dx, dc):
        return lax.ppermute(value, "help", help_pairs(xs, dx, dc))

    def to_help(value, dx):
        return lax.ppermute(value, "help", help_pairs(xs, -dx, 0))

    def together(*values):
        return lax.optimization_barrier(values)

    beside = [(i, i ^ 1) for i in range(groups)]
    across = [(i, i + 2) for i in range(0, groups - 2, 2)]
    across += [(i, i - 2) for i in range(3, groups, 2)]
    order = [(dx, dc) for dx in range(xs) for dc in range(2)]

    cut = SIZES[0]
    pts_y = lax.ppermute(points, "leaf", beside)
    w_y = [lax.ppermute(chunk, "leaf", beside) for chunk in (weights[:cut], weights[cut:])]
    sent = leaf_call(xs, pos, near_count, near_src, points, weights, interp)
    got = [
        lax.ppermute(sent[n], "help", help_pairs(xs, -dx, dc))
        for n, (dx, dc) in enumerate(order)
        if n
    ]
    pts_z = lax.ppermute(pts_y, "leaf", across)
    got, pts_z = together(got, pts_z)
    w_z = [lax.ppermute(w_y[0], "leaf", across)]
    msgs = [sent[0]] + [got[order.index((-dx % xs, dc)) - 1] for dx, dc in order[1:]]
    payload, targets = skel_call(xs, pos, skel_group, msgs)
    pieces = [payload]
    for mask in range(2, groups, 2):
        pieces.append(lax.ppermute(payload, "leaf", [(i, i ^ mask) for i in range(groups)]))

    payload, w_y[1] = together(payload, w_y[1])
    every, away, home = (0, 2 * helpers), (4, 2 * helpers), (0, 4)
    (own,) = near_call("near_own", pos, msgs, targets, every, [("own", (points,), [weights])], R)
    w_z.append(lax.ppermute(w_y[1], "leaf", across))
    pair_src = ("pair", (pts_y,), w_y)
    (pair,) = near_call("near_pair", pos, msgs, targets, away, [pair_src], R, after=[own])
    z_side = source_call(pts_z)
    sums, part = [], [pair]
    for c in range(2):
        if c == 1:
            pieces, part = together(pieces, part)
            alike = stack_call(pieces)
            side = lax.ppermute(alike, "leaf", beside)
            part = [alike]
        part = near_call(
            "near_next_away", pos, msgs, targets, away, [("next", z_side, w_z[c : c + 1])],
            SIZES[c], c * SIZES[0], [own, pair], part[:1],
        )
        kept, given = part[::2], part[1::2]
        sums.append((kept, [from_help(value, 0, 1) for value in given]))
    parts = []
    for c in range(2):
        kept, mates = sums[c]
        both = add_call(*zip(kept, mates))
        parts.append([to_help(value, dx + 1) for dx, value in enumerate(both)])
    sources = [pair_src, ("next", z_side, w_z)]
    home = near_call("near_home", pos, msgs, targets, home, sources, R, 0, [own], both[:1])
    v_own = far_call(groups, pos, far_nodes, skel_node, transfer, alike, side, home[:1])
    v_pair = stack_call([v_own, from_help(v_own, 0, 1)])
    values = [v_pair] + [from_help(v_pair, dx, 0) for dx in range(1, xs)]
    mate = [from_help(value, 0, 1) for value in home[2:]]
    mine = add_call(*[[home[c], *parts[c]] for c in range(2)])
    return final_call(xs, pos, interp, mine, mate, values)


def solution(mesh):
    placed = (
        P(None, ("leaf", "help")),
        P(None, ("leaf", "help")),
        P(("leaf", "help"), None, None),
        P(),
        P("leaf", "help"),
        P(("leaf", "help"), None),
        P("leaf", None),
        P(),
        P(),
    )
    return jax.shard_map(
        shards, mesh=mesh, in_specs=placed, out_specs=P(None, ("leaf", "help")), check_vma=False
    )
```

```python
import math
from functools import partial

import jax
import jax.numpy as jnp
from jax import lax
from jax.experimental import pallas as pl
from jax.experimental.pallas import tpu as pltpu
from jax.sharding import PartitionSpec as P

F = 64
R = 256
LEAF = 512
SK = 256
FL = 4
EXTRA = 8
SIZES = (128, 128)

BF = jnp.bfloat16
F32 = jnp.float32
LOG2E = 1.0 / math.log(2.0)
SCALE = math.sqrt(0.5 * LOG2E)
BIAS = 0.0625 * F * LOG2E
VMEM_LIMIT = 24 * 1024 * 1024
VMEM_WHOLE = 64 * 1024 * 1024


def dot(a, b):
    return jnp.dot(a, b, preferred_element_type=F32)


def dot_t(a, b):
    return lax.dot_general(a, b, (((1,), (1,)), ((), ())), preferred_element_type=F32)


def halves(x):
    hi = x.astype(BF)
    lo = (x - hi.astype(F32)).astype(BF)
    return hi, lo


def dot3(a, b, mul=dot):
    a_hi, a_lo = halves(a)
    b_hi, b_lo = halves(b)
    return mul(a_hi, b_hi) + mul(a_lo, b_hi) + mul(a_hi, b_lo)


def target_side(x):
    hi, lo = halves(x)
    both = hi.astype(F32) + lo.astype(F32)
    off = BIAS - 0.5 * jnp.sum(both * both, axis=0, keepdims=True)
    return jnp.concatenate([hi, lo, hi, lo], axis=0), off


def source_side(x):
    xt = x.T
    hi, lo = halves(xt)
    both = hi.astype(F32) + lo.astype(F32)
    off = BIAS - 0.5 * jnp.sum(both * both, axis=1, keepdims=True)
    return jnp.concatenate([hi, hi, lo, lo], axis=1), off


def near_body(
    xs, sets, leaves_at, rows, row, nacc, nout, *refs
):
    nset = len(sets)
    start, stop = leaves_at
    msgs, (t_ref, tb_ref), refs = refs[: 2 * xs], refs[2 * xs : 2 * xs + 2], refs[2 * xs + 2 :]
    if nacc:
        s_scr, sb_scr, w_scr, o_scr, k_scr, times_scr, list_ref, times_ref, sems = refs[-9:]
        outs = refs[-9 - nout : -9]
    else:
        o_scr, s_scr, sb_scr, w_scr, k_scr, times_scr, list_ref, times_ref, sems = refs[-9:]
    copies = [
        pltpu.make_async_copy(msgs[b].at[F : F + EXTRA, :128], times_ref.at[b], sems.at[b])
        for b in range(start // 2, stop // 2)
    ]
    for copy in copies:
        copy.start()
    at = 0
    for k, (_, ready, chunks) in enumerate(sets):
        heads = refs[at : at + 1 + ready]
        parts = refs[at + 1 + ready : at + 1 + ready + chunks]
        at += 1 + ready + chunks
        for leaf in range(2):
            cols = slice(leaf * LEAF, (leaf + 1) * LEAF)
            j = 2 * k + leaf
            if ready:
                s_scr[j] = heads[0][leaf]
                sb_scr[j] = heads[1][leaf]
            else:
                side, off = source_side(heads[0][:F, cols] * SCALE)
                s_scr[j] = side
                sb_scr[j] = jnp.broadcast_to(off, (LEAF, 128))
            top = 0
            for part in parts:
                hi, lo = halves(part[:, cols])
                w_scr[j, top : top + part.shape[0], :] = hi
                w_scr[j, rows + top : rows + top + part.shape[0], :] = lo
                top += part.shape[0]
    for t in range(start, stop):
        if nacc:
            o_scr[t - start] = sum(
                ref[t - (4 * xs - ref.shape[0]), row : row + rows, :] for ref in refs[at : at + nacc]
            )
        else:
            o_scr[t - start] = jnp.zeros((rows, LEAF), F32)

    x, core, group = place()
    leaves = 4 * xs
    odd = group % 2
    column = []
    for kind, _, _ in sets:
        relative = {"own": 1, "pair": 2 - 2 * odd, "next": 2 * odd}[kind]
        column.append(relative * leaves + 2 * (2 * x + core))

    for copy in copies:
        copy.wait()
    count = jnp.int32(0)
    list_ref[0] = 0
    for t in range(start, stop):
        for j in range(2 * nset):
            times = times_ref[t // 2, t % 2, column[j // 2] + j % 2]

            @pl.when(times > 0)
            def _(count=count, t=t, j=j, times=times):
                list_ref[count] = t * 8 + j
                times_scr[count] = times

            count = count + (times > 0).astype(jnp.int32)

    def block(index, slot):
        code = list_ref[jnp.minimum(index, jnp.maximum(count - 1, 0))]
        t, j = code // 8, code % 8
        side = t_ref[t]
        off = tb_ref[t][:1, :]
        for half in range(2):
            part = slice(half * 256, (half + 1) * 256)
            cross = dot(s_scr[j, part, :], side)
            src_off = sb_scr[j, part, :]
            src_off = jnp.concatenate([src_off] * (LEAF // 128), axis=1)
            k_hi, k_lo = halves(jnp.exp2(cross + src_off + off))
            k_scr[slot, part, :] = k_hi
            k_scr[slot, LEAF + half * 256 : LEAF + (half + 1) * 256, :] = k_lo

    def apply(index, slot):
        code = list_ref[index]
        t, j = code // 8 - start, code % 8
        factor = times_scr[index]
        for half in range(2):
            cols = slice(half * 256, (half + 1) * 256)
            both = dot(w_scr[j], k_scr[slot, :LEAF, cols])
            low = dot(w_scr[j, :rows, :], k_scr[slot, LEAF:, cols])
            o_scr[t, :, cols] = o_scr[t, :, cols] + factor * (both[:rows] + both[rows:] + low)

    @pl.when(count > 0)
    def _():
        block(0, 0)

    def pair(index, carry):
        block(2 * index + 1, 1)
        apply(2 * index, 0)

        @pl.when(2 * index + 1 < count)
        def _():
            block(2 * index + 2, 0)
            apply(2 * index + 1, 1)

        return carry

    lax.fori_loop(0, (count + 1) // 2, pair, jnp.int32(0))
    if nacc:
        t, top = 0, 0
        for ref in outs:
            tall = ref.shape[0]
            for leaf in range(2):
                cols = slice(leaf * LEAF, (leaf + 1) * LEAF)
                ref[:, cols] = o_scr[t + leaf, top : top + tall, :]
            t, top = (t, top + tall) if top + tall < rows else (t + 2, 0)


def near_call(name, msgs, targets, leaves_at, sources, rows, row=0, acc=(), after=()):
    nset = len(sources)
    start, stop = leaves_at
    vmem = pl.BlockSpec(memory_space=pltpu.VMEM)
    operands = [a for _, heads, chunks in sources for a in (*heads, *chunks)]
    scratch = [
        pltpu.VMEM((2 * nset, LEAF, 4 * F), BF),
        pltpu.VMEM((2 * nset, LEAF, 128), F32),
        pltpu.VMEM((2 * nset, 2 * rows, LEAF), BF),
        pltpu.VMEM((stop - start, rows, LEAF), F32),
        pltpu.VMEM((2, 2 * LEAF, LEAF), BF),
        pltpu.SMEM((2 * nset * (stop - start),), F32),
        pltpu.SMEM((2 * nset * (stop - start),), jnp.int32),
        pltpu.SMEM((len(msgs), EXTRA, 128), F32),
        pltpu.SemaphoreType.DMA((len(msgs),)),
    ]
    if not acc:
        out = [jax.ShapeDtypeStruct((stop - start, rows, LEAF), F32)]
        scratch.pop(3)
    else:
        operands += list(acc)
        talls = SIZES if rows == R else (rows,)
        out = [jax.ShapeDtypeStruct((tall, 2 * LEAF), F32) for tall in talls] * ((stop - start) // 2)
    sets = tuple((kind, len(heads) - 1, len(chunks)) for kind, heads, chunks in sources)
    return pl.pallas_call(
        partial(
            near_body, len(msgs) // 2, sets, leaves_at, rows, row, len(acc), len(out)
        ),
        name=name,
        out_shape=out,
        in_specs=[pl.BlockSpec(memory_space=pl.ANY)] * len(msgs)
        + [vmem] * (2 + len(operands))
        + [pl.BlockSpec(memory_space=pl.ANY)] * len(after),
        out_specs=[vmem] * len(out),
        scratch_shapes=scratch,
        compiler_params=pltpu.CompilerParams(vmem_limit_bytes=VMEM_LIMIT),
    )(*msgs, *targets, *operands, *after)


def source_body(pts_ref, side_ref, off_ref):
    for leaf in range(2):
        cols = slice(leaf * LEAF, (leaf + 1) * LEAF)
        side, off = source_side(pts_ref[:F, cols] * SCALE)
        side_ref[leaf] = side
        off_ref[leaf] = jnp.broadcast_to(off, (LEAF, 128))


def source_call(pts):
    vmem = pl.BlockSpec(memory_space=pltpu.VMEM)
    return pl.pallas_call(
        source_body,
        name="source_side",
        out_shape=[
            jax.ShapeDtypeStruct((2, LEAF, 4 * F), BF),
            jax.ShapeDtypeStruct((2, LEAF, 128), F32),
        ],
        in_specs=[vmem],
        out_specs=[vmem, vmem],
        compiler_params=pltpu.CompilerParams(vmem_limit_bytes=VMEM_LIMIT),
    )(pts)


def place():
    helper = lax.axis_index("help")
    return helper // 2, helper % 2, lax.axis_index("leaf")


def share_rows(xs):
    return R // (2 * xs) * SK // (2 * LEAF)


def leaf_body(xs, count_ref, src_ref, pts_in, w_in, interp_in, *refs):
    msgs = refs[: 2 * xs]
    pts_ref, w_ref, interp_ref, scr, sems = refs[2 * xs :]
    copies = [
        pltpu.make_async_copy(pts_in, pts_ref, sems.at[0]),
        pltpu.make_async_copy(w_in, w_ref, sems.at[1]),
        pltpu.make_async_copy(interp_in, interp_ref, sems.at[2]),
    ]
    for copy in copies:
        copy.start()
    x, core, group = place()
    leaves = 4 * xs
    lane = lax.broadcasted_iota(jnp.int32, (1, 128), 1) + (group - 1) * leaves
    times = []
    for leaf in range(2):
        row = jnp.zeros((1, 128), F32)
        for slot in range(src_ref.shape[1]):
            name = jnp.where(slot < count_ref[0, leaf], src_ref[leaf, slot], -1 - 128 * leaves)
            row = row + (lane == name).astype(F32)
        times.append(row)
    times = jnp.concatenate(times + [jnp.zeros((EXTRA - 2, 128), F32)], axis=0)
    for copy in copies:
        copy.wait()
    total = jnp.zeros((R, SK), F32)
    for leaf in range(2):
        total = total + dot3(w_ref[:, leaf * LEAF : (leaf + 1) * LEAF], interp_ref[leaf])
    scr[...] = total
    rows = R // (2 * xs)
    tall = share_rows(xs)
    for n, msg in enumerate(msgs):
        helper = 2 * lax.rem(x + n // 2, xs) + (core if n % 2 == 0 else 1 - core)
        msg[:F, :] = pts_ref[...]
        msg[F : F + EXTRA, :] = jnp.zeros((EXTRA, 2 * LEAF), F32)
        msg[F : F + EXTRA, :128] = times
        for i in range(rows // tall):
            at = pl.multiple_of(helper * rows + i * tall, tall)
            msg[F + EXTRA :, i * SK : (i + 1) * SK] = scr[pl.ds(at, tall), :]


def leaf_call(xs, near_count, near_src, points, weights, interp):
    vmem = pl.BlockSpec(memory_space=pltpu.VMEM)
    smem = pl.BlockSpec(memory_space=pltpu.SMEM)
    anywhere = pl.BlockSpec(memory_space=pl.ANY)
    height = F + EXTRA + share_rows(xs)
    return pl.pallas_call(
        partial(leaf_body, xs),
        name="leaf_up",
        out_shape=[jax.ShapeDtypeStruct((height, 2 * LEAF), F32)] * (2 * xs),
        in_specs=[smem, smem, anywhere, anywhere, anywhere],
        out_specs=[vmem] * (2 * xs),
        scratch_shapes=[
            pltpu.VMEM(points.shape, F32),
            pltpu.VMEM(weights.shape, F32),
            pltpu.VMEM(interp.shape, F32),
            pltpu.VMEM((R, SK), F32),
            pltpu.SemaphoreType.DMA((3,)),
        ],
        compiler_params=pltpu.CompilerParams(vmem_limit_bytes=VMEM_WHOLE),
    )(near_count, near_src, points, weights, interp)


def skel_body(xs, index_ref, *refs):
    msgs, (out_ref, side_ref, off_ref) = refs[:-3], refs[-3:]
    rows = R // (2 * xs)
    tall = share_rows(xs)
    total = jnp.zeros((2 * F, SK), F32)
    value = jnp.zeros((tall, 2 * LEAF), F32)
    spot = lax.broadcasted_iota(jnp.int32, (2 * LEAF, SK), 0)
    x, core, _ = place()
    for b, msg in enumerate(msgs):
        helper = 2 * lax.rem(x + b // 2, xs) + (core if b % 2 == 0 else 1 - core)
        side, off = target_side(msg[:F, :] * SCALE)
        for leaf in range(2):
            part = slice(leaf * LEAF, (leaf + 1) * LEAF)
            side_ref[2 * b + leaf] = side[:, part]
            off_ref[2 * b + leaf] = jnp.broadcast_to(off[:, part], (8, LEAF))
        hot = spot + helper * (2 * LEAF) == index_ref[...]
        total = total + dot(side[: 2 * F], hot.astype(F32).astype(BF))
        value = value + msg[F + EXTRA :, :]
    out_ref[:F, :] = total[:F] + total[F:]
    for i in range(rows // tall):
        out_ref[F + i * tall : F + (i + 1) * tall, :] = value[:, i * SK : (i + 1) * SK]


def skel_call(xs, index, msgs):
    rows = R // (2 * xs)
    leaves = 2 * len(msgs)
    vmem = pl.BlockSpec(memory_space=pltpu.VMEM)
    payload, *targets = pl.pallas_call(
        partial(skel_body, xs),
        name="skeleton",
        out_shape=[
            jax.ShapeDtypeStruct((F + rows, SK), F32),
            jax.ShapeDtypeStruct((leaves, 4 * F, LEAF), BF),
            jax.ShapeDtypeStruct((leaves, 8, LEAF), F32),
        ],
        in_specs=[vmem] * (1 + len(msgs)),
        out_specs=[vmem] * 3,
        compiler_params=pltpu.CompilerParams(vmem_limit_bytes=VMEM_LIMIT),
        cost_estimate=pl.CostEstimate(
            flops=5_000_000_000, bytes_accessed=8_000_000, transcendentals=0
        ),
    )(index, *msgs)
    return payload, targets


def stack_body(*refs):
    for n, ref in enumerate(refs[:-1]):
        refs[-1][n] = ref[...]


def stack_call(pieces):
    vmem = pl.BlockSpec(memory_space=pltpu.VMEM)
    return pl.pallas_call(
        stack_body,
        name="stack",
        out_shape=jax.ShapeDtypeStruct((len(pieces), *pieces[0].shape), F32),
        in_specs=[vmem] * len(pieces),
        out_specs=vmem,
        compiler_params=pltpu.CompilerParams(vmem_limit_bytes=VMEM_LIMIT),
    )(*pieces)


def upper_start(level, groups):
    return sum((groups >> step for step in range(1, level)))


def list_start(level, groups):
    return sum((groups >> step for step in range(level)))


def far_body(groups, rows, far_ref, node_ref, transfer_ref, alike_ref, beside_ref, *refs):
    out_ref, p_scr, u_scr, f_scr = refs[-4:]
    levels = groups.bit_length() - 1
    group = place()[2]
    start = [list_start(level, groups) for level in range(levels)]
    for n in range(groups // 2):
        same, other = group ^ (2 * n), group ^ (2 * n + 1)
        p_scr[same] = alike_ref[n, :F, :]
        u_scr[same] = alike_ref[n, F:, :]
        p_scr[other] = beside_ref[n, :F, :]
        u_scr[other] = beside_ref[n, F:, :]
    spot = lax.broadcasted_iota(jnp.int32, (2 * SK, SK), 0)
    for level in range(1, levels):
        for n in range(groups >> level):
            row = upper_start(level, groups) + n
            left = start[level - 1] + 2 * n
            hot = (spot == node_ref[row : row + 1, :]).astype(F32).astype(BF)
            hi, lo = halves(jnp.concatenate([p_scr[left], p_scr[left + 1]], axis=1))
            both = dot(jnp.concatenate([hi, lo], axis=0), hot)
            p_scr[start[level] + n] = both[:F] + both[F:]
            vals = jnp.concatenate([u_scr[left], u_scr[left + 1]], axis=1)
            u_scr[start[level] + n] = dot3(vals, transfer_ref[row])
    for level in range(levels):
        node = group >> level
        side, off = target_side(p_scr[start[level] + node])
        f_scr[level] = jnp.zeros((rows, SK), F32)

        def one(n, carry, level=level, node=node, side=side, off=off):
            hits = jnp.int32(0)
            for slot in range(FL):
                hits = hits + (far_ref[slot, start[level] + node] == n).astype(jnp.int32)

            @pl.when(hits > 0)
            def _():
                src, src_off = source_side(p_scr[start[level] + n])
                block = jnp.exp2(dot(src, side) + src_off + off)
                term = dot3(u_scr[start[level] + n], block)
                f_scr[level] = f_scr[level] + hits.astype(F32) * term

            return carry

        lax.fori_loop(0, groups >> level, one, jnp.int32(0))
    local = f_scr[levels - 1]
    for level in range(levels - 1, 0, -1):
        row = upper_start(level, groups) + (group >> level)
        bit = (group >> (level - 1)) & 1
        matrix = transfer_ref[row, pl.ds(pl.multiple_of(bit * SK, SK), SK), :]
        local = f_scr[level - 1] + dot3(local, matrix, dot_t)
    out_ref[...] = local


def far_call(groups, far_nodes, skel_node, transfer, alike, beside, after):
    rows = alike.shape[1] - F
    vmem = pl.BlockSpec(memory_space=pltpu.VMEM)
    smem = pl.BlockSpec(memory_space=pltpu.SMEM)
    nodes = 2 * groups
    return pl.pallas_call(
        partial(far_body, groups, rows),
        name="far",
        out_shape=jax.ShapeDtypeStruct((rows, SK), F32),
        in_specs=[smem, vmem, vmem, vmem, vmem]
        + [pl.BlockSpec(memory_space=pl.ANY)] * len(after),
        out_specs=vmem,
        scratch_shapes=[
            pltpu.VMEM((nodes, F, SK), F32),
            pltpu.VMEM((nodes, rows, SK), F32),
            pltpu.VMEM((groups.bit_length(), rows, SK), F32),
        ],
        compiler_params=pltpu.CompilerParams(vmem_limit_bytes=VMEM_LIMIT),
    )(far_nodes.T, skel_node, transfer, alike, beside, *after)


def final_body(xs, interp_ref, *refs):
    values, sums = refs[:xs], refs[xs:-2]
    out_ref, v_scr = refs[-2:]
    rows = R // (2 * xs)
    x, core, _ = place()
    for dx, ref in enumerate(values):
        for dc in range(2):
            helper = 2 * lax.rem(x + dx, xs) + (core if dc == 0 else 1 - core)
            v_scr[pl.ds(pl.multiple_of(helper * rows, rows), rows), :] = ref[dc]
    value = v_scr[...]
    for leaf in range(2):
        cols = slice(leaf * LEAF, (leaf + 1) * LEAF)
        total = dot3(value, interp_ref[leaf], dot_t)
        for c in range(2):
            part = slice(c * SIZES[0], SIZES[0] + c * SIZES[1])
            out_ref[part, cols] = total[part] + sums[c][:, cols] + sums[2 + c][:, cols]


def add_body(count, *refs):
    for n, out_ref in enumerate(refs[-(len(refs) // (count + 1)) :]):
        total = refs[n * count][...]
        for ref in refs[n * count + 1 : (n + 1) * count]:
            total = total + ref[...]
        out_ref[...] = total


def add_call(*sums):
    vmem = pl.BlockSpec(memory_space=pltpu.VMEM)
    operands = [value for terms in sums for value in terms]
    return pl.pallas_call(
        partial(add_body, len(sums[0])),
        name="add_parts",
        out_shape=[jax.ShapeDtypeStruct(terms[0].shape, F32) for terms in sums],
        in_specs=[vmem] * len(operands),
        out_specs=[vmem] * len(sums),
        compiler_params=pltpu.CompilerParams(vmem_limit_bytes=VMEM_LIMIT),
    )(*operands)


def final_call(xs, interp, home, mate, values):
    vmem = pl.BlockSpec(memory_space=pltpu.VMEM)
    return pl.pallas_call(
        partial(final_body, xs),
        name="join",
        out_shape=jax.ShapeDtypeStruct((R, 2 * LEAF), F32),
        in_specs=[vmem] * (1 + xs + 4),
        out_specs=vmem,
        scratch_shapes=[pltpu.VMEM((R, SK), F32)],
        compiler_params=pltpu.CompilerParams(vmem_limit_bytes=VMEM_LIMIT),
    )(interp, *values, *home, *mate)


def help_pairs(xs, dx, dc):
    return [
        (2 * ((x + dx) % xs) + (core ^ dc), 2 * x + core) for x in range(xs) for core in range(2)
    ]


def shards(
    points, weights, interp, transfer, near_count, near_src, skel_group, skel_node, far_nodes
):
    helpers = lax.axis_size("help")
    groups = lax.axis_size("leaf")
    xs = helpers // 2
    def from_help(value, dx, dc):
        return lax.ppermute(value, "help", help_pairs(xs, dx, dc))

    def to_help(value, dx):
        return lax.ppermute(value, "help", help_pairs(xs, -dx, 0))

    def together(*values):
        return lax.optimization_barrier(values)

    beside = [(i, i ^ 1) for i in range(groups)]
    across = [(i, i + 2) for i in range(0, groups - 2, 2)]
    across += [(i, i - 2) for i in range(3, groups, 2)]
    order = [(dx, dc) for dx in range(xs) for dc in range(2)]

    cut = SIZES[0]
    pts_y = lax.ppermute(points, "leaf", beside)
    w_y = [lax.ppermute(chunk, "leaf", beside) for chunk in (weights[:cut], weights[cut:])]
    sent = leaf_call(xs, near_count, near_src, points, weights, interp)
    got = [
        lax.ppermute(sent[n], "help", help_pairs(xs, -dx, dc))
        for n, (dx, dc) in enumerate(order)
        if n
    ]
    pts_z = lax.ppermute(pts_y, "leaf", across)
    pts_z, w_y[0] = together(pts_z, w_y[0])
    w_z = [lax.ppermute(w_y[0], "leaf", across)]
    msgs = [sent[0]] + [got[order.index((-dx % xs, dc)) - 1] for dx, dc in order[1:]]
    payload, targets = skel_call(xs, skel_group, msgs)
    pieces = [payload]
    for mask in range(2, groups, 2):
        pieces.append(lax.ppermute(payload, "leaf", [(i, i ^ mask) for i in range(groups)]))

    payload, w_y[1] = together(payload, w_y[1])
    every, away, home = (0, 2 * helpers), (4, 2 * helpers), (0, 4)
    (own,) = near_call("near_own", msgs, targets, every, [("own", (points,), [weights])], R)
    w_z.append(lax.ppermute(w_y[1], "leaf", across))
    pair_src = ("pair", (pts_y,), w_y)
    (pair,) = near_call("near_pair", msgs, targets, away, [pair_src], R, after=[own])
    z_side = source_call(pts_z)
    sums, part = [], [pair]
    for c in range(2):
        if c == 1:
            pieces, part = together(pieces, part)
            alike = stack_call(pieces)
            side = lax.ppermute(alike, "leaf", beside)
            part = [alike]
        part = near_call(
            "near_next_away", msgs, targets, away, [("next", z_side, w_z[c : c + 1])],
            SIZES[c], c * SIZES[0], [own, pair], part[:1],
        )
        kept, given = part[::2], part[1::2]
        sums.append((kept, [from_help(value, 0, 1) for value in given]))
    parts = []
    for c in range(2):
        kept, mates = sums[c]
        both = add_call(*zip(kept, mates))
        parts.append([to_help(value, dx + 1) for dx, value in enumerate(both)])
    sources = [pair_src, ("next", z_side, w_z)]
    home = near_call("near_home", msgs, targets, home, sources, R, 0, [own], both[:1])
    v_own = far_call(groups, far_nodes, skel_node, transfer, alike, side, home[:1])
    v_pair = stack_call([v_own, from_help(v_own, 0, 1)])
    values = [v_pair] + [from_help(v_pair, dx, 0) for dx in range(1, xs)]
    mate = [from_help(value, 0, 1) for value in home[2:]]
    mine = add_call(*[[home[c], *parts[c]] for c in range(2)])
    return final_call(xs, interp, mine, mate, values)


def solution(mesh):
    placed = (
        P(None, ("leaf", "help")),
        P(None, ("leaf", "help")),
        P(("leaf", "help"), None, None),
        P(),
        P("leaf", "help"),
        P(("leaf", "help"), None),
        P("leaf", None),
        P(),
        P(),
    )
    return jax.shard_map(
        shards, mesh=mesh, in_specs=placed, out_specs=P(None, ("leaf", "help")), check_vma=False
    )
```

```python
import math
from functools import partial

import jax
import jax.numpy as jnp
from jax import lax
from jax.experimental import pallas as pl
from jax.experimental.pallas import tpu as pltpu
from jax.sharding import PartitionSpec as P

F = 64
R = 256
LEAF = 512
SK = 256
FL = 4
EXTRA = 8
SIZES = (128, 128)

BF = jnp.bfloat16
F32 = jnp.float32
LOG2E = 1.0 / math.log(2.0)
SCALE = math.sqrt(0.5 * LOG2E)
BIAS = 0.0625 * F * LOG2E
VMEM_LIMIT = 24 * 1024 * 1024
VMEM_WHOLE = 64 * 1024 * 1024


def dot(a, b):
    return jnp.dot(a, b, preferred_element_type=F32)


def dot_t(a, b):
    return lax.dot_general(a, b, (((1,), (1,)), ((), ())), preferred_element_type=F32)


def halves(x):
    hi = x.astype(BF)
    lo = (x - hi.astype(F32)).astype(BF)
    return hi, lo


def dot3(a, b, mul=dot):
    a_hi, a_lo = halves(a)
    b_hi, b_lo = halves(b)
    return mul(a_hi, b_hi) + mul(a_lo, b_hi) + mul(a_hi, b_lo)


def target_side(x):
    hi, lo = halves(x)
    both = hi.astype(F32) + lo.astype(F32)
    off = BIAS - 0.5 * jnp.sum(both * both, axis=0, keepdims=True)
    return jnp.concatenate([hi, lo, hi, lo], axis=0), off


def source_side(x):
    xt = x.T
    hi, lo = halves(xt)
    both = hi.astype(F32) + lo.astype(F32)
    off = BIAS - 0.5 * jnp.sum(both * both, axis=1, keepdims=True)
    return jnp.concatenate([hi, hi, lo, lo], axis=1), off


def near_body(
    xs, sets, leaves_at, rows, row, nacc, nout, *refs
):
    nset = len(sets)
    start, stop = leaves_at
    msgs, (t_ref, tb_ref), refs = refs[: 2 * xs], refs[2 * xs : 2 * xs + 2], refs[2 * xs + 2 :]
    if nacc:
        s_scr, sb_scr, w_scr, o_scr, k_scr, times_scr, list_ref, times_ref, sems = refs[-9:]
        outs = refs[-9 - nout : -9]
    else:
        o_scr, s_scr, sb_scr, w_scr, k_scr, times_scr, list_ref, times_ref, sems = refs[-9:]
    copies = [
        pltpu.make_async_copy(msgs[b].at[F : F + EXTRA, :128], times_ref.at[b], sems.at[b])
        for b in range(start // 2, stop // 2)
    ]
    for copy in copies:
        copy.start()
    at = 0
    for k, (_, ready, chunks) in enumerate(sets):
        heads = refs[at : at + 1 + ready]
        parts = refs[at + 1 + ready : at + 1 + ready + chunks]
        at += 1 + ready + chunks
        for leaf in range(2):
            cols = slice(leaf * LEAF, (leaf + 1) * LEAF)
            j = 2 * k + leaf
            if ready:
                s_scr[j] = heads[0][leaf]
                sb_scr[j] = heads[1][leaf]
            else:
                side, off = source_side(heads[0][:F, cols] * SCALE)
                s_scr[j] = side
                sb_scr[j] = jnp.broadcast_to(off, (LEAF, 128))
            top = 0
            for part in parts:
                hi, lo = halves(part[:, cols])
                w_scr[j, top : top + part.shape[0], :] = hi
                w_scr[j, rows + top : rows + top + part.shape[0], :] = lo
                top += part.shape[0]
    for t in range(start, stop):
        if nacc:
            o_scr[t - start] = sum(
                ref[t - (4 * xs - ref.shape[0]), row : row + rows, :] for ref in refs[at : at + nacc]
            )
        else:
            o_scr[t - start] = jnp.zeros((rows, LEAF), F32)

    x, core, group = place()
    leaves = 4 * xs
    odd = group % 2
    column = []
    for kind, _, _ in sets:
        relative = {"own": 1, "pair": 2 - 2 * odd, "next": 2 * odd}[kind]
        column.append(relative * leaves + 2 * (2 * x + core))

    for copy in copies:
        copy.wait()
    count = jnp.int32(0)
    list_ref[0] = 0
    for t in range(start, stop):
        for j in range(2 * nset):
            times = times_ref[t // 2, t % 2, column[j // 2] + j % 2]

            @pl.when(times > 0)
            def _(count=count, t=t, j=j, times=times):
                list_ref[count] = t * 8 + j
                times_scr[count] = times

            count = count + (times > 0).astype(jnp.int32)

    def block(index, slot):
        code = list_ref[jnp.minimum(index, jnp.maximum(count - 1, 0))]
        t, j = code // 8, code % 8
        side = t_ref[t]
        off = tb_ref[t][:1, :]
        for half in range(2):
            part = slice(half * 256, (half + 1) * 256)
            cross = dot(s_scr[j, part, :], side)
            src_off = sb_scr[j, part, :]
            src_off = jnp.concatenate([src_off] * (LEAF // 128), axis=1)
            k_hi, k_lo = halves(jnp.exp2(cross + src_off + off))
            k_scr[slot, part, :] = k_hi
            k_scr[slot, LEAF + half * 256 : LEAF + (half + 1) * 256, :] = k_lo

    def apply(index, slot):
        code = list_ref[index]
        t, j = code // 8 - start, code % 8
        factor = times_scr[index]
        for half in range(2):
            cols = slice(half * 256, (half + 1) * 256)
            both = dot(w_scr[j], k_scr[slot, :LEAF, cols])
            low = dot(w_scr[j, :rows, :], k_scr[slot, LEAF:, cols])
            o_scr[t, :, cols] = o_scr[t, :, cols] + factor * (both[:rows] + both[rows:] + low)

    @pl.when(count > 0)
    def _():
        block(0, 0)

    def pair(index, carry):
        block(2 * index + 1, 1)
        apply(2 * index, 0)

        @pl.when(2 * index + 1 < count)
        def _():
            block(2 * index + 2, 0)
            apply(2 * index + 1, 1)

        return carry

    lax.fori_loop(0, (count + 1) // 2, pair, jnp.int32(0))
    if nacc:
        t, top = 0, 0
        for ref in outs:
            tall = ref.shape[0]
            for leaf in range(2):
                cols = slice(leaf * LEAF, (leaf + 1) * LEAF)
                ref[:, cols] = o_scr[t + leaf, top : top + tall, :]
            t, top = (t, top + tall) if top + tall < rows else (t + 2, 0)


def near_call(name, msgs, targets, leaves_at, sources, rows, row=0, acc=(), after=()):
    nset = len(sources)
    start, stop = leaves_at
    vmem = pl.BlockSpec(memory_space=pltpu.VMEM)
    operands = [a for _, heads, chunks in sources for a in (*heads, *chunks)]
    scratch = [
        pltpu.VMEM((2 * nset, LEAF, 4 * F), BF),
        pltpu.VMEM((2 * nset, LEAF, 128), F32),
        pltpu.VMEM((2 * nset, 2 * rows, LEAF), BF),
        pltpu.VMEM((stop - start, rows, LEAF), F32),
        pltpu.VMEM((2, 2 * LEAF, LEAF), BF),
        pltpu.SMEM((2 * nset * (stop - start),), F32),
        pltpu.SMEM((2 * nset * (stop - start),), jnp.int32),
        pltpu.SMEM((len(msgs), EXTRA, 128), F32),
        pltpu.SemaphoreType.DMA((len(msgs),)),
    ]
    if not acc:
        out = [jax.ShapeDtypeStruct((stop - start, rows, LEAF), F32)]
        scratch.pop(3)
    else:
        operands += list(acc)
        talls = SIZES if rows == R else (rows,)
        out = [jax.ShapeDtypeStruct((tall, 2 * LEAF), F32) for tall in talls] * ((stop - start) // 2)
    sets = tuple((kind, len(heads) - 1, len(chunks)) for kind, heads, chunks in sources)
    return pl.pallas_call(
        partial(
            near_body, len(msgs) // 2, sets, leaves_at, rows, row, len(acc), len(out)
        ),
        name=name,
        out_shape=out,
        in_specs=[pl.BlockSpec(memory_space=pl.ANY)] * len(msgs)
        + [vmem] * (2 + len(operands))
        + [pl.BlockSpec(memory_space=pl.ANY)] * len(after),
        out_specs=[vmem] * len(out),
        scratch_shapes=scratch,
        compiler_params=pltpu.CompilerParams(vmem_limit_bytes=VMEM_LIMIT),
    )(*msgs, *targets, *operands, *after)


def source_body(pts_ref, side_ref, off_ref):
    for leaf in range(2):
        cols = slice(leaf * LEAF, (leaf + 1) * LEAF)
        side, off = source_side(pts_ref[:F, cols] * SCALE)
        side_ref[leaf] = side
        off_ref[leaf] = jnp.broadcast_to(off, (LEAF, 128))


def source_call(pts):
    vmem = pl.BlockSpec(memory_space=pltpu.VMEM)
    return pl.pallas_call(
        source_body,
        name="source_side",
        out_shape=[
            jax.ShapeDtypeStruct((2, LEAF, 4 * F), BF),
            jax.ShapeDtypeStruct((2, LEAF, 128), F32),
        ],
        in_specs=[vmem],
        out_specs=[vmem, vmem],
        compiler_params=pltpu.CompilerParams(vmem_limit_bytes=VMEM_LIMIT),
    )(pts)


def place():
    helper = lax.axis_index("help")
    return helper // 2, helper % 2, lax.axis_index("leaf")


def share_rows(xs):
    return R // (2 * xs) * SK // (2 * LEAF)


def leaf_body(xs, count_ref, src_ref, pts_in, w_in, interp_in, *refs):
    msgs = refs[: 2 * xs]
    pts_ref, w_ref, interp_ref, scr, sems = refs[2 * xs :]
    copies = [
        pltpu.make_async_copy(pts_in, pts_ref, sems.at[0]),
        pltpu.make_async_copy(w_in, w_ref, sems.at[1]),
        pltpu.make_async_copy(interp_in, interp_ref, sems.at[2]),
    ]
    for copy in copies:
        copy.start()
    x, core, group = place()
    leaves = 4 * xs
    lane = lax.broadcasted_iota(jnp.int32, (1, 128), 1) + (group - 1) * leaves
    times = []
    for leaf in range(2):
        row = jnp.zeros((1, 128), F32)
        for slot in range(src_ref.shape[1]):
            name = jnp.where(slot < count_ref[0, leaf], src_ref[leaf, slot], -1 - 128 * leaves)
            row = row + (lane == name).astype(F32)
        times.append(row)
    times = jnp.concatenate(times + [jnp.zeros((EXTRA - 2, 128), F32)], axis=0)
    for copy in copies:
        copy.wait()
    total = jnp.zeros((R, SK), F32)
    for leaf in range(2):
        total = total + dot3(w_ref[:, leaf * LEAF : (leaf + 1) * LEAF], interp_ref[leaf])
    scr[...] = total
    rows = R // (2 * xs)
    tall = share_rows(xs)
    for n, msg in enumerate(msgs):
        helper = 2 * lax.rem(x + n // 2, xs) + (core if n % 2 == 0 else 1 - core)
        msg[:F, :] = pts_ref[...]
        msg[F : F + EXTRA, :] = jnp.zeros((EXTRA, 2 * LEAF), F32)
        msg[F : F + EXTRA, :128] = times
        for i in range(rows // tall):
            at = pl.multiple_of(helper * rows + i * tall, tall)
            msg[F + EXTRA :, i * SK : (i + 1) * SK] = scr[pl.ds(at, tall), :]


def leaf_call(xs, near_count, near_src, points, weights, interp):
    vmem = pl.BlockSpec(memory_space=pltpu.VMEM)
    smem = pl.BlockSpec(memory_space=pltpu.SMEM)
    anywhere = pl.BlockSpec(memory_space=pl.ANY)
    height = F + EXTRA + share_rows(xs)
    return pl.pallas_call(
        partial(leaf_body, xs),
        name="leaf_up",
        out_shape=[jax.ShapeDtypeStruct((height, 2 * LEAF), F32)] * (2 * xs),
        in_specs=[smem, smem, anywhere, anywhere, anywhere],
        out_specs=[vmem] * (2 * xs),
        scratch_shapes=[
            pltpu.VMEM(points.shape, F32),
            pltpu.VMEM(weights.shape, F32),
            pltpu.VMEM(interp.shape, F32),
            pltpu.VMEM((R, SK), F32),
            pltpu.SemaphoreType.DMA((3,)),
        ],
        compiler_params=pltpu.CompilerParams(vmem_limit_bytes=VMEM_WHOLE),
    )(near_count, near_src, points, weights, interp)


def skel_body(xs, index_ref, *refs):
    msgs, (out_ref, side_ref, off_ref) = refs[:-3], refs[-3:]
    rows = R // (2 * xs)
    tall = share_rows(xs)
    total = jnp.zeros((2 * F, SK), F32)
    value = jnp.zeros((tall, 2 * LEAF), F32)
    spot = lax.broadcasted_iota(jnp.int32, (2 * LEAF, SK), 0)
    x, core, _ = place()
    for b, msg in enumerate(msgs):
        helper = 2 * lax.rem(x + b // 2, xs) + (core if b % 2 == 0 else 1 - core)
        side, off = target_side(msg[:F, :] * SCALE)
        for leaf in range(2):
            part = slice(leaf * LEAF, (leaf + 1) * LEAF)
            side_ref[2 * b + leaf] = side[:, part]
            off_ref[2 * b + leaf] = jnp.broadcast_to(off[:, part], (8, LEAF))
        hot = spot + helper * (2 * LEAF) == index_ref[...]
        total = total + dot(side[: 2 * F], hot.astype(F32).astype(BF))
        value = value + msg[F + EXTRA :, :]
    out_ref[:F, :] = total[:F] + total[F:]
    for i in range(rows // tall):
        out_ref[F + i * tall : F + (i + 1) * tall, :] = value[:, i * SK : (i + 1) * SK]


def skel_call(xs, index, msgs):
    rows = R // (2 * xs)
    leaves = 2 * len(msgs)
    vmem = pl.BlockSpec(memory_space=pltpu.VMEM)
    payload, *targets = pl.pallas_call(
        partial(skel_body, xs),
        name="skeleton",
        out_shape=[
            jax.ShapeDtypeStruct((F + rows, SK), F32),
            jax.ShapeDtypeStruct((leaves, 4 * F, LEAF), BF),
            jax.ShapeDtypeStruct((leaves, 8, LEAF), F32),
        ],
        in_specs=[vmem] * (1 + len(msgs)),
        out_specs=[vmem] * 3,
        compiler_params=pltpu.CompilerParams(vmem_limit_bytes=VMEM_LIMIT),
        cost_estimate=pl.CostEstimate(
            flops=5_000_000_000, bytes_accessed=8_000_000, transcendentals=0
        ),
    )(index, *msgs)
    return payload, targets


def stack_body(*refs):
    for n, ref in enumerate(refs[:-1]):
        refs[-1][n] = ref[...]


def stack_call(pieces):
    vmem = pl.BlockSpec(memory_space=pltpu.VMEM)
    return pl.pallas_call(
        stack_body,
        name="stack",
        out_shape=jax.ShapeDtypeStruct((len(pieces), *pieces[0].shape), F32),
        in_specs=[vmem] * len(pieces),
        out_specs=vmem,
        compiler_params=pltpu.CompilerParams(vmem_limit_bytes=VMEM_LIMIT),
    )(*pieces)


def upper_start(level, groups):
    return sum((groups >> step for step in range(1, level)))


def list_start(level, groups):
    return sum((groups >> step for step in range(level)))


def far_body(groups, rows, far_ref, node_ref, transfer_ref, alike_ref, beside_ref, *refs):
    out_ref, p_scr, u_scr, f_scr = refs[-4:]
    levels = groups.bit_length() - 1
    group = place()[2]
    start = [list_start(level, groups) for level in range(levels)]
    for n in range(groups // 2):
        same, other = group ^ (2 * n), group ^ (2 * n + 1)
        p_scr[same] = alike_ref[n, :F, :]
        u_scr[same] = alike_ref[n, F:, :]
        p_scr[other] = beside_ref[n, :F, :]
        u_scr[other] = beside_ref[n, F:, :]
    spot = lax.broadcasted_iota(jnp.int32, (2 * SK, SK), 0)
    for level in range(1, levels):
        for n in range(groups >> level):
            row = upper_start(level, groups) + n
            left = start[level - 1] + 2 * n
            hot = (spot == node_ref[row : row + 1, :]).astype(F32).astype(BF)
            hi, lo = halves(jnp.concatenate([p_scr[left], p_scr[left + 1]], axis=1))
            both = dot(jnp.concatenate([hi, lo], axis=0), hot)
            p_scr[start[level] + n] = both[:F] + both[F:]
            vals = jnp.concatenate([u_scr[left], u_scr[left + 1]], axis=1)
            u_scr[start[level] + n] = dot3(vals, transfer_ref[row])
    for level in range(levels):
        node = group >> level
        side, off = target_side(p_scr[start[level] + node])
        f_scr[level] = jnp.zeros((rows, SK), F32)

        def one(n, carry, level=level, node=node, side=side, off=off):
            hits = jnp.int32(0)
            for slot in range(FL):
                hits = hits + (far_ref[slot, start[level] + node] == n).astype(jnp.int32)

            @pl.when(hits > 0)
            def _():
                src, src_off = source_side(p_scr[start[level] + n])
                block = jnp.exp2(dot(src, side) + src_off + off)
                term = dot3(u_scr[start[level] + n], block)
                f_scr[level] = f_scr[level] + hits.astype(F32) * term

            return carry

        lax.fori_loop(0, groups >> level, one, jnp.int32(0))
    local = f_scr[levels - 1]
    for level in range(levels - 1, 0, -1):
        row = upper_start(level, groups) + (group >> level)
        bit = (group >> (level - 1)) & 1
        matrix = transfer_ref[row, pl.ds(pl.multiple_of(bit * SK, SK), SK), :]
        local = f_scr[level - 1] + dot3(local, matrix, dot_t)
    out_ref[...] = local


def far_call(groups, far_nodes, skel_node, transfer, alike, beside, after):
    rows = alike.shape[1] - F
    vmem = pl.BlockSpec(memory_space=pltpu.VMEM)
    smem = pl.BlockSpec(memory_space=pltpu.SMEM)
    nodes = 2 * groups
    return pl.pallas_call(
        partial(far_body, groups, rows),
        name="far",
        out_shape=jax.ShapeDtypeStruct((rows, SK), F32),
        in_specs=[smem, vmem, vmem, vmem, vmem]
        + [pl.BlockSpec(memory_space=pl.ANY)] * len(after),
        out_specs=vmem,
        scratch_shapes=[
            pltpu.VMEM((nodes, F, SK), F32),
            pltpu.VMEM((nodes, rows, SK), F32),
            pltpu.VMEM((groups.bit_length(), rows, SK), F32),
        ],
        compiler_params=pltpu.CompilerParams(vmem_limit_bytes=VMEM_LIMIT),
    )(far_nodes.T, skel_node, transfer, alike, beside, *after)


def final_body(xs, interp_ref, *refs):
    values, sums = refs[:xs], refs[xs:-2]
    out_ref, v_scr = refs[-2:]
    rows = R // (2 * xs)
    x, core, _ = place()
    for dx, ref in enumerate(values):
        for dc in range(2):
            helper = 2 * lax.rem(x + dx, xs) + (core if dc == 0 else 1 - core)
            v_scr[pl.ds(pl.multiple_of(helper * rows, rows), rows), :] = ref[dc]
    value = v_scr[...]
    for leaf in range(2):
        cols = slice(leaf * LEAF, (leaf + 1) * LEAF)
        total = dot3(value, interp_ref[leaf], dot_t)
        for c in range(2):
            part = slice(c * SIZES[0], SIZES[0] + c * SIZES[1])
            out_ref[part, cols] = total[part] + sums[c][:, cols] + sums[2 + c][:, cols]


def add_body(count, *refs):
    for n, out_ref in enumerate(refs[-(len(refs) // (count + 1)) :]):
        total = refs[n * count][...]
        for ref in refs[n * count + 1 : (n + 1) * count]:
            total = total + ref[...]
        out_ref[...] = total


def add_call(*sums):
    vmem = pl.BlockSpec(memory_space=pltpu.VMEM)
    operands = [value for terms in sums for value in terms]
    return pl.pallas_call(
        partial(add_body, len(sums[0])),
        name="add_parts",
        out_shape=[jax.ShapeDtypeStruct(terms[0].shape, F32) for terms in sums],
        in_specs=[vmem] * len(operands),
        out_specs=[vmem] * len(sums),
        compiler_params=pltpu.CompilerParams(vmem_limit_bytes=VMEM_LIMIT),
    )(*operands)


def final_call(xs, interp, home, mate, values):
    vmem = pl.BlockSpec(memory_space=pltpu.VMEM)
    return pl.pallas_call(
        partial(final_body, xs),
        name="join",
        out_shape=jax.ShapeDtypeStruct((R, 2 * LEAF), F32),
        in_specs=[vmem] * (1 + xs + 4),
        out_specs=vmem,
        scratch_shapes=[pltpu.VMEM((R, SK), F32)],
        compiler_params=pltpu.CompilerParams(vmem_limit_bytes=VMEM_LIMIT),
    )(interp, *values, *home, *mate)


def help_pairs(xs, dx, dc):
    return [
        (2 * ((x + dx) % xs) + (core ^ dc), 2 * x + core) for x in range(xs) for core in range(2)
    ]


def shards(
    points, weights, interp, transfer, near_count, near_src, skel_group, skel_node, far_nodes
):
    helpers = lax.axis_size("help")
    groups = lax.axis_size("leaf")
    xs = helpers // 2
    def from_help(value, dx, dc):
        return lax.ppermute(value, "help", help_pairs(xs, dx, dc))

    def to_help(value, dx):
        return lax.ppermute(value, "help", help_pairs(xs, -dx, 0))

    def together(*values):
        return lax.optimization_barrier(values)

    beside = [(i, i ^ 1) for i in range(groups)]
    across = [(i, i + 2) for i in range(0, groups - 2, 2)]
    across += [(i, i - 2) for i in range(3, groups, 2)]
    order = [(dx, dc) for dx in range(xs) for dc in range(2)]

    cut = SIZES[0]
    pts_y = lax.ppermute(points, "leaf", beside)
    w_y = [lax.ppermute(chunk, "leaf", beside) for chunk in (weights[:cut], weights[cut:])]
    sent = leaf_call(xs, near_count, near_src, points, weights, interp)
    got = [
        lax.ppermute(sent[n], "help", help_pairs(xs, -dx, dc))
        for n, (dx, dc) in enumerate(order)
        if n
    ]
    pts_z = lax.ppermute(pts_y, "leaf", across)
    pts_z, w_y[0], got[0] = together(pts_z, w_y[0], got[0])
    w_z = [lax.ppermute(w_y[0], "leaf", across)]
    msgs = [sent[0]] + [got[order.index((-dx % xs, dc)) - 1] for dx, dc in order[1:]]
    payload, targets = skel_call(xs, skel_group, msgs)
    pieces = [payload]
    for mask in range(2, groups, 2):
        pieces.append(lax.ppermute(payload, "leaf", [(i, i ^ mask) for i in range(groups)]))

    payload, w_y[1] = together(payload, w_y[1])
    every, away, home = (0, 2 * helpers), (4, 2 * helpers), (0, 4)
    (own,) = near_call("near_own", msgs, targets, every, [("own", (points,), [weights])], R)
    w_z.append(lax.ppermute(w_y[1], "leaf", across))
    pair_src = ("pair", (pts_y,), w_y)
    (pair,) = near_call("near_pair", msgs, targets, away, [pair_src], R, after=[own])
    z_side = source_call(pts_z)
    sums, part = [], [pair]
    for c in range(2):
        if c == 1:
            pieces, part = together(pieces, part)
            alike = stack_call(pieces)
            side = lax.ppermute(alike, "leaf", beside)
            part = [alike]
        part = near_call(
            "near_next_away", msgs, targets, away, [("next", z_side, w_z[c : c + 1])],
            SIZES[c], c * SIZES[0], [own, pair], part[:1],
        )
        kept, given = part[::2], part[1::2]
        sums.append((kept, [from_help(value, 0, 1) for value in given]))
    parts = []
    for c in range(2):
        kept, mates = sums[c]
        both = add_call(*zip(kept, mates))
        parts.append([to_help(value, dx + 1) for dx, value in enumerate(both)])
    sources = [pair_src, ("next", z_side, w_z)]
    home = near_call("near_home", msgs, targets, home, sources, R, 0, [own], both[:1])
    v_own = far_call(groups, far_nodes, skel_node, transfer, alike, side, home[:1])
    v_pair = stack_call([v_own, from_help(v_own, 0, 1)])
    values = [v_pair] + [from_help(v_pair, dx, 0) for dx in range(1, xs)]
    mate = [from_help(value, 0, 1) for value in home[2:]]
    mine = add_call(*[[home[c], *parts[c]] for c in range(2)])
    return final_call(xs, interp, mine, mate, values)


def solution(mesh):
    placed = (
        P(None, ("leaf", "help")),
        P(None, ("leaf", "help")),
        P(("leaf", "help"), None, None),
        P(),
        P("leaf", "help"),
        P(("leaf", "help"), None),
        P("leaf", None),
        P(),
        P(),
    )
    return jax.shard_map(
        shards, mesh=mesh, in_specs=placed, out_specs=P(None, ("leaf", "help")), check_vma=False
    )
```

```python
import math
from functools import partial

import jax
import jax.numpy as jnp
from jax import lax
from jax.experimental import pallas as pl
from jax.experimental.pallas import tpu as pltpu
from jax.sharding import PartitionSpec as P

F = 64
R = 256
LEAF = 512
SK = 256
FL = 4
EXTRA = 8
HALF = F // 2
SIZES = (128, 128)

BF = jnp.bfloat16
F32 = jnp.float32
LOG2E = 1.0 / math.log(2.0)
SCALE = math.sqrt(0.5 * LOG2E)
BIAS = 0.0625 * F * LOG2E
VMEM_LIMIT = 24 * 1024 * 1024
VMEM_WHOLE = 64 * 1024 * 1024


def dot(a, b):
    return jnp.dot(a, b, preferred_element_type=F32)


def dot_t(a, b):
    return lax.dot_general(a, b, (((1,), (1,)), ((), ())), preferred_element_type=F32)


def halves(x):
    hi = x.astype(BF)
    lo = (x - hi.astype(F32)).astype(BF)
    return hi, lo


def dot3(a, b, mul=dot):
    a_hi, a_lo = halves(a)
    b_hi, b_lo = halves(b)
    return mul(a_hi, b_hi) + mul(a_lo, b_hi) + mul(a_hi, b_lo)


def target_side(x):
    hi, lo = halves(x)
    both = hi.astype(F32) + lo.astype(F32)
    off = BIAS - 0.5 * jnp.sum(both * both, axis=0, keepdims=True)
    return jnp.concatenate([hi, lo, hi, lo], axis=0), off


def source_side(x):
    xt = x.T
    hi, lo = halves(xt)
    both = hi.astype(F32) + lo.astype(F32)
    off = BIAS - 0.5 * jnp.sum(both * both, axis=1, keepdims=True)
    return jnp.concatenate([hi, hi, lo, lo], axis=1), off


def near_body(
    xs, sets, leaves_at, rows, row, nacc, nout, *refs
):
    nset = len(sets)
    start, stop = leaves_at
    msgs, (t_ref, tb_ref), refs = refs[: 2 * xs], refs[2 * xs : 2 * xs + 2], refs[2 * xs + 2 :]
    if nacc:
        s_scr, sb_scr, w_scr, o_scr, k_scr, times_scr, list_ref, times_ref, sems = refs[-9:]
        outs = refs[-9 - nout : -9]
    else:
        o_scr, s_scr, sb_scr, w_scr, k_scr, times_scr, list_ref, times_ref, sems = refs[-9:]
    copies = [
        pltpu.make_async_copy(msgs[b].at[F : F + EXTRA, :128], times_ref.at[b], sems.at[b])
        for b in range(start // 2, stop // 2)
    ]
    for copy in copies:
        copy.start()
    at = 0
    for k, (_, ready, chunks) in enumerate(sets):
        heads = refs[at : at + 1 + ready]
        parts = refs[at + 1 + ready : at + 1 + ready + chunks]
        at += 1 + ready + chunks
        for leaf in range(2):
            cols = slice(leaf * LEAF, (leaf + 1) * LEAF)
            j = 2 * k + leaf
            if ready:
                s_scr[j] = heads[0][leaf]
                sb_scr[j] = heads[1][leaf]
            else:
                side, off = source_side(heads[0][:F, cols] * SCALE)
                s_scr[j] = side
                sb_scr[j] = jnp.broadcast_to(off, (LEAF, 128))
            top = 0
            for part in parts:
                hi, lo = halves(part[:, cols])
                w_scr[j, top : top + part.shape[0], :] = hi
                w_scr[j, rows + top : rows + top + part.shape[0], :] = lo
                top += part.shape[0]
    for t in range(start, stop):
        if nacc:
            o_scr[t - start] = sum(
                ref[t - (4 * xs - ref.shape[0]), row : row + rows, :] for ref in refs[at : at + nacc]
            )
        else:
            o_scr[t - start] = jnp.zeros((rows, LEAF), F32)

    x, core, group = place()
    leaves = 4 * xs
    odd = group % 2
    column = []
    for kind, _, _ in sets:
        relative = {"own": 1, "pair": 2 - 2 * odd, "next": 2 * odd}[kind]
        column.append(relative * leaves + 2 * (2 * x + core))

    for copy in copies:
        copy.wait()
    count = jnp.int32(0)
    list_ref[0] = 0
    for t in range(start, stop):
        for j in range(2 * nset):
            times = times_ref[t // 2, t % 2, column[j // 2] + j % 2]

            @pl.when(times > 0)
            def _(count=count, t=t, j=j, times=times):
                list_ref[count] = t * 8 + j
                times_scr[count] = times

            count = count + (times > 0).astype(jnp.int32)

    def block(index, slot):
        code = list_ref[jnp.minimum(index, jnp.maximum(count - 1, 0))]
        t, j = code // 8, code % 8
        side = t_ref[t]
        off = tb_ref[t][:1, :]
        for half in range(2):
            part = slice(half * 256, (half + 1) * 256)
            cross = dot(s_scr[j, part, :], side)
            src_off = sb_scr[j, part, :]
            src_off = jnp.concatenate([src_off] * (LEAF // 128), axis=1)
            k_hi, k_lo = halves(jnp.exp2(cross + src_off + off))
            k_scr[slot, part, :] = k_hi
            k_scr[slot, LEAF + half * 256 : LEAF + (half + 1) * 256, :] = k_lo

    def apply(index, slot):
        code = list_ref[index]
        t, j = code // 8 - start, code % 8
        factor = times_scr[index]
        for half in range(2):
            cols = slice(half * 256, (half + 1) * 256)
            both = dot(w_scr[j], k_scr[slot, :LEAF, cols])
            low = dot(w_scr[j, :rows, :], k_scr[slot, LEAF:, cols])
            o_scr[t, :, cols] = o_scr[t, :, cols] + factor * (both[:rows] + both[rows:] + low)

    @pl.when(count > 0)
    def _():
        block(0, 0)

    def pair(index, carry):
        block(2 * index + 1, 1)
        apply(2 * index, 0)

        @pl.when(2 * index + 1 < count)
        def _():
            block(2 * index + 2, 0)
            apply(2 * index + 1, 1)

        return carry

    lax.fori_loop(0, (count + 1) // 2, pair, jnp.int32(0))
    if nacc:
        t, top = 0, 0
        for ref in outs:
            tall = ref.shape[0]
            for leaf in range(2):
                cols = slice(leaf * LEAF, (leaf + 1) * LEAF)
                ref[:, cols] = o_scr[t + leaf, top : top + tall, :]
            t, top = (t, top + tall) if top + tall < rows else (t + 2, 0)


def near_call(name, msgs, targets, leaves_at, sources, rows, row=0, acc=(), after=()):
    nset = len(sources)
    start, stop = leaves_at
    vmem = pl.BlockSpec(memory_space=pltpu.VMEM)
    operands = [a for _, heads, chunks in sources for a in (*heads, *chunks)]
    scratch = [
        pltpu.VMEM((2 * nset, LEAF, 4 * F), BF),
        pltpu.VMEM((2 * nset, LEAF, 128), F32),
        pltpu.VMEM((2 * nset, 2 * rows, LEAF), BF),
        pltpu.VMEM((stop - start, rows, LEAF), F32),
        pltpu.VMEM((2, 2 * LEAF, LEAF), BF),
        pltpu.SMEM((2 * nset * (stop - start),), F32),
        pltpu.SMEM((2 * nset * (stop - start),), jnp.int32),
        pltpu.SMEM((len(msgs), EXTRA, 128), F32),
        pltpu.SemaphoreType.DMA((len(msgs),)),
    ]
    if not acc:
        out = [jax.ShapeDtypeStruct((stop - start, rows, LEAF), F32)]
        scratch.pop(3)
    else:
        operands += list(acc)
        talls = SIZES if rows == R else (rows,)
        out = [jax.ShapeDtypeStruct((tall, 2 * LEAF), F32) for tall in talls] * ((stop - start) // 2)
    sets = tuple((kind, len(heads) - 1, len(chunks)) for kind, heads, chunks in sources)
    return pl.pallas_call(
        partial(
            near_body, len(msgs) // 2, sets, leaves_at, rows, row, len(acc), len(out)
        ),
        name=name,
        out_shape=out,
        in_specs=[pl.BlockSpec(memory_space=pl.ANY)] * len(msgs)
        + [vmem] * (2 + len(operands))
        + [pl.BlockSpec(memory_space=pl.ANY)] * len(after),
        out_specs=[vmem] * len(out),
        scratch_shapes=scratch,
        compiler_params=pltpu.CompilerParams(vmem_limit_bytes=VMEM_LIMIT),
    )(*msgs, *targets, *operands, *after)


def source_body(pts_ref, side_ref, off_ref):
    for leaf in range(2):
        cols = slice(leaf * LEAF, (leaf + 1) * LEAF)
        side, off = source_side(pts_ref[:F, cols] * SCALE)
        side_ref[leaf] = side
        off_ref[leaf] = jnp.broadcast_to(off, (LEAF, 128))


def source_call(pts):
    vmem = pl.BlockSpec(memory_space=pltpu.VMEM)
    return pl.pallas_call(
        source_body,
        name="source_side",
        out_shape=[
            jax.ShapeDtypeStruct((2, LEAF, 4 * F), BF),
            jax.ShapeDtypeStruct((2, LEAF, 128), F32),
        ],
        in_specs=[vmem],
        out_specs=[vmem, vmem],
        compiler_params=pltpu.CompilerParams(vmem_limit_bytes=VMEM_LIMIT),
    )(pts)


def place():
    helper = lax.axis_index("help")
    return helper // 2, helper % 2, lax.axis_index("leaf")


def share_rows(xs):
    return R // (2 * xs) * SK // (2 * LEAF)


def leaf_body(xs, count_ref, src_ref, pts_in, w_in, interp_in, *refs):
    msgs = refs[: 2 * xs]
    pts_ref, w_ref, interp_ref, scr, sems = refs[2 * xs :]
    copies = [
        pltpu.make_async_copy(pts_in, pts_ref, sems.at[0]),
        pltpu.make_async_copy(w_in, w_ref, sems.at[1]),
        pltpu.make_async_copy(interp_in, interp_ref, sems.at[2]),
    ]
    for copy in copies:
        copy.start()
    x, core, group = place()
    leaves = 4 * xs
    lane = lax.broadcasted_iota(jnp.int32, (1, 128), 1) + (group - 1) * leaves
    times = []
    for leaf in range(2):
        row = jnp.zeros((1, 128), F32)
        for slot in range(src_ref.shape[1]):
            name = jnp.where(slot < count_ref[0, leaf], src_ref[leaf, slot], -1 - 128 * leaves)
            row = row + (lane == name).astype(F32)
        times.append(row)
    times = jnp.concatenate(times + [jnp.zeros((EXTRA - 2, 128), F32)], axis=0)
    for copy in copies:
        copy.wait()
    total = jnp.zeros((R, SK), F32)
    for leaf in range(2):
        total = total + dot3(w_ref[:, leaf * LEAF : (leaf + 1) * LEAF], interp_ref[leaf])
    scr[...] = total
    rows = R // (2 * xs)
    tall = share_rows(xs)
    for n, msg in enumerate(msgs):
        helper = 2 * lax.rem(x + n // 2, xs) + (core if n % 2 == 0 else 1 - core)
        msg[:F, :] = pts_ref[...]
        msg[F : F + EXTRA, :] = jnp.zeros((EXTRA, 2 * LEAF), F32)
        msg[F : F + EXTRA, :128] = times
        for i in range(rows // tall):
            at = pl.multiple_of(helper * rows + i * tall, tall)
            msg[F + EXTRA :, i * SK : (i + 1) * SK] = scr[pl.ds(at, tall), :]


def leaf_call(xs, near_count, near_src, points, weights, interp):
    vmem = pl.BlockSpec(memory_space=pltpu.VMEM)
    smem = pl.BlockSpec(memory_space=pltpu.SMEM)
    anywhere = pl.BlockSpec(memory_space=pl.ANY)
    height = F + EXTRA + share_rows(xs)
    return pl.pallas_call(
        partial(leaf_body, xs),
        name="leaf_up",
        out_shape=[jax.ShapeDtypeStruct((height, 2 * LEAF), F32)] * (2 * xs),
        in_specs=[smem, smem, anywhere, anywhere, anywhere],
        out_specs=[vmem] * (2 * xs),
        scratch_shapes=[
            pltpu.VMEM(points.shape, F32),
            pltpu.VMEM(weights.shape, F32),
            pltpu.VMEM(interp.shape, F32),
            pltpu.VMEM((R, SK), F32),
            pltpu.SemaphoreType.DMA((3,)),
        ],
        compiler_params=pltpu.CompilerParams(vmem_limit_bytes=VMEM_WHOLE),
    )(near_count, near_src, points, weights, interp)


def skel_body(xs, index_ref, *refs):
    msgs, (out_ref, side_ref, off_ref, scr) = refs[:-4], refs[-4:]
    rows = R // (2 * xs)
    tall = share_rows(xs)
    total = jnp.zeros((2 * F, SK), F32)
    value = jnp.zeros((tall, 2 * LEAF), F32)
    spot = lax.broadcasted_iota(jnp.int32, (2 * LEAF, SK), 0)
    x, core, _ = place()
    for b, msg in enumerate(msgs):
        helper = 2 * lax.rem(x + b // 2, xs) + (core if b % 2 == 0 else 1 - core)
        side, off = target_side(msg[:F, :] * SCALE)
        for leaf in range(2):
            part = slice(leaf * LEAF, (leaf + 1) * LEAF)
            side_ref[2 * b + leaf] = side[:, part]
            off_ref[2 * b + leaf] = jnp.broadcast_to(off[:, part], (8, LEAF))
        hot = spot + helper * (2 * LEAF) == index_ref[...]
        total = total + dot(side[: 2 * F], hot.astype(F32).astype(BF))
        value = value + msg[F + EXTRA :, :]
    scr[...] = total[:F] + total[F:]
    out_ref[:HALF, :] = scr[pl.ds(pl.multiple_of(core * HALF, HALF), HALF), :]
    for i in range(rows // tall):
        out_ref[HALF + i * tall : HALF + (i + 1) * tall, :] = value[:, i * SK : (i + 1) * SK]


def skel_call(xs, index, msgs):
    rows = R // (2 * xs)
    leaves = 2 * len(msgs)
    vmem = pl.BlockSpec(memory_space=pltpu.VMEM)
    payload, *targets = pl.pallas_call(
        partial(skel_body, xs),
        name="skeleton",
        out_shape=[
            jax.ShapeDtypeStruct((HALF + rows, SK), F32),
            jax.ShapeDtypeStruct((leaves, 4 * F, LEAF), BF),
            jax.ShapeDtypeStruct((leaves, 8, LEAF), F32),
        ],
        in_specs=[vmem] * (1 + len(msgs)),
        out_specs=[vmem] * 3,
        scratch_shapes=[pltpu.VMEM((F, SK), F32)],
        compiler_params=pltpu.CompilerParams(vmem_limit_bytes=VMEM_LIMIT),
        cost_estimate=pl.CostEstimate(
            flops=5_000_000_000, bytes_accessed=8_000_000, transcendentals=0
        ),
    )(index, *msgs)
    return payload, targets


def stack_body(*refs):
    for n, ref in enumerate(refs[:-1]):
        refs[-1][n] = ref[...]


def stack_call(pieces):
    vmem = pl.BlockSpec(memory_space=pltpu.VMEM)
    return pl.pallas_call(
        stack_body,
        name="stack",
        out_shape=jax.ShapeDtypeStruct((len(pieces), *pieces[0].shape), F32),
        in_specs=[vmem] * len(pieces),
        out_specs=vmem,
        compiler_params=pltpu.CompilerParams(vmem_limit_bytes=VMEM_LIMIT),
    )(*pieces)


def points_body(alike_ref, beside_ref, out_ref):
    count = alike_ref.shape[0]
    for n in range(count):
        out_ref[n] = alike_ref[n, :HALF, :]
        out_ref[count + n] = beside_ref[n, :HALF, :]


def points_call(alike, beside):
    vmem = pl.BlockSpec(memory_space=pltpu.VMEM)
    return pl.pallas_call(
        points_body,
        name="points_of",
        out_shape=jax.ShapeDtypeStruct((2 * alike.shape[0], HALF, SK), F32),
        in_specs=[vmem, vmem],
        out_specs=vmem,
        compiler_params=pltpu.CompilerParams(vmem_limit_bytes=VMEM_LIMIT),
    )(alike, beside)


def upper_start(level, groups):
    return sum((groups >> step for step in range(1, level)))


def list_start(level, groups):
    return sum((groups >> step for step in range(level)))


def far_body(groups, rows, far_ref, node_ref, transfer_ref, alike_ref, beside_ref, mate_ref, *refs):
    out_ref, p_scr, u_scr, f_scr = refs[-4:]
    levels = groups.bit_length() - 1
    group = place()[2]
    start = [list_start(level, groups) for level in range(levels)]
    core = place()[1]
    here = pl.ds(pl.multiple_of(core * HALF, HALF), HALF)
    there = pl.ds(pl.multiple_of((1 - core) * HALF, HALF), HALF)
    for n in range(groups):
        node = group ^ (2 * (n % (groups // 2)) + n // (groups // 2))
        part = (alike_ref, beside_ref)[n // (groups // 2)]
        p_scr[node, here, :] = part[n % (groups // 2), :HALF, :]
        p_scr[node, there, :] = mate_ref[n]
        u_scr[node] = part[n % (groups // 2), HALF:, :]
    spot = lax.broadcasted_iota(jnp.int32, (2 * SK, SK), 0)
    for level in range(1, levels):
        for n in range(groups >> level):
            row = upper_start(level, groups) + n
            left = start[level - 1] + 2 * n
            hot = (spot == node_ref[row : row + 1, :]).astype(F32).astype(BF)
            hi, lo = halves(jnp.concatenate([p_scr[left], p_scr[left + 1]], axis=1))
            both = dot(jnp.concatenate([hi, lo], axis=0), hot)
            p_scr[start[level] + n] = both[:F] + both[F:]
            vals = jnp.concatenate([u_scr[left], u_scr[left + 1]], axis=1)
            u_scr[start[level] + n] = dot3(vals, transfer_ref[row])
    for level in range(levels):
        node = group >> level
        side, off = target_side(p_scr[start[level] + node])
        f_scr[level] = jnp.zeros((rows, SK), F32)

        def one(n, carry, level=level, node=node, side=side, off=off):
            hits = jnp.int32(0)
            for slot in range(FL):
                hits = hits + (far_ref[slot, start[level] + node] == n).astype(jnp.int32)

            @pl.when(hits > 0)
            def _():
                src, src_off = source_side(p_scr[start[level] + n])
                block = jnp.exp2(dot(src, side) + src_off + off)
                term = dot3(u_scr[start[level] + n], block)
                f_scr[level] = f_scr[level] + hits.astype(F32) * term

            return carry

        lax.fori_loop(0, groups >> level, one, jnp.int32(0))
    local = f_scr[levels - 1]
    for level in range(levels - 1, 0, -1):
        row = upper_start(level, groups) + (group >> level)
        bit = (group >> (level - 1)) & 1
        matrix = transfer_ref[row, pl.ds(pl.multiple_of(bit * SK, SK), SK), :]
        local = f_scr[level - 1] + dot3(local, matrix, dot_t)
    out_ref[...] = local


def far_call(groups, far_nodes, skel_node, transfer, alike, beside, mate, after):
    rows = alike.shape[1] - HALF
    vmem = pl.BlockSpec(memory_space=pltpu.VMEM)
    smem = pl.BlockSpec(memory_space=pltpu.SMEM)
    nodes = 2 * groups
    return pl.pallas_call(
        partial(far_body, groups, rows),
        name="far",
        out_shape=jax.ShapeDtypeStruct((rows, SK), F32),
        in_specs=[smem, vmem, vmem, vmem, vmem, vmem]
        + [pl.BlockSpec(memory_space=pl.ANY)] * len(after),
        out_specs=vmem,
        scratch_shapes=[
            pltpu.VMEM((nodes, F, SK), F32),
            pltpu.VMEM((nodes, rows, SK), F32),
            pltpu.VMEM((groups.bit_length(), rows, SK), F32),
        ],
        compiler_params=pltpu.CompilerParams(vmem_limit_bytes=VMEM_LIMIT),
    )(far_nodes.T, skel_node, transfer, alike, beside, mate, *after)


def final_body(xs, interp_ref, *refs):
    values, sums = refs[:xs], refs[xs:-2]
    out_ref, v_scr = refs[-2:]
    rows = R // (2 * xs)
    x, core, _ = place()
    for dx, ref in enumerate(values):
        for dc in range(2):
            helper = 2 * lax.rem(x + dx, xs) + (core if dc == 0 else 1 - core)
            v_scr[pl.ds(pl.multiple_of(helper * rows, rows), rows), :] = ref[dc]
    value = v_scr[...]
    for leaf in range(2):
        cols = slice(leaf * LEAF, (leaf + 1) * LEAF)
        total = dot3(value, interp_ref[leaf], dot_t)
        for c in range(2):
            part = slice(c * SIZES[0], SIZES[0] + c * SIZES[1])
            out_ref[part, cols] = total[part] + sums[c][:, cols] + sums[2 + c][:, cols]


def add_body(count, *refs):
    for n, out_ref in enumerate(refs[-(len(refs) // (count + 1)) :]):
        total = refs[n * count][...]
        for ref in refs[n * count + 1 : (n + 1) * count]:
            total = total + ref[...]
        out_ref[...] = total


def add_call(*sums):
    vmem = pl.BlockSpec(memory_space=pltpu.VMEM)
    operands = [value for terms in sums for value in terms]
    return pl.pallas_call(
        partial(add_body, len(sums[0])),
        name="add_parts",
        out_shape=[jax.ShapeDtypeStruct(terms[0].shape, F32) for terms in sums],
        in_specs=[vmem] * len(operands),
        out_specs=[vmem] * len(sums),
        compiler_params=pltpu.CompilerParams(vmem_limit_bytes=VMEM_LIMIT),
    )(*operands)


def final_call(xs, interp, home, mate, values):
    vmem = pl.BlockSpec(memory_space=pltpu.VMEM)
    return pl.pallas_call(
        partial(final_body, xs),
        name="join",
        out_shape=jax.ShapeDtypeStruct((R, 2 * LEAF), F32),
        in_specs=[vmem] * (1 + xs + 4),
        out_specs=vmem,
        scratch_shapes=[pltpu.VMEM((R, SK), F32)],
        compiler_params=pltpu.CompilerParams(vmem_limit_bytes=VMEM_LIMIT),
    )(interp, *values, *home, *mate)


def help_pairs(xs, dx, dc):
    return [
        (2 * ((x + dx) % xs) + (core ^ dc), 2 * x + core) for x in range(xs) for core in range(2)
    ]


def shards(
    points, weights, interp, transfer, near_count, near_src, skel_group, skel_node, far_nodes
):
    helpers = lax.axis_size("help")
    groups = lax.axis_size("leaf")
    xs = helpers // 2
    def from_help(value, dx, dc):
        return lax.ppermute(value, "help", help_pairs(xs, dx, dc))

    def to_help(value, dx):
        return lax.ppermute(value, "help", help_pairs(xs, -dx, 0))

    def together(*values):
        return lax.optimization_barrier(values)

    beside = [(i, i ^ 1) for i in range(groups)]
    across = [(i, i + 2) for i in range(0, groups - 2, 2)]
    across += [(i, i - 2) for i in range(3, groups, 2)]
    order = [(dx, dc) for dx in range(xs) for dc in range(2)]

    cut = SIZES[0]
    pts_y = lax.ppermute(points, "leaf", beside)
    w_y = [lax.ppermute(chunk, "leaf", beside) for chunk in (weights[:cut], weights[cut:])]
    sent = leaf_call(xs, near_count, near_src, points, weights, interp)
    got = [
        lax.ppermute(sent[n], "help", help_pairs(xs, -dx, dc))
        for n, (dx, dc) in enumerate(order)
        if n
    ]
    pts_z = lax.ppermute(pts_y, "leaf", across)
    pts_z, w_y[0], got[0] = together(pts_z, w_y[0], got[0])
    w_z = [lax.ppermute(w_y[0], "leaf", across)]
    msgs = [sent[0]] + [got[order.index((-dx % xs, dc)) - 1] for dx, dc in order[1:]]
    payload, targets = skel_call(xs, skel_group, msgs)
    pieces = [payload]
    for mask in range(2, groups, 2):
        pieces.append(lax.ppermute(payload, "leaf", [(i, i ^ mask) for i in range(groups)]))

    payload, w_y[1] = together(payload, w_y[1])
    every, away, home = (0, 2 * helpers), (4, 2 * helpers), (0, 4)
    (own,) = near_call("near_own", msgs, targets, every, [("own", (points,), [weights])], R)
    w_z.append(lax.ppermute(w_y[1], "leaf", across))
    pair_src = ("pair", (pts_y,), w_y)
    (pair,) = near_call("near_pair", msgs, targets, away, [pair_src], R, after=[own])
    z_side = source_call(pts_z)
    sums, part = [], [pair]
    for c in range(2):
        if c == 1:
            pieces, part = together(pieces, part)
            alike = stack_call(pieces)
            side = lax.ppermute(alike, "leaf", beside)
            part = [alike]
        part = near_call(
            "near_next_away", msgs, targets, away, [("next", z_side, w_z[c : c + 1])],
            SIZES[c], c * SIZES[0], [own, pair], part[:1],
        )
        kept, given = part[::2], part[1::2]
        sums.append((kept, [from_help(value, 0, 1) for value in given]))
    parts = []
    for c in range(2):
        kept, mates = sums[c]
        both = add_call(*zip(kept, mates))
        parts.append([to_help(value, dx + 1) for dx, value in enumerate(both)])
    sources = [pair_src, ("next", z_side, w_z)]
    home = near_call("near_home", msgs, targets, home, sources, R, 0, [own], both[:1])
    swapped = from_help(points_call(alike, side), 0, 1)
    v_own = far_call(groups, far_nodes, skel_node, transfer, alike, side, swapped, home[:1])
    v_pair = stack_call([v_own, from_help(v_own, 0, 1)])
    values = [v_pair] + [from_help(v_pair, dx, 0) for dx in range(1, xs)]
    mate = [from_help(value, 0, 1) for value in home[2:]]
    mine = add_call(*[[home[c], *parts[c]] for c in range(2)])
    return final_call(xs, interp, mine, mate, values)


def solution(mesh):
    placed = (
        P(None, ("leaf", "help")),
        P(None, ("leaf", "help")),
        P(("leaf", "help"), None, None),
        P(),
        P("leaf", "help"),
        P(("leaf", "help"), None),
        P("leaf", None),
        P(),
        P(),
    )
    return jax.shard_map(
        shards, mesh=mesh, in_specs=placed, out_specs=P(None, ("leaf", "help")), check_vma=False
    )
```

```python
import math
from functools import partial

import jax
import jax.numpy as jnp
from jax import lax
from jax.experimental import pallas as pl
from jax.experimental.pallas import tpu as pltpu
from jax.sharding import PartitionSpec as P

F = 64
R = 256
LEAF = 512
SK = 256
FL = 4
EXTRA = 8
HALF = F // 2
SIZES = (128, 128)

BF = jnp.bfloat16
F32 = jnp.float32
LOG2E = 1.0 / math.log(2.0)
SCALE = math.sqrt(0.5 * LOG2E)
BIAS = 0.0625 * F * LOG2E
VMEM_LIMIT = 24 * 1024 * 1024
VMEM_WHOLE = 64 * 1024 * 1024


def dot(a, b):
    return jnp.dot(a, b, preferred_element_type=F32)


def dot_t(a, b):
    return lax.dot_general(a, b, (((1,), (1,)), ((), ())), preferred_element_type=F32)


def halves(x):
    hi = x.astype(BF)
    lo = (x - hi.astype(F32)).astype(BF)
    return hi, lo


def dot3(a, b, mul=dot):
    a_hi, a_lo = halves(a)
    b_hi, b_lo = halves(b)
    return mul(a_hi, b_hi) + mul(a_lo, b_hi) + mul(a_hi, b_lo)


def target_side(x):
    hi, lo = halves(x)
    both = hi.astype(F32) + lo.astype(F32)
    off = BIAS - 0.5 * jnp.sum(both * both, axis=0, keepdims=True)
    return jnp.concatenate([hi, lo, hi, lo], axis=0), off


def source_side(x):
    xt = x.T
    hi, lo = halves(xt)
    both = hi.astype(F32) + lo.astype(F32)
    off = BIAS - 0.5 * jnp.sum(both * both, axis=1, keepdims=True)
    return jnp.concatenate([hi, hi, lo, lo], axis=1), off


def near_body(
    xs, sets, leaves_at, rows, row, nacc, nout, apart, *refs
):
    nset = len(sets)
    start, stop = leaves_at
    msgs, (t_ref, tb_ref), refs = refs[: 2 * xs], refs[2 * xs : 2 * xs + 2], refs[2 * xs + 2 :]
    if apart:
        s_scr, sb_scr, w_scr, o_scr, k_scr, times_scr, list_ref, times_ref, sems = refs[-9:]
        outs = refs[-9 - nout : -9]
    else:
        o_scr, s_scr, sb_scr, w_scr, k_scr, times_scr, list_ref, times_ref, sems = refs[-9:]
    copies = [
        pltpu.make_async_copy(msgs[b].at[F : F + EXTRA, :128], times_ref.at[b], sems.at[b])
        for b in range(start // 2, stop // 2)
    ]
    for copy in copies:
        copy.start()
    at = 0
    for k, (_, ready, chunks) in enumerate(sets):
        heads = refs[at : at + 1 + ready]
        parts = refs[at + 1 + ready : at + 1 + ready + chunks]
        at += 1 + ready + chunks
        for leaf in range(2):
            cols = slice(leaf * LEAF, (leaf + 1) * LEAF)
            j = 2 * k + leaf
            if ready:
                s_scr[j] = heads[0][leaf]
                sb_scr[j] = heads[1][leaf]
            else:
                side, off = source_side(heads[0][:F, cols] * SCALE)
                s_scr[j] = side
                sb_scr[j] = jnp.broadcast_to(off, (LEAF, 128))
            top = 0
            for part in parts:
                hi, lo = halves(part[:, cols])
                w_scr[j, top : top + part.shape[0], :] = hi
                w_scr[j, rows + top : rows + top + part.shape[0], :] = lo
                top += part.shape[0]
    for t in range(start, stop):
        if nacc:
            o_scr[t - start] = sum(
                ref[t - (4 * xs - ref.shape[0]), row : row + rows, :] for ref in refs[at : at + nacc]
            )
        else:
            o_scr[t - start] = jnp.zeros((rows, LEAF), F32)

    x, core, group = place()
    leaves = 4 * xs
    odd = group % 2
    column = []
    for kind, _, _ in sets:
        relative = {"own": 1, "pair": 2 - 2 * odd, "next": 2 * odd}[kind]
        column.append(relative * leaves + 2 * (2 * x + core))

    for copy in copies:
        copy.wait()
    count = jnp.int32(0)
    list_ref[0] = 0
    for t in range(start, stop):
        for j in range(2 * nset):
            times = times_ref[t // 2, t % 2, column[j // 2] + j % 2]

            @pl.when(times > 0)
            def _(count=count, t=t, j=j, times=times):
                list_ref[count] = t * 8 + j
                times_scr[count] = times

            count = count + (times > 0).astype(jnp.int32)

    def block(index, slot):
        code = list_ref[jnp.minimum(index, jnp.maximum(count - 1, 0))]
        t, j = code // 8, code % 8
        side = t_ref[t]
        off = tb_ref[t][:1, :]
        for half in range(2):
            part = slice(half * 256, (half + 1) * 256)
            cross = dot(s_scr[j, part, :], side)
            src_off = sb_scr[j, part, :]
            src_off = jnp.concatenate([src_off] * (LEAF // 128), axis=1)
            k_hi, k_lo = halves(jnp.exp2(cross + src_off + off))
            k_scr[slot, part, :] = k_hi
            k_scr[slot, LEAF + half * 256 : LEAF + (half + 1) * 256, :] = k_lo

    def apply(index, slot):
        code = list_ref[index]
        t, j = code // 8 - start, code % 8
        factor = times_scr[index]
        for half in range(2):
            cols = slice(half * 256, (half + 1) * 256)
            both = dot(w_scr[j], k_scr[slot, :LEAF, cols])
            low = dot(w_scr[j, :rows, :], k_scr[slot, LEAF:, cols])
            o_scr[t, :, cols] = o_scr[t, :, cols] + factor * (both[:rows] + both[rows:] + low)

    @pl.when(count > 0)
    def _():
        block(0, 0)

    def pair(index, carry):
        block(2 * index + 1, 1)
        apply(2 * index, 0)

        @pl.when(2 * index + 1 < count)
        def _():
            block(2 * index + 2, 0)
            apply(2 * index + 1, 1)

        return carry

    lax.fori_loop(0, (count + 1) // 2, pair, jnp.int32(0))
    if apart:
        t, top = 0, 0
        for ref in outs:
            tall = ref.shape[0]
            for leaf in range(2):
                cols = slice(leaf * LEAF, (leaf + 1) * LEAF)
                ref[:, cols] = o_scr[t + leaf, top : top + tall, :]
            t, top = (t, top + tall) if top + tall < rows else (t + 2, 0)


def near_call(name, msgs, targets, leaves_at, sources, rows, row=0, acc=(), after=(), apart=None):
    nset = len(sources)
    start, stop = leaves_at
    vmem = pl.BlockSpec(memory_space=pltpu.VMEM)
    operands = [a for _, heads, chunks in sources for a in (*heads, *chunks)]
    scratch = [
        pltpu.VMEM((2 * nset, LEAF, 4 * F), BF),
        pltpu.VMEM((2 * nset, LEAF, 128), F32),
        pltpu.VMEM((2 * nset, 2 * rows, LEAF), BF),
        pltpu.VMEM((stop - start, rows, LEAF), F32),
        pltpu.VMEM((2, 2 * LEAF, LEAF), BF),
        pltpu.SMEM((2 * nset * (stop - start),), F32),
        pltpu.SMEM((2 * nset * (stop - start),), jnp.int32),
        pltpu.SMEM((len(msgs), EXTRA, 128), F32),
        pltpu.SemaphoreType.DMA((len(msgs),)),
    ]
    apart = bool(acc) if apart is None else apart
    if not apart:
        out = [jax.ShapeDtypeStruct((stop - start, rows, LEAF), F32)]
        scratch.pop(3)
    else:
        operands += list(acc)
        talls = SIZES if rows == R else (rows,)
        out = [jax.ShapeDtypeStruct((tall, 2 * LEAF), F32) for tall in talls] * ((stop - start) // 2)
    sets = tuple((kind, len(heads) - 1, len(chunks)) for kind, heads, chunks in sources)
    return pl.pallas_call(
        partial(
            near_body, len(msgs) // 2, sets, leaves_at, rows, row, len(acc), len(out), apart
        ),
        name=name,
        out_shape=out,
        in_specs=[pl.BlockSpec(memory_space=pl.ANY)] * len(msgs)
        + [vmem] * (2 + len(operands))
        + [pl.BlockSpec(memory_space=pl.ANY)] * len(after),
        out_specs=[vmem] * len(out),
        scratch_shapes=scratch,
        compiler_params=pltpu.CompilerParams(vmem_limit_bytes=VMEM_LIMIT),
    )(*msgs, *targets, *operands, *after)


def source_body(pts_ref, side_ref, off_ref):
    for leaf in range(2):
        cols = slice(leaf * LEAF, (leaf + 1) * LEAF)
        side, off = source_side(pts_ref[:F, cols] * SCALE)
        side_ref[leaf] = side
        off_ref[leaf] = jnp.broadcast_to(off, (LEAF, 128))


def source_call(pts):
    vmem = pl.BlockSpec(memory_space=pltpu.VMEM)
    return pl.pallas_call(
        source_body,
        name="source_side",
        out_shape=[
            jax.ShapeDtypeStruct((2, LEAF, 4 * F), BF),
            jax.ShapeDtypeStruct((2, LEAF, 128), F32),
        ],
        in_specs=[vmem],
        out_specs=[vmem, vmem],
        compiler_params=pltpu.CompilerParams(vmem_limit_bytes=VMEM_LIMIT),
    )(pts)


def place():
    helper = lax.axis_index("help")
    return helper // 2, helper % 2, lax.axis_index("leaf")


def share_rows(xs):
    return R // (2 * xs) * SK // (2 * LEAF)


def leaf_body(xs, count_ref, src_ref, pts_in, w_in, interp_in, *refs):
    msgs = refs[: 2 * xs]
    pts_ref, w_ref, interp_ref, scr, sems = refs[2 * xs :]
    copies = [
        pltpu.make_async_copy(pts_in, pts_ref, sems.at[0]),
        pltpu.make_async_copy(w_in, w_ref, sems.at[1]),
        pltpu.make_async_copy(interp_in, interp_ref, sems.at[2]),
    ]
    for copy in copies:
        copy.start()
    x, core, group = place()
    leaves = 4 * xs
    lane = lax.broadcasted_iota(jnp.int32, (1, 128), 1) + (group - 1) * leaves
    times = []
    for leaf in range(2):
        row = jnp.zeros((1, 128), F32)
        for slot in range(src_ref.shape[1]):
            name = jnp.where(slot < count_ref[0, leaf], src_ref[leaf, slot], -1 - 128 * leaves)
            row = row + (lane == name).astype(F32)
        times.append(row)
    times = jnp.concatenate(times + [jnp.zeros((EXTRA - 2, 128), F32)], axis=0)
    for copy in copies:
        copy.wait()
    total = jnp.zeros((R, SK), F32)
    for leaf in range(2):
        total = total + dot3(w_ref[:, leaf * LEAF : (leaf + 1) * LEAF], interp_ref[leaf])
    scr[...] = total
    rows = R // (2 * xs)
    tall = share_rows(xs)
    for n, msg in enumerate(msgs):
        helper = 2 * lax.rem(x + n // 2, xs) + (core if n % 2 == 0 else 1 - core)
        msg[:F, :] = pts_ref[...]
        msg[F : F + EXTRA, :] = jnp.zeros((EXTRA, 2 * LEAF), F32)
        msg[F : F + EXTRA, :128] = times
        for i in range(rows // tall):
            at = pl.multiple_of(helper * rows + i * tall, tall)
            msg[F + EXTRA :, i * SK : (i + 1) * SK] = scr[pl.ds(at, tall), :]


def leaf_call(xs, near_count, near_src, points, weights, interp):
    vmem = pl.BlockSpec(memory_space=pltpu.VMEM)
    smem = pl.BlockSpec(memory_space=pltpu.SMEM)
    anywhere = pl.BlockSpec(memory_space=pl.ANY)
    height = F + EXTRA + share_rows(xs)
    return pl.pallas_call(
        partial(leaf_body, xs),
        name="leaf_up",
        out_shape=[jax.ShapeDtypeStruct((height, 2 * LEAF), F32)] * (2 * xs),
        in_specs=[smem, smem, anywhere, anywhere, anywhere],
        out_specs=[vmem] * (2 * xs),
        scratch_shapes=[
            pltpu.VMEM(points.shape, F32),
            pltpu.VMEM(weights.shape, F32),
            pltpu.VMEM(interp.shape, F32),
            pltpu.VMEM((R, SK), F32),
            pltpu.SemaphoreType.DMA((3,)),
        ],
        compiler_params=pltpu.CompilerParams(vmem_limit_bytes=VMEM_WHOLE),
    )(near_count, near_src, points, weights, interp)


def skel_body(xs, index_ref, *refs):
    msgs, (out_ref, side_ref, off_ref, scr) = refs[:-4], refs[-4:]
    rows = R // (2 * xs)
    tall = share_rows(xs)
    total = jnp.zeros((2 * F, SK), F32)
    value = jnp.zeros((tall, 2 * LEAF), F32)
    spot = lax.broadcasted_iota(jnp.int32, (2 * LEAF, SK), 0)
    x, core, _ = place()
    for b, msg in enumerate(msgs):
        helper = 2 * lax.rem(x + b // 2, xs) + (core if b % 2 == 0 else 1 - core)
        side, off = target_side(msg[:F, :] * SCALE)
        for leaf in range(2):
            part = slice(leaf * LEAF, (leaf + 1) * LEAF)
            side_ref[2 * b + leaf] = side[:, part]
            off_ref[2 * b + leaf] = jnp.broadcast_to(off[:, part], (8, LEAF))
        hot = spot + helper * (2 * LEAF) == index_ref[...]
        total = total + dot(side[: 2 * F], hot.astype(F32).astype(BF))
        value = value + msg[F + EXTRA :, :]
    scr[...] = total[:F] + total[F:]
    out_ref[:HALF, :] = scr[pl.ds(pl.multiple_of(core * HALF, HALF), HALF), :]
    for i in range(rows // tall):
        out_ref[HALF + i * tall : HALF + (i + 1) * tall, :] = value[:, i * SK : (i + 1) * SK]


def skel_call(xs, index, msgs):
    rows = R // (2 * xs)
    leaves = 2 * len(msgs)
    vmem = pl.BlockSpec(memory_space=pltpu.VMEM)
    payload, *targets = pl.pallas_call(
        partial(skel_body, xs),
        name="skeleton",
        out_shape=[
            jax.ShapeDtypeStruct((HALF + rows, SK), F32),
            jax.ShapeDtypeStruct((leaves, 4 * F, LEAF), BF),
            jax.ShapeDtypeStruct((leaves, 8, LEAF), F32),
        ],
        in_specs=[vmem] * (1 + len(msgs)),
        out_specs=[vmem] * 3,
        scratch_shapes=[pltpu.VMEM((F, SK), F32)],
        compiler_params=pltpu.CompilerParams(vmem_limit_bytes=VMEM_LIMIT),
        cost_estimate=pl.CostEstimate(
            flops=5_000_000_000, bytes_accessed=8_000_000, transcendentals=0
        ),
    )(index, *msgs)
    return payload, targets


def stack_body(*refs):
    for n, ref in enumerate(refs[:-1]):
        refs[-1][n] = ref[...]


def stack_call(pieces):
    vmem = pl.BlockSpec(memory_space=pltpu.VMEM)
    return pl.pallas_call(
        stack_body,
        name="stack",
        out_shape=jax.ShapeDtypeStruct((len(pieces), *pieces[0].shape), F32),
        in_specs=[vmem] * len(pieces),
        out_specs=vmem,
        compiler_params=pltpu.CompilerParams(vmem_limit_bytes=VMEM_LIMIT),
    )(*pieces)


def points_body(alike_ref, beside_ref, out_ref):
    count = alike_ref.shape[0]
    for n in range(count):
        out_ref[n] = alike_ref[n, :HALF, :]
        out_ref[count + n] = beside_ref[n, :HALF, :]


def points_call(alike, beside):
    vmem = pl.BlockSpec(memory_space=pltpu.VMEM)
    return pl.pallas_call(
        points_body,
        name="points_of",
        out_shape=jax.ShapeDtypeStruct((2 * alike.shape[0], HALF, SK), F32),
        in_specs=[vmem, vmem],
        out_specs=vmem,
        compiler_params=pltpu.CompilerParams(vmem_limit_bytes=VMEM_LIMIT),
    )(alike, beside)


def upper_start(level, groups):
    return sum((groups >> step for step in range(1, level)))


def list_start(level, groups):
    return sum((groups >> step for step in range(level)))


def far_body(groups, rows, far_ref, node_ref, transfer_ref, alike_ref, beside_ref, mate_ref, *refs):
    out_ref, p_scr, u_scr, f_scr = refs[-4:]
    levels = groups.bit_length() - 1
    group = place()[2]
    start = [list_start(level, groups) for level in range(levels)]
    core = place()[1]
    here = pl.ds(pl.multiple_of(core * HALF, HALF), HALF)
    there = pl.ds(pl.multiple_of((1 - core) * HALF, HALF), HALF)
    for n in range(groups):
        node = group ^ (2 * (n % (groups // 2)) + n // (groups // 2))
        part = (alike_ref, beside_ref)[n // (groups // 2)]
        p_scr[node, here, :] = part[n % (groups // 2), :HALF, :]
        p_scr[node, there, :] = mate_ref[n]
        u_scr[node] = part[n % (groups // 2), HALF:, :]
    spot = lax.broadcasted_iota(jnp.int32, (2 * SK, SK), 0)
    for level in range(1, levels):
        for n in range(groups >> level):
            row = upper_start(level, groups) + n
            left = start[level - 1] + 2 * n
            hot = (spot == node_ref[row : row + 1, :]).astype(F32).astype(BF)
            hi, lo = halves(jnp.concatenate([p_scr[left], p_scr[left + 1]], axis=1))
            both = dot(jnp.concatenate([hi, lo], axis=0), hot)
            p_scr[start[level] + n] = both[:F] + both[F:]
            vals = jnp.concatenate([u_scr[left], u_scr[left + 1]], axis=1)
            u_scr[start[level] + n] = dot3(vals, transfer_ref[row])
    for level in range(levels):
        node = group >> level
        side, off = target_side(p_scr[start[level] + node])
        f_scr[level] = jnp.zeros((rows, SK), F32)

        def one(n, carry, level=level, node=node, side=side, off=off):
            hits = jnp.int32(0)
            for slot in range(FL):
                hits = hits + (far_ref[slot, start[level] + node] == n).astype(jnp.int32)

            @pl.when(hits > 0)
            def _():
                src, src_off = source_side(p_scr[start[level] + n])
                block = jnp.exp2(dot(src, side) + src_off + off)
                term = dot3(u_scr[start[level] + n], block)
                f_scr[level] = f_scr[level] + hits.astype(F32) * term

            return carry

        lax.fori_loop(0, groups >> level, one, jnp.int32(0))
    local = f_scr[levels - 1]
    for level in range(levels - 1, 0, -1):
        row = upper_start(level, groups) + (group >> level)
        bit = (group >> (level - 1)) & 1
        matrix = transfer_ref[row, pl.ds(pl.multiple_of(bit * SK, SK), SK), :]
        local = f_scr[level - 1] + dot3(local, matrix, dot_t)
    out_ref[...] = local


def far_call(groups, far_nodes, skel_node, transfer, alike, beside, mate, after):
    rows = alike.shape[1] - HALF
    vmem = pl.BlockSpec(memory_space=pltpu.VMEM)
    smem = pl.BlockSpec(memory_space=pltpu.SMEM)
    nodes = 2 * groups
    return pl.pallas_call(
        partial(far_body, groups, rows),
        name="far",
        out_shape=jax.ShapeDtypeStruct((rows, SK), F32),
        in_specs=[smem, vmem, vmem, vmem, vmem, vmem]
        + [pl.BlockSpec(memory_space=pl.ANY)] * len(after),
        out_specs=vmem,
        scratch_shapes=[
            pltpu.VMEM((nodes, F, SK), F32),
            pltpu.VMEM((nodes, rows, SK), F32),
            pltpu.VMEM((groups.bit_length(), rows, SK), F32),
        ],
        compiler_params=pltpu.CompilerParams(vmem_limit_bytes=VMEM_LIMIT),
    )(far_nodes.T, skel_node, transfer, alike, beside, mate, *after)


def final_body(xs, interp_ref, *refs):
    values, sums = refs[:xs], refs[xs:-2]
    out_ref, v_scr = refs[-2:]
    rows = R // (2 * xs)
    x, core, _ = place()
    for dx, ref in enumerate(values):
        for dc in range(2):
            helper = 2 * lax.rem(x + dx, xs) + (core if dc == 0 else 1 - core)
            v_scr[pl.ds(pl.multiple_of(helper * rows, rows), rows), :] = ref[dc]
    value = v_scr[...]
    for leaf in range(2):
        cols = slice(leaf * LEAF, (leaf + 1) * LEAF)
        total = dot3(value, interp_ref[leaf], dot_t)
        for c in range(2):
            part = slice(c * SIZES[0], SIZES[0] + c * SIZES[1])
            out_ref[part, cols] = total[part] + sums[c][:, cols] + sums[2 + c][:, cols]


def add_body(count, *refs):
    for n, out_ref in enumerate(refs[-(len(refs) // (count + 1)) :]):
        total = refs[n * count][...]
        for ref in refs[n * count + 1 : (n + 1) * count]:
            total = total + ref[...]
        out_ref[...] = total


def add_call(*sums):
    vmem = pl.BlockSpec(memory_space=pltpu.VMEM)
    operands = [value for terms in sums for value in terms]
    return pl.pallas_call(
        partial(add_body, len(sums[0])),
        name="add_parts",
        out_shape=[jax.ShapeDtypeStruct(terms[0].shape, F32) for terms in sums],
        in_specs=[vmem] * len(operands),
        out_specs=[vmem] * len(sums),
        compiler_params=pltpu.CompilerParams(vmem_limit_bytes=VMEM_LIMIT),
    )(*operands)


def final_call(xs, interp, home, mate, values):
    vmem = pl.BlockSpec(memory_space=pltpu.VMEM)
    return pl.pallas_call(
        partial(final_body, xs),
        name="join",
        out_shape=jax.ShapeDtypeStruct((R, 2 * LEAF), F32),
        in_specs=[vmem] * (1 + xs + 4),
        out_specs=vmem,
        scratch_shapes=[pltpu.VMEM((R, SK), F32)],
        compiler_params=pltpu.CompilerParams(vmem_limit_bytes=VMEM_LIMIT),
    )(interp, *values, *home, *mate)


def help_pairs(xs, dx, dc):
    return [
        (2 * ((x + dx) % xs) + (core ^ dc), 2 * x + core) for x in range(xs) for core in range(2)
    ]


def shards(
    points, weights, interp, transfer, near_count, near_src, skel_group, skel_node, far_nodes
):
    helpers = lax.axis_size("help")
    groups = lax.axis_size("leaf")
    xs = helpers // 2
    def from_help(value, dx, dc):
        return lax.ppermute(value, "help", help_pairs(xs, dx, dc))

    def to_help(value, dx):
        return lax.ppermute(value, "help", help_pairs(xs, -dx, 0))

    def together(*values):
        return lax.optimization_barrier(values)

    beside = [(i, i ^ 1) for i in range(groups)]
    across = [(i, i + 2) for i in range(0, groups - 2, 2)]
    across += [(i, i - 2) for i in range(3, groups, 2)]
    order = [(dx, dc) for dx in range(xs) for dc in range(2)]

    cut = SIZES[0]
    pts_y = lax.ppermute(points, "leaf", beside)
    w_y = [lax.ppermute(chunk, "leaf", beside) for chunk in (weights[:cut], weights[cut:])]
    sent = leaf_call(xs, near_count, near_src, points, weights, interp)
    got = [
        lax.ppermute(sent[n], "help", help_pairs(xs, -dx, dc))
        for n, (dx, dc) in enumerate(order)
        if n
    ]
    pts_z = lax.ppermute(pts_y, "leaf", across)
    pts_z, w_y[0], got[0] = together(pts_z, w_y[0], got[0])
    w_z = [lax.ppermute(w_y[0], "leaf", across)]
    msgs = [sent[0]] + [got[order.index((-dx % xs, dc)) - 1] for dx, dc in order[1:]]
    payload, targets = skel_call(xs, skel_group, msgs)
    pieces = [payload]
    for mask in range(2, groups, 2):
        pieces.append(lax.ppermute(payload, "leaf", [(i, i ^ mask) for i in range(groups)]))

    payload, w_y[1] = together(payload, w_y[1])
    away, home = (4, 2 * helpers), (0, 4)
    own_src = ("own", (points,), [weights])
    (own,) = near_call("near_own", msgs, targets, away, [own_src], R)
    w_z.append(lax.ppermute(w_y[1], "leaf", across))
    pair_src = ("pair", (pts_y,), w_y)
    (pair,) = near_call("near_pair", msgs, targets, away, [pair_src], R, after=[own])
    z_side = source_call(pts_z)
    sums, part = [], [pair]
    for c in range(2):
        if c == 1:
            pieces, part = together(pieces, part)
            alike = stack_call(pieces)
            side = lax.ppermute(alike, "leaf", beside)
            part = [alike]
        part = near_call(
            "near_next_away", msgs, targets, away, [("next", z_side, w_z[c : c + 1])],
            SIZES[c], c * SIZES[0], [own, pair], part[:1],
        )
        kept, given = part[::2], part[1::2]
        sums.append((kept, [from_help(value, 0, 1) for value in given]))
    parts = []
    for c in range(2):
        kept, mates = sums[c]
        both = add_call(*zip(kept, mates))
        parts.append([to_help(value, dx + 1) for dx, value in enumerate(both)])
    sources = [own_src, pair_src, ("next", z_side, w_z)]
    home = near_call("near_home", msgs, targets, home, sources, R, after=both[:1], apart=True)
    swapped = from_help(points_call(alike, side), 0, 1)
    v_own = far_call(groups, far_nodes, skel_node, transfer, alike, side, swapped, home[:1])
    v_pair = stack_call([v_own, from_help(v_own, 0, 1)])
    values = [v_pair] + [from_help(v_pair, dx, 0) for dx in range(1, xs)]
    mate = [from_help(value, 0, 1) for value in home[2:]]
    mine = add_call(*[[home[c], *parts[c]] for c in range(2)])
    return final_call(xs, interp, mine, mate, values)


def solution(mesh):
    placed = (
        P(None, ("leaf", "help")),
        P(None, ("leaf", "help")),
        P(("leaf", "help"), None, None),
        P(),
        P("leaf", "help"),
        P(("leaf", "help"), None),
        P("leaf", None),
        P(),
        P(),
    )
    return jax.shard_map(
        shards, mesh=mesh, in_specs=placed, out_specs=P(None, ("leaf", "help")), check_vma=False
    )
```

```python
import math
from functools import partial

import jax
import jax.numpy as jnp
from jax import lax
from jax.experimental import pallas as pl
from jax.experimental.pallas import tpu as pltpu
from jax.sharding import PartitionSpec as P

F = 64
R = 256
LEAF = 512
SK = 256
FL = 4
EXTRA = 8
HALF = F // 2
SIZES = (128, 128)

BF = jnp.bfloat16
F32 = jnp.float32
LOG2E = 1.0 / math.log(2.0)
SCALE = math.sqrt(0.5 * LOG2E)
BIAS = 0.0625 * F * LOG2E
VMEM_LIMIT = 24 * 1024 * 1024
VMEM_WHOLE = 64 * 1024 * 1024


def dot(a, b):
    return jnp.dot(a, b, preferred_element_type=F32)


def dot_t(a, b):
    return lax.dot_general(a, b, (((1,), (1,)), ((), ())), preferred_element_type=F32)


def halves(x):
    hi = x.astype(BF)
    lo = (x - hi.astype(F32)).astype(BF)
    return hi, lo


def dot3(a, b, mul=dot):
    a_hi, a_lo = halves(a)
    b_hi, b_lo = halves(b)
    return mul(a_hi, b_hi) + mul(a_lo, b_hi) + mul(a_hi, b_lo)


def target_side(x):
    hi, lo = halves(x)
    both = hi.astype(F32) + lo.astype(F32)
    off = BIAS - 0.5 * jnp.sum(both * both, axis=0, keepdims=True)
    return jnp.concatenate([hi, lo, hi, lo], axis=0), off


def source_side(x):
    xt = x.T
    hi, lo = halves(xt)
    both = hi.astype(F32) + lo.astype(F32)
    off = BIAS - 0.5 * jnp.sum(both * both, axis=1, keepdims=True)
    return jnp.concatenate([hi, hi, lo, lo], axis=1), off


def near_body(
    xs, sets, leaves_at, rows, row, nacc, nout, apart, *refs
):
    nset = len(sets)
    start, stop = leaves_at
    msgs, (t_ref, tb_ref), refs = refs[: 2 * xs], refs[2 * xs : 2 * xs + 2], refs[2 * xs + 2 :]
    if apart:
        s_scr, sb_scr, w_scr, o_scr, k_scr, times_scr, list_ref, times_ref, sems = refs[-9:]
        outs = refs[-9 - nout : -9]
    else:
        o_scr, s_scr, sb_scr, w_scr, k_scr, times_scr, list_ref, times_ref, sems = refs[-9:]
    copies = [
        pltpu.make_async_copy(msgs[b].at[F : F + EXTRA, :128], times_ref.at[b], sems.at[b])
        for b in range(start // 2, stop // 2)
    ]
    for copy in copies:
        copy.start()
    at = 0
    for k, (_, ready, chunks) in enumerate(sets):
        heads = refs[at : at + 1 + ready]
        parts = refs[at + 1 + ready : at + 1 + ready + chunks]
        at += 1 + ready + chunks
        for leaf in range(2):
            cols = slice(leaf * LEAF, (leaf + 1) * LEAF)
            j = 2 * k + leaf
            if ready:
                s_scr[j] = heads[0][leaf]
                sb_scr[j] = heads[1][leaf]
            else:
                side, off = source_side(heads[0][:F, cols] * SCALE)
                s_scr[j] = side
                sb_scr[j] = jnp.broadcast_to(off, (LEAF, 128))
            top = 0
            for part in parts:
                hi, lo = halves(part[:, cols])
                w_scr[j, top : top + part.shape[0], :] = hi
                w_scr[j, rows + top : rows + top + part.shape[0], :] = lo
                top += part.shape[0]
    for t in range(start, stop):
        if nacc:
            o_scr[t - start] = sum(
                ref[t - start if ref.shape[0] < 4 * xs else t, row : row + rows, :]
                for ref in refs[at : at + nacc]
            )
        else:
            o_scr[t - start] = jnp.zeros((rows, LEAF), F32)

    x, core, group = place()
    leaves = 4 * xs
    odd = group % 2
    column = []
    for kind, _, _ in sets:
        relative = {"own": 1, "pair": 2 - 2 * odd, "next": 2 * odd}[kind]
        column.append(relative * leaves + 2 * (2 * x + core))

    for copy in copies:
        copy.wait()
    count = jnp.int32(0)
    list_ref[0] = 0
    for t in range(start, stop):
        for j in range(2 * nset):
            times = times_ref[t // 2, t % 2, column[j // 2] + j % 2]

            @pl.when(times > 0)
            def _(count=count, t=t, j=j, times=times):
                list_ref[count] = t * 8 + j
                times_scr[count] = times

            count = count + (times > 0).astype(jnp.int32)

    def block(index, slot):
        code = list_ref[jnp.minimum(index, jnp.maximum(count - 1, 0))]
        t, j = code // 8, code % 8
        side = t_ref[t]
        off = tb_ref[t][:1, :]
        for half in range(2):
            part = slice(half * 256, (half + 1) * 256)
            cross = dot(s_scr[j, part, :], side)
            src_off = sb_scr[j, part, :]
            src_off = jnp.concatenate([src_off] * (LEAF // 128), axis=1)
            k_hi, k_lo = halves(jnp.exp2(cross + src_off + off))
            k_scr[slot, part, :] = k_hi
            k_scr[slot, LEAF + half * 256 : LEAF + (half + 1) * 256, :] = k_lo

    def apply(index, slot):
        code = list_ref[index]
        t, j = code // 8 - start, code % 8
        factor = times_scr[index]
        for half in range(2):
            cols = slice(half * 256, (half + 1) * 256)
            both = dot(w_scr[j], k_scr[slot, :LEAF, cols])
            low = dot(w_scr[j, :rows, :], k_scr[slot, LEAF:, cols])
            o_scr[t, :, cols] = o_scr[t, :, cols] + factor * (both[:rows] + both[rows:] + low)

    @pl.when(count > 0)
    def _():
        block(0, 0)

    def pair(index, carry):
        block(2 * index + 1, 1)
        apply(2 * index, 0)

        @pl.when(2 * index + 1 < count)
        def _():
            block(2 * index + 2, 0)
            apply(2 * index + 1, 1)

        return carry

    lax.fori_loop(0, (count + 1) // 2, pair, jnp.int32(0))
    if apart:
        t, top = 0, 0
        for ref in outs:
            tall = ref.shape[0]
            for leaf in range(2):
                cols = slice(leaf * LEAF, (leaf + 1) * LEAF)
                ref[:, cols] = o_scr[t + leaf, top : top + tall, :]
            t, top = (t, top + tall) if top + tall < rows else (t + 2, 0)


def near_call(name, msgs, targets, leaves_at, sources, rows, row=0, acc=(), after=(), apart=None):
    nset = len(sources)
    start, stop = leaves_at
    vmem = pl.BlockSpec(memory_space=pltpu.VMEM)
    operands = [a for _, heads, chunks in sources for a in (*heads, *chunks)]
    scratch = [
        pltpu.VMEM((2 * nset, LEAF, 4 * F), BF),
        pltpu.VMEM((2 * nset, LEAF, 128), F32),
        pltpu.VMEM((2 * nset, 2 * rows, LEAF), BF),
        pltpu.VMEM((stop - start, rows, LEAF), F32),
        pltpu.VMEM((2, 2 * LEAF, LEAF), BF),
        pltpu.SMEM((2 * nset * (stop - start),), F32),
        pltpu.SMEM((2 * nset * (stop - start),), jnp.int32),
        pltpu.SMEM((len(msgs), EXTRA, 128), F32),
        pltpu.SemaphoreType.DMA((len(msgs),)),
    ]
    apart = bool(acc) if apart is None else apart
    if not apart:
        out = [jax.ShapeDtypeStruct((stop - start, rows, LEAF), F32)]
        scratch.pop(3)
    else:
        operands += list(acc)
        talls = SIZES if rows == R else (rows,)
        out = [jax.ShapeDtypeStruct((tall, 2 * LEAF), F32) for tall in talls] * ((stop - start) // 2)
    sets = tuple((kind, len(heads) - 1, len(chunks)) for kind, heads, chunks in sources)
    return pl.pallas_call(
        partial(
            near_body, len(msgs) // 2, sets, leaves_at, rows, row, len(acc), len(out), apart
        ),
        name=name,
        out_shape=out,
        in_specs=[pl.BlockSpec(memory_space=pl.ANY)] * len(msgs)
        + [vmem] * (2 + len(operands))
        + [pl.BlockSpec(memory_space=pl.ANY)] * len(after),
        out_specs=[vmem] * len(out),
        scratch_shapes=scratch,
        compiler_params=pltpu.CompilerParams(vmem_limit_bytes=VMEM_LIMIT),
    )(*msgs, *targets, *operands, *after)


def source_body(pts_ref, side_ref, off_ref):
    for leaf in range(2):
        cols = slice(leaf * LEAF, (leaf + 1) * LEAF)
        side, off = source_side(pts_ref[:F, cols] * SCALE)
        side_ref[leaf] = side
        off_ref[leaf] = jnp.broadcast_to(off, (LEAF, 128))


def source_call(pts):
    vmem = pl.BlockSpec(memory_space=pltpu.VMEM)
    return pl.pallas_call(
        source_body,
        name="source_side",
        out_shape=[
            jax.ShapeDtypeStruct((2, LEAF, 4 * F), BF),
            jax.ShapeDtypeStruct((2, LEAF, 128), F32),
        ],
        in_specs=[vmem],
        out_specs=[vmem, vmem],
        compiler_params=pltpu.CompilerParams(vmem_limit_bytes=VMEM_LIMIT),
    )(pts)


def place():
    helper = lax.axis_index("help")
    return helper // 2, helper % 2, lax.axis_index("leaf")


def share_rows(xs):
    return R // (2 * xs) * SK // (2 * LEAF)


def leaf_body(xs, count_ref, src_ref, pts_in, w_in, interp_in, *refs):
    msgs = refs[: 2 * xs]
    pts_ref, w_ref, interp_ref, scr, sems = refs[2 * xs :]
    copies = [
        pltpu.make_async_copy(pts_in, pts_ref, sems.at[0]),
        pltpu.make_async_copy(w_in, w_ref, sems.at[1]),
        pltpu.make_async_copy(interp_in, interp_ref, sems.at[2]),
    ]
    for copy in copies:
        copy.start()
    x, core, group = place()
    leaves = 4 * xs
    lane = lax.broadcasted_iota(jnp.int32, (1, 128), 1) + (group - 1) * leaves
    times = []
    for leaf in range(2):
        row = jnp.zeros((1, 128), F32)
        for slot in range(src_ref.shape[1]):
            name = jnp.where(slot < count_ref[0, leaf], src_ref[leaf, slot], -1 - 128 * leaves)
            row = row + (lane == name).astype(F32)
        times.append(row)
    times = jnp.concatenate(times + [jnp.zeros((EXTRA - 2, 128), F32)], axis=0)
    for copy in copies:
        copy.wait()
    total = jnp.zeros((R, SK), F32)
    for leaf in range(2):
        total = total + dot3(w_ref[:, leaf * LEAF : (leaf + 1) * LEAF], interp_ref[leaf])
    scr[...] = total
    rows = R // (2 * xs)
    tall = share_rows(xs)
    for n, msg in enumerate(msgs):
        helper = 2 * lax.rem(x + n // 2, xs) + (core if n % 2 == 0 else 1 - core)
        msg[:F, :] = pts_ref[...]
        msg[F : F + EXTRA, :] = jnp.zeros((EXTRA, 2 * LEAF), F32)
        msg[F : F + EXTRA, :128] = times
        for i in range(rows // tall):
            at = pl.multiple_of(helper * rows + i * tall, tall)
            msg[F + EXTRA :, i * SK : (i + 1) * SK] = scr[pl.ds(at, tall), :]


def leaf_call(xs, near_count, near_src, points, weights, interp):
    vmem = pl.BlockSpec(memory_space=pltpu.VMEM)
    smem = pl.BlockSpec(memory_space=pltpu.SMEM)
    anywhere = pl.BlockSpec(memory_space=pl.ANY)
    height = F + EXTRA + share_rows(xs)
    return pl.pallas_call(
        partial(leaf_body, xs),
        name="leaf_up",
        out_shape=[jax.ShapeDtypeStruct((height, 2 * LEAF), F32)] * (2 * xs),
        in_specs=[smem, smem, anywhere, anywhere, anywhere],
        out_specs=[vmem] * (2 * xs),
        scratch_shapes=[
            pltpu.VMEM(points.shape, F32),
            pltpu.VMEM(weights.shape, F32),
            pltpu.VMEM(interp.shape, F32),
            pltpu.VMEM((R, SK), F32),
            pltpu.SemaphoreType.DMA((3,)),
        ],
        compiler_params=pltpu.CompilerParams(vmem_limit_bytes=VMEM_WHOLE),
    )(near_count, near_src, points, weights, interp)


def skel_body(xs, index_ref, *refs):
    msgs, (out_ref, side_ref, off_ref, scr) = refs[:-4], refs[-4:]
    rows = R // (2 * xs)
    tall = share_rows(xs)
    total = jnp.zeros((2 * F, SK), F32)
    value = jnp.zeros((tall, 2 * LEAF), F32)
    spot = lax.broadcasted_iota(jnp.int32, (2 * LEAF, SK), 0)
    x, core, _ = place()
    for b, msg in enumerate(msgs):
        helper = 2 * lax.rem(x + b // 2, xs) + (core if b % 2 == 0 else 1 - core)
        side, off = target_side(msg[:F, :] * SCALE)
        for leaf in range(2):
            part = slice(leaf * LEAF, (leaf + 1) * LEAF)
            side_ref[2 * b + leaf] = side[:, part]
            off_ref[2 * b + leaf] = jnp.broadcast_to(off[:, part], (8, LEAF))
        hot = spot + helper * (2 * LEAF) == index_ref[...]
        total = total + dot(side[: 2 * F], hot.astype(F32).astype(BF))
        value = value + msg[F + EXTRA :, :]
    scr[...] = total[:F] + total[F:]
    out_ref[:HALF, :] = scr[pl.ds(pl.multiple_of(core * HALF, HALF), HALF), :]
    for i in range(rows // tall):
        out_ref[HALF + i * tall : HALF + (i + 1) * tall, :] = value[:, i * SK : (i + 1) * SK]


def skel_call(xs, index, msgs):
    rows = R // (2 * xs)
    leaves = 2 * len(msgs)
    vmem = pl.BlockSpec(memory_space=pltpu.VMEM)
    payload, *targets = pl.pallas_call(
        partial(skel_body, xs),
        name="skeleton",
        out_shape=[
            jax.ShapeDtypeStruct((HALF + rows, SK), F32),
            jax.ShapeDtypeStruct((leaves, 4 * F, LEAF), BF),
            jax.ShapeDtypeStruct((leaves, 8, LEAF), F32),
        ],
        in_specs=[vmem] * (1 + len(msgs)),
        out_specs=[vmem] * 3,
        scratch_shapes=[pltpu.VMEM((F, SK), F32)],
        compiler_params=pltpu.CompilerParams(vmem_limit_bytes=VMEM_LIMIT),
        cost_estimate=pl.CostEstimate(
            flops=5_000_000_000, bytes_accessed=8_000_000, transcendentals=0
        ),
    )(index, *msgs)
    return payload, targets


def stack_body(*refs):
    for n, ref in enumerate(refs[:-1]):
        refs[-1][n] = ref[...]


def stack_call(pieces):
    vmem = pl.BlockSpec(memory_space=pltpu.VMEM)
    return pl.pallas_call(
        stack_body,
        name="stack",
        out_shape=jax.ShapeDtypeStruct((len(pieces), *pieces[0].shape), F32),
        in_specs=[vmem] * len(pieces),
        out_specs=vmem,
        compiler_params=pltpu.CompilerParams(vmem_limit_bytes=VMEM_LIMIT),
    )(*pieces)


def points_body(alike_ref, beside_ref, out_ref):
    count = alike_ref.shape[0]
    for n in range(count):
        out_ref[n] = alike_ref[n, :HALF, :]
        out_ref[count + n] = beside_ref[n, :HALF, :]


def points_call(alike, beside):
    vmem = pl.BlockSpec(memory_space=pltpu.VMEM)
    return pl.pallas_call(
        points_body,
        name="points_of",
        out_shape=jax.ShapeDtypeStruct((2 * alike.shape[0], HALF, SK), F32),
        in_specs=[vmem, vmem],
        out_specs=vmem,
        compiler_params=pltpu.CompilerParams(vmem_limit_bytes=VMEM_LIMIT),
    )(alike, beside)


def upper_start(level, groups):
    return sum((groups >> step for step in range(1, level)))


def list_start(level, groups):
    return sum((groups >> step for step in range(level)))


def far_body(groups, rows, far_ref, node_ref, transfer_ref, alike_ref, beside_ref, mate_ref, *refs):
    out_ref, p_scr, u_scr, f_scr = refs[-4:]
    levels = groups.bit_length() - 1
    group = place()[2]
    start = [list_start(level, groups) for level in range(levels)]
    core = place()[1]
    here = pl.ds(pl.multiple_of(core * HALF, HALF), HALF)
    there = pl.ds(pl.multiple_of((1 - core) * HALF, HALF), HALF)
    for n in range(groups):
        node = group ^ (2 * (n % (groups // 2)) + n // (groups // 2))
        part = (alike_ref, beside_ref)[n // (groups // 2)]
        p_scr[node, here, :] = part[n % (groups // 2), :HALF, :]
        p_scr[node, there, :] = mate_ref[n]
        u_scr[node] = part[n % (groups // 2), HALF:, :]
    spot = lax.broadcasted_iota(jnp.int32, (2 * SK, SK), 0)
    for level in range(1, levels):
        for n in range(groups >> level):
            row = upper_start(level, groups) + n
            left = start[level - 1] + 2 * n
            hot = (spot == node_ref[row : row + 1, :]).astype(F32).astype(BF)
            hi, lo = halves(jnp.concatenate([p_scr[left], p_scr[left + 1]], axis=1))
            both = dot(jnp.concatenate([hi, lo], axis=0), hot)
            p_scr[start[level] + n] = both[:F] + both[F:]
            vals = jnp.concatenate([u_scr[left], u_scr[left + 1]], axis=1)
            u_scr[start[level] + n] = dot3(vals, transfer_ref[row])
    for level in range(levels):
        node = group >> level
        side, off = target_side(p_scr[start[level] + node])
        f_scr[level] = jnp.zeros((rows, SK), F32)

        def one(n, carry, level=level, node=node, side=side, off=off):
            hits = jnp.int32(0)
            for slot in range(FL):
                hits = hits + (far_ref[slot, start[level] + node] == n).astype(jnp.int32)

            @pl.when(hits > 0)
            def _():
                src, src_off = source_side(p_scr[start[level] + n])
                block = jnp.exp2(dot(src, side) + src_off + off)
                term = dot3(u_scr[start[level] + n], block)
                f_scr[level] = f_scr[level] + hits.astype(F32) * term

            return carry

        lax.fori_loop(0, groups >> level, one, jnp.int32(0))
    local = f_scr[levels - 1]
    for level in range(levels - 1, 0, -1):
        row = upper_start(level, groups) + (group >> level)
        bit = (group >> (level - 1)) & 1
        matrix = transfer_ref[row, pl.ds(pl.multiple_of(bit * SK, SK), SK), :]
        local = f_scr[level - 1] + dot3(local, matrix, dot_t)
    out_ref[...] = local


def far_call(groups, far_nodes, skel_node, transfer, alike, beside, mate, after):
    rows = alike.shape[1] - HALF
    vmem = pl.BlockSpec(memory_space=pltpu.VMEM)
    smem = pl.BlockSpec(memory_space=pltpu.SMEM)
    nodes = 2 * groups
    return pl.pallas_call(
        partial(far_body, groups, rows),
        name="far",
        out_shape=jax.ShapeDtypeStruct((rows, SK), F32),
        in_specs=[smem, vmem, vmem, vmem, vmem, vmem]
        + [pl.BlockSpec(memory_space=pl.ANY)] * len(after),
        out_specs=vmem,
        scratch_shapes=[
            pltpu.VMEM((nodes, F, SK), F32),
            pltpu.VMEM((nodes, rows, SK), F32),
            pltpu.VMEM((groups.bit_length(), rows, SK), F32),
        ],
        compiler_params=pltpu.CompilerParams(vmem_limit_bytes=VMEM_LIMIT),
    )(far_nodes.T, skel_node, transfer, alike, beside, mate, *after)


def final_body(xs, interp_ref, *refs):
    values, sums = refs[:xs], refs[xs:-2]
    out_ref, v_scr = refs[-2:]
    rows = R // (2 * xs)
    x, core, _ = place()
    for dx, ref in enumerate(values):
        for dc in range(2):
            helper = 2 * lax.rem(x + dx, xs) + (core if dc == 0 else 1 - core)
            v_scr[pl.ds(pl.multiple_of(helper * rows, rows), rows), :] = ref[dc]
    value = v_scr[...]
    for leaf in range(2):
        cols = slice(leaf * LEAF, (leaf + 1) * LEAF)
        total = dot3(value, interp_ref[leaf], dot_t)
        for c in range(2):
            part = slice(c * SIZES[0], SIZES[0] + c * SIZES[1])
            out_ref[part, cols] = total[part] + sums[c][:, cols] + sums[2 + c][:, cols]


def add_body(count, *refs):
    for n, out_ref in enumerate(refs[-(len(refs) // (count + 1)) :]):
        total = refs[n * count][...]
        for ref in refs[n * count + 1 : (n + 1) * count]:
            total = total + ref[...]
        out_ref[...] = total


def add_call(*sums):
    vmem = pl.BlockSpec(memory_space=pltpu.VMEM)
    operands = [value for terms in sums for value in terms]
    return pl.pallas_call(
        partial(add_body, len(sums[0])),
        name="add_parts",
        out_shape=[jax.ShapeDtypeStruct(terms[0].shape, F32) for terms in sums],
        in_specs=[vmem] * len(operands),
        out_specs=[vmem] * len(sums),
        compiler_params=pltpu.CompilerParams(vmem_limit_bytes=VMEM_LIMIT),
    )(*operands)


def final_call(xs, interp, home, mate, values):
    vmem = pl.BlockSpec(memory_space=pltpu.VMEM)
    return pl.pallas_call(
        partial(final_body, xs),
        name="join",
        out_shape=jax.ShapeDtypeStruct((R, 2 * LEAF), F32),
        in_specs=[vmem] * (1 + xs + 4),
        out_specs=vmem,
        scratch_shapes=[pltpu.VMEM((R, SK), F32)],
        compiler_params=pltpu.CompilerParams(vmem_limit_bytes=VMEM_LIMIT),
    )(interp, *values, *home, *mate)


def help_pairs(xs, dx, dc):
    return [
        (2 * ((x + dx) % xs) + (core ^ dc), 2 * x + core) for x in range(xs) for core in range(2)
    ]


def shards(
    points, weights, interp, transfer, near_count, near_src, skel_group, skel_node, far_nodes
):
    helpers = lax.axis_size("help")
    groups = lax.axis_size("leaf")
    xs = helpers // 2
    def from_help(value, dx, dc):
        return lax.ppermute(value, "help", help_pairs(xs, dx, dc))

    def to_help(value, dx):
        return lax.ppermute(value, "help", help_pairs(xs, -dx, 0))

    def together(*values):
        return lax.optimization_barrier(values)

    beside = [(i, i ^ 1) for i in range(groups)]
    across = [(i, i + 2) for i in range(0, groups - 2, 2)]
    across += [(i, i - 2) for i in range(3, groups, 2)]
    order = [(dx, dc) for dx in range(xs) for dc in range(2)]

    cut = SIZES[0]
    pts_y = lax.ppermute(points, "leaf", beside)
    w_y = [lax.ppermute(chunk, "leaf", beside) for chunk in (weights[:cut], weights[cut:])]
    sent = leaf_call(xs, near_count, near_src, points, weights, interp)
    got = [
        lax.ppermute(sent[n], "help", help_pairs(xs, -dx, dc))
        for n, (dx, dc) in enumerate(order)
        if n
    ]
    pts_z = lax.ppermute(pts_y, "leaf", across)
    pts_z, w_y[0], got[0] = together(pts_z, w_y[0], got[0])
    w_z = [lax.ppermute(w_y[0], "leaf", across)]
    msgs = [sent[0]] + [got[order.index((-dx % xs, dc)) - 1] for dx, dc in order[1:]]
    payload, targets = skel_call(xs, skel_group, msgs)
    pieces = [payload]
    for mask in range(2, groups, 2):
        pieces.append(lax.ppermute(payload, "leaf", [(i, i ^ mask) for i in range(groups)]))

    payload, w_y[1] = together(payload, w_y[1])
    away, home = (4, 2 * helpers), (0, 4)
    own_src = ("own", (points,), [weights])
    (own,) = near_call("near_own", msgs, targets, away, [own_src], R)
    w_z.append(lax.ppermute(w_y[1], "leaf", across))
    pair_src = ("pair", (pts_y,), w_y)
    (pair,) = near_call("near_pair", msgs, targets, away, [pair_src], R, after=[own])
    z_side = source_call(pts_z)
    sums, part = [], [pair]
    for c in range(2):
        if c == 1:
            (own_home,) = near_call(
                "near_own_home", msgs, targets, home, [own_src], R, after=part[:1]
            )
            pieces, own_home = together(pieces, own_home)
            alike = stack_call(pieces)
            side = lax.ppermute(alike, "leaf", beside)
            part = [alike]
        part = near_call(
            "near_next_away", msgs, targets, away, [("next", z_side, w_z[c : c + 1])],
            SIZES[c], c * SIZES[0], [own, pair], part[:1],
        )
        kept, given = part[::2], part[1::2]
        sums.append((kept, [from_help(value, 0, 1) for value in given]))
    parts = []
    for c in range(2):
        kept, mates = sums[c]
        both = add_call(*zip(kept, mates))
        parts.append([to_help(value, dx + 1) for dx, value in enumerate(both)])
    sources = [pair_src, ("next", z_side, w_z)]
    home = near_call("near_home", msgs, targets, home, sources, R, 0, [own_home], both[:1])
    swapped = from_help(points_call(alike, side), 0, 1)
    v_own = far_call(groups, far_nodes, skel_node, transfer, alike, side, swapped, home[:1])
    v_pair = stack_call([v_own, from_help(v_own, 0, 1)])
    values = [v_pair] + [from_help(v_pair, dx, 0) for dx in range(1, xs)]
    mate = [from_help(value, 0, 1) for value in home[2:]]
    mine = add_call(*[[home[c], *parts[c]] for c in range(2)])
    return final_call(xs, interp, mine, mate, values)


def solution(mesh):
    placed = (
        P(None, ("leaf", "help")),
        P(None, ("leaf", "help")),
        P(("leaf", "help"), None, None),
        P(),
        P("leaf", "help"),
        P(("leaf", "help"), None),
        P("leaf", None),
        P(),
        P(),
    )
    return jax.shard_map(
        shards, mesh=mesh, in_specs=placed, out_specs=P(None, ("leaf", "help")), check_vma=False
    )
```

```python
import math
from functools import partial

import jax
import jax.numpy as jnp
from jax import lax
from jax.experimental import pallas as pl
from jax.experimental.pallas import tpu as pltpu
from jax.sharding import PartitionSpec as P

F = 64
R = 256
LEAF = 512
SK = 256
FL = 4
EXTRA = 8
HALF = F // 2
SIZES = (128, 128)

BF = jnp.bfloat16
F32 = jnp.float32
LOG2E = 1.0 / math.log(2.0)
SCALE = math.sqrt(0.5 * LOG2E)
BIAS = 0.0625 * F * LOG2E
VMEM_LIMIT = 24 * 1024 * 1024
VMEM_WHOLE = 64 * 1024 * 1024


def dot(a, b):
    return jnp.dot(a, b, preferred_element_type=F32)


def dot_t(a, b):
    return lax.dot_general(a, b, (((1,), (1,)), ((), ())), preferred_element_type=F32)


def halves(x):
    hi = x.astype(BF)
    lo = (x - hi.astype(F32)).astype(BF)
    return hi, lo


def dot3(a, b, mul=dot):
    a_hi, a_lo = halves(a)
    b_hi, b_lo = halves(b)
    return mul(a_hi, b_hi) + mul(a_lo, b_hi) + mul(a_hi, b_lo)


def target_side(x):
    hi, lo = halves(x)
    both = hi.astype(F32) + lo.astype(F32)
    off = BIAS - 0.5 * jnp.sum(both * both, axis=0, keepdims=True)
    return jnp.concatenate([hi, lo, hi, lo], axis=0), off


def source_side(x):
    xt = x.T
    hi, lo = halves(xt)
    both = hi.astype(F32) + lo.astype(F32)
    off = BIAS - 0.5 * jnp.sum(both * both, axis=1, keepdims=True)
    return jnp.concatenate([hi, hi, lo, lo], axis=1), off


def near_body(
    xs, sets, leaves_at, rows, row, nacc, nout, *refs
):
    nset = len(sets)
    start, stop = leaves_at
    msgs, (t_ref, tb_ref), refs = refs[: 2 * xs], refs[2 * xs : 2 * xs + 2], refs[2 * xs + 2 :]
    if nacc:
        s_scr, sb_scr, w_scr, o_scr, k_scr, times_scr, list_ref, times_ref, sems = refs[-9:]
        outs = refs[-9 - nout : -9]
    else:
        o_scr, s_scr, sb_scr, w_scr, k_scr, times_scr, list_ref, times_ref, sems = refs[-9:]
    copies = [
        pltpu.make_async_copy(msgs[b].at[F : F + EXTRA, :128], times_ref.at[b], sems.at[b])
        for b in range(start // 2, stop // 2)
    ]
    for copy in copies:
        copy.start()
    at = 0
    for k, (_, ready, chunks) in enumerate(sets):
        heads = refs[at : at + 1 + ready]
        parts = refs[at + 1 + ready : at + 1 + ready + chunks]
        at += 1 + ready + chunks
        for leaf in range(2):
            cols = slice(leaf * LEAF, (leaf + 1) * LEAF)
            j = 2 * k + leaf
            if ready:
                s_scr[j] = heads[0][leaf]
                sb_scr[j] = heads[1][leaf]
            else:
                side, off = source_side(heads[0][:F, cols] * SCALE)
                s_scr[j] = side
                sb_scr[j] = jnp.broadcast_to(off, (LEAF, 128))
            top = 0
            for part in parts:
                hi, lo = halves(part[:, cols])
                w_scr[j, top : top + part.shape[0], :] = hi
                w_scr[j, rows + top : rows + top + part.shape[0], :] = lo
                top += part.shape[0]
    for t in range(start, stop):
        if nacc:
            o_scr[t - start] = sum(
                ref[t - (4 * xs - ref.shape[0]), row : row + rows, :] for ref in refs[at : at + nacc]
            )
        else:
            o_scr[t - start] = jnp.zeros((rows, LEAF), F32)

    x, core, group = place()
    leaves = 4 * xs
    odd = group % 2
    column = []
    for kind, _, _ in sets:
        relative = {"own": 1, "pair": 2 - 2 * odd, "next": 2 * odd}[kind]
        column.append(relative * leaves + 2 * (2 * x + core))

    for copy in copies:
        copy.wait()
    count = jnp.int32(0)
    list_ref[0] = 0
    for t in range(start, stop):
        for j in range(2 * nset):
            times = times_ref[t // 2, t % 2, column[j // 2] + j % 2]

            @pl.when(times > 0)
            def _(count=count, t=t, j=j, times=times):
                list_ref[count] = t * 8 + j
                times_scr[count] = times

            count = count + (times > 0).astype(jnp.int32)

    def block(index, slot):
        code = list_ref[jnp.minimum(index, jnp.maximum(count - 1, 0))]
        t, j = code // 8, code % 8
        side = t_ref[t]
        off = tb_ref[t][:1, :]
        for half in range(2):
            part = slice(half * 256, (half + 1) * 256)
            cross = dot(s_scr[j, part, :], side)
            src_off = sb_scr[j, part, :]
            src_off = jnp.concatenate([src_off] * (LEAF // 128), axis=1)
            k_hi, k_lo = halves(jnp.exp2(cross + src_off + off))
            k_scr[slot, part, :] = k_hi
            k_scr[slot, LEAF + half * 256 : LEAF + (half + 1) * 256, :] = k_lo

    def apply(index, slot):
        code = list_ref[index]
        t, j = code // 8 - start, code % 8
        factor = times_scr[index]
        for half in range(2):
            cols = slice(half * 256, (half + 1) * 256)
            high = w_scr[j, :rows, :]
            both = dot(jnp.concatenate([high, high], axis=1), k_scr[slot, :, cols])
            low = dot(w_scr[j, rows:, :], k_scr[slot, :LEAF, cols])
            o_scr[t, :, cols] = o_scr[t, :, cols] + factor * (both + low)

    @pl.when(count > 0)
    def _():
        block(0, 0)

    def pair(index, carry):
        block(2 * index + 1, 1)
        apply(2 * index, 0)

        @pl.when(2 * index + 1 < count)
        def _():
            block(2 * index + 2, 0)
            apply(2 * index + 1, 1)

        return carry

    lax.fori_loop(0, (count + 1) // 2, pair, jnp.int32(0))
    if nacc:
        t, top = 0, 0
        for ref in outs:
            tall = ref.shape[0]
            for leaf in range(2):
                cols = slice(leaf * LEAF, (leaf + 1) * LEAF)
                ref[:, cols] = o_scr[t + leaf, top : top + tall, :]
            t, top = (t, top + tall) if top + tall < rows else (t + 2, 0)


def near_call(name, msgs, targets, leaves_at, sources, rows, row=0, acc=(), after=()):
    nset = len(sources)
    start, stop = leaves_at
    vmem = pl.BlockSpec(memory_space=pltpu.VMEM)
    operands = [a for _, heads, chunks in sources for a in (*heads, *chunks)]
    scratch = [
        pltpu.VMEM((2 * nset, LEAF, 4 * F), BF),
        pltpu.VMEM((2 * nset, LEAF, 128), F32),
        pltpu.VMEM((2 * nset, 2 * rows, LEAF), BF),
        pltpu.VMEM((stop - start, rows, LEAF), F32),
        pltpu.VMEM((2, 2 * LEAF, LEAF), BF),
        pltpu.SMEM((2 * nset * (stop - start),), F32),
        pltpu.SMEM((2 * nset * (stop - start),), jnp.int32),
        pltpu.SMEM((len(msgs), EXTRA, 128), F32),
        pltpu.SemaphoreType.DMA((len(msgs),)),
    ]
    if not acc:
        out = [jax.ShapeDtypeStruct((stop - start, rows, LEAF), F32)]
        scratch.pop(3)
    else:
        operands += list(acc)
        talls = SIZES if rows == R else (rows,)
        out = [jax.ShapeDtypeStruct((tall, 2 * LEAF), F32) for tall in talls] * ((stop - start) // 2)
    sets = tuple((kind, len(heads) - 1, len(chunks)) for kind, heads, chunks in sources)
    return pl.pallas_call(
        partial(
            near_body, len(msgs) // 2, sets, leaves_at, rows, row, len(acc), len(out)
        ),
        name=name,
        out_shape=out,
        in_specs=[pl.BlockSpec(memory_space=pl.ANY)] * len(msgs)
        + [vmem] * (2 + len(operands))
        + [pl.BlockSpec(memory_space=pl.ANY)] * len(after),
        out_specs=[vmem] * len(out),
        scratch_shapes=scratch,
        compiler_params=pltpu.CompilerParams(vmem_limit_bytes=VMEM_LIMIT),
    )(*msgs, *targets, *operands, *after)


def source_body(pts_ref, side_ref, off_ref):
    for leaf in range(2):
        cols = slice(leaf * LEAF, (leaf + 1) * LEAF)
        side, off = source_side(pts_ref[:F, cols] * SCALE)
        side_ref[leaf] = side
        off_ref[leaf] = jnp.broadcast_to(off, (LEAF, 128))


def source_call(pts):
    vmem = pl.BlockSpec(memory_space=pltpu.VMEM)
    return pl.pallas_call(
        source_body,
        name="source_side",
        out_shape=[
            jax.ShapeDtypeStruct((2, LEAF, 4 * F), BF),
            jax.ShapeDtypeStruct((2, LEAF, 128), F32),
        ],
        in_specs=[vmem],
        out_specs=[vmem, vmem],
        compiler_params=pltpu.CompilerParams(vmem_limit_bytes=VMEM_LIMIT),
    )(pts)


def place():
    helper = lax.axis_index("help")
    return helper // 2, helper % 2, lax.axis_index("leaf")


def share_rows(xs):
    return R // (2 * xs) * SK // (2 * LEAF)


def leaf_body(xs, count_ref, src_ref, pts_in, w_in, interp_in, *refs):
    msgs = refs[: 2 * xs]
    pts_ref, w_ref, interp_ref, scr, sems = refs[2 * xs :]
    copies = [
        pltpu.make_async_copy(pts_in, pts_ref, sems.at[0]),
        pltpu.make_async_copy(w_in, w_ref, sems.at[1]),
        pltpu.make_async_copy(interp_in, interp_ref, sems.at[2]),
    ]
    for copy in copies:
        copy.start()
    x, core, group = place()
    leaves = 4 * xs
    lane = lax.broadcasted_iota(jnp.int32, (1, 128), 1) + (group - 1) * leaves
    times = []
    for leaf in range(2):
        row = jnp.zeros((1, 128), F32)
        for slot in range(src_ref.shape[1]):
            name = jnp.where(slot < count_ref[0, leaf], src_ref[leaf, slot], -1 - 128 * leaves)
            row = row + (lane == name).astype(F32)
        times.append(row)
    times = jnp.concatenate(times + [jnp.zeros((EXTRA - 2, 128), F32)], axis=0)
    for copy in copies:
        copy.wait()
    total = jnp.zeros((R, SK), F32)
    for leaf in range(2):
        total = total + dot3(w_ref[:, leaf * LEAF : (leaf + 1) * LEAF], interp_ref[leaf])
    scr[...] = total
    rows = R // (2 * xs)
    tall = share_rows(xs)
    for n, msg in enumerate(msgs):
        helper = 2 * lax.rem(x + n // 2, xs) + (core if n % 2 == 0 else 1 - core)
        msg[:F, :] = pts_ref[...]
        msg[F : F + EXTRA, :] = jnp.zeros((EXTRA, 2 * LEAF), F32)
        msg[F : F + EXTRA, :128] = times
        for i in range(rows // tall):
            at = pl.multiple_of(helper * rows + i * tall, tall)
            msg[F + EXTRA :, i * SK : (i + 1) * SK] = scr[pl.ds(at, tall), :]


def leaf_call(xs, near_count, near_src, points, weights, interp):
    vmem = pl.BlockSpec(memory_space=pltpu.VMEM)
    smem = pl.BlockSpec(memory_space=pltpu.SMEM)
    anywhere = pl.BlockSpec(memory_space=pl.ANY)
    height = F + EXTRA + share_rows(xs)
    return pl.pallas_call(
        partial(leaf_body, xs),
        name="leaf_up",
        out_shape=[jax.ShapeDtypeStruct((height, 2 * LEAF), F32)] * (2 * xs),
        in_specs=[smem, smem, anywhere, anywhere, anywhere],
        out_specs=[vmem] * (2 * xs),
        scratch_shapes=[
            pltpu.VMEM(points.shape, F32),
            pltpu.VMEM(weights.shape, F32),
            pltpu.VMEM(interp.shape, F32),
            pltpu.VMEM((R, SK), F32),
            pltpu.SemaphoreType.DMA((3,)),
        ],
        compiler_params=pltpu.CompilerParams(vmem_limit_bytes=VMEM_WHOLE),
    )(near_count, near_src, points, weights, interp)


def skel_body(xs, index_ref, *refs):
    msgs, (out_ref, side_ref, off_ref, scr) = refs[:-4], refs[-4:]
    rows = R // (2 * xs)
    tall = share_rows(xs)
    total = jnp.zeros((2 * F, SK), F32)
    value = jnp.zeros((tall, 2 * LEAF), F32)
    spot = lax.broadcasted_iota(jnp.int32, (2 * LEAF, SK), 0)
    x, core, _ = place()
    for b, msg in enumerate(msgs):
        helper = 2 * lax.rem(x + b // 2, xs) + (core if b % 2 == 0 else 1 - core)
        side, off = target_side(msg[:F, :] * SCALE)
        for leaf in range(2):
            part = slice(leaf * LEAF, (leaf + 1) * LEAF)
            side_ref[2 * b + leaf] = side[:, part]
            off_ref[2 * b + leaf] = jnp.broadcast_to(off[:, part], (8, LEAF))
        hot = spot + helper * (2 * LEAF) == index_ref[...]
        total = total + dot(side[: 2 * F], hot.astype(F32).astype(BF))
        value = value + msg[F + EXTRA :, :]
    scr[...] = total[:F] + total[F:]
    out_ref[:HALF, :] = scr[pl.ds(pl.multiple_of(core * HALF, HALF), HALF), :]
    for i in range(rows // tall):
        out_ref[HALF + i * tall : HALF + (i + 1) * tall, :] = value[:, i * SK : (i + 1) * SK]


def skel_call(xs, index, msgs):
    rows = R // (2 * xs)
    leaves = 2 * len(msgs)
    vmem = pl.BlockSpec(memory_space=pltpu.VMEM)
    payload, *targets = pl.pallas_call(
        partial(skel_body, xs),
        name="skeleton",
        out_shape=[
            jax.ShapeDtypeStruct((HALF + rows, SK), F32),
            jax.ShapeDtypeStruct((leaves, 4 * F, LEAF), BF),
            jax.ShapeDtypeStruct((leaves, 8, LEAF), F32),
        ],
        in_specs=[vmem] * (1 + len(msgs)),
        out_specs=[vmem] * 3,
        scratch_shapes=[pltpu.VMEM((F, SK), F32)],
        compiler_params=pltpu.CompilerParams(vmem_limit_bytes=VMEM_LIMIT),
        cost_estimate=pl.CostEstimate(
            flops=5_000_000_000, bytes_accessed=8_000_000, transcendentals=0
        ),
    )(index, *msgs)
    return payload, targets


def stack_body(*refs):
    for n, ref in enumerate(refs[:-1]):
        refs[-1][n] = ref[...]


def stack_call(pieces):
    vmem = pl.BlockSpec(memory_space=pltpu.VMEM)
    return pl.pallas_call(
        stack_body,
        name="stack",
        out_shape=jax.ShapeDtypeStruct((len(pieces), *pieces[0].shape), F32),
        in_specs=[vmem] * len(pieces),
        out_specs=vmem,
        compiler_params=pltpu.CompilerParams(vmem_limit_bytes=VMEM_LIMIT),
    )(*pieces)


def points_body(alike_ref, beside_ref, out_ref):
    count = alike_ref.shape[0]
    for n in range(count):
        out_ref[n] = alike_ref[n, :HALF, :]
        out_ref[count + n] = beside_ref[n, :HALF, :]


def points_call(alike, beside):
    vmem = pl.BlockSpec(memory_space=pltpu.VMEM)
    return pl.pallas_call(
        points_body,
        name="points_of",
        out_shape=jax.ShapeDtypeStruct((2 * alike.shape[0], HALF, SK), F32),
        in_specs=[vmem, vmem],
        out_specs=vmem,
        compiler_params=pltpu.CompilerParams(vmem_limit_bytes=VMEM_LIMIT),
    )(alike, beside)


def upper_start(level, groups):
    return sum((groups >> step for step in range(1, level)))


def list_start(level, groups):
    return sum((groups >> step for step in range(level)))


def far_body(groups, rows, far_ref, node_ref, transfer_ref, alike_ref, beside_ref, mate_ref, *refs):
    out_ref, p_scr, u_scr, f_scr = refs[-4:]
    levels = groups.bit_length() - 1
    group = place()[2]
    start = [list_start(level, groups) for level in range(levels)]
    core = place()[1]
    here = pl.ds(pl.multiple_of(core * HALF, HALF), HALF)
    there = pl.ds(pl.multiple_of((1 - core) * HALF, HALF), HALF)
    for n in range(groups):
        node = group ^ (2 * (n % (groups // 2)) + n // (groups // 2))
        part = (alike_ref, beside_ref)[n // (groups // 2)]
        p_scr[node, here, :] = part[n % (groups // 2), :HALF, :]
        p_scr[node, there, :] = mate_ref[n]
        u_scr[node] = part[n % (groups // 2), HALF:, :]
    spot = lax.broadcasted_iota(jnp.int32, (2 * SK, SK), 0)
    for level in range(1, levels):
        for n in range(groups >> level):
            row = upper_start(level, groups) + n
            left = start[level - 1] + 2 * n
            hot = (spot == node_ref[row : row + 1, :]).astype(F32).astype(BF)
            hi, lo = halves(jnp.concatenate([p_scr[left], p_scr[left + 1]], axis=1))
            both = dot(jnp.concatenate([hi, lo], axis=0), hot)
            p_scr[start[level] + n] = both[:F] + both[F:]
            vals = jnp.concatenate([u_scr[left], u_scr[left + 1]], axis=1)
            u_scr[start[level] + n] = dot3(vals, transfer_ref[row])
    for level in range(levels):
        node = group >> level
        side, off = target_side(p_scr[start[level] + node])
        f_scr[level] = jnp.zeros((rows, SK), F32)

        def one(n, carry, level=level, node=node, side=side, off=off):
            hits = jnp.int32(0)
            for slot in range(FL):
                hits = hits + (far_ref[slot, start[level] + node] == n).astype(jnp.int32)

            @pl.when(hits > 0)
            def _():
                src, src_off = source_side(p_scr[start[level] + n])
                block = jnp.exp2(dot(src, side) + src_off + off)
                term = dot3(u_scr[start[level] + n], block)
                f_scr[level] = f_scr[level] + hits.astype(F32) * term

            return carry

        lax.fori_loop(0, groups >> level, one, jnp.int32(0))
    local = f_scr[levels - 1]
    for level in range(levels - 1, 0, -1):
        row = upper_start(level, groups) + (group >> level)
        bit = (group >> (level - 1)) & 1
        matrix = transfer_ref[row, pl.ds(pl.multiple_of(bit * SK, SK), SK), :]
        local = f_scr[level - 1] + dot3(local, matrix, dot_t)
    out_ref[...] = local


def far_call(groups, far_nodes, skel_node, transfer, alike, beside, mate, after):
    rows = alike.shape[1] - HALF
    vmem = pl.BlockSpec(memory_space=pltpu.VMEM)
    smem = pl.BlockSpec(memory_space=pltpu.SMEM)
    nodes = 2 * groups
    return pl.pallas_call(
        partial(far_body, groups, rows),
        name="far",
        out_shape=jax.ShapeDtypeStruct((rows, SK), F32),
        in_specs=[smem, vmem, vmem, vmem, vmem, vmem]
        + [pl.BlockSpec(memory_space=pl.ANY)] * len(after),
        out_specs=vmem,
        scratch_shapes=[
            pltpu.VMEM((nodes, F, SK), F32),
            pltpu.VMEM((nodes, rows, SK), F32),
            pltpu.VMEM((groups.bit_length(), rows, SK), F32),
        ],
        compiler_params=pltpu.CompilerParams(vmem_limit_bytes=VMEM_LIMIT),
    )(far_nodes.T, skel_node, transfer, alike, beside, mate, *after)


def final_body(xs, interp_ref, *refs):
    values, sums = refs[:xs], refs[xs:-2]
    out_ref, v_scr = refs[-2:]
    rows = R // (2 * xs)
    x, core, _ = place()
    for dx, ref in enumerate(values):
        for dc in range(2):
            helper = 2 * lax.rem(x + dx, xs) + (core if dc == 0 else 1 - core)
            v_scr[pl.ds(pl.multiple_of(helper * rows, rows), rows), :] = ref[dc]
    value = v_scr[...]
    for leaf in range(2):
        cols = slice(leaf * LEAF, (leaf + 1) * LEAF)
        total = dot3(value, interp_ref[leaf], dot_t)
        for c in range(2):
            part = slice(c * SIZES[0], SIZES[0] + c * SIZES[1])
            out_ref[part, cols] = total[part] + sums[c][:, cols] + sums[2 + c][:, cols]


def add_body(count, *refs):
    for n, out_ref in enumerate(refs[-(len(refs) // (count + 1)) :]):
        total = refs[n * count][...]
        for ref in refs[n * count + 1 : (n + 1) * count]:
            total = total + ref[...]
        out_ref[...] = total


def add_call(*sums):
    vmem = pl.BlockSpec(memory_space=pltpu.VMEM)
    operands = [value for terms in sums for value in terms]
    return pl.pallas_call(
        partial(add_body, len(sums[0])),
        name="add_parts",
        out_shape=[jax.ShapeDtypeStruct(terms[0].shape, F32) for terms in sums],
        in_specs=[vmem] * len(operands),
        out_specs=[vmem] * len(sums),
        compiler_params=pltpu.CompilerParams(vmem_limit_bytes=VMEM_LIMIT),
    )(*operands)


def final_call(xs, interp, home, mate, values):
    vmem = pl.BlockSpec(memory_space=pltpu.VMEM)
    return pl.pallas_call(
        partial(final_body, xs),
        name="join",
        out_shape=jax.ShapeDtypeStruct((R, 2 * LEAF), F32),
        in_specs=[vmem] * (1 + xs + 4),
        out_specs=vmem,
        scratch_shapes=[pltpu.VMEM((R, SK), F32)],
        compiler_params=pltpu.CompilerParams(vmem_limit_bytes=VMEM_LIMIT),
    )(interp, *values, *home, *mate)


def help_pairs(xs, dx, dc):
    return [
        (2 * ((x + dx) % xs) + (core ^ dc), 2 * x + core) for x in range(xs) for core in range(2)
    ]


def shards(
    points, weights, interp, transfer, near_count, near_src, skel_group, skel_node, far_nodes
):
    helpers = lax.axis_size("help")
    groups = lax.axis_size("leaf")
    xs = helpers // 2
    def from_help(value, dx, dc):
        return lax.ppermute(value, "help", help_pairs(xs, dx, dc))

    def to_help(value, dx):
        return lax.ppermute(value, "help", help_pairs(xs, -dx, 0))

    def together(*values):
        return lax.optimization_barrier(values)

    beside = [(i, i ^ 1) for i in range(groups)]
    across = [(i, i + 2) for i in range(0, groups - 2, 2)]
    across += [(i, i - 2) for i in range(3, groups, 2)]
    order = [(dx, dc) for dx in range(xs) for dc in range(2)]

    cut = SIZES[0]
    pts_y = lax.ppermute(points, "leaf", beside)
    w_y = [lax.ppermute(chunk, "leaf", beside) for chunk in (weights[:cut], weights[cut:])]
    sent = leaf_call(xs, near_count, near_src, points, weights, interp)
    got = [
        lax.ppermute(sent[n], "help", help_pairs(xs, -dx, dc))
        for n, (dx, dc) in enumerate(order)
        if n
    ]
    pts_z = lax.ppermute(pts_y, "leaf", across)
    pts_z, w_y[0], got[0] = together(pts_z, w_y[0], got[0])
    w_z = [lax.ppermute(w_y[0], "leaf", across)]
    msgs = [sent[0]] + [got[order.index((-dx % xs, dc)) - 1] for dx, dc in order[1:]]
    payload, targets = skel_call(xs, skel_group, msgs)
    pieces = [payload]
    for mask in range(2, groups, 2):
        pieces.append(lax.ppermute(payload, "leaf", [(i, i ^ mask) for i in range(groups)]))

    payload, w_y[1] = together(payload, w_y[1])
    every, away, home = (0, 2 * helpers), (4, 2 * helpers), (0, 4)
    (own,) = near_call("near_own", msgs, targets, every, [("own", (points,), [weights])], R)
    w_z.append(lax.ppermute(w_y[1], "leaf", across))
    pair_src = ("pair", (pts_y,), w_y)
    (pair,) = near_call("near_pair", msgs, targets, away, [pair_src], R, after=[own])
    z_side = source_call(pts_z)
    sums, part = [], [pair]
    for c in range(2):
        if c == 1:
            pieces, part = together(pieces, part)
            alike = stack_call(pieces)
            side = lax.ppermute(alike, "leaf", beside)
            part = [alike]
        part = near_call(
            "near_next_away", msgs, targets, away, [("next", z_side, w_z[c : c + 1])],
            SIZES[c], c * SIZES[0], [own, pair], part[:1],
        )
        kept, given = part[::2], part[1::2]
        sums.append((kept, [from_help(value, 0, 1) for value in given]))
    parts = []
    for c in range(2):
        kept, mates = sums[c]
        both = add_call(*zip(kept, mates))
        parts.append([to_help(value, dx + 1) for dx, value in enumerate(both)])
    sources = [pair_src, ("next", z_side, w_z)]
    home = near_call("near_home", msgs, targets, home, sources, R, 0, [own], both[:1])
    swapped = from_help(points_call(alike, side), 0, 1)
    v_own = far_call(groups, far_nodes, skel_node, transfer, alike, side, swapped, home[:1])
    v_pair = stack_call([v_own, from_help(v_own, 0, 1)])
    values = [v_pair] + [from_help(v_pair, dx, 0) for dx in range(1, xs)]
    mate = [from_help(value, 0, 1) for value in home[2:]]
    mine = add_call(*[[home[c], *parts[c]] for c in range(2)])
    return final_call(xs, interp, mine, mate, values)


def solution(mesh):
    placed = (
        P(None, ("leaf", "help")),
        P(None, ("leaf", "help")),
        P(("leaf", "help"), None, None),
        P(),
        P("leaf", "help"),
        P(("leaf", "help"), None),
        P("leaf", None),
        P(),
        P(),
    )
    return jax.shard_map(
        shards, mesh=mesh, in_specs=placed, out_specs=P(None, ("leaf", "help")), check_vma=False
    )
```

```python
import math
from functools import partial

import jax
import jax.numpy as jnp
from jax import lax
from jax.experimental import pallas as pl
from jax.experimental.pallas import tpu as pltpu
from jax.sharding import PartitionSpec as P

F = 64
R = 256
LEAF = 512
SK = 256
FL = 4
EXTRA = 8
HALF = F // 2
SIZES = (128, 128)

BF = jnp.bfloat16
F32 = jnp.float32
LOG2E = 1.0 / math.log(2.0)
SCALE = math.sqrt(0.5 * LOG2E)
BIAS = 0.0625 * F * LOG2E
VMEM_LIMIT = 24 * 1024 * 1024
VMEM_WHOLE = 64 * 1024 * 1024


def dot(a, b):
    return jnp.dot(a, b, preferred_element_type=F32)


def dot_t(a, b):
    return lax.dot_general(a, b, (((1,), (1,)), ((), ())), preferred_element_type=F32)


def halves(x):
    hi = x.astype(BF)
    lo = (x - hi.astype(F32)).astype(BF)
    return hi, lo


def dot3(a, b, mul=dot):
    a_hi, a_lo = halves(a)
    b_hi, b_lo = halves(b)
    return mul(a_hi, b_hi) + mul(a_lo, b_hi) + mul(a_hi, b_lo)


def target_side(x):
    hi, lo = halves(x)
    both = hi.astype(F32) + lo.astype(F32)
    off = BIAS - 0.5 * jnp.sum(both * both, axis=0, keepdims=True)
    return jnp.concatenate([hi, lo, hi, lo], axis=0), off


def source_side(x):
    xt = x.T
    hi, lo = halves(xt)
    both = hi.astype(F32) + lo.astype(F32)
    off = BIAS - 0.5 * jnp.sum(both * both, axis=1, keepdims=True)
    return jnp.concatenate([hi, hi, lo, lo], axis=1), off


def near_body(
    xs, sets, leaves_at, rows, row, nacc, nout, *refs
):
    nset = len(sets)
    start, stop = leaves_at
    msgs, (t_ref, tb_ref), refs = refs[: 2 * xs], refs[2 * xs : 2 * xs + 2], refs[2 * xs + 2 :]
    if nacc:
        s_scr, sb_scr, w_scr, o_scr, k_scr, times_scr, list_ref, times_ref, sems = refs[-9:]
        outs = refs[-9 - nout : -9]
    else:
        o_scr, s_scr, sb_scr, w_scr, k_scr, times_scr, list_ref, times_ref, sems = refs[-9:]
    copies = [
        pltpu.make_async_copy(msgs[b].at[F : F + EXTRA, :128], times_ref.at[b], sems.at[b])
        for b in range(start // 2, stop // 2)
    ]
    for copy in copies:
        copy.start()
    at = 0
    for k, (_, ready, chunks) in enumerate(sets):
        heads = refs[at : at + 1 + ready]
        parts = refs[at + 1 + ready : at + 1 + ready + chunks]
        at += 1 + ready + chunks
        for leaf in range(2):
            cols = slice(leaf * LEAF, (leaf + 1) * LEAF)
            j = 2 * k + leaf
            if ready:
                s_scr[j] = heads[0][leaf]
                sb_scr[j] = heads[1][leaf]
            else:
                side, off = source_side(heads[0][:F, cols] * SCALE)
                s_scr[j] = side
                sb_scr[j] = jnp.broadcast_to(off, (LEAF, 128))
            top = 0
            for part in parts:
                hi, lo = halves(part[:, cols])
                w_scr[j, top : top + part.shape[0], :] = hi
                w_scr[j, rows + top : rows + top + part.shape[0], :] = lo
                top += part.shape[0]
    for t in range(start, stop):
        if nacc:
            o_scr[t - start] = sum(
                ref[t - (4 * xs - ref.shape[0]), row : row + rows, :] for ref in refs[at : at + nacc]
            )
        else:
            o_scr[t - start] = jnp.zeros((rows, LEAF), F32)

    x, core, group = place()
    leaves = 4 * xs
    odd = group % 2
    column = []
    for kind, _, _ in sets:
        relative = {"own": 1, "pair": 2 - 2 * odd, "next": 2 * odd}[kind]
        column.append(relative * leaves + 2 * (2 * x + core))

    for copy in copies:
        copy.wait()
    count = jnp.int32(0)
    list_ref[0] = 0
    for t in range(start, stop):
        for j in range(2 * nset):
            times = times_ref[t // 2, t % 2, column[j // 2] + j % 2]

            @pl.when(times > 0)
            def _(count=count, t=t, j=j, times=times):
                list_ref[count] = t * 8 + j
                times_scr[count] = times

            count = count + (times > 0).astype(jnp.int32)

    def block(index, slot):
        code = list_ref[jnp.minimum(index, jnp.maximum(count - 1, 0))]
        t, j = code // 8, code % 8
        side = t_ref[t]
        off = tb_ref[t][:1, :]
        for half in range(2):
            part = slice(half * 256, (half + 1) * 256)
            cross = dot(s_scr[j, part, :], side)
            src_off = sb_scr[j, part, :]
            src_off = jnp.concatenate([src_off] * (LEAF // 128), axis=1)
            k_hi, k_lo = halves(jnp.exp2(cross + src_off + off))
            k_scr[slot, part, :] = k_hi
            k_scr[slot, LEAF + half * 256 : LEAF + (half + 1) * 256, :] = k_lo

    def apply(index, slot):
        code = list_ref[index]
        t, j = code // 8 - start, code % 8
        factor = times_scr[index]
        for half in range(2):
            cols = slice(half * 256, (half + 1) * 256)
            both = dot(w_scr[j], k_scr[slot, :LEAF, cols])
            low = dot(w_scr[j, :rows, :], k_scr[slot, LEAF:, cols])
            o_scr[t, :, cols] = o_scr[t, :, cols] + factor * (both[:rows] + both[rows:] + low)

    @pl.when(count > 0)
    def _():
        block(0, 0)

    def pair(index, carry):
        block(2 * index + 1, 1)
        apply(2 * index, 0)

        @pl.when(2 * index + 1 < count)
        def _():
            block(2 * index + 2, 0)
            apply(2 * index + 1, 1)

        return carry

    lax.fori_loop(0, (count + 1) // 2, pair, jnp.int32(0))
    if nacc:
        t, top = 0, 0
        for ref in outs:
            tall = ref.shape[0]
            for leaf in range(2):
                cols = slice(leaf * LEAF, (leaf + 1) * LEAF)
                ref[:, cols] = o_scr[t + leaf, top : top + tall, :]
            t, top = (t, top + tall) if top + tall < rows else (t + 2, 0)


def near_call(name, msgs, targets, leaves_at, sources, rows, row=0, acc=(), after=()):
    nset = len(sources)
    start, stop = leaves_at
    vmem = pl.BlockSpec(memory_space=pltpu.VMEM)
    operands = [a for _, heads, chunks in sources for a in (*heads, *chunks)]
    scratch = [
        pltpu.VMEM((2 * nset, LEAF, 4 * F), BF),
        pltpu.VMEM((2 * nset, LEAF, 128), F32),
        pltpu.VMEM((2 * nset, 2 * rows, LEAF), BF),
        pltpu.VMEM((stop - start, rows, LEAF), F32),
        pltpu.VMEM((2, 2 * LEAF, LEAF), BF),
        pltpu.SMEM((2 * nset * (stop - start),), F32),
        pltpu.SMEM((2 * nset * (stop - start),), jnp.int32),
        pltpu.SMEM((len(msgs), EXTRA, 128), F32),
        pltpu.SemaphoreType.DMA((len(msgs),)),
    ]
    if not acc:
        out = [jax.ShapeDtypeStruct((stop - start, rows, LEAF), F32)]
        scratch.pop(3)
    else:
        operands += list(acc)
        talls = SIZES if rows == R else (rows,)
        out = [jax.ShapeDtypeStruct((tall, 2 * LEAF), F32) for tall in talls] * ((stop - start) // 2)
    sets = tuple((kind, len(heads) - 1, len(chunks)) for kind, heads, chunks in sources)
    return pl.pallas_call(
        partial(
            near_body, len(msgs) // 2, sets, leaves_at, rows, row, len(acc), len(out)
        ),
        name=name,
        out_shape=out,
        in_specs=[pl.BlockSpec(memory_space=pl.ANY)] * len(msgs)
        + [vmem] * (2 + len(operands))
        + [pl.BlockSpec(memory_space=pl.ANY)] * len(after),
        out_specs=[vmem] * len(out),
        scratch_shapes=scratch,
        compiler_params=pltpu.CompilerParams(vmem_limit_bytes=VMEM_LIMIT),
    )(*msgs, *targets, *operands, *after)


def source_body(pts_ref, side_ref, off_ref):
    for leaf in range(2):
        cols = slice(leaf * LEAF, (leaf + 1) * LEAF)
        side, off = source_side(pts_ref[:F, cols] * SCALE)
        side_ref[leaf] = side
        off_ref[leaf] = jnp.broadcast_to(off, (LEAF, 128))


def source_call(pts):
    vmem = pl.BlockSpec(memory_space=pltpu.VMEM)
    return pl.pallas_call(
        source_body,
        name="source_side",
        out_shape=[
            jax.ShapeDtypeStruct((2, LEAF, 4 * F), BF),
            jax.ShapeDtypeStruct((2, LEAF, 128), F32),
        ],
        in_specs=[vmem],
        out_specs=[vmem, vmem],
        compiler_params=pltpu.CompilerParams(vmem_limit_bytes=VMEM_LIMIT),
    )(pts)


def place():
    helper = lax.axis_index("help")
    return helper // 2, helper % 2, lax.axis_index("leaf")


def share_rows(xs):
    return R // (2 * xs) * SK // (2 * LEAF)


def leaf_body(xs, count_ref, src_ref, pts_in, w_in, interp_in, *refs):
    msgs = refs[: 2 * xs]
    pts_ref, w_ref, interp_ref, scr, sems = refs[2 * xs :]
    copies = [
        pltpu.make_async_copy(pts_in, pts_ref, sems.at[0]),
        pltpu.make_async_copy(w_in, w_ref, sems.at[1]),
        pltpu.make_async_copy(interp_in, interp_ref, sems.at[2]),
    ]
    for copy in copies:
        copy.start()
    x, core, group = place()
    leaves = 4 * xs
    lane = lax.broadcasted_iota(jnp.int32, (1, 128), 1) + (group - 1) * leaves
    times = []
    for leaf in range(2):
        row = jnp.zeros((1, 128), F32)
        for slot in range(src_ref.shape[1]):
            name = jnp.where(slot < count_ref[0, leaf], src_ref[leaf, slot], -1 - 128 * leaves)
            row = row + (lane == name).astype(F32)
        times.append(row)
    times = jnp.concatenate(times + [jnp.zeros((EXTRA - 2, 128), F32)], axis=0)
    for copy in copies:
        copy.wait()
    total = jnp.zeros((R, SK), F32)
    for leaf in range(2):
        total = total + dot3(w_ref[:, leaf * LEAF : (leaf + 1) * LEAF], interp_ref[leaf])
    scr[...] = total
    rows = R // (2 * xs)
    tall = share_rows(xs)
    for n, msg in enumerate(msgs):
        helper = 2 * lax.rem(x + n // 2, xs) + (core if n % 2 == 0 else 1 - core)
        msg[:F, :] = pts_ref[...]
        msg[F : F + EXTRA, :] = jnp.zeros((EXTRA, 2 * LEAF), F32)
        msg[F : F + EXTRA, :128] = times
        for i in range(rows // tall):
            at = pl.multiple_of(helper * rows + i * tall, tall)
            msg[F + EXTRA :, i * SK : (i + 1) * SK] = scr[pl.ds(at, tall), :]


def leaf_call(xs, near_count, near_src, points, weights, interp):
    vmem = pl.BlockSpec(memory_space=pltpu.VMEM)
    smem = pl.BlockSpec(memory_space=pltpu.SMEM)
    anywhere = pl.BlockSpec(memory_space=pl.ANY)
    height = F + EXTRA + share_rows(xs)
    return pl.pallas_call(
        partial(leaf_body, xs),
        name="leaf_up",
        out_shape=[jax.ShapeDtypeStruct((height, 2 * LEAF), F32)] * (2 * xs),
        in_specs=[smem, smem, anywhere, anywhere, anywhere],
        out_specs=[vmem] * (2 * xs),
        scratch_shapes=[
            pltpu.VMEM(points.shape, F32),
            pltpu.VMEM(weights.shape, F32),
            pltpu.VMEM(interp.shape, F32),
            pltpu.VMEM((R, SK), F32),
            pltpu.SemaphoreType.DMA((3,)),
        ],
        compiler_params=pltpu.CompilerParams(vmem_limit_bytes=VMEM_WHOLE),
    )(near_count, near_src, points, weights, interp)


def skel_body(xs, index_ref, *refs):
    msgs, (out_ref, side_ref, off_ref, scr) = refs[:-4], refs[-4:]
    rows = R // (2 * xs)
    tall = share_rows(xs)
    total = jnp.zeros((2 * F, SK), F32)
    value = jnp.zeros((tall, 2 * LEAF), F32)
    spot = lax.broadcasted_iota(jnp.int32, (2 * LEAF, SK), 0)
    x, core, _ = place()
    for b, msg in enumerate(msgs):
        helper = 2 * lax.rem(x + b // 2, xs) + (core if b % 2 == 0 else 1 - core)
        side, off = target_side(msg[:F, :] * SCALE)
        for leaf in range(2):
            part = slice(leaf * LEAF, (leaf + 1) * LEAF)
            side_ref[2 * b + leaf] = side[:, part]
            off_ref[2 * b + leaf] = jnp.broadcast_to(off[:, part], (8, LEAF))
        hot = spot + helper * (2 * LEAF) == index_ref[...]
        total = total + dot(side[: 2 * F], hot.astype(F32).astype(BF))
        value = value + msg[F + EXTRA :, :]
    scr[...] = total[:F] + total[F:]
    out_ref[:HALF, :] = scr[pl.ds(pl.multiple_of(core * HALF, HALF), HALF), :]
    for i in range(rows // tall):
        out_ref[HALF + i * tall : HALF + (i + 1) * tall, :] = value[:, i * SK : (i + 1) * SK]


def skel_call(xs, index, msgs):
    rows = R // (2 * xs)
    leaves = 2 * len(msgs)
    vmem = pl.BlockSpec(memory_space=pltpu.VMEM)
    payload, *targets = pl.pallas_call(
        partial(skel_body, xs),
        name="skeleton",
        out_shape=[
            jax.ShapeDtypeStruct((HALF + rows, SK), F32),
            jax.ShapeDtypeStruct((leaves, 4 * F, LEAF), BF),
            jax.ShapeDtypeStruct((leaves, 8, LEAF), F32),
        ],
        in_specs=[vmem] * (1 + len(msgs)),
        out_specs=[vmem] * 3,
        scratch_shapes=[pltpu.VMEM((F, SK), F32)],
        compiler_params=pltpu.CompilerParams(vmem_limit_bytes=VMEM_LIMIT),
        cost_estimate=pl.CostEstimate(
            flops=5_000_000_000, bytes_accessed=8_000_000, transcendentals=0
        ),
    )(index, *msgs)
    return payload, targets


def stack_body(*refs):
    for n, ref in enumerate(refs[:-1]):
        refs[-1][n] = ref[...]


def stack_call(pieces):
    vmem = pl.BlockSpec(memory_space=pltpu.VMEM)
    return pl.pallas_call(
        stack_body,
        name="stack",
        out_shape=jax.ShapeDtypeStruct((len(pieces), *pieces[0].shape), F32),
        in_specs=[vmem] * len(pieces),
        out_specs=vmem,
        compiler_params=pltpu.CompilerParams(vmem_limit_bytes=VMEM_LIMIT),
    )(*pieces)


def points_body(alike_ref, beside_ref, out_ref):
    count = alike_ref.shape[0]
    for n in range(count):
        out_ref[n] = alike_ref[n, :HALF, :]
        out_ref[count + n] = beside_ref[n, :HALF, :]


def points_call(alike, beside):
    vmem = pl.BlockSpec(memory_space=pltpu.VMEM)
    return pl.pallas_call(
        points_body,
        name="points_of",
        out_shape=jax.ShapeDtypeStruct((2 * alike.shape[0], HALF, SK), F32),
        in_specs=[vmem, vmem],
        out_specs=vmem,
        compiler_params=pltpu.CompilerParams(vmem_limit_bytes=VMEM_LIMIT),
    )(alike, beside)


def upper_start(level, groups):
    return sum((groups >> step for step in range(1, level)))


def list_start(level, groups):
    return sum((groups >> step for step in range(level)))


def far_body(groups, rows, far_ref, node_ref, transfer_ref, alike_ref, beside_ref, mate_ref, *refs):
    out_ref, p_scr, u_scr, f_scr = refs[-4:]
    levels = groups.bit_length() - 1
    group = place()[2]
    start = [list_start(level, groups) for level in range(levels)]
    core = place()[1]
    here = pl.ds(pl.multiple_of(core * HALF, HALF), HALF)
    there = pl.ds(pl.multiple_of((1 - core) * HALF, HALF), HALF)
    for n in range(groups):
        node = group ^ (2 * (n % (groups // 2)) + n // (groups // 2))
        part = (alike_ref, beside_ref)[n // (groups // 2)]
        p_scr[node, here, :] = part[n % (groups // 2), :HALF, :]
        p_scr[node, there, :] = mate_ref[n]
        u_scr[node] = part[n % (groups // 2), HALF:, :]
    spot = lax.broadcasted_iota(jnp.int32, (2 * SK, SK), 0)
    for level in range(1, levels):
        for n in range(groups >> level):
            row = upper_start(level, groups) + n
            left = start[level - 1] + 2 * n
            hot = (spot == node_ref[row : row + 1, :]).astype(F32).astype(BF)
            hi, lo = halves(jnp.concatenate([p_scr[left], p_scr[left + 1]], axis=1))
            both = dot(jnp.concatenate([hi, lo], axis=0), hot)
            p_scr[start[level] + n] = both[:F] + both[F:]
            vals = jnp.concatenate([u_scr[left], u_scr[left + 1]], axis=1)
            u_scr[start[level] + n] = dot3(vals, transfer_ref[row])
    for level in range(levels):
        node = group >> level
        side, off = target_side(p_scr[start[level] + node])
        f_scr[level] = jnp.zeros((rows, SK), F32)

        def one(n, carry, level=level, node=node, side=side, off=off):
            hits = jnp.int32(0)
            for slot in range(FL):
                hits = hits + (far_ref[slot, start[level] + node] == n).astype(jnp.int32)

            @pl.when(hits > 0)
            def _():
                src, src_off = source_side(p_scr[start[level] + n])
                block = jnp.exp2(dot(src, side) + src_off + off)
                term = dot3(u_scr[start[level] + n], block)
                f_scr[level] = f_scr[level] + hits.astype(F32) * term

            return carry

        lax.fori_loop(0, groups >> level, one, jnp.int32(0))
    local = f_scr[levels - 1]
    for level in range(levels - 1, 0, -1):
        row = upper_start(level, groups) + (group >> level)
        bit = (group >> (level - 1)) & 1
        matrix = transfer_ref[row, pl.ds(pl.multiple_of(bit * SK, SK), SK), :]
        local = f_scr[level - 1] + dot3(local, matrix, dot_t)
    out_ref[...] = local


def far_call(groups, far_nodes, skel_node, transfer, alike, beside, mate, after):
    rows = alike.shape[1] - HALF
    vmem = pl.BlockSpec(memory_space=pltpu.VMEM)
    smem = pl.BlockSpec(memory_space=pltpu.SMEM)
    nodes = 2 * groups
    return pl.pallas_call(
        partial(far_body, groups, rows),
        name="far",
        out_shape=jax.ShapeDtypeStruct((rows, SK), F32),
        in_specs=[smem, vmem, vmem, vmem, vmem, vmem]
        + [pl.BlockSpec(memory_space=pl.ANY)] * len(after),
        out_specs=vmem,
        scratch_shapes=[
            pltpu.VMEM((nodes, F, SK), F32),
            pltpu.VMEM((nodes, rows, SK), F32),
            pltpu.VMEM((groups.bit_length(), rows, SK), F32),
        ],
        compiler_params=pltpu.CompilerParams(vmem_limit_bytes=VMEM_LIMIT),
    )(far_nodes.T, skel_node, transfer, alike, beside, mate, *after)


def final_body(xs, interp_ref, *refs):
    values, sums = refs[:xs], refs[xs:-2]
    out_ref, v_scr = refs[-2:]
    rows = R // (2 * xs)
    x, core, _ = place()
    for dx, ref in enumerate(values):
        for dc in range(2):
            helper = 2 * lax.rem(x + dx, xs) + (core if dc == 0 else 1 - core)
            v_scr[pl.ds(pl.multiple_of(helper * rows, rows), rows), :] = ref[dc]
    value = v_scr[...]
    for leaf in range(2):
        cols = slice(leaf * LEAF, (leaf + 1) * LEAF)
        total = dot3(value, interp_ref[leaf], dot_t)
        for c in range(2):
            part = slice(c * SIZES[0], SIZES[0] + c * SIZES[1])
            out_ref[part, cols] = total[part] + sums[c][:, cols] + sums[2 + c][:, cols]


def add_body(count, *refs):
    for n, out_ref in enumerate(refs[-(len(refs) // (count + 1)) :]):
        total = refs[n * count][...]
        for ref in refs[n * count + 1 : (n + 1) * count]:
            total = total + ref[...]
        out_ref[...] = total


def add_call(*sums):
    vmem = pl.BlockSpec(memory_space=pltpu.VMEM)
    operands = [value for terms in sums for value in terms]
    return pl.pallas_call(
        partial(add_body, len(sums[0])),
        name="add_parts",
        out_shape=[jax.ShapeDtypeStruct(terms[0].shape, F32) for terms in sums],
        in_specs=[vmem] * len(operands),
        out_specs=[vmem] * len(sums),
        compiler_params=pltpu.CompilerParams(vmem_limit_bytes=VMEM_LIMIT),
    )(*operands)


def final_call(xs, interp, home, mate, values):
    vmem = pl.BlockSpec(memory_space=pltpu.VMEM)
    return pl.pallas_call(
        partial(final_body, xs),
        name="join",
        out_shape=jax.ShapeDtypeStruct((R, 2 * LEAF), F32),
        in_specs=[vmem] * (1 + xs + 4),
        out_specs=vmem,
        scratch_shapes=[pltpu.VMEM((R, SK), F32)],
        compiler_params=pltpu.CompilerParams(vmem_limit_bytes=VMEM_LIMIT),
    )(interp, *values, *home, *mate)


def help_pairs(xs, dx, dc):
    return [
        (2 * ((x + dx) % xs) + (core ^ dc), 2 * x + core) for x in range(xs) for core in range(2)
    ]


def shards(
    points, weights, interp, transfer, near_count, near_src, skel_group, skel_node, far_nodes
):
    helpers = lax.axis_size("help")
    groups = lax.axis_size("leaf")
    xs = helpers // 2
    def from_help(value, dx, dc):
        return lax.ppermute(value, "help", help_pairs(xs, dx, dc))

    def to_help(value, dx):
        return lax.ppermute(value, "help", help_pairs(xs, -dx, 0))

    def together(*values):
        return lax.optimization_barrier(values)

    beside = [(i, i ^ 1) for i in range(groups)]
    across = [(i, i + 2) for i in range(0, groups - 2, 2)]
    across += [(i, i - 2) for i in range(3, groups, 2)]
    order = [(dx, dc) for dx in range(xs) for dc in range(2)]

    cut = SIZES[0]
    pts_y = lax.ppermute(points, "leaf", beside)
    w_y = [lax.ppermute(chunk, "leaf", beside) for chunk in (weights[:cut], weights[cut:])]
    sent = leaf_call(xs, near_count, near_src, points, weights, interp)
    got = [
        lax.ppermute(sent[n], "help", help_pairs(xs, -dx, dc))
        for n, (dx, dc) in enumerate(order)
        if n
    ]
    pts_z = lax.ppermute(pts_y, "leaf", across)
    sides = [source_call(points), source_call(pts_y)]
    pts_z, w_y[0], got[0], (own_side, pair_side) = together(pts_z, w_y[0], got[0], sides)
    w_z = [lax.ppermute(w_y[0], "leaf", across)]
    msgs = [sent[0]] + [got[order.index((-dx % xs, dc)) - 1] for dx, dc in order[1:]]
    payload, targets = skel_call(xs, skel_group, msgs)
    pieces = [payload]
    for mask in range(2, groups, 2):
        pieces.append(lax.ppermute(payload, "leaf", [(i, i ^ mask) for i in range(groups)]))

    payload, w_y[1] = together(payload, w_y[1])
    every, away, home = (0, 2 * helpers), (4, 2 * helpers), (0, 4)
    (own,) = near_call("near_own", msgs, targets, every, [("own", own_side, [weights])], R)
    w_z.append(lax.ppermute(w_y[1], "leaf", across))
    pair_src = ("pair", pair_side, w_y)
    (pair,) = near_call("near_pair", msgs, targets, away, [pair_src], R, after=[own])
    z_side = source_call(pts_z)
    sums, part = [], [pair]
    for c in range(2):
        if c == 1:
            pieces, part = together(pieces, part)
            alike = stack_call(pieces)
            side = lax.ppermute(alike, "leaf", beside)
            part = [alike]
        part = near_call(
            "near_next_away", msgs, targets, away, [("next", z_side, w_z[c : c + 1])],
            SIZES[c], c * SIZES[0], [own, pair], part[:1],
        )
        kept, given = part[::2], part[1::2]
        sums.append((kept, [from_help(value, 0, 1) for value in given]))
    parts = []
    for c in range(2):
        kept, mates = sums[c]
        both = add_call(*zip(kept, mates))
        parts.append([to_help(value, dx + 1) for dx, value in enumerate(both)])
    sources = [pair_src, ("next", z_side, w_z)]
    home = near_call("near_home", msgs, targets, home, sources, R, 0, [own], both[:1])
    swapped = from_help(points_call(alike, side), 0, 1)
    v_own = far_call(groups, far_nodes, skel_node, transfer, alike, side, swapped, home[:1])
    v_pair = stack_call([v_own, from_help(v_own, 0, 1)])
    values = [v_pair] + [from_help(v_pair, dx, 0) for dx in range(1, xs)]
    mate = [from_help(value, 0, 1) for value in home[2:]]
    mine = add_call(*[[home[c], *parts[c]] for c in range(2)])
    return final_call(xs, interp, mine, mate, values)


def solution(mesh):
    placed = (
        P(None, ("leaf", "help")),
        P(None, ("leaf", "help")),
        P(("leaf", "help"), None, None),
        P(),
        P("leaf", "help"),
        P(("leaf", "help"), None),
        P("leaf", None),
        P(),
        P(),
    )
    return jax.shard_map(
        shards, mesh=mesh, in_specs=placed, out_specs=P(None, ("leaf", "help")), check_vma=False
    )
```
